32 devices in a mesh: dp: 4 (over y, core), fsdp: 8 (over z, x).
Axes of the slice: x: 2, y: 2, z: 4, core: 2. Of those that a mesh axis runs over, the one named last changes fastest.
Arguments:
- tokens: bfloat16 [131072, 512], P(('dp', 'fsdp')), may hold values from -6 to 6
- cotangent: bfloat16 [131072, 512], P(('dp', 'fsdp')), may hold values from -6 to 6
- w_qkv: bfloat16 [512, 1536], P('fsdp', 'dp'), may hold values from -0.03125 to 0.03125
- w_out: bfloat16 [512, 512], P('fsdp', 'dp'), may hold values from -0.5 to 0.5
- w_in: bfloat16 [512, 2048], P('fsdp', 'dp'), may hold values from -0.25 to 0.25
- w_back: bfloat16 [2048, 512], P('fsdp', 'dp'), may hold values from -0.125 to 0.125
- vec_params: bfloat16 [8, 512], P('dp', 'fsdp'), may hold values from -7.2 to 24
- b_in: bfloat16 [2048], P(('dp', 'fsdp')), may hold values from -3 to 3
- item_lengths: int32 [32, 4], P(('dp', 'fsdp')), may hold values from 256 to 4096, as said below
- bucket_counts: int32 [32, 3], P(('dp', 'fsdp')), may hold values from 0 to 1, as said below
Outputs:
- layer_out: bfloat16 [131072, 512], P(('dp', 'fsdp'))
- tokens_grad: bfloat16 [131072, 512], P(('dp', 'fsdp'))
- grad_qkv: float32 [512, 1536], P('fsdp', 'dp')
- grad_out: float32 [512, 512], P('fsdp', 'dp')
- grad_in: float32 [512, 2048], P('fsdp', 'dp')
- grad_back: float32 [2048, 512], P('fsdp', 'dp')
- grad_vec: float32 [8, 512], P('dp', 'fsdp')
- grad_bias_in: float32 [2048], P(('dp', 'fsdp'))
The draws below stay inside these ranges and needn't reach their ends.
Inputs may be any that keep to these rules, and one draw needn't show every extreme that they name: `item_lengths`: slots of one microbatch hold that microbatch's item length; an item of a 4-slot microbatch has more than 2048 rows, of a 2-slot one more than 1024, of a 1-slot one 1024 // 4 or more, and none more than its microbatch's rows. `bucket_counts`: each row (c0, c1, c2) has 4 c0 + 2 c1 + c2 = 4 and c0 >= 1; microbatches lie in that order.
All inputs are finite; a program needn't handle non-finite values.
Results may differ from the reference program's by a relative error of at most 0.012.
Values may be sent and summed in bfloat16 or wider, within the bound.
A program may use at most 384 MiB of HBM per device.

```python
import jax
import jax.numpy as jnp
from jax import lax

D = 512
HEADS = 8
FF = 2048
BAND = 30
SLOT_ROWS = 1024
BLOCK = 512
SLOTS = 4
ROWS_DEV = 4096
GROUPS = 32
TOKENS = 131072


def shared_counts(key):
    key = jax.random.fold_in(key, 11)
    key_four, key_two = jax.random.split(key)
    four_count = jax.random.randint(key_four, (GROUPS,), 1, SLOTS // 4 + 1, dtype=jnp.int32)
    rest_slots = SLOTS - 4 * four_count
    two_count = jax.random.randint(key_two, (GROUPS,), 0, 1 << 20, dtype=jnp.int32) % (rest_slots // 2 + 1)
    group_ids = jnp.arange(GROUPS, dtype=jnp.int32)
    last_group = group_ids == GROUPS - 1
    four_count = jnp.where(last_group, 1, four_count)
    two_count = jnp.where(last_group, 0, two_count)
    one_count = SLOTS - 4 * four_count - 2 * two_count
    return jnp.stack([four_count, two_count, one_count], axis=1).astype(jnp.int32)


def draw_bucket_counts(key, part):
    return shared_counts(key)


def draw_item_lengths(key, part):
    counts = shared_counts(key)
    key = jax.random.fold_in(key, 23)
    slot_ids = jnp.arange(SLOTS, dtype=jnp.int32)[None, :]
    four_end = 4 * counts[:, 0:1]
    two_end = four_end + 2 * counts[:, 1:2]
    start_slot = jnp.where(slot_ids < four_end, slot_ids // 4 * 4, jnp.where(slot_ids < two_end, four_end + (slot_ids - four_end) // 2 * 2, slot_ids))
    span_slots = jnp.where(slot_ids < four_end, 4, jnp.where(slot_ids < two_end, 2, 1))
    raw_draw = jax.random.randint(key, (GROUPS, SLOTS), 0, 1 << 20, dtype=jnp.int32)
    item_draw = jnp.take_along_axis(raw_draw, start_slot, axis=1)
    low_end = jnp.where(span_slots == 1, SLOT_ROWS // 4, span_slots // 2 * SLOT_ROWS + 1)
    choices_count = span_slots * SLOT_ROWS - low_end + 1
    lengths = low_end + item_draw % choices_count
    group_ids = jnp.arange(GROUPS, dtype=jnp.int32)[:, None]
    lengths = jnp.where((group_ids == 0) & (start_slot == 0), 4 * SLOT_ROWS, lengths)
    return lengths.astype(jnp.int32)


def draw_vec_params(key, part):
    key = jax.random.fold_in(key, 37)
    unit_draw = jax.random.uniform(key, (8, D), jnp.float32)
    normal_draw = jax.random.normal(jax.random.fold_in(key, 1), (8, D), jnp.float32)
    lower = jnp.array([5.6, 0.0, 0.7, 0.0, 0.0, 1.0, 8.0, 2.0], dtype=jnp.float32)[:, None]
    upper = jnp.array([10.4, 0.0, 1.3, 0.0, 0.0, 3.0, 24.0, 6.0], dtype=jnp.float32)[:, None]
    spread = jnp.array([0.0, 2.4, 0.0, 0.3, 0.3, 0.0, 0.0, 0.0], dtype=jnp.float32)[:, None]
    return (lower + (upper - lower) * unit_draw + spread * jnp.clip(normal_draw, -3.0, 3.0)).astype(jnp.bfloat16)


def steps_of(key, dims, cuts, least, largest):
    def one(dim, shards_of):
        draws = jax.random.uniform(jax.random.fold_in(jax.random.fold_in(key, 6), dim), (shards_of,), jnp.float32, least / len(cuts), largest / len(cuts))
        return jnp.repeat(jnp.exp(draws), dims[dim] // shards_of).reshape((-1,) + (1,) * (len(dims) - dim - 1))

    level = one(*cuts[0])
    for cut in cuts[1:]:
        level = level * one(*cut)
    return level


def centred(key, extent, scale, most, pieces=(), held_as=jnp.bfloat16):
    level = steps_of(key, extent, pieces, -0.22, 0.18) if pieces else 1.0
    entries = jax.random.normal(key, extent, jnp.float32) * scale * level
    return jnp.minimum(jnp.maximum(entries, -most), most).astype(held_as)


def setup_inputs(seed: int = 0) -> dict:
    streams_of = jax.random.split(jax.random.key(seed), 11)
    tokens = centred(streams_of[0], (TOKENS, D), 1.0, 6.0, ((0, 32),))
    cotangent = centred(streams_of[1], (TOKENS, D), 1.0, 6.0, ((0, 32),))
    w_qkv = centred(streams_of[2], (D, 3 * D), (64 * D) ** -0.5, 0.03125, ((0, 8), (1, 4)))
    w_out = centred(streams_of[3], (D, D), (D // 4) ** -0.5, 0.5, ((0, 8), (1, 4)))
    w_in = centred(streams_of[4], (D, FF), D ** -0.5, 0.25, ((0, 8), (1, 4)))
    w_back = centred(streams_of[5], (FF, D), FF ** -0.5, 0.125, ((0, 8), (1, 4)))
    vec_params = draw_vec_params(jax.random.fold_in(streams_of[10], 71), 0)
    b_in = centred(streams_of[7], (FF,), 0.5, 3.0, ((0, 32),))
    item_lengths = draw_item_lengths(jax.random.fold_in(streams_of[10], 71), 0)
    bucket_counts = draw_bucket_counts(jax.random.fold_in(streams_of[10], 71), 0)
    return dict(tokens=tokens, cotangent=cotangent, w_qkv=w_qkv, w_out=w_out, w_in=w_in, w_back=w_back, vec_params=vec_params, b_in=b_in, item_lengths=item_lengths, bucket_counts=bucket_counts)


@jax.custom_vjp
def low(v):
    return lax.optimization_barrier(v.astype(jnp.bfloat16)).astype(jnp.float32)

@jax.custom_vjp
def low_back(v):
    return v

def low_keep(v):
    return (low(v), None)

def low_pass(kept, grad):
    return (grad,)

def back_keep(v):
    return (v, None)

def back_low(kept, grad):
    return (low(grad),)
low.defvjp(low_keep, low_pass)
low_back.defvjp(back_keep, back_low)
norm_eps = 1e-05
exact = lax.Precision.HIGHEST

def layout(counts, lengths, slot_count, slot_rows):
    slot_ids = jnp.arange(slot_count, dtype=jnp.int32)
    four_end = 4 * counts[0]
    two_end = four_end + 2 * counts[1]
    start_slot = jnp.where(slot_ids < four_end, slot_ids // 4 * 4, jnp.where(slot_ids < two_end, four_end + (slot_ids - four_end) // 2 * 2, slot_ids))
    item_rows = jnp.broadcast_to(start_slot[:, None], (slot_count, slot_rows)).reshape(-1)
    length_rows = jnp.broadcast_to(lengths[:, None], (slot_count, slot_rows)).reshape(-1)
    row_ids = jnp.arange(slot_count * slot_rows, dtype=jnp.int32)
    place_rows = (row_ids // slot_rows - item_rows) * slot_rows + row_ids % slot_rows
    valid_rows = (place_rows < length_rows).astype(jnp.float32)
    same_item = (start_slot[:, None] == start_slot[None, :]).astype(jnp.float32)
    inv_length = 1.0 / lengths.astype(jnp.float32)
    return (item_rows, valid_rows, same_item, inv_length)

def band_mask(item_pad, valid_pad, item_rows, block_id):
    first_row = block_id * BLOCK
    query_row = first_row + jnp.arange(BLOCK, dtype=jnp.int32)
    key_row = first_row - BAND + jnp.arange(BLOCK + 2 * BAND, dtype=jnp.int32)
    item_query = lax.dynamic_slice_in_dim(item_rows, first_row, BLOCK, 0)
    item_key = lax.dynamic_slice_in_dim(item_pad, first_row, BLOCK + 2 * BAND, 0)
    valid_key = lax.dynamic_slice_in_dim(valid_pad, first_row, BLOCK + 2 * BAND, 0)
    offset = query_row[:, None] - key_row[None, :]
    return (jnp.abs(offset) <= BAND) & (item_query[:, None] == item_key[None, :]) & ((valid_key[None, :] > 0.5) | (offset == 0))

def block_inputs(query_all, key_pad, value_pad, block_id):
    first_row = block_id * BLOCK
    model_width = query_all.shape[1]
    head_size = model_width // HEADS
    block_query = lax.dynamic_slice_in_dim(query_all, first_row, BLOCK, 0).reshape(BLOCK, HEADS, head_size)
    block_keys = lax.dynamic_slice_in_dim(key_pad, first_row, BLOCK + 2 * BAND, 0).reshape(BLOCK + 2 * BAND, HEADS, head_size)
    block_values = lax.dynamic_slice_in_dim(value_pad, first_row, BLOCK + 2 * BAND, 0).reshape(BLOCK + 2 * BAND, HEADS, head_size)
    return (block_query, block_keys, block_values)

def normed(values_in, gain, shift):
    row_mean = lax.optimization_barrier(jnp.mean(values_in, axis=-1, keepdims=True))
    centered = values_in - row_mean
    inv_std = lax.rsqrt(lax.optimization_barrier(jnp.mean(centered * centered, axis=-1, keepdims=True)) + norm_eps)
    return centered * inv_std * gain + shift

def far_field(query_in, keys_in, values_in, valid_rows, same_item, inv_length):
    slot_count = same_item.shape[0]
    row_count, model_width = query_in.shape
    shape_four = (slot_count, row_count // slot_count, HEADS, model_width // HEADS)
    query_four = query_in.reshape(shape_four)
    keys_four = keys_in.reshape(shape_four)
    values_four = values_in.reshape(shape_four)
    valid_four = valid_rows.reshape(slot_count, row_count // slot_count, 1, 1)
    lift_query = jax.nn.elu(query_four) + 1.0
    lift_keys = (jax.nn.elu(keys_four) + 1.0) * valid_four
    bent_query = jnp.tanh(query_four)
    bent_keys = jnp.tanh(keys_four) * valid_four
    state_one = jnp.einsum('srhd,srhe->shde', lift_keys, values_four, precision=exact)
    state_one = jnp.einsum('st,thde->shde', same_item, state_one, precision=exact)
    total_one = jnp.einsum('st,thd->shd', same_item, lax.optimization_barrier(jnp.sum(lift_keys, axis=1)), precision=exact)
    numer = jnp.einsum('srhd,shde->srhe', lift_query, state_one, precision=exact)
    denom = jnp.einsum('srhd,shd->srh', lift_query, total_one, precision=exact)
    state_two = jnp.einsum('srhd,srhe->shde', bent_keys, values_four, precision=exact)
    state_two = jnp.einsum('st,thde->shde', same_item, state_two, precision=exact)
    far_two = jnp.einsum('srhd,shde->srhe', bent_query, state_two, precision=exact) * inv_length.reshape(slot_count, 1, 1, 1)
    return ((numer / denom[..., None]).reshape(row_count, model_width), far_two.reshape(row_count, model_width))

def near_field(query_all, key_all, value_all, item_rows, valid_rows):
    row_count, model_width = query_all.shape
    score_scale = (model_width // HEADS) ** (-0.5)
    key_pad = jnp.pad(key_all, ((BAND, BAND), (0, 0)))
    value_pad = jnp.pad(value_all, ((BAND, BAND), (0, 0)))
    item_pad = jnp.pad(item_rows, (BAND, BAND), constant_values=-1)
    valid_pad = jnp.pad(valid_rows, (BAND, BAND))

    def one_block(block_id):
        mask_now = band_mask(item_pad, valid_pad, item_rows, block_id)
        block_query, block_keys, block_values = block_inputs(query_all, key_pad, value_pad, block_id)
        scores = low_back(jnp.einsum('qhd,khd->hqk', block_query, block_keys, precision=exact) * score_scale)
        scores = jnp.where(mask_now[None], scores, -1e+30)
        exp_scores = jnp.exp(scores - lax.optimization_barrier(jnp.max(scores, axis=-1, keepdims=True)))
        probs = low(exp_scores / lax.optimization_barrier(jnp.sum(exp_scores, axis=-1, keepdims=True)))
        return jnp.einsum('hqk,khd->qhd', probs, block_values, precision=exact).reshape(BLOCK, model_width)
    outputs = lax.map(jax.checkpoint(one_block), jnp.arange(row_count // BLOCK, dtype=jnp.int32))
    return outputs.reshape(row_count, model_width)

def matmul(left_side, right_side):
    return jnp.dot(left_side, right_side, precision=exact, preferred_element_type=jnp.float32)

def forward(tokens_in, params, meta):
    qkv_w, out_w, in_w, back_w, vecs, in_bias = params
    item_rows, valid_rows, same_item, inv_length = meta
    model_width = tokens_in.shape[1]
    h_one = low(normed(tokens_in, vecs[0], vecs[1]))
    qkv = low(low_back(matmul(h_one, qkv_w)))
    query_all = qkv[:, :model_width]
    key_all = qkv[:, model_width:2 * model_width]
    value_all = qkv[:, 2 * model_width:]
    near_out = low_back(near_field(query_all, key_all, value_all, item_rows, valid_rows))
    far_a, far_b = far_field(query_all, key_all, value_all, valid_rows, same_item, inv_length)
    mixed = low(vecs[5] * near_out + vecs[6] * far_a + vecs[7] * far_b)
    resid = tokens_in + low_back(matmul(mixed, out_w))
    h_two = low(normed(resid, vecs[2], vecs[3]))
    pre_act = low_back(matmul(h_two, in_w) + in_bias)
    act = low(jax.nn.gelu(pre_act))
    ffn_out = low_back(matmul(act, back_w) + vecs[4])
    return valid_rows[:, None] * (resid + ffn_out)

def reference(tokens, cotangent, w_qkv, w_out, w_in, w_back, vec_params, b_in, item_lengths, bucket_counts):
    weights = tuple((weight.astype(jnp.float32) for weight in (w_qkv, w_out, w_in, w_back, vec_params, b_in)))
    rows_in = tokens.astype(jnp.float32).reshape(GROUPS, ROWS_DEV, D)
    seeds_in = cotangent.astype(jnp.float32).reshape(GROUPS, ROWS_DEV, D)

    def one_group(totals, inputs):
        group_rows, group_seed, lengths, counts = inputs
        meta = layout(counts, lengths, SLOTS, SLOT_ROWS)

        def run(tokens_in, *params):
            return forward(tokens_in, params, meta)
        result, pull = jax.vjp(run, group_rows, *weights)
        grads = pull(group_seed)
        totals = tuple((total + grad for total, grad in zip(totals, grads[1:])))
        return (totals, (result.astype(jnp.bfloat16), grads[0].astype(jnp.bfloat16)))
    zeros = tuple((jnp.zeros_like(weight) for weight in weights))
    totals, (outputs, input_grads) = lax.scan(one_group, zeros, (rows_in, seeds_in, item_lengths, bucket_counts))
    return (outputs.reshape(TOKENS, D), input_grads.reshape(TOKENS, D), totals[0], totals[1], totals[2], totals[3], totals[4], totals[5])
```

```python
import functools
import math

import jax
import jax.numpy as jnp
import numpy as np
from jax import lax
from jax.experimental import pallas as pl
from jax.experimental.pallas import tpu as pltpu
from jax.sharding import PartitionSpec as P

HEADS = 8
BAND = 30
QB = 64
HALO = 32
KW = QB + 2 * HALO
GW = 256

norm_eps = 1e-05
f32 = jnp.float32
bf16 = jnp.bfloat16
exact = lax.Precision.HIGHEST
VMEM_LIMIT = 60 * 1024 * 1024


def nn(a, b):
    return lax.dot_general(a, b, (((1,), (0,)), ((), ())), preferred_element_type=f32)


def nt(a, b):
    return lax.dot_general(a, b, (((1,), (1,)), ((), ())), preferred_element_type=f32)


def tn(a, b):
    return lax.dot_general(a, b, (((0,), (0,)), ((), ())), preferred_element_type=f32)


def nt_exact(a, b):
    return lax.dot_general(
        a, b, (((1,), (1,)), ((), ())), preferred_element_type=f32, precision=exact
    )


def lift(t):
    return jnp.where(t > 0, t + 1.0, jnp.exp(jnp.minimum(t, 0.0)))


def moments(x):
    mean = jnp.mean(x, axis=-1, keepdims=True)
    cen = x - mean
    inv = lax.rsqrt(jnp.mean(cen * cen, axis=-1, keepdims=True) + norm_eps)
    return cen * inv, inv


def fold8(x):
    return jnp.sum(x.reshape(x.shape[0] // 8, 8, x.shape[1]), axis=0)


def row_valid(step, rows, width, length):
    ids = step * rows + lax.broadcasted_iota(jnp.int32, (rows, width), 0)
    return ids < length


def same_head(head):
    r = lax.broadcasted_iota(jnp.int32, (GW, GW), 0) // head
    c = lax.broadcasted_iota(jnp.int32, (GW, GW), 1) // head
    return r == c


def spread_rows(x, mask_low):
    return jnp.concatenate([x] * (GW // QB), axis=0) * mask_low


def pick_heads(x, head):
    lane = lax.broadcasted_iota(jnp.int32, (QB, GW), 1) // head
    out = x[:QB]
    for h in range(1, GW // QB):
        out = jnp.where(lane == h, x[h * QB : (h + 1) * QB], out)
    return out


def qkv_kernel(len_ref, tok_ref, vec_ref, w_ref, qkv_ref, m1_ref, m2_ref, c_ref, st_ref, t_ref):
    step = pl.program_id(0)
    rows, width = tok_ref.shape
    groups = width // GW
    head = width // HEADS
    length = len_ref[0, 0]

    @pl.when(step == 0)
    def _():
        st_ref[...] = jnp.zeros_like(st_ref)
        t_ref[...] = jnp.zeros_like(t_ref)

    z, _ = moments(tok_ref[...].astype(f32))
    h = (z * vec_ref[0:1] + vec_ref[1:2]).astype(bf16)
    qkv_ref[:, :width] = nn(h, w_ref[:, :width]).astype(bf16)
    valid = row_valid(step, rows, GW, length)
    for g in range(groups):
        kc = slice(width + g * GW, width + (g + 1) * GW)
        vc = slice(2 * width + g * GW, 2 * width + (g + 1) * GW)
        k = nn(h, w_ref[:, kc]).astype(bf16)
        v = nn(h, w_ref[:, vc]).astype(bf16)
        qkv_ref[:, kc] = k
        qkv_ref[:, vc] = v
        kw = k.astype(f32)
        phi = jnp.where(valid, lift(kw), 0.0)
        bent = jnp.where(valid, jnp.tanh(kw), 0.0)
        both = jnp.concatenate([phi.astype(bf16), bent.astype(bf16)], axis=1)
        st_ref[g] += tn(v, both)
        t_ref[g] += fold8(phi)

    @pl.when(step == pl.num_programs(0) - 1)
    def _():
        mask = same_head(head).astype(f32)
        inv_len = 1.0 / length.astype(f32)
        ones = jnp.ones((8, GW), f32)
        for g in range(groups):
            tb = jnp.sum(t_ref[g], axis=0, keepdims=True) * mask
            s1 = st_ref[g][:, :GW] * mask
            s2 = st_ref[g][:, GW:] * mask
            c_col = jnp.sum(s1, axis=1, keepdims=True) / jnp.sum(tb, axis=1, keepdims=True)
            c_row = nt_exact(ones, s1) / nt_exact(ones, tb)
            m1_ref[g, :GW] = (s1 - c_col * tb).astype(bf16)
            m1_ref[g, GW:] = tb.astype(bf16)
            m2_ref[g] = (s2 * inv_len).astype(bf16)
            c_ref[g] = c_row


def first_pass(length, tokens, vecs, w_qkv, tile):
    rows, width = tokens.shape
    groups = width // GW
    const = lambda *shape: pl.BlockSpec(shape, lambda i: (0,) * len(shape))
    return pl.pallas_call(
        qkv_kernel,
        grid=(rows // tile,),
        in_specs=[
            pl.BlockSpec(memory_space=pltpu.SMEM),
            pl.BlockSpec((tile, width), lambda i: (i, 0)),
            const(8, width),
            const(width, 3 * width),
        ],
        out_specs=[
            pl.BlockSpec((tile, 3 * width), lambda i: (i, 0)),
            const(groups, 2 * GW, GW),
            const(groups, GW, GW),
            const(groups, 8, GW),
        ],
        out_shape=[
            jax.ShapeDtypeStruct((rows, 3 * width), bf16),
            jax.ShapeDtypeStruct((groups, 2 * GW, GW), bf16),
            jax.ShapeDtypeStruct((groups, GW, GW), bf16),
            jax.ShapeDtypeStruct((groups, 8, GW), f32),
        ],
        scratch_shapes=[
            pltpu.VMEM((groups, GW, 2 * GW), f32),
            pltpu.VMEM((groups, 8, GW), f32),
        ],
        compiler_params=pltpu.CompilerParams(vmem_limit_bytes=VMEM_LIMIT),
        cost_estimate=pl.CostEstimate(
            flops=2 * rows * width * 4 * width, bytes_accessed=rows * width * 8, transcendentals=0
        ),
        name="first_pass",
    )(length, tokens, vecs, w_qkv)


def mix_kernel(
    len_ref,
    q_ref,
    k_lo,
    k_ref,
    k_hi,
    v_lo,
    v_ref,
    v_hi,
    m1_ref,
    m2_ref,
    c_ref,
    band_ref,
    hm_ref,
    near_ref,
    fa_ref,
    fb_ref,
    rn_ref,
    p_ref,
    kk,
    vv,
):
    step = pl.program_id(0)
    rows, width = q_ref.shape
    groups = width // GW
    head = width // HEADS
    scale = head ** (-0.5)
    length = len_ref[0, 0]
    kk[:HALO] = k_lo[...]
    kk[HALO : HALO + rows] = k_ref[...]
    kk[HALO + rows :] = k_hi[...]
    vv[:HALO] = v_lo[...]
    vv[HALO : HALO + rows] = v_ref[...]
    vv[HALO + rows :] = v_hi[...]
    hm = hm_ref[...]
    for b in range(rows // QB):
        base = step * rows + b * QB - HALO
        key = base + lax.broadcasted_iota(jnp.int32, (KW, GW), 0)
        bias = jnp.where((key >= 0) & (key < length), band_ref[...], -1e30)
        for g in range(groups):
            cols = slice(g * GW, (g + 1) * GW)
            qs = spread_rows(q_ref[b * QB : (b + 1) * QB, cols] * scale, hm)
            s = nt(kk[b * QB : b * QB + KW, cols], qs) + bias
            e = jnp.exp(s - jnp.max(s, axis=0, keepdims=True))
            p = (e * (1.0 / jnp.sum(e, axis=0, keepdims=True))).astype(bf16)
            p_ref[b, :, cols] = p
            o = tn(p, vv[b * QB : b * QB + KW, cols])
            near_ref[b * QB : (b + 1) * QB, cols] = pick_heads(o, head).astype(bf16)
    for g in range(groups):
        cols = slice(g * GW, (g + 1) * GW)
        q = q_ref[:, cols].astype(f32)
        both = nt(lift(q).astype(bf16), m1_ref[g])
        rn = 1.0 / both[:, GW:]
        rn_ref[:, cols] = rn.astype(bf16)
        fa_ref[:, cols] = (both[:, :GW] * rn).astype(bf16)
        fb_ref[:, cols] = nt(jnp.tanh(q).astype(bf16), m2_ref[g]).astype(bf16)


def halo_specs(tile, width, col, rows):
    per = tile // HALO
    last = rows // HALO - 1
    return [
        pl.BlockSpec((HALO, width), lambda i: (jnp.maximum(i * per - 1, 0), col)),
        pl.BlockSpec((tile, width), lambda i: (i, col)),
        pl.BlockSpec((HALO, width), lambda i: (jnp.minimum((i + 1) * per, last), col)),
    ]


def band_table(head):
    key = np.arange(KW)[:, None] - HALO
    query = np.arange(GW)[None, :] % QB
    return np.where(np.abs(key - query) <= BAND, 0.0, -1e30).astype(np.float32)


def head_table(head):
    r = np.arange(GW)[:, None] // QB
    c = np.arange(GW)[None, :] // head
    return (r == c).astype(np.float32)


def second_pass(length, qkv, m1, m2, c, tile):
    rows = qkv.shape[0]
    width = qkv.shape[1] // 3
    groups = width // GW
    const = lambda *shape: pl.BlockSpec(shape, lambda i: (0,) * len(shape))
    block = pl.BlockSpec((tile, width), lambda i: (i, 0))
    head = width // HEADS
    return pl.pallas_call(
        mix_kernel,
        grid=(rows // tile,),
        in_specs=[
            pl.BlockSpec(memory_space=pltpu.SMEM),
            block,
            *halo_specs(tile, width, 1, rows),
            *halo_specs(tile, width, 2, rows),
            const(groups, 2 * GW, GW),
            const(groups, GW, GW),
            const(groups, 8, GW),
            const(KW, GW),
            const(GW, GW),
        ],
        out_specs=[
            block,
            block,
            block,
            block,
            pl.BlockSpec((tile // QB, KW, width), lambda i: (i, 0, 0)),
        ],
        out_shape=[jax.ShapeDtypeStruct((rows, width), bf16)] * 4
        + [jax.ShapeDtypeStruct((rows // QB, KW, width), bf16)],
        scratch_shapes=[pltpu.VMEM((tile + 2 * HALO, width), bf16)] * 2,
        compiler_params=pltpu.CompilerParams(vmem_limit_bytes=VMEM_LIMIT),
        cost_estimate=pl.CostEstimate(
            flops=2 * rows * width * 4 * width, bytes_accessed=rows * width * 18, transcendentals=0
        ),
        name="second_pass",
    )(
        length,
        qkv,
        qkv,
        qkv,
        qkv,
        qkv,
        qkv,
        qkv,
        m1,
        m2,
        c,
        jnp.asarray(band_table(head)),
        jnp.asarray(head_table(head), bf16),
    )


def ffn_kernel(
    chunk,
    len_ref,
    tok_ref,
    cot_ref,
    near_ref,
    fa_ref,
    fb_ref,
    rn_ref,
    q_ref,
    c_ref,
    vec_ref,
    bin_ref,
    wout_ref,
    win_ref,
    wback_ref,
    out_ref,
    datt_ref,
    dmix_ref,
    dn_ref,
    gin_ref,
    gback_ref,
    gout_ref,
    gvec_ref,
    gbias_ref,
    m3_ref,
    m4_ref,
    dt_ref,
    a_in,
    a_back,
    a_out,
    a_st,
    a_bent,
):
    step = pl.program_id(0)
    rows, width = tok_ref.shape
    hidden = win_ref.shape[1]
    groups = width // GW
    head = width // HEADS
    length = len_ref[0, 0]

    @pl.when(step == 0)
    def _():
        a_in[...] = jnp.zeros_like(a_in)
        a_back[...] = jnp.zeros_like(a_back)
        a_out[...] = jnp.zeros_like(a_out)
        a_st[...] = jnp.zeros_like(a_st)
        a_bent[...] = jnp.zeros_like(a_bent)
        gvec_ref[...] = jnp.zeros_like(gvec_ref)
        gbias_ref[...] = jnp.zeros_like(gbias_ref)

    c_row = jnp.concatenate([c_ref[g, 0:1] for g in range(groups)], axis=1)
    near = near_ref[...].astype(f32)
    fac = fa_ref[...].astype(f32)
    far_b = fb_ref[...].astype(f32)
    mixed = (
        vec_ref[5:6] * near + vec_ref[6:7] * (fac + c_row) + vec_ref[7:8] * far_b
    ).astype(bf16)
    resid = tok_ref[...].astype(f32) + nn(mixed, wout_ref[...])
    z2, r2 = moments(resid)
    h2 = (z2 * vec_ref[2:3] + vec_ref[3:4]).astype(bf16)
    valid = row_valid(step, rows, width, length)
    seed = jnp.where(valid, cot_ref[...].astype(f32), 0.0)
    d_ffn = seed.astype(bf16)
    s0 = math.sqrt(2.0 / math.pi)
    s1 = s0 * 0.044715
    ffn = jnp.zeros((rows, width), f32)
    dh2 = jnp.zeros((rows, width), f32)
    for lo in range(0, hidden, chunk):
        cols = slice(lo, lo + chunk)
        x = nn(h2, win_ref[:, cols]) + bin_ref[0:1, cols]
        x2 = x * x
        t = jnp.tanh(x * (s0 + s1 * x2))
        half = 0.5 + 0.5 * t
        act = x * half
        slope = half + (act - act * half) * (2 * s0 + 6 * s1 * x2)
        act = act.astype(bf16)
        ffn += nn(act, wback_ref[cols, :])
        a_back[:, cols] += tn(d_ffn, act)
        d_pre = slope * nt(d_ffn, wback_ref[cols, :])
        gbias_ref[:, cols] += fold8(d_pre)
        d_pre = d_pre.astype(bf16)
        a_in[:, cols] += tn(h2, d_pre)
        dh2 += nt(d_pre, win_ref[:, cols])
    out_ref[...] = jnp.where(valid, resid + ffn + vec_ref[4:5], 0.0).astype(bf16)
    gvec_ref[2] += fold8(dh2 * z2)
    gvec_ref[3] += fold8(dh2)
    gvec_ref[4] += fold8(seed)
    dz = dh2 * vec_ref[2:3]
    d_resid = seed + r2 * (
        dz
        - jnp.mean(dz, axis=-1, keepdims=True)
        - z2 * jnp.mean(dz * z2, axis=-1, keepdims=True)
    )
    d_attn = d_resid.astype(bf16)
    datt_ref[...] = d_attn
    a_out[...] += tn(mixed, d_attn)
    d_mix = nt(d_attn, wout_ref[...])
    dmix_ref[...] = d_mix.astype(bf16)
    gvec_ref[5] += fold8(d_mix * near)
    gvec_ref[6] += fold8(d_mix * fac)
    gvec_ref[7] += fold8(d_mix * far_b)
    gvec_ref[0] += fold8(d_mix)
    d_num = (vec_ref[6:7] * d_mix * rn_ref[...].astype(f32)).astype(bf16)
    dn_ref[...] = d_num
    d_den = (d_num.astype(f32) * fac).astype(bf16)
    d_far = (vec_ref[7:8] * d_mix).astype(bf16)
    for g in range(groups):
        cols = slice(g * GW, (g + 1) * GW)
        q = q_ref[:, cols].astype(f32)
        a_st[g] += tn(lift(q).astype(bf16), jnp.concatenate([d_num[:, cols], d_den[:, cols]], axis=1))
        a_bent[g] += tn(jnp.tanh(q).astype(bf16), d_far[:, cols])

    @pl.when(step == pl.num_programs(0) - 1)
    def _():
        mask = same_head(head).astype(f32)
        inv_len = 1.0 / length.astype(f32)
        ones = jnp.ones((8, GW), f32)
        for g in range(groups):
            m3_ref[g] = (a_st[g][:, :GW] * mask).astype(bf16)
            m4_ref[g] = (a_bent[g] * mask * inv_len).astype(bf16)
            dt_ref[g] = -nt_exact(ones, a_st[g][:, GW:] * mask)
        gin_ref[...] = a_in[...].astype(gin_ref.dtype)
        gback_ref[...] = a_back[...].astype(gback_ref.dtype)
        gout_ref[...] = a_out[...].astype(gout_ref.dtype)
        gvec_ref[6] += gvec_ref[0] * c_row


def third_pass(length, tokens, cot, near, fa, fb, rn, qkv, c, vecs, b_in, w_out, w_in, w_back, tile, chunk):
    rows, width = tokens.shape
    hidden = w_in.shape[1]
    groups = width // GW
    const = lambda *shape: pl.BlockSpec(shape, lambda i: (0,) * len(shape))
    block = pl.BlockSpec((tile, width), lambda i: (i, 0))
    sds = jax.ShapeDtypeStruct
    return pl.pallas_call(
        functools.partial(ffn_kernel, chunk),
        grid=(rows // tile,),
        in_specs=[pl.BlockSpec(memory_space=pltpu.SMEM)]
        + [block] * 7
        + [
            const(groups, 8, GW),
            const(8, width),
            const(1, hidden),
            const(width, width),
            const(width, hidden),
            const(hidden, width),
        ],
        out_specs=[block] * 4
        + [
            const(width, hidden),
            const(width, hidden),
            const(width, width),
            const(8, 8, width),
            const(8, hidden),
            const(groups, GW, GW),
            const(groups, GW, GW),
            const(groups, 8, GW),
        ],
        out_shape=[sds((rows, width), bf16)] * 4
        + [
            sds((width, hidden), bf16),
            sds((width, hidden), bf16),
            sds((width, width), bf16),
            sds((8, 8, width), f32),
            sds((8, hidden), f32),
            sds((groups, GW, GW), bf16),
            sds((groups, GW, GW), bf16),
            sds((groups, 8, GW), f32),
        ],
        scratch_shapes=[
            pltpu.VMEM((width, hidden), f32),
            pltpu.VMEM((width, hidden), f32),
            pltpu.VMEM((width, width), f32),
            pltpu.VMEM((groups, GW, 2 * GW), f32),
            pltpu.VMEM((groups, GW, GW), f32),
        ],
        compiler_params=pltpu.CompilerParams(vmem_limit_bytes=VMEM_LIMIT),
        cost_estimate=pl.CostEstimate(
            flops=2 * rows * width * (6 * hidden + 4 * width),
            bytes_accessed=rows * width * 22,
            transcendentals=0,
        ),
        name="third_pass",
    )(length, tokens, cot, near, fa, fb, rn, qkv, c, vecs, b_in, w_out, w_in, w_back)


def back_kernel(
    len_ref,
    q_ref,
    k_lo,
    k_ref,
    k_hi,
    v_lo,
    v_ref,
    v_hi,
    p_ref,
    dmix_ref,
    qkv_ref,
    tok_ref,
    datt_ref,
    dn_ref,
    fa_ref,
    dmp_ref,
    m1_ref,
    m2_ref,
    m3_ref,
    m4_ref,
    dt_ref,
    c_ref,
    vec_ref,
    w_ref,
    hm_ref,
    dtok_ref,
    gqkv_ref,
    gvec_ref,
    kk,
    vv,
    dq_s,
    dk_s,
    dv_s,
    a_qkv,
):
    step = pl.program_id(0)
    steps = pl.num_programs(0) - 1
    rows, width = q_ref.shape
    groups = width // GW
    head = width // HEADS
    scale = head ** (-0.5)
    length = len_ref[0, 0]

    @pl.when(step == 0)
    def _():
        dk_s[: 2 * HALO] = jnp.zeros((2 * HALO, width), f32)
        dv_s[: 2 * HALO] = jnp.zeros((2 * HALO, width), f32)
        a_qkv[...] = jnp.zeros_like(a_qkv)
        gvec_ref[...] = jnp.zeros_like(gvec_ref)

    @pl.when(step < steps)
    def _():
        kk[:HALO] = k_lo[...]
        kk[HALO : HALO + rows] = k_ref[...]
        kk[HALO + rows :] = k_hi[...]
        vv[:HALO] = v_lo[...]
        vv[HALO : HALO + rows] = v_ref[...]
        vv[HALO + rows :] = v_hi[...]
        hm = hm_ref[...]
        slot = lax.rem(step, 2)
        for g in range(groups):
            cols = slice(g * GW, (g + 1) * GW)
            for b in range(rows // QB):
                here = slice(b * QB, (b + 1) * QB)
                window = slice(b * QB, b * QB + KW)
                qs = spread_rows(q_ref[here, cols] * scale, hm)
                d_near = (vec_ref[5:6, cols] * dmix_ref[here, cols].astype(f32)).astype(bf16)
                ds = spread_rows(d_near, hm)
                p = p_ref[b, :, cols]
                pw = p.astype(f32)
                t = pw * nt(vv[window, cols], ds)
                d_s = (t - pw * jnp.sum(t, axis=0, keepdims=True)).astype(bf16)
                dk = nn(d_s, qs)
                dv = nn(p, ds)
                dq_s[slot, here, cols] = pick_heads(tn(d_s, kk[window, cols]), head) * scale
                lo = pl.multiple_of(step * rows + b * QB, QB)
                dk_s[pl.ds(lo, QB), cols] += dk[:QB]
                dk_s[pl.ds(lo + QB, QB), cols] = dk[QB:]
                dv_s[pl.ds(lo, QB), cols] += dv[:QB]
                dv_s[pl.ds(lo + QB, QB), cols] = dv[QB:]

    @pl.when(step > 0)
    def _():
        slot = lax.rem(step + 1, 2)
        z1, r1 = moments(tok_ref[...].astype(f32))
        h1 = (z1 * vec_ref[0:1] + vec_ref[1:2]).astype(bf16)
        valid = row_valid(step - 1, rows, GW, length)
        lo = pl.multiple_of((step - 1) * rows + HALO, HALO)
        dqs, dks, dvs = [], [], []
        for g in range(groups):
            cols = slice(g * GW, (g + 1) * GW)
            q = qkv_ref[:, g * GW : (g + 1) * GW].astype(f32)
            k = qkv_ref[:, width + g * GW : width + (g + 1) * GW].astype(f32)
            v = qkv_ref[:, 2 * width + g * GW : 2 * width + (g + 1) * GW]
            d_num = dn_ref[:, cols]
            d_den = (d_num.astype(f32) * -fa_ref[:, cols].astype(f32)).astype(bf16)
            d_far = (vec_ref[7:8, cols] * dmp_ref[:, cols].astype(f32)).astype(bf16)
            bent_q = jnp.tanh(q)
            dq = (
                dq_s[slot, :, cols]
                + nn(jnp.concatenate([d_num, d_den], axis=1), m1_ref[g]) * jnp.minimum(lift(q), 1.0)
                + nn(d_far, m2_ref[g]) * (1.0 - bent_q * bent_q)
            )
            lift_k = lift(k)
            bent_k = jnp.tanh(k)
            v_cen = (v.astype(f32) - c_ref[g, 0:1]).astype(bf16)
            dk = (nt(v_cen, m3_ref[g]) + dt_ref[g, 0:1]) * jnp.minimum(lift_k, 1.0) + nt(
                v, m4_ref[g]
            ) * (1.0 - bent_k * bent_k)
            both = jnp.concatenate([lift_k.astype(bf16), bent_k.astype(bf16)], axis=1)
            dv = nn(both, jnp.concatenate([m3_ref[g], m4_ref[g]], axis=0))
            dqs.append(dq.astype(bf16))
            dks.append((dk_s[pl.ds(lo, rows), cols] + jnp.where(valid, dk, 0.0)).astype(bf16))
            dvs.append((dv_s[pl.ds(lo, rows), cols] + jnp.where(valid, dv, 0.0)).astype(bf16))
        d_qkv = jnp.concatenate(dqs + dks + dvs, axis=1)
        a_qkv[...] += tn(h1, d_qkv)
        dh1 = nt(d_qkv, w_ref[...])
        gvec_ref[0] += fold8(dh1 * z1)
        gvec_ref[1] += fold8(dh1)
        dz = dh1 * vec_ref[0:1]
        dtok_ref[...] = (
            datt_ref[...].astype(f32)
            + r1
            * (
                dz
                - jnp.mean(dz, axis=-1, keepdims=True)
                - z1 * jnp.mean(dz * z1, axis=-1, keepdims=True)
            )
        ).astype(bf16)

    @pl.when(step == steps)
    def _():
        gqkv_ref[...] = a_qkv[...].astype(gqkv_ref.dtype)


def fourth_pass(
    length, qkv, p, d_mix, tokens, d_attn, d_num, fa, m1, m2, m3, m4, dt, c, vecs, w_qkv, tile
):
    rows, width = tokens.shape
    groups = width // GW
    steps = rows // tile
    const = lambda *shape: pl.BlockSpec(shape, lambda i: (0,) * len(shape))
    now = lambda i: jnp.minimum(i, steps - 1)
    old = lambda i: jnp.maximum(i - 1, 0)
    per = tile // HALO
    last = rows // HALO - 1

    def halo(col):
        return [
            pl.BlockSpec((HALO, width), lambda i: (jnp.maximum(now(i) * per - 1, 0), col)),
            pl.BlockSpec((tile, width), lambda i: (now(i), col)),
            pl.BlockSpec((HALO, width), lambda i: (jnp.minimum((now(i) + 1) * per, last), col)),
        ]

    block = pl.BlockSpec((tile, width), lambda i: (now(i), 0))
    late = pl.BlockSpec((tile, width), lambda i: (old(i), 0))
    head = width // HEADS
    sds = jax.ShapeDtypeStruct
    return pl.pallas_call(
        back_kernel,
        grid=(steps + 1,),
        in_specs=[
            pl.BlockSpec(memory_space=pltpu.SMEM),
            block,
            *halo(1),
            *halo(2),
            pl.BlockSpec((tile // QB, KW, width), lambda i: (now(i), 0, 0)),
            block,
            pl.BlockSpec((tile, 3 * width), lambda i: (old(i), 0)),
            late,
            late,
            late,
            late,
            late,
            const(groups, 2 * GW, GW),
            const(groups, GW, GW),
            const(groups, GW, GW),
            const(groups, GW, GW),
            const(groups, 8, GW),
            const(groups, 8, GW),
            const(8, width),
            const(width, 3 * width),
            const(GW, GW),
        ],
        out_specs=[late, const(width, 3 * width), const(2, 8, width)],
        out_shape=[
            sds((rows, width), bf16),
            sds((width, 3 * width), bf16),
            sds((2, 8, width), f32),
        ],
        scratch_shapes=[
            pltpu.VMEM((tile + 2 * HALO, width), bf16),
            pltpu.VMEM((tile + 2 * HALO, width), bf16),
            pltpu.VMEM((2, tile, width), f32),
            pltpu.VMEM((rows + 2 * HALO, width), f32),
            pltpu.VMEM((rows + 2 * HALO, width), f32),
            pltpu.VMEM((width, 3 * width), f32),
        ],
        compiler_params=pltpu.CompilerParams(vmem_limit_bytes=VMEM_LIMIT),
        cost_estimate=pl.CostEstimate(
            flops=2 * rows * width * 14 * width, bytes_accessed=rows * width * 24, transcendentals=0
        ),
        name="fourth_pass",
    )(
        length,
        qkv,
        qkv,
        qkv,
        qkv,
        qkv,
        qkv,
        qkv,
        p,
        d_mix,
        qkv,
        tokens,
        d_attn,
        d_num,
        fa,
        d_mix,
        m1,
        m2,
        m3,
        m4,
        dt,
        c,
        vecs,
        w_qkv,
        jnp.asarray(head_table(head), bf16),
    )


TILES = dict(one=512, two=512, three=512, chunk=512, four=512)


def layer(tokens, cot, w_qkv, w_out, w_in, w_back, vecs, b_in, lengths, T=TILES):
    qkv, m1, m2, c = first_pass(lengths, tokens, vecs, w_qkv, T["one"])
    near, fa, fb, rn, p = second_pass(lengths, qkv, m1, m2, c, T["two"])
    (out, d_attn, d_mix, d_num, g_in, g_back, g_out, g_vec, g_bias, m3, m4, dt) = third_pass(
        lengths, tokens, cot, near, fa, fb, rn, qkv, c, vecs, b_in, w_out, w_in, w_back, T["three"], T["chunk"]
    )
    d_tok, g_qkv, g_vec1 = fourth_pass(
        lengths, qkv, p, d_mix, tokens, d_attn, d_num, fa, m1, m2, m3, m4, dt, c, vecs, w_qkv, T["four"]
    )
    grad_vec = jnp.concatenate([jnp.sum(g_vec1, axis=1), jnp.sum(g_vec, axis=1)[2:]], axis=0)
    return out, d_tok, g_qkv, g_out, g_in, g_back, grad_vec, jnp.sum(g_bias, axis=0)


def collect(w_qkv, w_out, w_in, w_back, vec_params, b_in):
    section_one = (
        lax.all_gather(w_qkv, "fsdp", axis=0, tiled=True),
        lax.all_gather(w_out, "fsdp", axis=0, tiled=True),
        lax.all_gather(w_in, "fsdp", axis=0, tiled=True),
        lax.all_gather(w_back, "fsdp", axis=0, tiled=True),
        lax.all_gather(vec_params, "fsdp", axis=1, tiled=True),
        lax.all_gather(b_in, "fsdp", axis=0, tiled=True),
    )
    return (
        lax.all_gather(section_one[0], "dp", axis=1, tiled=True),
        lax.all_gather(section_one[1], "dp", axis=1, tiled=True),
        lax.all_gather(section_one[2], "dp", axis=1, tiled=True),
        lax.all_gather(section_one[3], "dp", axis=1, tiled=True),
        lax.all_gather(section_one[4], "dp", axis=0, tiled=True),
        lax.all_gather(section_one[5], "dp", axis=0, tiled=True),
    )


def spread(grad_qkv, grad_out, grad_in, grad_back, grad_vec, grad_bias_in):
    section_one = (
        lax.psum_scatter(
            grad_qkv.astype(jnp.bfloat16), "dp", scatter_dimension=1, tiled=True
        ).astype(jnp.float32),
        lax.psum_scatter(
            grad_out.astype(jnp.bfloat16), "dp", scatter_dimension=1, tiled=True
        ).astype(jnp.float32),
        lax.psum_scatter(
            grad_in.astype(jnp.bfloat16), "dp", scatter_dimension=1, tiled=True
        ).astype(jnp.float32),
        lax.psum_scatter(
            grad_back.astype(jnp.bfloat16), "dp", scatter_dimension=0, tiled=True
        ).astype(jnp.float32),
        lax.psum_scatter(
            grad_vec.astype(jnp.bfloat16), "dp", scatter_dimension=0, tiled=True
        ).astype(jnp.float32),
        lax.psum_scatter(
            grad_bias_in.astype(jnp.bfloat16), "dp", scatter_dimension=0, tiled=True
        ).astype(jnp.float32),
    )
    return (
        lax.psum_scatter(section_one[0], "fsdp", scatter_dimension=0, tiled=True),
        lax.psum_scatter(section_one[1], "fsdp", scatter_dimension=0, tiled=True),
        lax.psum_scatter(section_one[2], "fsdp", scatter_dimension=0, tiled=True),
        lax.psum_scatter(section_one[3], "fsdp", scatter_dimension=1, tiled=True).T,
        lax.psum_scatter(section_one[4], "fsdp", scatter_dimension=1, tiled=True),
        lax.psum_scatter(section_one[5], "fsdp", scatter_dimension=0, tiled=True),
    )


def shards(
    tokens, cotangent, w_qkv, w_out, w_in, w_back, vec_params, b_in, item_lengths, bucket_counts
):
    qkv_w, out_w, in_w, back_w, vecs, in_bias = collect(
        w_qkv, w_out, w_in, w_back, vec_params, b_in
    )
    out, d_tok, g_qkv, g_out, g_in, g_back, g_vec, g_bias = layer(
        tokens,
        cotangent,
        qkv_w,
        out_w,
        in_w,
        back_w,
        vecs.astype(f32),
        in_bias.astype(f32)[None],
        item_lengths,
    )
    return (out, d_tok) + spread(g_qkv, g_out, g_in, g_back, g_vec, g_bias)


def solution(mesh):
    in_specs = (
        P(("dp", "fsdp"), None),
        P(("dp", "fsdp"), None),
        P("fsdp", "dp"),
        P("fsdp", "dp"),
        P("fsdp", "dp"),
        P("fsdp", "dp"),
        P("dp", "fsdp"),
        P(("dp", "fsdp")),
        P(("dp", "fsdp"), None),
        P(("dp", "fsdp"), None),
    )
    out_specs = (
        P(("dp", "fsdp"), None),
        P(("dp", "fsdp"), None),
        P("fsdp", "dp"),
        P("fsdp", "dp"),
        P("fsdp", "dp"),
        P("fsdp", "dp"),
        P("dp", "fsdp"),
        P(("dp", "fsdp")),
    )
    return jax.shard_map(shards, mesh=mesh, in_specs=in_specs, out_specs=out_specs, check_vma=False)
```

```python
import functools
import math

import jax
import jax.numpy as jnp
import numpy as np
from jax import lax
from jax.experimental import pallas as pl
from jax.experimental.pallas import tpu as pltpu
from jax.sharding import PartitionSpec as P

HEADS = 8
BAND = 30
QB = 64
HALO = 32
KW = QB + 2 * HALO
GW = 256

norm_eps = 1e-05
f32 = jnp.float32
bf16 = jnp.bfloat16
exact = lax.Precision.HIGHEST
VMEM_LIMIT = 60 * 1024 * 1024


def nn(a, b):
    return lax.dot_general(a, b, (((1,), (0,)), ((), ())), preferred_element_type=f32)


def nt(a, b):
    return lax.dot_general(a, b, (((1,), (1,)), ((), ())), preferred_element_type=f32)


def tn(a, b):
    return lax.dot_general(a, b, (((0,), (0,)), ((), ())), preferred_element_type=f32)


def nt_exact(a, b):
    return lax.dot_general(
        a, b, (((1,), (1,)), ((), ())), preferred_element_type=f32, precision=exact
    )


def first_part(cols):
    return 128 * ((cols // 128 + 1) // 2) if cols >= 256 else cols // 2


def lift(t):
    return jnp.where(t > 0, t + 1.0, jnp.exp(jnp.minimum(t, 0.0)))


def moments(x):
    mean = jnp.mean(x, axis=-1, keepdims=True)
    cen = x - mean
    inv = lax.rsqrt(jnp.mean(cen * cen, axis=-1, keepdims=True) + norm_eps)
    return cen * inv, inv


def fold8(x):
    return jnp.sum(x.reshape(x.shape[0] // 8, 8, x.shape[1]), axis=0)


def row_valid(step, rows, width, length):
    ids = step * rows + lax.broadcasted_iota(jnp.int32, (rows, width), 0)
    return ids < length


def same_head(head):
    r = lax.broadcasted_iota(jnp.int32, (GW, GW), 0) // head
    c = lax.broadcasted_iota(jnp.int32, (GW, GW), 1) // head
    return r == c


def spread_rows(x, mask_low):
    return jnp.concatenate([x] * (GW // QB), axis=0) * mask_low


def pick_heads(x, head):
    lane = lax.broadcasted_iota(jnp.int32, (QB, GW), 1) // head
    out = x[:QB]
    for h in range(1, GW // QB):
        out = jnp.where(lane == h, x[h * QB : (h + 1) * QB], out)
    return out


def cut_blocks(ref, acc, lo=0, step=None, swap=False):
    n_dp, n_fsdp, r, c = ref.shape
    step = c if step is None else step
    for d in range(n_dp):
        for f in range(n_fsdp):
            if swap:
                block = acc[d * r : (d + 1) * r, f * c : (f + 1) * c]
            else:
                block = acc[f * r : (f + 1) * r, d * step + lo : d * step + lo + c]
            ref[d, f] = block.astype(ref.dtype)


def qkv_kernel(len_ref, tok_ref, vec_ref, w_ref, qkv_ref, m1_ref, m2_ref, c_ref, st_ref, t_ref):
    step = pl.program_id(0)
    rows, width = tok_ref.shape
    groups = width // GW
    head = width // HEADS
    length = len_ref[0, 0]

    @pl.when(step == 0)
    def _():
        st_ref[...] = jnp.zeros_like(st_ref)
        t_ref[...] = jnp.zeros_like(t_ref)

    z, _ = moments(tok_ref[...].astype(f32))
    h = (z * vec_ref[0:1] + vec_ref[1:2]).astype(bf16)
    qkv_ref[:, :width] = nn(h, w_ref[:, :width]).astype(bf16)
    valid = row_valid(step, rows, GW, length)
    for g in range(groups):
        kc = slice(width + g * GW, width + (g + 1) * GW)
        vc = slice(2 * width + g * GW, 2 * width + (g + 1) * GW)
        k = nn(h, w_ref[:, kc]).astype(bf16)
        v = nn(h, w_ref[:, vc]).astype(bf16)
        qkv_ref[:, kc] = k
        qkv_ref[:, vc] = v
        kw = k.astype(f32)
        phi = jnp.where(valid, lift(kw), 0.0)
        bent = jnp.where(valid, jnp.tanh(kw), 0.0)
        both = jnp.concatenate([phi.astype(bf16), bent.astype(bf16)], axis=1)
        st_ref[g] += tn(v, both)
        t_ref[g] += fold8(phi)

    @pl.when(step == pl.num_programs(0) - 1)
    def _():
        mask = same_head(head).astype(f32)
        inv_len = 1.0 / length.astype(f32)
        ones = jnp.ones((8, GW), f32)
        for g in range(groups):
            tb = jnp.sum(t_ref[g], axis=0, keepdims=True) * mask
            s1 = st_ref[g][:, :GW] * mask
            s2 = st_ref[g][:, GW:] * mask
            c_col = jnp.sum(s1, axis=1, keepdims=True) / jnp.sum(tb, axis=1, keepdims=True)
            c_row = nt_exact(ones, s1) / nt_exact(ones, tb)
            m1_ref[g, :GW] = (s1 - c_col * tb).astype(bf16)
            m1_ref[g, GW:] = tb.astype(bf16)
            m2_ref[g] = (s2 * inv_len).astype(bf16)
            c_ref[g] = c_row


def first_pass(length, tokens, vecs, w_qkv, tile):
    rows, width = tokens.shape
    groups = width // GW
    const = lambda *shape: pl.BlockSpec(shape, lambda i: (0,) * len(shape))
    return pl.pallas_call(
        qkv_kernel,
        grid=(rows // tile,),
        in_specs=[
            pl.BlockSpec(memory_space=pltpu.SMEM),
            pl.BlockSpec((tile, width), lambda i: (i, 0)),
            const(8, width),
            const(width, 3 * width),
        ],
        out_specs=[
            pl.BlockSpec((tile, 3 * width), lambda i: (i, 0)),
            const(groups, 2 * GW, GW),
            const(groups, GW, GW),
            const(groups, 8, GW),
        ],
        out_shape=[
            jax.ShapeDtypeStruct((rows, 3 * width), bf16),
            jax.ShapeDtypeStruct((groups, 2 * GW, GW), bf16),
            jax.ShapeDtypeStruct((groups, GW, GW), bf16),
            jax.ShapeDtypeStruct((groups, 8, GW), f32),
        ],
        scratch_shapes=[
            pltpu.VMEM((groups, GW, 2 * GW), f32),
            pltpu.VMEM((groups, 8, GW), f32),
        ],
        compiler_params=pltpu.CompilerParams(vmem_limit_bytes=VMEM_LIMIT),
        cost_estimate=pl.CostEstimate(
            flops=2 * rows * width * 4 * width, bytes_accessed=rows * width * 8, transcendentals=0
        ),
        name="first_pass",
    )(length, tokens, vecs, w_qkv)


def mix_kernel(
    len_ref,
    q_ref,
    k_lo,
    k_ref,
    k_hi,
    v_lo,
    v_ref,
    v_hi,
    m1_ref,
    m2_ref,
    c_ref,
    band_ref,
    hm_ref,
    near_ref,
    fa_ref,
    fb_ref,
    rn_ref,
    p_ref,
    kk,
    vv,
):
    step = pl.program_id(0)
    rows, width = q_ref.shape
    groups = width // GW
    head = width // HEADS
    scale = head ** (-0.5)
    length = len_ref[0, 0]
    kk[:HALO] = k_lo[...]
    kk[HALO : HALO + rows] = k_ref[...]
    kk[HALO + rows :] = k_hi[...]
    vv[:HALO] = v_lo[...]
    vv[HALO : HALO + rows] = v_ref[...]
    vv[HALO + rows :] = v_hi[...]
    hm = hm_ref[...]
    for b in range(rows // QB):
        base = step * rows + b * QB - HALO
        key = base + lax.broadcasted_iota(jnp.int32, (KW, GW), 0)
        bias = jnp.where((key >= 0) & (key < length), band_ref[...], -1e30)
        for g in range(groups):
            cols = slice(g * GW, (g + 1) * GW)
            qs = spread_rows(q_ref[b * QB : (b + 1) * QB, cols] * scale, hm)
            s = nt(kk[b * QB : b * QB + KW, cols], qs) + bias
            e = jnp.exp(s - jnp.max(s, axis=0, keepdims=True))
            p = (e * (1.0 / jnp.sum(e, axis=0, keepdims=True))).astype(bf16)
            p_ref[b, :, cols] = p
            o = tn(p, vv[b * QB : b * QB + KW, cols])
            near_ref[b * QB : (b + 1) * QB, cols] = pick_heads(o, head).astype(bf16)
    for g in range(groups):
        cols = slice(g * GW, (g + 1) * GW)
        q = q_ref[:, cols].astype(f32)
        both = nt(lift(q).astype(bf16), m1_ref[g])
        rn = 1.0 / both[:, GW:]
        rn_ref[:, cols] = rn.astype(bf16)
        fa_ref[:, cols] = (both[:, :GW] * rn).astype(bf16)
        fb_ref[:, cols] = nt(jnp.tanh(q).astype(bf16), m2_ref[g]).astype(bf16)


def halo_specs(tile, width, col, rows):
    per = tile // HALO
    last = rows // HALO - 1
    return [
        pl.BlockSpec((HALO, width), lambda i: (jnp.maximum(i * per - 1, 0), col)),
        pl.BlockSpec((tile, width), lambda i: (i, col)),
        pl.BlockSpec((HALO, width), lambda i: (jnp.minimum((i + 1) * per, last), col)),
    ]


def band_table(head):
    key = np.arange(KW)[:, None] - HALO
    query = np.arange(GW)[None, :] % QB
    return np.where(np.abs(key - query) <= BAND, 0.0, -1e30).astype(np.float32)


def head_table(head):
    r = np.arange(GW)[:, None] // QB
    c = np.arange(GW)[None, :] // head
    return (r == c).astype(np.float32)


def second_pass(length, qkv, m1, m2, c, tile):
    rows = qkv.shape[0]
    width = qkv.shape[1] // 3
    groups = width // GW
    const = lambda *shape: pl.BlockSpec(shape, lambda i: (0,) * len(shape))
    block = pl.BlockSpec((tile, width), lambda i: (i, 0))
    head = width // HEADS
    return pl.pallas_call(
        mix_kernel,
        grid=(rows // tile,),
        in_specs=[
            pl.BlockSpec(memory_space=pltpu.SMEM),
            block,
            *halo_specs(tile, width, 1, rows),
            *halo_specs(tile, width, 2, rows),
            const(groups, 2 * GW, GW),
            const(groups, GW, GW),
            const(groups, 8, GW),
            const(KW, GW),
            const(GW, GW),
        ],
        out_specs=[
            block,
            block,
            block,
            block,
            pl.BlockSpec((tile // QB, KW, width), lambda i: (i, 0, 0)),
        ],
        out_shape=[jax.ShapeDtypeStruct((rows, width), bf16)] * 4
        + [jax.ShapeDtypeStruct((rows // QB, KW, width), bf16)],
        scratch_shapes=[pltpu.VMEM((tile + 2 * HALO, width), bf16)] * 2,
        compiler_params=pltpu.CompilerParams(vmem_limit_bytes=VMEM_LIMIT),
        cost_estimate=pl.CostEstimate(
            flops=2 * rows * width * 4 * width, bytes_accessed=rows * width * 18, transcendentals=0
        ),
        name="second_pass",
    )(
        length,
        qkv,
        qkv,
        qkv,
        qkv,
        qkv,
        qkv,
        qkv,
        m1,
        m2,
        c,
        jnp.asarray(band_table(head)),
        jnp.asarray(head_table(head), bf16),
    )


def ffn_kernel(
    chunk,
    len_ref,
    tok_ref,
    cot_ref,
    near_ref,
    fa_ref,
    fb_ref,
    rn_ref,
    q_ref,
    c_ref,
    vec_ref,
    bin_ref,
    wout_ref,
    win_ref,
    wback_ref,
    out_ref,
    datt_ref,
    dmix_ref,
    dn_ref,
    gin_ref,
    gback_ref,
    gout_ref,
    gvec_ref,
    gbias_ref,
    m3_ref,
    m4_ref,
    dt_ref,
    a_in,
    a_back,
    a_out,
    a_st,
    a_bent,
):
    step = pl.program_id(0)
    rows, width = tok_ref.shape
    hidden = win_ref.shape[1]
    groups = width // GW
    head = width // HEADS
    length = len_ref[0, 0]

    @pl.when(step == 0)
    def _():
        a_in[...] = jnp.zeros_like(a_in)
        a_back[...] = jnp.zeros_like(a_back)
        a_out[...] = jnp.zeros_like(a_out)
        a_st[...] = jnp.zeros_like(a_st)
        a_bent[...] = jnp.zeros_like(a_bent)
        gvec_ref[...] = jnp.zeros_like(gvec_ref)
        gbias_ref[...] = jnp.zeros_like(gbias_ref)

    c_row = jnp.concatenate([c_ref[g, 0:1] for g in range(groups)], axis=1)
    near = near_ref[...].astype(f32)
    fac = fa_ref[...].astype(f32)
    far_b = fb_ref[...].astype(f32)
    mixed = (
        vec_ref[5:6] * near + vec_ref[6:7] * (fac + c_row) + vec_ref[7:8] * far_b
    ).astype(bf16)
    resid = tok_ref[...].astype(f32) + nn(mixed, wout_ref[...])
    z2, r2 = moments(resid)
    h2 = (z2 * vec_ref[2:3] + vec_ref[3:4]).astype(bf16)
    valid = row_valid(step, rows, width, length)
    seed = jnp.where(valid, cot_ref[...].astype(f32), 0.0)
    d_ffn = seed.astype(bf16)
    s0 = math.sqrt(2.0 / math.pi)
    s1 = s0 * 0.044715
    ffn = jnp.zeros((rows, width), f32)
    dh2 = jnp.zeros((rows, width), f32)
    for lo in range(0, hidden, chunk):
        cols = slice(lo, lo + chunk)
        x = nn(h2, win_ref[:, cols]) + bin_ref[0:1, cols]
        x2 = x * x
        t = jnp.tanh(x * (s0 + s1 * x2))
        half = 0.5 + 0.5 * t
        act = x * half
        slope = half + (act - act * half) * (2 * s0 + 6 * s1 * x2)
        act = act.astype(bf16)
        ffn += nn(act, wback_ref[cols, :])
        a_back[:, cols] += tn(d_ffn, act)
        d_pre = slope * nt(d_ffn, wback_ref[cols, :])
        gbias_ref[:, cols] += fold8(d_pre)
        d_pre = d_pre.astype(bf16)
        a_in[:, cols] += tn(h2, d_pre)
        dh2 += nt(d_pre, win_ref[:, cols])
    out_ref[...] = jnp.where(valid, resid + ffn + vec_ref[4:5], 0.0).astype(bf16)
    gvec_ref[2] += fold8(dh2 * z2)
    gvec_ref[3] += fold8(dh2)
    gvec_ref[4] += fold8(seed)
    dz = dh2 * vec_ref[2:3]
    d_resid = seed + r2 * (
        dz
        - jnp.mean(dz, axis=-1, keepdims=True)
        - z2 * jnp.mean(dz * z2, axis=-1, keepdims=True)
    )
    d_attn = d_resid.astype(bf16)
    datt_ref[...] = d_attn
    a_out[...] += tn(mixed, d_attn)
    d_mix = nt(d_attn, wout_ref[...])
    dmix_ref[...] = d_mix.astype(bf16)
    gvec_ref[5] += fold8(d_mix * near)
    gvec_ref[6] += fold8(d_mix * fac)
    gvec_ref[7] += fold8(d_mix * far_b)
    gvec_ref[0] += fold8(d_mix)
    d_num = (vec_ref[6:7] * d_mix * rn_ref[...].astype(f32)).astype(bf16)
    dn_ref[...] = d_num
    d_den = (d_num.astype(f32) * fac).astype(bf16)
    d_far = (vec_ref[7:8] * d_mix).astype(bf16)
    for g in range(groups):
        cols = slice(g * GW, (g + 1) * GW)
        q = q_ref[:, cols].astype(f32)
        a_st[g] += tn(lift(q).astype(bf16), jnp.concatenate([d_num[:, cols], d_den[:, cols]], axis=1))
        a_bent[g] += tn(jnp.tanh(q).astype(bf16), d_far[:, cols])

    @pl.when(step == pl.num_programs(0) - 1)
    def _():
        mask = same_head(head).astype(f32)
        inv_len = 1.0 / length.astype(f32)
        ones = jnp.ones((8, GW), f32)
        for g in range(groups):
            m3_ref[g] = (a_st[g][:, :GW] * mask).astype(bf16)
            m4_ref[g] = (a_bent[g] * mask * inv_len).astype(bf16)
            dt_ref[g] = -nt_exact(ones, a_st[g][:, GW:] * mask)
        cut_blocks(gin_ref, a_in)
        cut_blocks(gback_ref, a_back, swap=True)
        cut_blocks(gout_ref, a_out)
        gvec_ref[6] += gvec_ref[0] * c_row


def third_pass(ways, length, tokens, cot, near, fa, fb, rn, qkv, c, vecs, b_in, w_out, w_in, w_back, tile, chunk):
    rows, width = tokens.shape
    hidden = w_in.shape[1]
    groups = width // GW
    n_dp, n_fsdp = ways
    const = lambda *shape: pl.BlockSpec(shape, lambda i: (0,) * len(shape))
    block = pl.BlockSpec((tile, width), lambda i: (i, 0))
    sds = jax.ShapeDtypeStruct
    return pl.pallas_call(
        functools.partial(ffn_kernel, chunk),
        grid=(rows // tile,),
        in_specs=[pl.BlockSpec(memory_space=pltpu.SMEM)]
        + [block] * 7
        + [
            const(groups, 8, GW),
            const(8, width),
            const(1, hidden),
            const(width, width),
            const(width, hidden),
            const(hidden, width),
        ],
        out_specs=[block] * 4
        + [
            const(n_dp, n_fsdp, width // n_fsdp, hidden // n_dp),
            const(n_dp, n_fsdp, width // n_dp, hidden // n_fsdp),
            const(n_dp, n_fsdp, width // n_fsdp, width // n_dp),
            const(8, 8, width),
            const(8, hidden),
            const(groups, GW, GW),
            const(groups, GW, GW),
            const(groups, 8, GW),
        ],
        out_shape=[sds((rows, width), bf16)] * 4
        + [
            sds((n_dp, n_fsdp, width // n_fsdp, hidden // n_dp), bf16),
            sds((n_dp, n_fsdp, width // n_dp, hidden // n_fsdp), bf16),
            sds((n_dp, n_fsdp, width // n_fsdp, width // n_dp), bf16),
            sds((8, 8, width), f32),
            sds((8, hidden), f32),
            sds((groups, GW, GW), bf16),
            sds((groups, GW, GW), bf16),
            sds((groups, 8, GW), f32),
        ],
        scratch_shapes=[
            pltpu.VMEM((width, hidden), f32),
            pltpu.VMEM((width, hidden), f32),
            pltpu.VMEM((width, width), f32),
            pltpu.VMEM((groups, GW, 2 * GW), f32),
            pltpu.VMEM((groups, GW, GW), f32),
        ],
        compiler_params=pltpu.CompilerParams(vmem_limit_bytes=VMEM_LIMIT),
        cost_estimate=pl.CostEstimate(
            flops=2 * rows * width * (6 * hidden + 4 * width),
            bytes_accessed=rows * width * 22,
            transcendentals=0,
        ),
        name="third_pass",
    )(length, tokens, cot, near, fa, fb, rn, qkv, c, vecs, b_in, w_out, w_in, w_back)


def back_kernel(
    len_ref,
    q_ref,
    k_lo,
    k_ref,
    k_hi,
    v_lo,
    v_ref,
    v_hi,
    p_ref,
    dmix_ref,
    qkv_ref,
    tok_ref,
    datt_ref,
    dn_ref,
    fa_ref,
    dmp_ref,
    m1_ref,
    m2_ref,
    m3_ref,
    m4_ref,
    dt_ref,
    c_ref,
    vec_ref,
    w_ref,
    hm_ref,
    dtok_ref,
    ga_ref,
    gb_ref,
    gvec_ref,
    kk,
    vv,
    dq_s,
    dk_s,
    dv_s,
    a_qkv,
):
    step = pl.program_id(0)
    steps = pl.num_programs(0) - 1
    rows, width = q_ref.shape
    groups = width // GW
    head = width // HEADS
    scale = head ** (-0.5)
    length = len_ref[0, 0]

    @pl.when(step == 0)
    def _():
        dk_s[: 2 * HALO] = jnp.zeros((2 * HALO, width), f32)
        dv_s[: 2 * HALO] = jnp.zeros((2 * HALO, width), f32)
        a_qkv[...] = jnp.zeros_like(a_qkv)
        gvec_ref[...] = jnp.zeros_like(gvec_ref)

    @pl.when(step < steps)
    def _():
        kk[:HALO] = k_lo[...]
        kk[HALO : HALO + rows] = k_ref[...]
        kk[HALO + rows :] = k_hi[...]
        vv[:HALO] = v_lo[...]
        vv[HALO : HALO + rows] = v_ref[...]
        vv[HALO + rows :] = v_hi[...]
        hm = hm_ref[...]
        slot = lax.rem(step, 2)
        for g in range(groups):
            cols = slice(g * GW, (g + 1) * GW)
            for b in range(rows // QB):
                here = slice(b * QB, (b + 1) * QB)
                window = slice(b * QB, b * QB + KW)
                qs = spread_rows(q_ref[here, cols] * scale, hm)
                d_near = (vec_ref[5:6, cols] * dmix_ref[here, cols].astype(f32)).astype(bf16)
                ds = spread_rows(d_near, hm)
                p = p_ref[b, :, cols]
                pw = p.astype(f32)
                t = pw * nt(vv[window, cols], ds)
                d_s = (t - pw * jnp.sum(t, axis=0, keepdims=True)).astype(bf16)
                dk = nn(d_s, qs)
                dv = nn(p, ds)
                dq_s[slot, here, cols] = pick_heads(tn(d_s, kk[window, cols]), head) * scale
                lo = pl.multiple_of(step * rows + b * QB, QB)
                dk_s[pl.ds(lo, QB), cols] += dk[:QB]
                dk_s[pl.ds(lo + QB, QB), cols] = dk[QB:]
                dv_s[pl.ds(lo, QB), cols] += dv[:QB]
                dv_s[pl.ds(lo + QB, QB), cols] = dv[QB:]

    @pl.when(step > 0)
    def _():
        slot = lax.rem(step + 1, 2)
        z1, r1 = moments(tok_ref[...].astype(f32))
        h1 = (z1 * vec_ref[0:1] + vec_ref[1:2]).astype(bf16)
        valid = row_valid(step - 1, rows, GW, length)
        lo = pl.multiple_of((step - 1) * rows + HALO, HALO)
        dqs, dks, dvs = [], [], []
        for g in range(groups):
            cols = slice(g * GW, (g + 1) * GW)
            q = qkv_ref[:, g * GW : (g + 1) * GW].astype(f32)
            k = qkv_ref[:, width + g * GW : width + (g + 1) * GW].astype(f32)
            v = qkv_ref[:, 2 * width + g * GW : 2 * width + (g + 1) * GW]
            d_num = dn_ref[:, cols]
            d_den = (d_num.astype(f32) * -fa_ref[:, cols].astype(f32)).astype(bf16)
            d_far = (vec_ref[7:8, cols] * dmp_ref[:, cols].astype(f32)).astype(bf16)
            bent_q = jnp.tanh(q)
            dq = (
                dq_s[slot, :, cols]
                + nn(jnp.concatenate([d_num, d_den], axis=1), m1_ref[g]) * jnp.minimum(lift(q), 1.0)
                + nn(d_far, m2_ref[g]) * (1.0 - bent_q * bent_q)
            )
            lift_k = lift(k)
            bent_k = jnp.tanh(k)
            v_cen = (v.astype(f32) - c_ref[g, 0:1]).astype(bf16)
            dk = (nt(v_cen, m3_ref[g]) + dt_ref[g, 0:1]) * jnp.minimum(lift_k, 1.0) + nt(
                v, m4_ref[g]
            ) * (1.0 - bent_k * bent_k)
            both = jnp.concatenate([lift_k.astype(bf16), bent_k.astype(bf16)], axis=1)
            dv = nn(both, jnp.concatenate([m3_ref[g], m4_ref[g]], axis=0))
            dqs.append(dq.astype(bf16))
            dks.append((dk_s[pl.ds(lo, rows), cols] + jnp.where(valid, dk, 0.0)).astype(bf16))
            dvs.append((dv_s[pl.ds(lo, rows), cols] + jnp.where(valid, dv, 0.0)).astype(bf16))
        d_qkv = jnp.concatenate(dqs + dks + dvs, axis=1)
        a_qkv[...] += tn(h1, d_qkv)
        dh1 = nt(d_qkv, w_ref[...])
        gvec_ref[0] += fold8(dh1 * z1)
        gvec_ref[1] += fold8(dh1)
        dz = dh1 * vec_ref[0:1]
        dtok_ref[...] = (
            datt_ref[...].astype(f32)
            + r1
            * (
                dz
                - jnp.mean(dz, axis=-1, keepdims=True)
                - z1 * jnp.mean(dz * z1, axis=-1, keepdims=True)
            )
        ).astype(bf16)

    @pl.when(step == steps)
    def _():
        step_cols = ga_ref.shape[3] + gb_ref.shape[3]
        cut_blocks(ga_ref, a_qkv, 0, step_cols)
        cut_blocks(gb_ref, a_qkv, ga_ref.shape[3], step_cols)


def fourth_pass(
    ways, length, qkv, p, d_mix, tokens, d_attn, d_num, fa, m1, m2, m3, m4, dt, c, vecs, w_qkv, tile
):
    rows, width = tokens.shape
    groups = width // GW
    steps = rows // tile
    n_dp, n_fsdp = ways
    part = first_part(3 * width // n_dp)
    const = lambda *shape: pl.BlockSpec(shape, lambda i: (0,) * len(shape))
    now = lambda i: jnp.minimum(i, steps - 1)
    old = lambda i: jnp.maximum(i - 1, 0)
    per = tile // HALO
    last = rows // HALO - 1

    def halo(col):
        return [
            pl.BlockSpec((HALO, width), lambda i: (jnp.maximum(now(i) * per - 1, 0), col)),
            pl.BlockSpec((tile, width), lambda i: (now(i), col)),
            pl.BlockSpec((HALO, width), lambda i: (jnp.minimum((now(i) + 1) * per, last), col)),
        ]

    block = pl.BlockSpec((tile, width), lambda i: (now(i), 0))
    late = pl.BlockSpec((tile, width), lambda i: (old(i), 0))
    head = width // HEADS
    sds = jax.ShapeDtypeStruct
    return pl.pallas_call(
        back_kernel,
        grid=(steps + 1,),
        in_specs=[
            pl.BlockSpec(memory_space=pltpu.SMEM),
            block,
            *halo(1),
            *halo(2),
            pl.BlockSpec((tile // QB, KW, width), lambda i: (now(i), 0, 0)),
            block,
            pl.BlockSpec((tile, 3 * width), lambda i: (old(i), 0)),
            late,
            late,
            late,
            late,
            late,
            const(groups, 2 * GW, GW),
            const(groups, GW, GW),
            const(groups, GW, GW),
            const(groups, GW, GW),
            const(groups, 8, GW),
            const(groups, 8, GW),
            const(8, width),
            const(width, 3 * width),
            const(GW, GW),
        ],
        out_specs=[
            late,
            const(n_dp, n_fsdp, width // n_fsdp, part),
            const(n_dp, n_fsdp, width // n_fsdp, 3 * width // n_dp - part),
            const(2, 8, width),
        ],
        out_shape=[
            sds((rows, width), bf16),
            sds((n_dp, n_fsdp, width // n_fsdp, part), bf16),
            sds((n_dp, n_fsdp, width // n_fsdp, 3 * width // n_dp - part), bf16),
            sds((2, 8, width), f32),
        ],
        scratch_shapes=[
            pltpu.VMEM((tile + 2 * HALO, width), bf16),
            pltpu.VMEM((tile + 2 * HALO, width), bf16),
            pltpu.VMEM((2, tile, width), f32),
            pltpu.VMEM((rows + 2 * HALO, width), f32),
            pltpu.VMEM((rows + 2 * HALO, width), f32),
            pltpu.VMEM((width, 3 * width), f32),
        ],
        compiler_params=pltpu.CompilerParams(vmem_limit_bytes=VMEM_LIMIT),
        cost_estimate=pl.CostEstimate(
            flops=2 * rows * width * 14 * width, bytes_accessed=rows * width * 24, transcendentals=0
        ),
        name="fourth_pass",
    )(
        length,
        qkv,
        qkv,
        qkv,
        qkv,
        qkv,
        qkv,
        qkv,
        p,
        d_mix,
        qkv,
        tokens,
        d_attn,
        d_num,
        fa,
        d_mix,
        m1,
        m2,
        m3,
        m4,
        dt,
        c,
        vecs,
        w_qkv,
        jnp.asarray(head_table(head), bf16),
    )


TILES = dict(one=512, two=512, three=512, chunk=512, four=512)


def layer(ways, tokens, cot, w_qkv, w_out, w_in, w_back, vecs, b_in, lengths, T=TILES):
    qkv, m1, m2, c = first_pass(lengths, tokens, vecs, w_qkv, T["one"])
    near, fa, fb, rn, p = second_pass(lengths, qkv, m1, m2, c, T["two"])
    (out, d_attn, d_mix, d_num, g_in, g_back, g_out, g_vec, g_bias, m3, m4, dt) = third_pass(
        ways, lengths, tokens, cot, near, fa, fb, rn, qkv, c, vecs, b_in, w_out, w_in, w_back, T["three"], T["chunk"]
    )
    d_tok, g_a, g_b, g_vec1 = fourth_pass(
        ways, lengths, qkv, p, d_mix, tokens, d_attn, d_num, fa, m1, m2, m3, m4, dt, c, vecs, w_qkv, T["four"]
    )
    grad_vec = jnp.concatenate([jnp.sum(g_vec1, axis=1), jnp.sum(g_vec, axis=1)[2:]], axis=0)
    return out, d_tok, g_a, g_b, g_out, g_in, g_back, grad_vec, jnp.sum(g_bias, axis=0)


MESH = pl.DeviceIdType.MESH


class Place:
    def __init__(self, n_dp, n_fsdp):
        self.m = n_fsdp // 2
        self.nh = n_dp // 2
        d = lax.axis_index("dp")
        f = lax.axis_index("fsdp")
        self.dh, self.dl = d // 2, lax.rem(d, 2)
        self.fh, self.fl = f // 2, lax.rem(f, 2)

    def dev(self, dh=None, dl=None, fh=None, fl=None):
        dh = self.dh if dh is None else dh
        dl = self.dl if dl is None else dl
        fh = self.fh if fh is None else fh
        fl = self.fl if fl is None else fl
        return {"dp": dh * 2 + dl, "fsdp": fh * 2 + fl}

    def partners(self):
        out = [self.dev(fh=lax.rem(self.fh + o, self.m)) for o in range(1, self.m)]
        out += [self.dev(dh=lax.rem(self.dh + o, self.nh)) for o in range(1, self.nh)]
        return out + [self.dev(fl=1 - self.fl), self.dev(dl=1 - self.dl)]


def greet(place):
    barrier = pltpu.get_barrier_semaphore()
    who = place.partners()
    for dev in who:
        pl.semaphore_signal(barrier, inc=1, device_id=dev, device_id_type=MESH)
    pl.semaphore_wait(barrier, len(who))


def copy_to(src, dst, send, recv, dev):
    return pltpu.make_async_remote_copy(
        src_ref=src, dst_ref=dst, send_sem=send, recv_sem=recv, device_id=dev, device_id_type=MESH
    )


class Gather:
    def __init__(self, place, shard, got, sems, local, first, order):
        self.p, self.shard, self.got, self.order = place, shard, got, order
        self.send, self.recv, self.local, self.first = sems[0], sems[1], local, first

    def own(self):
        p = self.p
        return pltpu.make_async_copy(self.shard, self.got.at[p.dh, p.dl, p.fh, p.fl], self.local)

    def stage(self, k):
        p, g = self.p, self.got
        i = self.first
        if k == 0:
            out = []
            for o in range(1, p.m):
                out.append(
                    copy_to(self.shard, g.at[p.dh, p.dl, p.fh, p.fl], self.send.at[i + o - 1],
                            self.recv.at[i + o - 1], p.dev(fh=lax.rem(p.fh + o, p.m)))
                )
            return out
        i += p.m - 1
        x_first = self.order == "x"
        if k == 3:
            ref = g.at[:, p.dl]
            return [copy_to(ref, ref, self.send.at[i + p.nh], self.recv.at[i + p.nh], p.dev(dl=1 - p.dl))]
        if (k == 1) == x_first:
            ref = g.at[p.dh, p.dl, :, p.fl] if k == 1 else g.at[:, p.dl, :, p.fl]
            return [copy_to(ref, ref, self.send.at[i], self.recv.at[i], p.dev(fl=1 - p.fl))]
        ref = g.at[p.dh, p.dl, :, p.fl] if k == 1 else g.at[p.dh, p.dl]
        return [
            copy_to(ref, ref, self.send.at[i + o], self.recv.at[i + o], p.dev(dh=lax.rem(p.dh + o, p.nh)))
            for o in range(1, p.nh)
        ]

    @staticmethod
    def count(n_dp, n_fsdp):
        return n_fsdp // 2 - 1 + 1 + n_dp // 2 - 1 + 1


def gather_kernel(n_dp, n_fsdp, orders, rounds, *refs):
    n = len(orders)
    shards, gots = refs[:n], refs[n : 2 * n]
    send, recv, local = refs[2 * n :]
    place = Place(n_dp, n_fsdp)
    per = Gather.count(n_dp, n_fsdp)
    pieces = [Gather(place, shards[j], gots[j], (send, recv), local.at[j], j * per, orders[j]) for j in range(n)]
    owns = [p.own() for p in pieces]
    for o in owns:
        o.start()
    greet(place)
    flight = {}
    for j, k in rounds:
        if k == 1:
            owns[j].wait()
        if k > 0:
            for c in flight[j, k - 1]:
                c.wait()
        if k < 4:
            flight[j, k] = pieces[j].stage(k)
            for c in flight[j, k]:
                c.start()


def gather_all(mesh_shape, arrays, orders, rounds, cid=0, vmem=False):
    n_dp, n_fsdp = mesh_shape["dp"], mesh_shape["fsdp"]
    n = len(arrays)
    per = Gather.count(n_dp, n_fsdp)
    sp = pl.BlockSpec(memory_space=pltpu.VMEM) if vmem else pl.BlockSpec(memory_space=pl.ANY)
    return pl.pallas_call(
        functools.partial(gather_kernel, n_dp, n_fsdp, orders, rounds),
        in_specs=[sp] * n,
        out_specs=[sp] * n,
        out_shape=[jax.ShapeDtypeStruct((n_dp // 2, 2, n_fsdp // 2, 2) + a.shape, a.dtype) for a in arrays],
        scratch_shapes=[
            pltpu.SemaphoreType.DMA((n * per,)),
            pltpu.SemaphoreType.DMA((n * per,)),
            pltpu.SemaphoreType.DMA((n,)),
        ],
        compiler_params=pltpu.CompilerParams(collective_id=cid, has_side_effects=True, vmem_limit_bytes=VMEM_LIMIT),
        name="gather_weights",
    )(*arrays)


class Scatter:
    def __init__(self, place, src, out, bufs, send, recv, local, order):
        self.p, self.src, self.out, self.order = place, src, out, order
        self.acc, self.r0, self.r1, self.r2, self.r3 = bufs
        self.send, self.recv, self.local = send, recv, local

    @staticmethod
    def count(n_dp, n_fsdp):
        return 1 + 1 + (n_dp // 2 - 1) + (n_fsdp // 2 - 1)

    @staticmethod
    def scratch(n_dp, n_fsdp, r, c, order, dtype):
        nh, m = n_dp // 2, n_fsdp // 2
        if order == "x":
            one, two = (nh, m, r, c), (nh - 1, m, r, c)
        else:
            one, two = (nh - 1, m, 2, r, c), (m, r, c)
        shapes = [(nh, m, 2, r, c), (nh, m, 2, r, c), one, two, (m - 1, r, c)]
        return [pltpu.VMEM(s, dtype) for s in shapes]

    def own(self):
        return pltpu.make_async_copy(self.src.at[:, self.p.dl], self.acc, self.local)

    def stage(self, k):
        p = self.p
        if k == 0:
            ref = self.src.at[:, 1 - p.dl]
            return [copy_to(ref, self.r0, self.send.at[0], self.recv.at[0], p.dev(dl=1 - p.dl))]
        if k == 3:
            i = p.nh
            out = []
            for o in range(1, p.m):
                fh = lax.rem(p.fh + o, p.m)
                out.append(
                    copy_to(self.acc.at[p.dh, fh, p.fl], self.r3.at[o - 1], self.send.at[i + o], self.recv.at[i + o],
                            p.dev(fh=fh))
                )
            return out
        if (k == 1) == (self.order == "x"):
            ref = self.acc.at[:, :, 1 - p.fl] if k == 1 else self.acc.at[p.dh, :, 1 - p.fl]
            dst = self.r1 if k == 1 else self.r2
            return [copy_to(ref, dst, self.send.at[1], self.recv.at[1], p.dev(fl=1 - p.fl))]
        out = []
        for o in range(1, p.nh):
            dh = lax.rem(p.dh + o, p.nh)
            ref = self.acc.at[dh] if k == 1 else self.acc.at[dh, :, p.fl]
            dst = self.r1.at[o - 1] if k == 1 else self.r2.at[o - 1]
            out.append(copy_to(ref, dst, self.send.at[1 + o], self.recv.at[1 + o], p.dev(dh=dh)))
        return out

    def add(self, k):
        p, acc = self.p, self.acc
        nh, m = p.nh, p.m
        dt = acc.dtype

        def put(index, others):
            total = acc[index].astype(f32)
            for o in others:
                total = total + o.astype(f32)
            acc[index] = total.astype(dt)

        if k == 3:
            total = acc[p.dh, p.fh, p.fl].astype(f32)
            for o in range(1, m):
                total = total + self.r3[o - 1].astype(f32)
            self.out[...] = total
            return

        @pl.loop(0, m)
        def _(i):
            if k == 0:
                for a in range(nh):
                    for b in range(2):
                        put((a, i, b), [self.r0[a, i, b]])
            elif k == 1 and self.order == "x":
                for a in range(nh):
                    put((a, i, p.fl), [self.r1[a, i]])
            elif k == 1:
                for b in range(2):
                    put((p.dh, i, b), [self.r1[o - 1, i, b] for o in range(1, nh)])
            elif self.order == "x":
                put((p.dh, i, p.fl), [self.r2[o - 1, i] for o in range(1, nh)])
            else:
                put((p.dh, i, p.fl), [self.r2[i]])


def scatter_kernel(n_dp, n_fsdp, orders, *refs):
    n = len(orders)
    srcs, outs = refs[:n], refs[n : 2 * n]
    bufs = [refs[2 * n + 5 * j : 2 * n + 5 * (j + 1)] for j in range(n)]
    sems = refs[7 * n :]
    place = Place(n_dp, n_fsdp)
    pieces = [
        Scatter(place, srcs[j], outs[j], bufs[j], sems[2 * j], sems[2 * j + 1], sems[2 * n].at[j], orders[j])
        for j in range(n)
    ]
    owns = [p.own() for p in pieces]
    for o in owns:
        o.start()
    greet(place)
    flight = {}
    for j in range(n):
        flight[j] = pieces[j].stage(0)
        for c in flight[j]:
            c.start()
    for o in owns:
        o.wait()
    for k in range(4):
        for j in range(n):
            for c in flight[j]:
                c.wait()
            pieces[j].add(k)
            if k < 3:
                flight[j] = pieces[j].stage(k + 1)
                for c in flight[j]:
                    c.start()


def scatter_all(mesh_shape, arrays, orders, cid):
    n_dp, n_fsdp = mesh_shape["dp"], mesh_shape["fsdp"]
    n = len(arrays)
    per = Scatter.count(n_dp, n_fsdp)
    scratch = []
    for a, order in zip(arrays, orders):
        scratch += Scatter.scratch(n_dp, n_fsdp, a.shape[-2], a.shape[-1], order, a.dtype)
    scratch += [pltpu.SemaphoreType.DMA((per,))] * (2 * n) + [pltpu.SemaphoreType.DMA((n,))]
    return pl.pallas_call(
        functools.partial(scatter_kernel, n_dp, n_fsdp, orders),
        in_specs=[pl.BlockSpec(memory_space=pl.ANY)] * n,
        out_specs=[pl.BlockSpec(memory_space=pltpu.VMEM)] * n,
        out_shape=[jax.ShapeDtypeStruct(a.shape[-2:], f32) for a in arrays],
        scratch_shapes=scratch,
        compiler_params=pltpu.CompilerParams(
            collective_id=cid, has_side_effects=True, vmem_limit_bytes=VMEM_LIMIT
        ),
        name="scatter_grads",
    )(*arrays)


def shards(
    tokens, cotangent, w_qkv, w_out, w_in, w_back, vec_params, b_in, item_lengths, bucket_counts, *, ways
):
    n_dp, n_fsdp = ways
    shape = {"dp": n_dp, "fsdp": n_fsdp}
    width = tokens.shape[1]
    cols = width // n_fsdp
    part = first_part(w_qkv.shape[1])
    small = jnp.zeros((16, 128), bf16).at[:2, :cols].set(vec_params).at[2, :cols].set(b_in)
    pieces = [w_qkv[:, :part], w_qkv[:, part:], w_in, w_back, w_out, small]
    orders = ["x", "y", "x", "y", "y", "x"]
    rounds = [(j, k) for k in range(5) for j in (0, 1, 5, 2, 3, 4)]
    got = gather_all(shape, pieces, orders, rounds, cid=0)

    def whole(g):
        return g.reshape(n_dp, n_fsdp, *g.shape[-2:])

    def lay(g):
        g = whole(g)
        return g.transpose(1, 2, 0, 3).reshape(n_fsdp * g.shape[2], n_dp * g.shape[3])

    qkv_w = jnp.concatenate([whole(got[0]), whole(got[1])], axis=3)
    qkv_w = lay(qkv_w)
    small = whole(got[5])
    vecs = small[:, :, :2, :cols].transpose(0, 2, 1, 3).reshape(2 * n_dp, width).astype(f32)
    in_bias = small[:, :, 2, :cols].reshape(1, -1).astype(f32)
    out, d_tok, g_a, g_b, g_out, g_in, g_back, g_vec, g_bias = layer(
        ways, tokens, cotangent, qkv_w, lay(got[4]), lay(got[2]), lay(got[3]), vecs, in_bias, item_lengths
    )
    g_vec = g_vec.reshape(n_dp, 2, n_fsdp, cols).transpose(0, 2, 1, 3)
    g_bias = g_bias.reshape(n_dp, n_fsdp, 1, cols)
    g_small = jnp.zeros((n_dp, n_fsdp, 8, 128), f32)
    g_small = g_small.at[:, :, :2, :cols].set(g_vec).at[:, :, 2:3, :cols].set(g_bias)
    grads = [g_a, g_b, g_in, g_back, g_out, g_small]
    grads = [g.reshape(n_dp // 2, 2, n_fsdp // 2, 2, *g.shape[2:]) for g in grads]
    r_a, r_b, r_in, r_back, r_out, r_small = scatter_all(shape, grads, ["x", "y", "x", "y", "y", "x"], cid=1)
    return (
        out,
        d_tok,
        jnp.concatenate([r_a, r_b], axis=1),
        r_out,
        r_in,
        r_back.T,
        r_small[:2, :cols],
        r_small[2, :cols],
    )


def solution(mesh):
    in_specs = (
        P(("dp", "fsdp"), None),
        P(("dp", "fsdp"), None),
        P("fsdp", "dp"),
        P("fsdp", "dp"),
        P("fsdp", "dp"),
        P("fsdp", "dp"),
        P("dp", "fsdp"),
        P(("dp", "fsdp")),
        P(("dp", "fsdp"), None),
        P(("dp", "fsdp"), None),
    )
    out_specs = (
        P(("dp", "fsdp"), None),
        P(("dp", "fsdp"), None),
        P("fsdp", "dp"),
        P("fsdp", "dp"),
        P("fsdp", "dp"),
        P("fsdp", "dp"),
        P("dp", "fsdp"),
        P(("dp", "fsdp")),
    )
    ways = (mesh.shape["dp"], mesh.shape["fsdp"])
    body = functools.partial(shards, ways=ways)
    return jax.shard_map(body, mesh=mesh, in_specs=in_specs, out_specs=out_specs, check_vma=False)
```

```python
import functools
import math

import jax
import jax.numpy as jnp
import numpy as np
from jax import lax
from jax.experimental import pallas as pl
from jax.experimental.pallas import tpu as pltpu
from jax.sharding import PartitionSpec as P

HEADS = 8
BAND = 30
QB = 64
HALO = 32
KW = QB + 2 * HALO
GW = 256

norm_eps = 1e-05
f32 = jnp.float32
bf16 = jnp.bfloat16
exact = lax.Precision.HIGHEST
VMEM_LIMIT = 60 * 1024 * 1024


def nn(a, b):
    return lax.dot_general(a, b, (((1,), (0,)), ((), ())), preferred_element_type=f32)


def nt(a, b):
    return lax.dot_general(a, b, (((1,), (1,)), ((), ())), preferred_element_type=f32)


def tn(a, b):
    return lax.dot_general(a, b, (((0,), (0,)), ((), ())), preferred_element_type=f32)


def nt_exact(a, b):
    return lax.dot_general(
        a, b, (((1,), (1,)), ((), ())), preferred_element_type=f32, precision=exact
    )


def first_part(cols):
    return 128 * ((cols // 128 + 1) // 2) if cols >= 256 else cols // 2


def lift(t):
    return jnp.where(t > 0, t + 1.0, jnp.exp(jnp.minimum(t, 0.0)))


def moments(x):
    mean = jnp.mean(x, axis=-1, keepdims=True)
    cen = x - mean
    inv = lax.rsqrt(jnp.mean(cen * cen, axis=-1, keepdims=True) + norm_eps)
    return cen * inv, inv


def fold8(x):
    return jnp.sum(x.reshape(x.shape[0] // 8, 8, x.shape[1]), axis=0)


def row_valid(step, rows, width, length):
    ids = step * rows + lax.broadcasted_iota(jnp.int32, (rows, width), 0)
    return ids < length


def same_head(head):
    r = lax.broadcasted_iota(jnp.int32, (GW, GW), 0) // head
    c = lax.broadcasted_iota(jnp.int32, (GW, GW), 1) // head
    return r == c


def spread_rows(x, mask_low):
    return jnp.concatenate([x] * (GW // QB), axis=0) * mask_low


def pick_heads(x, head):
    lane = lax.broadcasted_iota(jnp.int32, (QB, GW), 1) // head
    out = x[:QB]
    for h in range(1, GW // QB):
        out = jnp.where(lane == h, x[h * QB : (h + 1) * QB], out)
    return out


def join_blocks(ref, got, lo=0, step=None):
    n_dp, n_fsdp, r, c = got.shape
    step = c if step is None else step
    for d in range(n_dp):
        for f in range(n_fsdp):
            ref[f * r : (f + 1) * r, d * step + lo : d * step + lo + c] = got[d, f]


def cut_blocks(ref, acc, lo=0, step=None, swap=False):
    n_dp, n_fsdp, r, c = ref.shape
    step = c if step is None else step
    for d in range(n_dp):
        for f in range(n_fsdp):
            if swap:
                block = acc[d * r : (d + 1) * r, f * c : (f + 1) * c]
            else:
                block = acc[f * r : (f + 1) * r, d * step + lo : d * step + lo + c]
            ref[d, f] = block.astype(ref.dtype)


def band_table(head):
    key = np.arange(KW)[:, None] - HALO
    query = np.arange(GW)[None, :] % QB
    return np.where(np.abs(key - query) <= BAND, 0.0, -1e30).astype(np.float32)


def head_table(head):
    r = np.arange(GW)[:, None] // QB
    c = np.arange(GW)[None, :] // head
    return (r == c).astype(np.float32)


MESH = pl.DeviceIdType.MESH


class Place:
    def __init__(self, n_dp, n_fsdp):
        self.m = n_fsdp // 2
        self.nh = n_dp // 2
        d = lax.axis_index("dp")
        f = lax.axis_index("fsdp")
        self.dh, self.dl = d // 2, lax.rem(d, 2)
        self.fh, self.fl = f // 2, lax.rem(f, 2)

    def dev(self, dh=None, dl=None, fh=None, fl=None):
        dh = self.dh if dh is None else dh
        dl = self.dl if dl is None else dl
        fh = self.fh if fh is None else fh
        fl = self.fl if fl is None else fl
        return {"dp": dh * 2 + dl, "fsdp": fh * 2 + fl}

    def partners(self):
        out = [self.dev(fh=lax.rem(self.fh + o, self.m)) for o in range(1, self.m)]
        out += [self.dev(dh=lax.rem(self.dh + o, self.nh)) for o in range(1, self.nh)]
        return out + [self.dev(fl=1 - self.fl), self.dev(dl=1 - self.dl)]


def greet(place):
    barrier = pltpu.get_barrier_semaphore()
    who = place.partners()
    for dev in who:
        pl.semaphore_signal(barrier, inc=1, device_id=dev, device_id_type=MESH)
    pl.semaphore_wait(barrier, len(who))


def copy_to(src, dst, send, recv, dev):
    return pltpu.make_async_remote_copy(
        src_ref=src, dst_ref=dst, send_sem=send, recv_sem=recv, device_id=dev, device_id_type=MESH
    )


class Gather:
    def __init__(self, place, shard, got, send, recv, local, order):
        self.p, self.shard, self.got, self.order = place, shard, got, order
        self.send, self.recv, self.local = send, recv, local

    @staticmethod
    def count(n_dp, n_fsdp):
        return n_fsdp // 2 - 1 + 1 + n_dp // 2 - 1 + 1

    def own(self):
        p = self.p
        return pltpu.make_async_copy(self.shard, self.got.at[p.dh, p.dl, p.fh, p.fl], self.local)

    def stage(self, k):
        p, g = self.p, self.got
        if k == 0:
            out = []
            for o in range(1, p.m):
                to = p.dev(fh=lax.rem(p.fh + o, p.m))
                dst = g.at[p.dh, p.dl, p.fh, p.fl]
                out.append(copy_to(self.shard, dst, self.send.at[o - 1], self.recv.at[o - 1], to))
            return out
        i = p.m - 1
        if k == 3:
            ref = g.at[:, p.dl]
            return [copy_to(ref, ref, self.send.at[i], self.recv.at[i], p.dev(dl=1 - p.dl))]
        if (k == 1) == (self.order == "x"):
            ref = g.at[p.dh, p.dl, :, p.fl] if k == 1 else g.at[:, p.dl, :, p.fl]
            return [copy_to(ref, ref, self.send.at[i + 1], self.recv.at[i + 1], p.dev(fl=1 - p.fl))]
        ref = g.at[p.dh, p.dl, :, p.fl] if k == 1 else g.at[p.dh, p.dl]
        out = []
        for o in range(1, p.nh):
            to = p.dev(dh=lax.rem(p.dh + o, p.nh))
            out.append(copy_to(ref, ref, self.send.at[i + 1 + o], self.recv.at[i + 1 + o], to))
        return out

    def start(self, k):
        for c in self.stage(k):
            c.start()

    def wait(self, k):
        if k == 0:
            self.own().wait()
        for c in self.stage(k):
            c.wait()

    def turn(self, k):
        self.wait(k)
        self.start(k + 1)


def front_kernel(
    ways,
    plan,
    len_ref,
    tok_ref,
    wqkv,
    win,
    wback,
    wout,
    vec_in,
    bias_in,
    band_ref,
    hm_ref,
    qkv_ref,
    near_ref,
    fa_ref,
    fb_ref,
    rn_ref,
    p_ref,
    m1_ref,
    m2_ref,
    c_ref,
    w_ref,
    vec_ref,
    bin_ref,
    g_in,
    g_back,
    g_out,
    all_s,
    st_ref,
    t_ref,
    ga,
    gb,
    small,
    g_small,
    send,
    recv,
    local,
):
    step = pl.program_id(0)
    steps = pl.num_programs(0) // 2
    rows, width = tok_ref.shape
    groups = width // GW
    head = width // HEADS
    scale = head ** (-0.5)
    length = len_ref[0, 0]
    n_dp, n_fsdp = ways
    cols = vec_in.shape[1]
    place = Place(n_dp, n_fsdp)
    part = ga.shape[-1]
    half_in = win.shape[1] // 2
    half_back = wback.shape[0] // 2

    def piece(j, shard, got, order):
        return Gather(place, shard, got, send.at[j], recv.at[j], local.at[j], order)

    first = [
        piece(0, small, g_small, "x"),
        piece(1, wqkv.at[:, pl.ds(0, part)], ga, "x"),
        piece(2, wqkv.at[:, pl.ds(part, wqkv.shape[1] - part)], gb, "y"),
    ]
    rest = []
    for i in range(2):
        cut = pl.ds(i * half_in, half_in)
        rest.append(piece(3 + i, win.at[:, cut], g_in.at[:, :, :, :, :, cut], "x"))
    for i in range(2):
        cut = pl.ds(i * half_back, half_back)
        rest.append(piece(5 + i, wback.at[cut], g_back.at[:, :, :, :, cut], "y"))
    rest.append(piece(7, wout, g_out, "y"))
    sets = [[rest[0], rest[2]], [rest[1], rest[3], rest[4]]]

    @pl.when(step == 0)
    def _():
        small[...] = jnp.zeros_like(small)
        small[:2, :cols] = vec_in[...]
        small[2:3, :cols] = bias_in[...]
        for x in first + rest:
            x.own().start()
        greet(place)
        for x in first:
            x.start(0)
        for k in range(3):
            for x in first:
                x.turn(k)
            if k == 1:
                for x in sets[0] + sets[1]:
                    x.start(0)
        st_ref[...] = jnp.zeros_like(st_ref)
        t_ref[...] = jnp.zeros_like(t_ref)
        all_s[:HALO] = jnp.zeros((HALO, 3 * width), bf16)
        all_s[HALO + steps * rows :] = jnp.zeros((HALO, 3 * width), bf16)
        for x in first:
            x.wait(3)
        join_pairs(w_ref, ga, 0, wqkv.shape[1])
        join_pairs(w_ref, gb, part, wqkv.shape[1])
        lane = lax.broadcasted_iota(jnp.int32, (128, width), 0)
        col = lax.broadcasted_iota(jnp.int32, (128, width), 1)

        def place_small(f, total):
            spot = ((lane + f * cols == col) & (lane < cols)).astype(bf16)
            block = jnp.concatenate(
                [g_small[d // 2, d % 2, f // 2, lax.rem(f, 2)] for d in range(n_dp)], axis=0
            )
            return total + nn(block, spot)

        total = lax.fori_loop(0, n_fsdp, place_small, jnp.zeros((16 * n_dp, width), f32))
        for d in range(n_dp):
            vec_ref[2 * d : 2 * d + 2] = total[16 * d : 16 * d + 2]
            bin_ref[0:1, d * width : (d + 1) * width] = total[16 * d + 2 : 16 * d + 3]

    for at, moves in plan.items():

        @pl.when(step == at)
        def _(moves=moves):
            for which, k in moves:
                for x in sets[which]:
                    if k < 3:
                        x.turn(k)
                    else:
                        x.wait(k)

    @pl.when(step < steps)
    def _():
        z, _ = moments(tok_ref[...].astype(f32))
        h = (z * vec_ref[0:1] + vec_ref[1:2]).astype(bf16)
        lo = pl.multiple_of(HALO + step * rows, HALO)
        q = nn(h, w_ref[:, :width]).astype(bf16)
        qkv_ref[:, :width] = q
        all_s[pl.ds(lo, rows), :width] = q
        valid = row_valid(step, rows, GW, length)
        for g in range(groups):
            kc = slice(width + g * GW, width + (g + 1) * GW)
            vc = slice(2 * width + g * GW, 2 * width + (g + 1) * GW)
            k = nn(h, w_ref[:, kc]).astype(bf16)
            v = nn(h, w_ref[:, vc]).astype(bf16)
            qkv_ref[:, kc] = k
            qkv_ref[:, vc] = v
            all_s[pl.ds(lo, rows), kc] = k
            all_s[pl.ds(lo, rows), vc] = v
            kw = k.astype(f32)
            phi = jnp.where(valid, lift(kw), 0.0)
            bent = jnp.where(valid, jnp.tanh(kw), 0.0)
            both = jnp.concatenate([phi.astype(bf16), bent.astype(bf16)], axis=1)
            st_ref[g] += tn(v, both)
            t_ref[g] += fold8(phi)

    @pl.when(step == steps - 1)
    def _():
        mask = same_head(head).astype(f32)
        inv_len = 1.0 / length.astype(f32)
        ones = jnp.ones((8, GW), f32)
        for g in range(groups):
            tb = jnp.sum(t_ref[g], axis=0, keepdims=True) * mask
            s1 = st_ref[g][:, :GW] * mask
            s2 = st_ref[g][:, GW:] * mask
            c_col = jnp.sum(s1, axis=1, keepdims=True) / jnp.sum(tb, axis=1, keepdims=True)
            c_row = nt_exact(ones, s1) / nt_exact(ones, tb)
            m1_ref[g, :GW] = (s1 - c_col * tb).astype(bf16)
            m1_ref[g, GW:] = tb.astype(bf16)
            m2_ref[g] = (s2 * inv_len).astype(bf16)
            c_ref[g] = c_row

    @pl.when(step >= steps)
    def _():
        hm = hm_ref[...]
        at = (step - steps) * rows
        for b in range(rows // QB):
            base = at + b * QB - HALO
            key = base + lax.broadcasted_iota(jnp.int32, (KW, GW), 0)
            bias = jnp.where((key >= 0) & (key < length), band_ref[...], -1e30)
            here = pl.ds(pl.multiple_of(at + b * QB + HALO, HALO), QB)
            window = pl.ds(pl.multiple_of(at + b * QB, QB), KW)
            for g in range(groups):
                cut = slice(g * GW, (g + 1) * GW)
                kc = slice(width + g * GW, width + (g + 1) * GW)
                vc = slice(2 * width + g * GW, 2 * width + (g + 1) * GW)
                qs = spread_rows(all_s[here, cut] * scale, hm)
                s = nt(all_s[window, kc], qs) + bias
                e = jnp.exp(s - jnp.max(s, axis=0, keepdims=True))
                p = (e * (1.0 / jnp.sum(e, axis=0, keepdims=True))).astype(bf16)
                p_ref[b, :, cut] = p
                o = tn(p, all_s[window, vc])
                near_ref[b * QB : (b + 1) * QB, cut] = pick_heads(o, head).astype(bf16)
        for g in range(groups):
            cut = slice(g * GW, (g + 1) * GW)
            q = all_s[pl.ds(pl.multiple_of(at + HALO, HALO), rows), cut].astype(f32)
            both = nt(lift(q).astype(bf16), m1_ref[g])
            rn = 1.0 / both[:, GW:]
            rn_ref[:, cut] = rn.astype(bf16)
            fa_ref[:, cut] = (both[:, :GW] * rn).astype(bf16)
            fb_ref[:, cut] = nt(jnp.tanh(q).astype(bf16), m2_ref[g]).astype(bf16)


def join_pairs(ref, got, lo, step):
    nh, _, m, _, r, c = got.shape
    for d in range(2 * nh):
        for f in range(2 * m):
            ref[f * r : (f + 1) * r, d * step + lo : d * step + lo + c] = got[d // 2, d % 2, f // 2, f % 2]


def front_pass(ways, length, tokens, w_qkv, w_in, w_back, w_out, vec, bias, tile, plan):
    rows, width = tokens.shape
    groups = width // GW
    n_dp, n_fsdp = ways
    nh, m = n_dp // 2, n_fsdp // 2
    steps = rows // tile
    head = width // HEADS
    part = first_part(w_qkv.shape[1])
    const = lambda *shape: pl.BlockSpec(shape, lambda i: (0,) * len(shape))
    early = lambda i: (jnp.minimum(i, steps - 1), 0)
    late = pl.BlockSpec((tile, width), lambda i: (jnp.maximum(i - steps, 0), 0))
    hbm = pl.BlockSpec(memory_space=pl.ANY)
    sds = jax.ShapeDtypeStruct
    got = lambda r, c: (nh, 2, m, 2, r, c)
    hidden = w_in.shape[1] * n_dp
    pieces = 8
    per = Gather.count(n_dp, n_fsdp)
    return pl.pallas_call(
        functools.partial(front_kernel, ways, plan),
        grid=(2 * steps,),
        in_specs=[
            pl.BlockSpec(memory_space=pltpu.SMEM),
            pl.BlockSpec((tile, width), early),
            hbm,
            hbm,
            hbm,
            hbm,
            const(*vec.shape),
            const(*bias.shape),
            const(KW, GW),
            const(GW, GW),
        ],
        out_specs=[
            pl.BlockSpec((tile, 3 * width), early),
            late,
            late,
            late,
            late,
            pl.BlockSpec((tile // QB, KW, width), lambda i: (jnp.maximum(i - steps, 0), 0, 0)),
            const(groups, 2 * GW, GW),
            const(groups, GW, GW),
            const(groups, 8, GW),
            const(width, 3 * width),
            const(8, width),
            const(1, hidden),
            hbm,
            hbm,
            hbm,
        ],
        out_shape=[sds((rows, 3 * width), bf16)]
        + [sds((rows, width), bf16)] * 4
        + [
            sds((rows // QB, KW, width), bf16),
            sds((groups, 2 * GW, GW), bf16),
            sds((groups, GW, GW), bf16),
            sds((groups, 8, GW), f32),
            sds((width, 3 * width), bf16),
            sds((8, width), f32),
            sds((1, hidden), f32),
            sds(got(*w_in.shape), bf16),
            sds(got(*w_back.shape), bf16),
            sds(got(*w_out.shape), bf16),
        ],
        scratch_shapes=[
            pltpu.VMEM((rows + 2 * HALO, 3 * width), bf16),
            pltpu.VMEM((groups, GW, 2 * GW), f32),
            pltpu.VMEM((groups, 8, GW), f32),
            pltpu.VMEM(got(w_qkv.shape[0], part), bf16),
            pltpu.VMEM(got(w_qkv.shape[0], w_qkv.shape[1] - part), bf16),
            pltpu.VMEM((16, 128), bf16),
            pltpu.VMEM(got(16, 128), bf16),
            pltpu.SemaphoreType.DMA((pieces, per)),
            pltpu.SemaphoreType.DMA((pieces, per)),
            pltpu.SemaphoreType.DMA((pieces,)),
        ],
        compiler_params=pltpu.CompilerParams(
            collective_id=0, has_side_effects=True, vmem_limit_bytes=VMEM_LIMIT
        ),
        cost_estimate=pl.CostEstimate(
            flops=2 * rows * width * 8 * width, bytes_accessed=rows * width * 24, transcendentals=0
        ),
        name="front_pass",
    )(
        length,
        tokens,
        w_qkv,
        w_in,
        w_back,
        w_out,
        vec,
        bias,
        jnp.asarray(band_table(head)),
        jnp.asarray(head_table(head), bf16),
    )


def ffn_kernel(
    chunk,
    len_ref,
    tok_ref,
    cot_ref,
    near_ref,
    fa_ref,
    fb_ref,
    rn_ref,
    q_ref,
    c_ref,
    vec_ref,
    bin_ref,
    gw_out,
    gw_in,
    gw_back,
    out_ref,
    datt_ref,
    dmix_ref,
    dn_ref,
    gin_ref,
    gback_ref,
    gout_ref,
    gvec_ref,
    gbias_ref,
    m3_ref,
    m4_ref,
    dt_ref,
    a_in,
    a_back,
    a_out,
    a_st,
    a_bent,
    wout_ref,
    win_ref,
    wback_ref,
):
    step = pl.program_id(0)
    rows, width = tok_ref.shape
    hidden = win_ref.shape[1]
    groups = width // GW
    head = width // HEADS
    length = len_ref[0, 0]

    @pl.when(step == 0)
    def _():
        join_blocks(wout_ref, gw_out)
        join_blocks(win_ref, gw_in)
        join_blocks(wback_ref, gw_back)
        a_in[...] = jnp.zeros_like(a_in)
        a_back[...] = jnp.zeros_like(a_back)
        a_out[...] = jnp.zeros_like(a_out)
        a_st[...] = jnp.zeros_like(a_st)
        a_bent[...] = jnp.zeros_like(a_bent)
        gvec_ref[...] = jnp.zeros_like(gvec_ref)
        gbias_ref[...] = jnp.zeros_like(gbias_ref)

    c_row = jnp.concatenate([c_ref[g, 0:1] for g in range(groups)], axis=1)
    near = near_ref[...].astype(f32)
    fac = fa_ref[...].astype(f32)
    far_b = fb_ref[...].astype(f32)
    mixed = (
        vec_ref[5:6] * near + vec_ref[6:7] * (fac + c_row) + vec_ref[7:8] * far_b
    ).astype(bf16)
    resid = tok_ref[...].astype(f32) + nn(mixed, wout_ref[...])
    z2, r2 = moments(resid)
    h2 = (z2 * vec_ref[2:3] + vec_ref[3:4]).astype(bf16)
    valid = row_valid(step, rows, width, length)
    seed = jnp.where(valid, cot_ref[...].astype(f32), 0.0)
    d_ffn = seed.astype(bf16)
    s0 = math.sqrt(2.0 / math.pi)
    s1 = s0 * 0.044715
    ffn = jnp.zeros((rows, width), f32)
    dh2 = jnp.zeros((rows, width), f32)
    for lo in range(0, hidden, chunk):
        cols = slice(lo, lo + chunk)
        x = nn(h2, win_ref[:, cols]) + bin_ref[0:1, cols]
        x2 = x * x
        t = jnp.tanh(x * (s0 + s1 * x2))
        half = 0.5 + 0.5 * t
        act = x * half
        slope = half + (act - act * half) * (2 * s0 + 6 * s1 * x2)
        act = act.astype(bf16)
        ffn += nn(act, wback_ref[cols, :])
        a_back[:, cols] += tn(d_ffn, act)
        d_pre = slope * nt(d_ffn, wback_ref[cols, :])
        gbias_ref[:, cols] += fold8(d_pre)
        d_pre = d_pre.astype(bf16)
        a_in[:, cols] += tn(h2, d_pre)
        dh2 += nt(d_pre, win_ref[:, cols])
    out_ref[...] = jnp.where(valid, resid + ffn + vec_ref[4:5], 0.0).astype(bf16)
    gvec_ref[2] += fold8(dh2 * z2)
    gvec_ref[3] += fold8(dh2)
    gvec_ref[4] += fold8(seed)
    dz = dh2 * vec_ref[2:3]
    d_resid = seed + r2 * (
        dz
        - jnp.mean(dz, axis=-1, keepdims=True)
        - z2 * jnp.mean(dz * z2, axis=-1, keepdims=True)
    )
    d_attn = d_resid.astype(bf16)
    datt_ref[...] = d_attn
    a_out[...] += tn(mixed, d_attn)
    d_mix = nt(d_attn, wout_ref[...])
    dmix_ref[...] = d_mix.astype(bf16)
    gvec_ref[5] += fold8(d_mix * near)
    gvec_ref[6] += fold8(d_mix * fac)
    gvec_ref[7] += fold8(d_mix * far_b)
    gvec_ref[0] += fold8(d_mix)
    d_num = (vec_ref[6:7] * d_mix * rn_ref[...].astype(f32)).astype(bf16)
    dn_ref[...] = d_num
    d_den = (d_num.astype(f32) * fac).astype(bf16)
    d_far = (vec_ref[7:8] * d_mix).astype(bf16)
    for g in range(groups):
        cols = slice(g * GW, (g + 1) * GW)
        q = q_ref[:, cols].astype(f32)
        a_st[g] += tn(lift(q).astype(bf16), jnp.concatenate([d_num[:, cols], d_den[:, cols]], axis=1))
        a_bent[g] += tn(jnp.tanh(q).astype(bf16), d_far[:, cols])

    @pl.when(step == pl.num_programs(0) - 1)
    def _():
        mask = same_head(head).astype(f32)
        inv_len = 1.0 / length.astype(f32)
        ones = jnp.ones((8, GW), f32)
        for g in range(groups):
            m3_ref[g] = (a_st[g][:, :GW] * mask).astype(bf16)
            m4_ref[g] = (a_bent[g] * mask * inv_len).astype(bf16)
            dt_ref[g] = -nt_exact(ones, a_st[g][:, GW:] * mask)
        cut_blocks(gin_ref, a_in)
        cut_blocks(gback_ref, a_back, swap=True)
        cut_blocks(gout_ref, a_out)
        gvec_ref[6] += gvec_ref[0] * c_row


def third_pass(ways, length, tokens, cot, near, fa, fb, rn, qkv, c, vecs, b_in, w_out, w_in, w_back, tile, chunk):
    rows, width = tokens.shape
    hidden = w_in.shape[0] * w_in.shape[3]
    groups = width // GW
    n_dp, n_fsdp = ways
    const = lambda *shape: pl.BlockSpec(shape, lambda i: (0,) * len(shape))
    block = pl.BlockSpec((tile, width), lambda i: (i, 0))
    sds = jax.ShapeDtypeStruct
    return pl.pallas_call(
        functools.partial(ffn_kernel, chunk),
        grid=(rows // tile,),
        in_specs=[pl.BlockSpec(memory_space=pltpu.SMEM)]
        + [block] * 7
        + [
            const(groups, 8, GW),
            const(8, width),
            const(1, hidden),
            const(*w_out.shape),
            const(*w_in.shape),
            const(*w_back.shape),
        ],
        out_specs=[block] * 4
        + [
            const(n_dp, n_fsdp, width // n_fsdp, hidden // n_dp),
            const(n_dp, n_fsdp, width // n_dp, hidden // n_fsdp),
            const(n_dp, n_fsdp, width // n_fsdp, width // n_dp),
            const(8, 8, width),
            const(8, hidden),
            const(groups, GW, GW),
            const(groups, GW, GW),
            const(groups, 8, GW),
        ],
        out_shape=[sds((rows, width), bf16)] * 4
        + [
            sds((n_dp, n_fsdp, width // n_fsdp, hidden // n_dp), bf16),
            sds((n_dp, n_fsdp, width // n_dp, hidden // n_fsdp), bf16),
            sds((n_dp, n_fsdp, width // n_fsdp, width // n_dp), bf16),
            sds((8, 8, width), f32),
            sds((8, hidden), f32),
            sds((groups, GW, GW), bf16),
            sds((groups, GW, GW), bf16),
            sds((groups, 8, GW), f32),
        ],
        scratch_shapes=[
            pltpu.VMEM((width, hidden), f32),
            pltpu.VMEM((width, hidden), f32),
            pltpu.VMEM((width, width), f32),
            pltpu.VMEM((groups, GW, 2 * GW), f32),
            pltpu.VMEM((groups, GW, GW), f32),
            pltpu.VMEM((width, width), bf16),
            pltpu.VMEM((width, hidden), bf16),
            pltpu.VMEM((hidden, width), bf16),
        ],
        compiler_params=pltpu.CompilerParams(vmem_limit_bytes=VMEM_LIMIT),
        cost_estimate=pl.CostEstimate(
            flops=2 * rows * width * (6 * hidden + 4 * width),
            bytes_accessed=rows * width * 22,
            transcendentals=0,
        ),
        name="third_pass",
    )(length, tokens, cot, near, fa, fb, rn, qkv, c, vecs, b_in, w_out, w_in, w_back)


class Scatter:
    def __init__(self, place, src, out, bufs, send, recv, local, order):
        self.p, self.src, self.out, self.order = place, src, out, order
        self.acc, self.r0, self.r1, self.r2, self.r3 = bufs
        self.send, self.recv, self.local = send, recv, local

    @staticmethod
    def count(n_dp, n_fsdp):
        return 1 + 1 + (n_dp // 2 - 1) + (n_fsdp // 2 - 1)

    @staticmethod
    def scratch(n_dp, n_fsdp, r, c, order, dtype):
        nh, m = n_dp // 2, n_fsdp // 2
        if order == "x":
            one, two = (nh, m, r, c), (nh - 1, m, r, c)
        else:
            one, two = (nh - 1, m, 2, r, c), (m, r, c)
        shapes = [(nh, m, 2, r, c), (nh, m, 2, r, c), one, two, (m - 1, r, c)]
        return [pltpu.VMEM(s, dtype) for s in shapes]

    def own(self):
        return pltpu.make_async_copy(self.src.at[:, self.p.dl], self.acc, self.local)

    def stage(self, k):
        p = self.p
        if k == 0:
            ref = self.src.at[:, 1 - p.dl]
            return [copy_to(ref, self.r0, self.send.at[0], self.recv.at[0], p.dev(dl=1 - p.dl))]
        if k == 3:
            i = p.nh
            out = []
            for o in range(1, p.m):
                fh = lax.rem(p.fh + o, p.m)
                out.append(
                    copy_to(self.acc.at[p.dh, fh, p.fl], self.r3.at[o - 1], self.send.at[i + o], self.recv.at[i + o],
                            p.dev(fh=fh))
                )
            return out
        if (k == 1) == (self.order == "x"):
            ref = self.acc.at[:, :, 1 - p.fl] if k == 1 else self.acc.at[p.dh, :, 1 - p.fl]
            dst = self.r1 if k == 1 else self.r2
            return [copy_to(ref, dst, self.send.at[1], self.recv.at[1], p.dev(fl=1 - p.fl))]
        out = []
        for o in range(1, p.nh):
            dh = lax.rem(p.dh + o, p.nh)
            ref = self.acc.at[dh] if k == 1 else self.acc.at[dh, :, p.fl]
            dst = self.r1.at[o - 1] if k == 1 else self.r2.at[o - 1]
            out.append(copy_to(ref, dst, self.send.at[1 + o], self.recv.at[1 + o], p.dev(dh=dh)))
        return out

    def start(self, k):
        for c in self.stage(k):
            c.start()

    def turn(self, k):
        if k == 0:
            self.own().wait()
        for c in self.stage(k):
            c.wait()
        self.add(k)
        if k < 3:
            self.start(k + 1)

    def add(self, k):
        p, acc = self.p, self.acc
        nh, m = p.nh, p.m
        dt = acc.dtype

        def put(index, others):
            total = acc[index].astype(f32)
            for o in others:
                total = total + o.astype(f32)
            acc[index] = total.astype(dt)

        if k == 3:
            total = acc[p.dh, p.fh, p.fl].astype(f32)
            for o in range(1, m):
                total = total + self.r3[o - 1].astype(f32)
            self.out[...] = total
            return

        @pl.loop(0, m)
        def _(i):
            if k == 0:
                for a in range(nh):
                    for b in range(2):
                        put((a, i, b), [self.r0[a, i, b]])
            elif k == 1 and self.order == "x":
                for a in range(nh):
                    put((a, i, p.fl), [self.r1[a, i]])
            elif k == 1:
                for b in range(2):
                    put((p.dh, i, b), [self.r1[o - 1, i, b] for o in range(1, nh)])
            elif self.order == "x":
                put((p.dh, i, p.fl), [self.r2[o - 1, i] for o in range(1, nh)])
            else:
                put((p.dh, i, p.fl), [self.r2[i]])


def back_kernel(
    ways,
    plan,
    len_ref,
    q_ref,
    k_lo,
    k_ref,
    k_hi,
    v_lo,
    v_ref,
    v_hi,
    p_ref,
    dmix_ref,
    qkv_ref,
    tok_ref,
    datt_ref,
    dn_ref,
    fa_ref,
    dmp_ref,
    m1_ref,
    m2_ref,
    m3_ref,
    m4_ref,
    dt_ref,
    c_ref,
    vec_ref,
    w_ref,
    hm_ref,
    gv_ref,
    gbias_ref,
    s_in,
    s_back,
    s_out,
    dtok_ref,
    oqkv_ref,
    oin_ref,
    oback_ref,
    oout_ref,
    ovec_ref,
    obias_ref,
    kk,
    vv,
    dq_s,
    dk_s,
    dv_s,
    a_qkv,
    gvec_ref,
    ga_ref,
    gb_ref,
    gs_ref,
    rows_s,
    back_t,
    small_o,
    *rest,
):
    step = pl.program_id(0)
    steps = pl.num_programs(0) - 1
    rows, width = q_ref.shape
    groups = width // GW
    head = width // HEADS
    scale = head ** (-0.5)
    length = len_ref[0, 0]
    place = Place(*ways)
    n_dp, n_fsdp = ways
    cols = ovec_ref.shape[1]
    part = ga_ref.shape[-1]
    send, recv, local = rest[30:]

    def piece(j, src, out, order):
        return Scatter(place, src, out, rest[5 * j : 5 * j + 5], send.at[j], recv.at[j], local.at[j], order)

    ffn = [
        piece(0, s_in, oin_ref, "x"),
        piece(1, s_back, back_t, "y"),
        piece(2, s_out, oout_ref, "y"),
    ]
    last = [
        piece(3, ga_ref, oqkv_ref.at[:, pl.ds(0, part)], "x"),
        piece(4, gb_ref, oqkv_ref.at[:, pl.ds(part, oqkv_ref.shape[1] - part)], "y"),
        piece(5, gs_ref, small_o, "x"),
    ]

    @pl.when(step == 0)
    def _():
        dk_s[: 2 * HALO] = jnp.zeros((2 * HALO, width), f32)
        dv_s[: 2 * HALO] = jnp.zeros((2 * HALO, width), f32)
        a_qkv[...] = jnp.zeros_like(a_qkv)
        gvec_ref[...] = jnp.zeros_like(gvec_ref)
        for x in ffn:
            x.own().start()
        greet(place)
        for x in ffn:
            x.start(0)

    for at, moves in plan.items():

        @pl.when(step == at)
        def _(moves=moves):
            for k in moves:
                for x in ffn:
                    x.turn(k)

    @pl.when(step < steps)
    def _():
        kk[:HALO] = k_lo[...]
        kk[HALO : HALO + rows] = k_ref[...]
        kk[HALO + rows :] = k_hi[...]
        vv[:HALO] = v_lo[...]
        vv[HALO : HALO + rows] = v_ref[...]
        vv[HALO + rows :] = v_hi[...]
        hm = hm_ref[...]
        slot = lax.rem(step, 2)
        for g in range(groups):
            cut = slice(g * GW, (g + 1) * GW)
            for b in range(rows // QB):
                here = slice(b * QB, (b + 1) * QB)
                window = slice(b * QB, b * QB + KW)
                qs = spread_rows(q_ref[here, cut] * scale, hm)
                d_near = (vec_ref[5:6, cut] * dmix_ref[here, cut].astype(f32)).astype(bf16)
                ds = spread_rows(d_near, hm)
                p = p_ref[b, :, cut]
                pw = p.astype(f32)
                t = pw * nt(vv[window, cut], ds)
                d_s = (t - pw * jnp.sum(t, axis=0, keepdims=True)).astype(bf16)
                dk = nn(d_s, qs)
                dv = nn(p, ds)
                dq_s[slot, here, cut] = pick_heads(tn(d_s, kk[window, cut]), head) * scale
                lo = pl.ds(pl.multiple_of(lax.rem(step * rows + b * QB, 3 * rows), QB), QB)
                hi = pl.ds(pl.multiple_of(lax.rem(step * rows + (b + 1) * QB, 3 * rows), QB), QB)
                dk_s[lo, cut] += dk[:QB]
                dk_s[hi, cut] = dk[QB:]
                dv_s[lo, cut] += dv[:QB]
                dv_s[hi, cut] = dv[QB:]

    @pl.when(step > 0)
    def _():
        slot = lax.rem(step + 1, 2)
        z1, r1 = moments(tok_ref[...].astype(f32))
        h1 = (z1 * vec_ref[0:1] + vec_ref[1:2]).astype(bf16)
        valid = row_valid(step - 1, rows, GW, length)
        lo = pl.ds(pl.multiple_of(lax.rem((step - 1) * rows, 3 * rows) + HALO, HALO), rows - HALO)
        hi = pl.ds(pl.multiple_of(lax.rem(step * rows, 3 * rows), HALO), HALO)
        dqs, dks, dvs = [], [], []
        for g in range(groups):
            cut = slice(g * GW, (g + 1) * GW)
            q = qkv_ref[:, g * GW : (g + 1) * GW].astype(f32)
            k = qkv_ref[:, width + g * GW : width + (g + 1) * GW].astype(f32)
            v = qkv_ref[:, 2 * width + g * GW : 2 * width + (g + 1) * GW]
            d_num = dn_ref[:, cut]
            d_den = (d_num.astype(f32) * -fa_ref[:, cut].astype(f32)).astype(bf16)
            d_far = (vec_ref[7:8, cut] * dmp_ref[:, cut].astype(f32)).astype(bf16)
            bent_q = jnp.tanh(q)
            dq = (
                dq_s[slot, :, cut]
                + nn(jnp.concatenate([d_num, d_den], axis=1), m1_ref[g]) * jnp.minimum(lift(q), 1.0)
                + nn(d_far, m2_ref[g]) * (1.0 - bent_q * bent_q)
            )
            lift_k = lift(k)
            bent_k = jnp.tanh(k)
            v_cen = (v.astype(f32) - c_ref[g, 0:1]).astype(bf16)
            dk = (nt(v_cen, m3_ref[g]) + dt_ref[g, 0:1]) * jnp.minimum(lift_k, 1.0) + nt(
                v, m4_ref[g]
            ) * (1.0 - bent_k * bent_k)
            both = jnp.concatenate([lift_k.astype(bf16), bent_k.astype(bf16)], axis=1)
            dv = nn(both, jnp.concatenate([m3_ref[g], m4_ref[g]], axis=0))
            dqs.append(dq.astype(bf16))
            dks.append((jnp.concatenate([dk_s[lo, cut], dk_s[hi, cut]], axis=0) + jnp.where(valid, dk, 0.0)).astype(bf16))
            dvs.append((jnp.concatenate([dv_s[lo, cut], dv_s[hi, cut]], axis=0) + jnp.where(valid, dv, 0.0)).astype(bf16))
        d_qkv = jnp.concatenate(dqs + dks + dvs, axis=1)
        a_qkv[...] += tn(h1, d_qkv)
        dh1 = nt(d_qkv, w_ref[...])
        gvec_ref[0] += fold8(dh1 * z1)
        gvec_ref[1] += fold8(dh1)
        dz = dh1 * vec_ref[0:1]
        dtok_ref[...] = (
            datt_ref[...].astype(f32)
            + r1
            * (
                dz
                - jnp.mean(dz, axis=-1, keepdims=True)
                - z1 * jnp.mean(dz * z1, axis=-1, keepdims=True)
            )
        ).astype(bf16)

    @pl.when(step == steps)
    def _():
        oback_ref[...] = back_t[...].T
        step_cols = oqkv_ref.shape[1]
        cut_pairs(ga_ref, a_qkv, 0, step_cols)
        cut_pairs(gb_ref, a_qkv, part, step_cols)
        gs_ref[...] = jnp.zeros_like(gs_ref)
        rows_s[0:2] = jnp.sum(gvec_ref[...], axis=1)
        rows_s[2:8] = jnp.sum(gv_ref[2:8], axis=1)
        bias = jnp.sum(gbias_ref[...], axis=0, keepdims=True)
        for d in range(n_dp):
            pair = rows_s[2 * d : 2 * d + 2]
            for f in range(n_fsdp):
                spot = slice(f * cols, (f + 1) * cols)
                gs_ref[d // 2, d % 2, f // 2, f % 2, 0:2, :cols] = pair[:, spot]
                gs_ref[d // 2, d % 2, f // 2, f % 2, 2:3, :cols] = bias[:, d * width + f * cols : d * width + (f + 1) * cols]
        for x in last:
            x.own().start()
            x.start(0)
        for k in range(4):
            for x in last:
                x.turn(k)
        ovec_ref[...] = small_o[0:2, :cols]
        obias_ref[...] = small_o[2:3, :cols]


def cut_pairs(ref, acc, lo, step):
    nh, _, m, _, r, c = ref.shape
    for d in range(2 * nh):
        for f in range(2 * m):
            block = acc[f * r : (f + 1) * r, d * step + lo : d * step + lo + c]
            ref[d // 2, d % 2, f // 2, f % 2] = block.astype(ref.dtype)


def back_pass(
    ways, length, qkv, p, d_mix, tokens, d_attn, d_num, fa, m1, m2, m3, m4, dt, c, vecs, w_qkv, gv, gbias, s_in, s_back, s_out, tile, plan
):
    rows, width = tokens.shape
    groups = width // GW
    steps = rows // tile
    n_dp, n_fsdp = ways
    r, c_all = width // n_fsdp, 3 * width // n_dp
    part = first_part(c_all)
    nh, m = n_dp // 2, n_fsdp // 2
    hbm = pl.BlockSpec(memory_space=pl.ANY)
    back_shape = s_back.shape[-2:]
    outs = [
        (r, c_all),
        s_in.shape[-2:],
        back_shape[::-1],
        s_out.shape[-2:],
        (2, width // n_fsdp),
        (1, gbias.shape[1] // (n_dp * n_fsdp)),
    ]
    kinds = [
        (*s_in.shape[-2:], "x", bf16),
        (*back_shape, "y", bf16),
        (*s_out.shape[-2:], "y", bf16),
        (r, part, "x", bf16),
        (r, c_all - part, "y", bf16),
        (8, 128, "x", f32),
    ]
    bufs = [b for k in kinds for b in Scatter.scratch(n_dp, n_fsdp, *k)]
    per = Scatter.count(n_dp, n_fsdp)
    got = lambda *s: (nh, 2, m, 2, *s)
    const = lambda *shape: pl.BlockSpec(shape, lambda i: (0,) * len(shape))
    now = lambda i: jnp.minimum(i, steps - 1)
    old = lambda i: jnp.maximum(i - 1, 0)
    per = tile // HALO
    last = rows // HALO - 1

    def halo(col):
        return [
            pl.BlockSpec((HALO, width), lambda i: (jnp.maximum(now(i) * per - 1, 0), col)),
            pl.BlockSpec((tile, width), lambda i: (now(i), col)),
            pl.BlockSpec((HALO, width), lambda i: (jnp.minimum((now(i) + 1) * per, last), col)),
        ]

    block = pl.BlockSpec((tile, width), lambda i: (now(i), 0))
    late = pl.BlockSpec((tile, width), lambda i: (old(i), 0))
    head = width // HEADS
    sds = jax.ShapeDtypeStruct
    return pl.pallas_call(
        functools.partial(back_kernel, ways, plan),
        grid=(steps + 1,),
        in_specs=[
            pl.BlockSpec(memory_space=pltpu.SMEM),
            block,
            *halo(1),
            *halo(2),
            pl.BlockSpec((tile // QB, KW, width), lambda i: (now(i), 0, 0)),
            block,
            pl.BlockSpec((tile, 3 * width), lambda i: (old(i), 0)),
            late,
            late,
            late,
            late,
            late,
            const(groups, 2 * GW, GW),
            const(groups, GW, GW),
            const(groups, GW, GW),
            const(groups, GW, GW),
            const(groups, 8, GW),
            const(groups, 8, GW),
            const(8, width),
            const(width, 3 * width),
            const(GW, GW),
            const(*gv.shape),
            const(*gbias.shape),
            hbm,
            hbm,
            hbm,
        ],
        out_specs=[late] + [const(*s) for s in outs],
        out_shape=[sds((rows, width), bf16)] + [sds(s, f32) for s in outs],
        scratch_shapes=[
            pltpu.VMEM((tile + 2 * HALO, width), bf16),
            pltpu.VMEM((tile + 2 * HALO, width), bf16),
            pltpu.VMEM((2, tile, width), f32),
            pltpu.VMEM((3 * tile, width), f32),
            pltpu.VMEM((3 * tile, width), f32),
            pltpu.VMEM((width, 3 * width), f32),
            pltpu.VMEM((2, 8, width), f32),
            pltpu.VMEM(got(r, part), bf16),
            pltpu.VMEM(got(r, c_all - part), bf16),
            pltpu.VMEM(got(8, 128), f32),
            pltpu.VMEM((8, width), f32),
            pltpu.VMEM(back_shape, f32),
            pltpu.VMEM((8, 128), f32),
            *bufs,
            pltpu.SemaphoreType.DMA((6, per)),
            pltpu.SemaphoreType.DMA((6, per)),
            pltpu.SemaphoreType.DMA((6,)),
        ],
        compiler_params=pltpu.CompilerParams(
            collective_id=1, has_side_effects=True, vmem_limit_bytes=VMEM_LIMIT
        ),
        cost_estimate=pl.CostEstimate(
            flops=2 * rows * width * 14 * width, bytes_accessed=rows * width * 24, transcendentals=0
        ),
        name="back_pass",
    )(
        length,
        qkv,
        qkv,
        qkv,
        qkv,
        qkv,
        qkv,
        qkv,
        p,
        d_mix,
        qkv,
        tokens,
        d_attn,
        d_num,
        fa,
        d_mix,
        m1,
        m2,
        m3,
        m4,
        dt,
        c,
        vecs,
        w_qkv,
        jnp.asarray(head_table(head), bf16),
        gv,
        gbias,
        s_in,
        s_back,
        s_out,
    )


TILE = 512
CHUNK = 512
FRONT_PLAN = {2: [(0, 0)], 4: [(0, 1), (1, 0)], 6: [(0, 2)], 7: [(1, 1)], 10: [(0, 3), (1, 2)], 13: [(1, 3)]}
BACK_PLAN = {2: [0], 4: [1], 5: [2], 7: [3]}


def shards(
    tokens, cotangent, w_qkv, w_out, w_in, w_back, vec_params, b_in, item_lengths, bucket_counts, *, ways
):
    n_dp, n_fsdp = ways
    (
        qkv,
        near,
        fa,
        fb,
        rn,
        p,
        m1,
        m2,
        c,
        qkv_w,
        vecs,
        in_bias,
        g_in,
        g_back,
        g_out,
    ) = front_pass(
        ways, item_lengths, tokens, w_qkv, w_in, w_back, w_out, vec_params, b_in[None], TILE, FRONT_PLAN
    )

    def blocks(g):
        return g.reshape(n_dp, n_fsdp, *g.shape[-2:])

    def pairs(g):
        return g.reshape(n_dp // 2, 2, n_fsdp // 2, 2, *g.shape[-2:])

    (out, d_attn, d_mix, d_num, s_in, s_back, s_out, g_vec, g_bias, m3, m4, dt) = third_pass(
        ways,
        item_lengths,
        tokens,
        cotangent,
        near,
        fa,
        fb,
        rn,
        qkv,
        c,
        vecs,
        in_bias,
        blocks(g_out),
        blocks(g_in),
        blocks(g_back),
        TILE,
        CHUNK,
    )
    d_tok, r_qkv, r_in, r_back, r_out, r_vec, r_bias = back_pass(
        ways,
        item_lengths,
        qkv,
        p,
        d_mix,
        tokens,
        d_attn,
        d_num,
        fa,
        m1,
        m2,
        m3,
        m4,
        dt,
        c,
        vecs,
        qkv_w,
        g_vec,
        g_bias,
        pairs(s_in),
        pairs(s_back),
        pairs(s_out),
        TILE,
        BACK_PLAN,
    )
    return (out, d_tok, r_qkv, r_out, r_in, r_back, r_vec, r_bias[0])


def solution(mesh):
    in_specs = (
        P(("dp", "fsdp"), None),
        P(("dp", "fsdp"), None),
        P("fsdp", "dp"),
        P("fsdp", "dp"),
        P("fsdp", "dp"),
        P("fsdp", "dp"),
        P("dp", "fsdp"),
        P(("dp", "fsdp")),
        P(("dp", "fsdp"), None),
        P(("dp", "fsdp"), None),
    )
    out_specs = (
        P(("dp", "fsdp"), None),
        P(("dp", "fsdp"), None),
        P("fsdp", "dp"),
        P("fsdp", "dp"),
        P("fsdp", "dp"),
        P("fsdp", "dp"),
        P("dp", "fsdp"),
        P(("dp", "fsdp")),
    )
    ways = (mesh.shape["dp"], mesh.shape["fsdp"])
    body = functools.partial(shards, ways=ways)
    return jax.shard_map(body, mesh=mesh, in_specs=in_specs, out_specs=out_specs, check_vma=False)
```

```python
import functools
import math

import jax
import jax.numpy as jnp
import numpy as np
from jax import lax
from jax.experimental import pallas as pl
from jax.experimental.pallas import tpu as pltpu
from jax.sharding import PartitionSpec as P

HEADS = 8
BAND = 30
QB = 64
HALO = 32
KW = QB + 2 * HALO
GW = 256

norm_eps = 1e-05
f32 = jnp.float32
bf16 = jnp.bfloat16
exact = lax.Precision.HIGHEST
VMEM_LIMIT = 60 * 1024 * 1024


def nn(a, b):
    return lax.dot_general(a, b, (((1,), (0,)), ((), ())), preferred_element_type=f32)


def nt(a, b):
    return lax.dot_general(a, b, (((1,), (1,)), ((), ())), preferred_element_type=f32)


def tn(a, b):
    return lax.dot_general(a, b, (((0,), (0,)), ((), ())), preferred_element_type=f32)


def nt_exact(a, b):
    return lax.dot_general(
        a, b, (((1,), (1,)), ((), ())), preferred_element_type=f32, precision=exact
    )


def first_part(cols):
    return 128 * ((cols // 128 + 1) // 2) if cols >= 256 else cols // 2


def lift(t):
    return jnp.where(t > 0, t + 1, jnp.exp(jnp.minimum(t, 0)))


def moments(x):
    mean = jnp.mean(x, axis=-1, keepdims=True)
    cen = x - mean
    inv = lax.rsqrt(jnp.mean(cen * cen, axis=-1, keepdims=True) + norm_eps)
    return cen * inv, inv


def fold8(x):
    return jnp.sum(x.reshape(x.shape[0] // 8, 8, x.shape[1]), axis=0)


def row_valid(step, rows, width, length):
    ids = step * rows + lax.broadcasted_iota(jnp.int32, (rows, width), 0)
    return ids < length


def same_head(head):
    r = lax.broadcasted_iota(jnp.int32, (GW, GW), 0) // head
    c = lax.broadcasted_iota(jnp.int32, (GW, GW), 1) // head
    return r == c


def spread_rows(x, mask_low):
    return jnp.concatenate([x] * (GW // QB), axis=0) * mask_low


def pick_heads(x, head):
    lane = lax.broadcasted_iota(jnp.int32, (QB, GW), 1) // head
    out = x[:QB]
    for h in range(1, GW // QB):
        out = jnp.where(lane == h, x[h * QB : (h + 1) * QB], out)
    return out


def turned(hidden, n_fsdp):
    return hidden // n_fsdp >= 128


def join_blocks(ref, got, lo=0, step=None):
    n_dp, n_fsdp, r, c = got.shape
    step = c if step is None else step
    for d in range(n_dp):
        for f in range(n_fsdp):
            ref[f * r : (f + 1) * r, d * step + lo : d * step + lo + c] = got[d, f]


def cut_blocks(ref, acc):
    n_dp, n_fsdp, r, c = ref.shape
    for d in range(n_dp):
        for f in range(n_fsdp):
            ref[d, f] = acc[f * r : (f + 1) * r, d * c : (d + 1) * c].astype(ref.dtype)


def cut_turned(ref, acc):
    n_dp, n_fsdp, r, c = ref.shape
    width, hidden = acc.shape
    wide, deep = width // n_dp, hidden // n_fsdp
    for d in range(n_dp):
        for f in range(n_fsdp):
            block = acc[d * wide : (d + 1) * wide, f * deep : (f + 1) * deep]
            ref[d, f] = (block if turned(hidden, n_fsdp) else block.T).astype(ref.dtype)


def band_table(head):
    key = np.arange(KW)[:, None] - HALO
    query = np.arange(GW)[None, :] % QB
    return np.where(np.abs(key - query) <= BAND, 0.0, -1e30).astype(np.float32)


def head_table(head):
    r = np.arange(GW)[:, None] // QB
    c = np.arange(GW)[None, :] // head
    return (r == c).astype(np.float32)


MESH = pl.DeviceIdType.MESH


class Place:
    def __init__(self, n_dp, n_fsdp):
        self.m = n_fsdp // 2
        self.nh = n_dp // 2
        d = lax.axis_index("dp")
        f = lax.axis_index("fsdp")
        self.dh, self.dl = d // 2, lax.rem(d, 2)
        self.fh, self.fl = f // 2, lax.rem(f, 2)

    def dev(self, dh=None, dl=None, fh=None, fl=None):
        dh = self.dh if dh is None else dh
        dl = self.dl if dl is None else dl
        fh = self.fh if fh is None else fh
        fl = self.fl if fl is None else fl
        return {"dp": dh * 2 + dl, "fsdp": fh * 2 + fl}

    def partners(self):
        out = [self.dev(fh=lax.rem(self.fh + o, self.m)) for o in range(1, self.m)]
        out += [self.dev(dh=lax.rem(self.dh + o, self.nh)) for o in range(1, self.nh)]
        return out + [self.dev(fl=1 - self.fl), self.dev(dl=1 - self.dl)]


def greet(place):
    barrier = pltpu.get_barrier_semaphore()
    who = place.partners()
    for dev in who:
        pl.semaphore_signal(barrier, inc=1, device_id=dev, device_id_type=MESH)
    pl.semaphore_wait(barrier, len(who))


def copy_to(src, dst, send, recv, dev):
    return pltpu.make_async_remote_copy(
        src_ref=src, dst_ref=dst, send_sem=send, recv_sem=recv, device_id=dev, device_id_type=MESH
    )


class Gather:
    def __init__(self, place, shard, got, send, recv, local, order, way=None):
        self.p, self.shard, self.got, self.order, self.way = place, shard, got, order, way
        self.send, self.recv, self.local = send, recv, local

    @staticmethod
    def count(n_dp, n_fsdp):
        return n_fsdp // 2 - 1 + 1 + n_dp // 2 - 1 + 1

    def own(self):
        p = self.p
        src = self.shard if self.way is None else self.way
        return pltpu.make_async_copy(src, self.got.at[p.dh, p.dl, p.fh, p.fl], self.local)

    def fetch(self):
        return pltpu.make_async_copy(self.shard, self.way, self.local)

    def stage(self, k):
        p, g = self.p, self.got
        if k == 0:
            out = []
            for o in range(1, p.m):
                to = p.dev(fh=lax.rem(p.fh + o, p.m))
                dst = g.at[p.dh, p.dl, p.fh, p.fl]
                out.append(copy_to(self.shard, dst, self.send.at[o - 1], self.recv.at[o - 1], to))
            return out
        i = p.m - 1
        if k == 3:
            ref = g.at[:, p.dl]
            return [copy_to(ref, ref, self.send.at[i], self.recv.at[i], p.dev(dl=1 - p.dl))]
        if (k == 1) == (self.order == "x"):
            ref = g.at[p.dh, p.dl, :, p.fl] if k == 1 else g.at[:, p.dl, :, p.fl]
            return [copy_to(ref, ref, self.send.at[i + 1], self.recv.at[i + 1], p.dev(fl=1 - p.fl))]
        ref = g.at[p.dh, p.dl, :, p.fl] if k == 1 else g.at[p.dh, p.dl]
        out = []
        for o in range(1, p.nh):
            to = p.dev(dh=lax.rem(p.dh + o, p.nh))
            out.append(copy_to(ref, ref, self.send.at[i + 1 + o], self.recv.at[i + 1 + o], to))
        return out

    def start(self, k):
        for c in self.stage(k):
            c.start()

    def wait(self, k):
        if k == 0:
            self.own().wait()
        for c in self.stage(k):
            c.wait()

    def turn(self, k):
        self.wait(k)
        self.start(k + 1)


def front_kernel(
    ways,
    plan,
    qkv_steps,
    len_ref,
    tok_ref,
    wqkv,
    win,
    wback,
    wout,
    vec_in,
    bias_in,
    band_ref,
    hm_ref,
    qkv_ref,
    near_ref,
    fa_ref,
    fb_ref,
    rn_ref,
    p_ref,
    h1t_ref,
    m1_ref,
    m2_ref,
    c_ref,
    w_ref,
    vec_ref,
    bin_ref,
    g_in,
    g_back,
    g_out,
    all_s,
    st_ref,
    t_ref,
    ga,
    gb,
    small,
    g_small,
    way_in,
    way_back,
    way_out,
    send,
    recv,
    local,
):
    step = pl.program_id(0)
    steps = qkv_steps
    rows, width = tok_ref.shape
    groups = width // GW
    head = width // HEADS
    scale = head ** (-0.5)
    length = len_ref[0, 0]
    n_dp, n_fsdp = ways
    cols = vec_in.shape[1]
    place = Place(n_dp, n_fsdp)
    part = ga.shape[-1]
    half_in = win.shape[1] // 2
    half_back = wback.shape[0] // 2

    def piece(j, shard, got, order, way=None):
        return Gather(place, shard, got, send.at[j], recv.at[j], local.at[j], order, way)

    first = [
        piece(0, small, g_small, "x"),
        piece(1, wqkv.at[:, pl.ds(0, part)], ga, "x"),
        piece(2, wqkv.at[:, pl.ds(part, wqkv.shape[1] - part)], gb, "y"),
    ]
    rest = []
    for i in range(2):
        cut = pl.ds(i * half_in, half_in)
        rest.append(piece(3 + i, win.at[:, cut], g_in.at[:, :, :, :, :, cut], "x", way_in.at[:, cut]))
    for i in range(2):
        cut = pl.ds(i * half_back, half_back)
        rest.append(piece(5 + i, wback.at[cut], g_back.at[:, :, :, :, cut], "y", way_back.at[cut]))
    rest.append(piece(7, wout, g_out, "y", way_out))
    sets = [[rest[0], rest[2]], [rest[1], rest[3], rest[4]]]

    @pl.when(step == 0)
    def _():
        small[...] = jnp.zeros_like(small)
        small[:2, :cols] = vec_in[...]
        small[2:3, :cols] = bias_in[...]
        for x in first:
            x.own().start()
        for x in rest:
            x.fetch().start()
        greet(place)
        for x in first:
            x.start(0)
        for k in range(3):
            for x in first:
                x.turn(k)
            if k == 0:
                for x in rest:
                    x.fetch().wait()
                    x.own().start()
            if k == 1:
                for x in sets[0] + sets[1]:
                    x.start(0)
        st_ref[...] = jnp.zeros_like(st_ref)
        t_ref[...] = jnp.zeros_like(t_ref)
        all_s[:HALO] = jnp.zeros((HALO, 3 * width), bf16)
        all_s[HALO + steps * rows :] = jnp.zeros((HALO, 3 * width), bf16)
        for x in first:
            x.wait(3)
        join_pairs(w_ref, ga, 0, wqkv.shape[1])
        join_pairs(w_ref, gb, part, wqkv.shape[1])
        lane = lax.broadcasted_iota(jnp.int32, (128, width), 0)
        col = lax.broadcasted_iota(jnp.int32, (128, width), 1)

        def place_small(f, total):
            spot = ((lane + f * cols == col) & (lane < cols)).astype(bf16)
            block = jnp.concatenate(
                [g_small[d // 2, d % 2, f // 2, lax.rem(f, 2)] for d in range(n_dp)], axis=0
            )
            return total + nn(block, spot)

        total = lax.fori_loop(0, n_fsdp, place_small, jnp.zeros((16 * n_dp, width), f32))
        for d in range(n_dp):
            vec_ref[2 * d : 2 * d + 2] = total[16 * d : 16 * d + 2]
            bin_ref[0:1, d * width : (d + 1) * width] = total[16 * d + 2 : 16 * d + 3]

    def advance(at, moves):
        @pl.when(step == at)
        def _():
            for which, k in moves:
                for x in sets[which]:
                    if k < 3:
                        x.turn(k)
                    else:
                        x.wait(k)

    for at, moves in plan.items():
        if at < 2 * steps:
            advance(at, moves)

    @pl.when(step < steps)
    def _():
        z, _ = moments(tok_ref[...].astype(f32))
        h = (z * vec_ref[0:1] + vec_ref[1:2]).astype(bf16)
        h1t_ref[...] = h.T
        lo = pl.multiple_of(HALO + step * rows, HALO)
        q = nn(h, w_ref[:, :width]).astype(bf16)
        qkv_ref[:, :width] = q
        all_s[pl.ds(lo, rows), :width] = q
        valid = row_valid(step, rows, GW, length)
        for g in range(groups):
            kc = slice(width + g * GW, width + (g + 1) * GW)
            vc = slice(2 * width + g * GW, 2 * width + (g + 1) * GW)
            k = nn(h, w_ref[:, kc]).astype(bf16)
            v = nn(h, w_ref[:, vc]).astype(bf16)
            qkv_ref[:, kc] = k
            qkv_ref[:, vc] = v
            all_s[pl.ds(lo, rows), kc] = k
            all_s[pl.ds(lo, rows), vc] = v
            phi = jnp.where(valid, lift(k), 0)
            bent = jnp.where(valid, jnp.tanh(k), 0)
            st_ref[g] += tn(v, jnp.concatenate([phi, bent], axis=1))
            t_ref[g] += fold8(phi.astype(f32))

    @pl.when(step == steps - 1)
    def _():
        mask = same_head(head).astype(f32)
        inv_len = 1.0 / length.astype(f32)
        ones = jnp.ones((8, GW), f32)
        for g in range(groups):
            tb = jnp.sum(t_ref[g], axis=0, keepdims=True) * mask
            s1 = st_ref[g][:, :GW] * mask
            s2 = st_ref[g][:, GW:] * mask
            c_row = (nt_exact(ones, s1) / nt_exact(ones, tb)).astype(bf16).astype(f32)
            c_col = jnp.broadcast_to(c_row[0:1], (GW, GW)).T
            m1_ref[g, :GW] = (s1 - c_col * tb).astype(bf16)
            m1_ref[g, GW:] = tb.astype(bf16)
            m2_ref[g] = (s2 * inv_len).astype(bf16)
            c_ref[g] = c_row

    @pl.when(step >= steps)
    def _():
        hm = hm_ref[...]
        at = (step - steps) * rows
        for b in range(rows // QB):
            base = at + b * QB - HALO
            key = base + lax.broadcasted_iota(jnp.int32, (KW, GW), 0)
            bias = jnp.where((key >= 0) & (key < length), band_ref[...], -1e30)
            here = pl.ds(pl.multiple_of(at + b * QB + HALO, HALO), QB)
            window = pl.ds(pl.multiple_of(at + b * QB, QB), KW)
            for g in range(groups):
                cut = slice(g * GW, (g + 1) * GW)
                kc = slice(width + g * GW, width + (g + 1) * GW)
                vc = slice(2 * width + g * GW, 2 * width + (g + 1) * GW)
                qs = spread_rows(all_s[here, cut] * scale, hm)
                s = nt(all_s[window, kc], qs) + bias
                e = jnp.exp(s - jnp.max(s, axis=0, keepdims=True))
                p = (e * (1.0 / jnp.sum(e, axis=0, keepdims=True))).astype(bf16)
                p_ref[b, :, cut] = p
                o = tn(p, all_s[window, vc])
                near_ref[b * QB : (b + 1) * QB, cut] = pick_heads(o, head).astype(bf16)
        for g in range(groups):
            cut = slice(g * GW, (g + 1) * GW)
            q = all_s[pl.ds(pl.multiple_of(at + HALO, HALO), rows), cut]
            both = nt(lift(q), m1_ref[g])
            rn = 1.0 / both[:, GW:]
            rn_ref[:, cut] = rn.astype(bf16)
            fa_ref[:, cut] = (both[:, :GW] * rn).astype(bf16)
            fb_ref[:, cut] = nt(jnp.tanh(q), m2_ref[g]).astype(bf16)

    advance(2 * steps - 1, plan[2 * steps])


def join_pairs(ref, got, lo, step):
    nh, _, m, _, r, c = got.shape
    for d in range(2 * nh):
        for f in range(2 * m):
            ref[f * r : (f + 1) * r, d * step + lo : d * step + lo + c] = got[d // 2, d % 2, f // 2, f % 2]


def front_pass(ways, length, tokens, w_qkv, w_in, w_back, w_out, vec, bias, tile, plan):
    rows, width = tokens.shape
    groups = width // GW
    n_dp, n_fsdp = ways
    nh, m = n_dp // 2, n_fsdp // 2
    steps = rows // tile
    head = width // HEADS
    part = first_part(w_qkv.shape[1])
    const = lambda *shape: pl.BlockSpec(shape, lambda i: (0,) * len(shape))
    early = lambda i: (jnp.minimum(i, steps - 1), 0)
    late = pl.BlockSpec((tile, width), lambda i: (jnp.maximum(i - steps, 0), 0))
    hbm = pl.BlockSpec(memory_space=pl.ANY)
    sds = jax.ShapeDtypeStruct
    got = lambda r, c: (nh, 2, m, 2, r, c)
    hidden = w_in.shape[1] * n_dp
    pieces = 8
    per = Gather.count(n_dp, n_fsdp)
    return pl.pallas_call(
        functools.partial(front_kernel, ways, plan, steps),
        grid=(2 * steps,),
        in_specs=[
            pl.BlockSpec(memory_space=pltpu.SMEM),
            pl.BlockSpec((tile, width), early),
            hbm,
            hbm,
            hbm,
            hbm,
            const(*vec.shape),
            const(*bias.shape),
            const(KW, GW),
            const(GW, GW),
        ],
        out_specs=[
            pl.BlockSpec((tile, 3 * width), early),
            late,
            late,
            late,
            late,
            pl.BlockSpec((tile // QB, KW, width), lambda i: (jnp.maximum(i - steps, 0), 0, 0)),
            pl.BlockSpec((width, tile), lambda i: (0, jnp.minimum(i, steps - 1))),
            const(groups, 2 * GW, GW),
            const(groups, GW, GW),
            const(groups, 8, GW),
            const(width, 3 * width),
            const(8, width),
            const(1, hidden),
            hbm,
            hbm,
            hbm,
        ],
        out_shape=[sds((rows, 3 * width), bf16)]
        + [sds((rows, width), bf16)] * 4
        + [
            sds((rows // QB, KW, width), bf16),
            sds((width, rows), bf16),
            sds((groups, 2 * GW, GW), bf16),
            sds((groups, GW, GW), bf16),
            sds((groups, 8, GW), f32),
            sds((width, 3 * width), bf16),
            sds((8, width), f32),
            sds((1, hidden), f32),
            sds(got(*w_in.shape), bf16),
            sds(got(*w_back.shape), bf16),
            sds(got(*w_out.shape), bf16),
        ],
        scratch_shapes=[
            pltpu.VMEM((rows + 2 * HALO, 3 * width), bf16),
            pltpu.VMEM((groups, GW, 2 * GW), f32),
            pltpu.VMEM((groups, 8, GW), f32),
            pltpu.VMEM(got(w_qkv.shape[0], part), bf16),
            pltpu.VMEM(got(w_qkv.shape[0], w_qkv.shape[1] - part), bf16),
            pltpu.VMEM((16, 128), bf16),
            pltpu.VMEM(got(16, 128), bf16),
            pltpu.VMEM(w_in.shape, bf16),
            pltpu.VMEM(w_back.shape, bf16),
            pltpu.VMEM(w_out.shape, bf16),
            pltpu.SemaphoreType.DMA((pieces, per)),
            pltpu.SemaphoreType.DMA((pieces, per)),
            pltpu.SemaphoreType.DMA((pieces,)),
        ],
        compiler_params=pltpu.CompilerParams(
            collective_id=0, has_side_effects=True, vmem_limit_bytes=VMEM_LIMIT
        ),
        cost_estimate=pl.CostEstimate(
            flops=2 * rows * width * 8 * width, bytes_accessed=rows * width * 24, transcendentals=0
        ),
        name="front_pass",
    )(
        length,
        tokens,
        w_qkv,
        w_in,
        w_back,
        w_out,
        vec,
        bias,
        jnp.asarray(band_table(head)),
        jnp.asarray(head_table(head), bf16),
    )


def ffn_kernel(
    chunk,
    len_ref,
    tok_ref,
    cot_ref,
    near_ref,
    fa_ref,
    fb_ref,
    rn_ref,
    q_ref,
    c_ref,
    vec_ref,
    bin_ref,
    gw_out,
    gw_in,
    gw_back,
    out_ref,
    datt_ref,
    dmix_ref,
    dn_ref,
    gin_ref,
    gback_ref,
    gout_ref,
    gvec_ref,
    gbias_ref,
    m3_ref,
    m4_ref,
    dt_ref,
    a_in,
    a_back,
    a_out,
    a_st,
    a_bent,
    wout_ref,
    win_ref,
    wback_ref,
):
    step = pl.program_id(0)
    rows, width = tok_ref.shape
    hidden = win_ref.shape[1]
    groups = width // GW
    head = width // HEADS
    length = len_ref[0, 0]

    @pl.when(step == 0)
    def _():
        join_blocks(wout_ref, gw_out)
        join_blocks(win_ref, gw_in)
        join_blocks(wback_ref, gw_back)
        a_in[...] = jnp.zeros_like(a_in)
        a_back[...] = jnp.zeros_like(a_back)
        a_out[...] = jnp.zeros_like(a_out)
        a_st[...] = jnp.zeros_like(a_st)
        a_bent[...] = jnp.zeros_like(a_bent)
        gvec_ref[...] = jnp.zeros_like(gvec_ref)
        gbias_ref[...] = jnp.zeros_like(gbias_ref)

    c_row = jnp.concatenate([c_ref[g, 0:1] for g in range(groups)], axis=1)
    near = near_ref[...].astype(f32)
    fac = fa_ref[...].astype(f32)
    far_b = fb_ref[...].astype(f32)
    mixed = (
        vec_ref[5:6] * near + vec_ref[6:7] * (fac + c_row) + vec_ref[7:8] * far_b
    ).astype(bf16)
    resid = tok_ref[...].astype(f32) + nn(mixed, wout_ref[...])
    z2, r2 = moments(resid)
    h2 = (z2 * vec_ref[2:3] + vec_ref[3:4]).astype(bf16)
    valid = row_valid(step, rows, width, length)
    seed = jnp.where(valid, cot_ref[...].astype(f32), 0.0)
    d_ffn = seed.astype(bf16)
    s0 = math.sqrt(2.0 / math.pi)
    s1 = s0 * 0.044715
    ffn = jnp.zeros((rows, width), f32)
    dh2 = jnp.zeros((rows, width), f32)
    for lo in range(0, hidden, chunk):
        cols = slice(lo, lo + chunk)
        x = nn(h2, win_ref[:, cols]) + bin_ref[0:1, cols]
        x2 = x * x
        t = jnp.tanh(x * (s0 + s1 * x2))
        half = 0.5 + 0.5 * t
        act = x * half
        slope = half + (act - act * half) * (2 * s0 + 6 * s1 * x2)
        act = act.astype(bf16)
        ffn += nn(act, wback_ref[cols, :])
        a_back[:, cols] += tn(d_ffn, act)
        d_pre = slope * nt(d_ffn, wback_ref[cols, :])
        gbias_ref[:, cols] += fold8(d_pre)
        d_pre = d_pre.astype(bf16)
        a_in[:, cols] += tn(h2, d_pre)
        dh2 += nt(d_pre, win_ref[:, cols])
    out_ref[...] = jnp.where(valid, resid + ffn + vec_ref[4:5], 0.0).astype(bf16)
    gvec_ref[2] += fold8(dh2 * z2)
    gvec_ref[3] += fold8(dh2)
    gvec_ref[4] += fold8(seed)
    dz = dh2 * vec_ref[2:3]
    d_resid = seed + r2 * (
        dz
        - jnp.mean(dz, axis=-1, keepdims=True)
        - z2 * jnp.mean(dz * z2, axis=-1, keepdims=True)
    )
    d_attn = d_resid.astype(bf16)
    datt_ref[...] = d_attn
    a_out[...] += tn(mixed, d_attn)
    d_mix = nt(d_attn, wout_ref[...])
    dmix_ref[...] = d_mix.astype(bf16)
    gvec_ref[5] += fold8(d_mix * near)
    gvec_ref[6] += fold8(d_mix * fac)
    gvec_ref[7] += fold8(d_mix * far_b)
    gvec_ref[0] += fold8(d_mix)
    d_num = (vec_ref[6:7] * d_mix * rn_ref[...].astype(f32)).astype(bf16)
    dn_ref[...] = d_num
    d_den = (d_num.astype(f32) * fac).astype(bf16)
    d_far = (vec_ref[7:8] * d_mix).astype(bf16)
    for g in range(groups):
        cols = slice(g * GW, (g + 1) * GW)
        q = q_ref[:, cols]
        a_st[g] += tn(lift(q), jnp.concatenate([d_num[:, cols], d_den[:, cols]], axis=1))
        a_bent[g] += tn(jnp.tanh(q), d_far[:, cols])

    @pl.when(step == pl.num_programs(0) - 1)
    def _():
        mask = same_head(head).astype(f32)
        inv_len = 1.0 / length.astype(f32)
        ones = jnp.ones((8, GW), f32)
        for g in range(groups):
            m3_ref[g] = (a_st[g][:, :GW] * mask).astype(bf16)
            m4_ref[g] = (a_bent[g] * mask * inv_len).astype(bf16)
            dt_ref[g] = -nt_exact(ones, a_st[g][:, GW:] * mask)
        cut_blocks(gin_ref, a_in)
        cut_turned(gback_ref, a_back)
        cut_blocks(gout_ref, a_out)
        gvec_ref[6] += gvec_ref[0] * c_row


def third_pass(ways, length, tokens, cot, near, fa, fb, rn, qkv, c, vecs, b_in, w_out, w_in, w_back, tile, chunk):
    rows, width = tokens.shape
    hidden = w_in.shape[0] * w_in.shape[3]
    groups = width // GW
    n_dp, n_fsdp = ways
    back = (width // n_dp, hidden // n_fsdp)
    back = back if turned(hidden, n_fsdp) else back[::-1]
    const = lambda *shape: pl.BlockSpec(shape, lambda i: (0,) * len(shape))
    block = pl.BlockSpec((tile, width), lambda i: (i, 0))
    sds = jax.ShapeDtypeStruct
    return pl.pallas_call(
        functools.partial(ffn_kernel, chunk),
        grid=(rows // tile,),
        in_specs=[pl.BlockSpec(memory_space=pltpu.SMEM)]
        + [block] * 7
        + [
            const(groups, 8, GW),
            const(8, width),
            const(1, hidden),
            const(*w_out.shape),
            const(*w_in.shape),
            const(*w_back.shape),
        ],
        out_specs=[block] * 4
        + [
            const(n_dp, n_fsdp, width // n_fsdp, hidden // n_dp),
            const(n_dp, n_fsdp, *back),
            const(n_dp, n_fsdp, width // n_fsdp, width // n_dp),
            const(8, 8, width),
            const(8, hidden),
            const(groups, GW, GW),
            const(groups, GW, GW),
            const(groups, 8, GW),
        ],
        out_shape=[sds((rows, width), bf16)] * 4
        + [
            sds((n_dp, n_fsdp, width // n_fsdp, hidden // n_dp), bf16),
            sds((n_dp, n_fsdp, *back), bf16),
            sds((n_dp, n_fsdp, width // n_fsdp, width // n_dp), bf16),
            sds((8, 8, width), f32),
            sds((8, hidden), f32),
            sds((groups, GW, GW), bf16),
            sds((groups, GW, GW), bf16),
            sds((groups, 8, GW), f32),
        ],
        scratch_shapes=[
            pltpu.VMEM((width, hidden), f32),
            pltpu.VMEM((width, hidden), f32),
            pltpu.VMEM((width, width), f32),
            pltpu.VMEM((groups, GW, 2 * GW), f32),
            pltpu.VMEM((groups, GW, GW), f32),
            pltpu.VMEM((width, width), bf16),
            pltpu.VMEM((width, hidden), bf16),
            pltpu.VMEM((hidden, width), bf16),
        ],
        compiler_params=pltpu.CompilerParams(vmem_limit_bytes=VMEM_LIMIT),
        cost_estimate=pl.CostEstimate(
            flops=2 * rows * width * (6 * hidden + 4 * width),
            bytes_accessed=rows * width * 22,
            transcendentals=0,
        ),
        name="third_pass",
    )(length, tokens, cot, near, fa, fb, rn, qkv, c, vecs, b_in, w_out, w_in, w_back)


class Scatter:
    def __init__(self, place, src, out, bufs, send, recv, local, order):
        self.p, self.src, self.out, self.order = place, src, out, order
        self.acc, self.r0, self.r1, self.r2, self.r3 = bufs
        self.send, self.recv, self.local = send, recv, local

    @staticmethod
    def count(n_dp, n_fsdp):
        return 1 + 1 + (n_dp // 2 - 1) + (n_fsdp // 2 - 1)

    @staticmethod
    def scratch(n_dp, n_fsdp, r, c, order, dtype):
        nh, m = n_dp // 2, n_fsdp // 2
        if order == "x":
            one, two = (nh, m, r, c), (nh - 1, m, r, c)
        else:
            one, two = (nh - 1, m, 2, r, c), (m, r, c)
        shapes = [(nh, m, 2, r, c), (nh, m, 2, r, c), one, two, (m - 1, r, c)]
        return [pltpu.VMEM(s, dtype) for s in shapes]

    def own(self):
        return pltpu.make_async_copy(self.src.at[:, self.p.dl], self.acc, self.local)

    def stage(self, k):
        p = self.p
        if k == 0:
            ref = self.src.at[:, 1 - p.dl]
            return [copy_to(ref, self.r0, self.send.at[0], self.recv.at[0], p.dev(dl=1 - p.dl))]
        if k == 3:
            i = p.nh
            out = []
            for o in range(1, p.m):
                fh = lax.rem(p.fh + o, p.m)
                out.append(
                    copy_to(self.acc.at[p.dh, fh, p.fl], self.r3.at[o - 1], self.send.at[i + o], self.recv.at[i + o],
                            p.dev(fh=fh))
                )
            return out
        if (k == 1) == (self.order == "x"):
            ref = self.acc.at[:, :, 1 - p.fl] if k == 1 else self.acc.at[p.dh, :, 1 - p.fl]
            dst = self.r1 if k == 1 else self.r2
            return [copy_to(ref, dst, self.send.at[1], self.recv.at[1], p.dev(fl=1 - p.fl))]
        out = []
        for o in range(1, p.nh):
            dh = lax.rem(p.dh + o, p.nh)
            ref = self.acc.at[dh] if k == 1 else self.acc.at[dh, :, p.fl]
            dst = self.r1.at[o - 1] if k == 1 else self.r2.at[o - 1]
            out.append(copy_to(ref, dst, self.send.at[1 + o], self.recv.at[1 + o], p.dev(dh=dh)))
        return out

    def start(self, k):
        for c in self.stage(k):
            c.start()

    def turn(self, k):
        if k == 0:
            self.own().wait()
        for c in self.stage(k):
            c.wait()
        self.add(k)
        if k < 3:
            self.start(k + 1)

    def add(self, k):
        p, acc = self.p, self.acc
        nh, m = p.nh, p.m
        dt = acc.dtype

        def put(index, others):
            total = acc[index].astype(f32)
            for o in others:
                total = total + o.astype(f32)
            acc[index] = total.astype(dt)

        if k == 3:
            total = acc[p.dh, p.fh, p.fl].astype(f32)
            for o in range(1, m):
                total = total + self.r3[o - 1].astype(f32)
            self.out[...] = total
            return

        @pl.loop(0, m)
        def _(i):
            if k == 0:
                for a in range(nh):
                    for b in range(2):
                        put((a, i, b), [self.r0[a, i, b]])
            elif k == 1 and self.order == "x":
                for a in range(nh):
                    put((a, i, p.fl), [self.r1[a, i]])
            elif k == 1:
                for b in range(2):
                    put((p.dh, i, b), [self.r1[o - 1, i, b] for o in range(1, nh)])
            elif self.order == "x":
                put((p.dh, i, p.fl), [self.r2[o - 1, i] for o in range(1, nh)])
            else:
                put((p.dh, i, p.fl), [self.r2[i]])


def back_kernel(
    ways,
    plan,
    late_plan,
    len_ref,
    q_ref,
    k_lo,
    k_ref,
    k_hi,
    v_lo,
    v_ref,
    v_hi,
    p_ref,
    dmix_ref,
    dn_ref,
    fa_ref,
    tok_ref,
    datt_ref,
    h1t_ref,
    m1_ref,
    m2_ref,
    m3_ref,
    m4_ref,
    dt_ref,
    c_ref,
    vec_ref,
    w_ref,
    hm_ref,
    gv_ref,
    gbias_ref,
    s_in,
    s_back,
    s_out,
    dtok_ref,
    oqkv_ref,
    oin_ref,
    oback_ref,
    oout_ref,
    ovec_ref,
    obias_ref,
    kk,
    vv,
    far_s,
    dp_s,
    ds_s,
    all_d,
    carry,
    gvec_s,
    ga_ref,
    gb_ref,
    gs_ref,
    rows_s,
    back_t,
    small_o,
    late_src,
    late_got,
    *rest,
):
    step = pl.program_id(0)
    rows, width = q_ref.shape
    total = h1t_ref.shape[1]
    steps = total // rows
    groups = width // GW
    head = width // HEADS
    scale = head ** (-0.5)
    length = len_ref[0, 0]
    n_dp, n_fsdp = ways
    place = Place(n_dp, n_fsdp)
    cols = ovec_ref.shape[1]
    c_all = oqkv_ref.shape[1]
    part = ga_ref.shape[-1]
    send, recv, local, late_send, late_recv = rest[30:]
    final = steps + 1 + place.nh
    last_rows = tok_ref.shape[0]

    def piece(j, src, out, order):
        return Scatter(place, src, out, rest[5 * j : 5 * j + 5], send.at[j], recv.at[j], local.at[j], order)

    early = [
        piece(0, s_in, oin_ref, "x"),
        piece(1, s_back, back_t, "y"),
        piece(2, s_out, oout_ref, "y"),
        piece(5, gs_ref, small_o, "x"),
    ]
    last = [
        piece(3, ga_ref, oqkv_ref.at[:, pl.ds(0, part)], "x"),
        piece(4, gb_ref, oqkv_ref.at[:, pl.ds(part, c_all - part)], "y"),
    ]

    @pl.when(step == 0)
    def _():
        for x in early[:3]:
            x.own().start()
        greet_all(place)
        for x in early[:3]:
            x.start(0)
        carry[...] = jnp.zeros_like(carry)
        gvec_s[...] = jnp.zeros_like(gvec_s)
        gs_ref[...] = jnp.zeros_like(gs_ref)
        late_src[...] = jnp.zeros_like(late_src)
        rows_s[0:2] = jnp.zeros((2, width), f32)
        rows_s[2:8] = jnp.sum(gv_ref[2:8], axis=1)
        bias = jnp.sum(gbias_ref[...], axis=0, keepdims=True)
        for d in range(n_dp):
            pair = rows_s[2 * d : 2 * d + 2]
            for f in range(n_fsdp):
                spot = slice(f * cols, (f + 1) * cols)
                at = d * width + f * cols
                gs_ref[d // 2, d % 2, f // 2, f % 2, 0:2, :cols] = pair[:, spot]
                gs_ref[d // 2, d % 2, f // 2, f % 2, 2:3, :cols] = bias[:, at : at + cols]
        early[3].own().start()
        early[3].start(0)

    for at, moves in plan.items():

        @pl.when(step == at)
        def _(moves=moves):
            for k in moves:
                for x in early:
                    x.turn(k)

    def far_keys(at, slot, live):
        valid = row_valid(at, rows, GW, length) & live
        here = pl.ds(pl.multiple_of(at * rows + HALO, HALO), rows)
        for g in range(groups):
            cut = slice(g * GW, (g + 1) * GW)
            kc = slice(width + g * GW, width + (g + 1) * GW)
            vc = slice(2 * width + g * GW, 2 * width + (g + 1) * GW)
            k = kk[slot, HALO : HALO + rows, cut]
            v = vv[slot, HALO : HALO + rows, cut]
            lift_k = lift(k)
            bent_k = jnp.tanh(k)
            bent = bent_k.astype(f32)
            v_cen = v - c_ref[g, 0:1].astype(bf16)
            dk = (nt(v_cen, m3_ref[g]) + dt_ref[g, 0:1]) * jnp.minimum(lift_k, 1.0).astype(f32)
            dk += nt(v, m4_ref[g]) * (1.0 - bent * bent)
            both = jnp.concatenate([lift_k, bent_k], axis=1)
            dv = nn(both, jnp.concatenate([m3_ref[g], m4_ref[g]], axis=0))
            all_d[here, kc] = (all_d[here, kc].astype(f32) + jnp.where(valid, dk, 0.0)).astype(bf16)
            all_d[here, vc] = (all_d[here, vc].astype(f32) + jnp.where(valid, dv, 0.0)).astype(bf16)

    @pl.when(step < steps)
    def _():
        slot = lax.rem(step, 2)
        kk[slot, :HALO] = k_lo[...]
        kk[slot, HALO : HALO + rows] = k_ref[...]
        kk[slot, HALO + rows :] = k_hi[...]
        vv[slot, :HALO] = v_lo[...]
        vv[slot, HALO : HALO + rows] = v_ref[...]
        vv[slot, HALO + rows :] = v_hi[...]
        hm = hm_ref[...]
        blend = vec_ref[...].astype(bf16)
        base = step * rows
        for g in range(groups):
            cut = slice(g * GW, (g + 1) * GW)
            kc = slice(width + g * GW, width + (g + 1) * GW)
            vc = slice(2 * width + g * GW, 2 * width + (g + 1) * GW)
            q = q_ref[:, cut]
            d_num = dn_ref[:, cut]
            d_den = -d_num * fa_ref[:, cut]
            d_mix = dmix_ref[:, cut]
            bent = jnp.tanh(q).astype(f32)
            far = nn(jnp.concatenate([d_num, d_den], axis=1), m1_ref[g]) * jnp.minimum(lift(q), 1.0).astype(f32)
            far_s[:, cut] = far + nn(blend[7:8, cut] * d_mix, m2_ref[g]) * (1.0 - bent * bent)
            for b in range(rows // QB):
                here = slice(b * QB, (b + 1) * QB)
                window = slice(b * QB, b * QB + KW)
                ds = spread_rows(blend[5:6, cut] * dmix_ref[here, cut], hm)
                dp_s[g, b] = nt(vv[slot, window, cut], ds)
            for b in range(rows // QB):
                pw = p_ref[b, :, cut].astype(f32)
                t = pw * dp_s[g, b]
                ds_s[g, b] = (t - pw * jnp.sum(t, axis=0, keepdims=True)).astype(bf16)
            old_k = carry[0, :, cut]
            old_v = carry[1, :, cut]
            for b in range(rows // QB):
                here = slice(b * QB, (b + 1) * QB)
                window = slice(b * QB, b * QB + KW)
                d_s = ds_s[g, b]
                dk = nn(d_s, spread_rows(q_ref[here, cut] * scale, hm))
                dv = nn(p_ref[b, :, cut], spread_rows(blend[5:6, cut] * dmix_ref[here, cut], hm))
                dq = pick_heads(tn(d_s, kk[slot, window, cut]), head) * scale + far_s[here, cut]
                lo = pl.ds(pl.multiple_of(base + b * QB, QB), QB)
                all_d[pl.ds(pl.multiple_of(base + b * QB + HALO, HALO), QB), cut] = dq.astype(bf16)
                all_d[lo, kc] = (old_k + dk[:QB]).astype(bf16)
                all_d[lo, vc] = (old_v + dv[:QB]).astype(bf16)
                old_k = dk[QB:]
                old_v = dv[QB:]
            carry[0, :, cut] = old_k
            carry[1, :, cut] = old_v
        far_keys(jnp.maximum(step - 1, 0), 1 - slot, step > 0)

    @pl.when(step == steps)
    def _():
        all_d[total:, width : 2 * width] = carry[0].astype(bf16)
        all_d[total:, 2 * width :] = carry[1].astype(bf16)
        far_keys(steps - 1, (steps - 1) % 2, True)

    for dh in range(n_dp // 2):

        @pl.when(step == steps + 1 + dh)
        def _(dh=dh):
            grad = nn(h1t_ref[...], all_d[HALO : HALO + total, dh * 2 * c_all : (dh + 1) * 2 * c_all])
            r = ga_ref.shape[-2]
            for dl in range(2):
                for f in range(n_fsdp):
                    block = grad[f * r : (f + 1) * r, dl * c_all : (dl + 1) * c_all].astype(bf16)
                    ga_ref[dh, dl, f // 2, f % 2] = block[:, :part]
                    gb_ref[dh, dl, f // 2, f % 2] = block[:, part:]

    @pl.when(step == final)
    def _():
        for x in last:
            x.own().start()
            x.start(0)

    for at, moves in late_plan.items():

        @pl.when(step == final + at)
        def _(moves=moves):
            for k in moves:
                for x in last:
                    x.turn(k)

    @pl.when(step >= final)
    def _():
        here = pl.ds(pl.multiple_of((step - final) * last_rows + HALO, HALO), last_rows)
        z1, r1 = moments(tok_ref[...].astype(f32))
        dh1 = nt(all_d[here], w_ref[...])
        gvec_s[0] += fold8(dh1 * z1)
        gvec_s[1] += fold8(dh1)
        dz = dh1 * vec_ref[0:1]
        dtok_ref[...] = (
            datt_ref[...].astype(f32)
            + r1
            * (
                dz
                - jnp.mean(dz, axis=-1, keepdims=True)
                - z1 * jnp.mean(dz * z1, axis=-1, keepdims=True)
            )
        ).astype(bf16)

    @pl.when(step == final + total // last_rows - 1)
    def _():
        rows_s[0:2] = jnp.sum(gvec_s[...], axis=1)
        for f in range(n_fsdp):
            late_src[f, 0:2, :cols] = rows_s[0:2, f * cols : (f + 1) * cols]
        d, f = lax.axis_index("dp"), lax.axis_index("fsdp")
        me = d * n_fsdp + f

        def late(o):
            to = lax.rem(f + o, n_fsdp)
            return copy_to(
                late_src.at[to], late_got.at[me], late_send.at[o], late_recv.at[me], {"dp": 0, "fsdp": to}
            )

        @pl.when(d > 0)
        def _():
            late(0).start()

        for o in range(1, n_fsdp):
            late(o).start()
        oback_ref[...] = back_t[...].T if turned(gbias_ref.shape[1], n_fsdp) else back_t[...]
        for x in last:
            x.turn(3)

        @pl.when(d > 0)
        def _():
            late(0).wait_send()
            ovec_ref[...] = small_o[0:2, :cols]

        for o in range(1, n_fsdp):
            late(o).wait_send()

        @pl.when(d == 0)
        def _():
            late_got[me] = late_src[f]

            @pl.loop(0, n_dp * n_fsdp)
            def _(s):
                @pl.when(s != me)
                def _():
                    copy_to(
                        late_src.at[0], late_got.at[s], late_send.at[0], late_recv.at[s], {"dp": 0, "fsdp": 0}
                    ).wait_recv()

            ovec_ref[...] = jnp.sum(late_got[...], axis=0)[0:2, :cols]

        obias_ref[...] = small_o[2:3, :cols]


def greet_all(place):
    d, f = lax.axis_index("dp"), lax.axis_index("fsdp")
    n_dp, n_fsdp = 2 * place.nh, 2 * place.m
    barrier = pltpu.get_barrier_semaphore()
    who = place.partners()
    for dev in who:
        pl.semaphore_signal(barrier, inc=1, device_id=dev, device_id_type=MESH)

    @pl.when(d == 0)
    def _():
        @pl.loop(0, n_dp)
        def _(i):
            @pl.loop(0, n_fsdp)
            def _(j):
                @pl.when((i != 0) | (j != f))
                def _():
                    pl.semaphore_signal(barrier, inc=1, device_id={"dp": i, "fsdp": j}, device_id_type=MESH)

    pl.semaphore_wait(barrier, len(who) + n_fsdp - (d == 0).astype(jnp.int32))


def back_pass(
    ways,
    length,
    qkv,
    p,
    d_mix,
    tokens,
    d_attn,
    d_num,
    fa,
    h1t,
    m1,
    m2,
    m3,
    m4,
    dt,
    c,
    vecs,
    w_qkv,
    gv,
    gbias,
    s_in,
    s_back,
    s_out,
    tile,
    last_tile,
    plan,
    late_plan,
):
    rows, width = tokens.shape
    groups = width // GW
    steps = rows // tile
    n_dp, n_fsdp = ways
    nh, m = n_dp // 2, n_fsdp // 2
    r, c_all = width // n_fsdp, 3 * width // n_dp
    part = first_part(c_all)
    per = Scatter.count(n_dp, n_fsdp)
    final = steps + 1 + nh
    hbm = pl.BlockSpec(memory_space=pl.ANY)
    back_shape = s_back.shape[-2:]
    outs = [
        (r, c_all),
        s_in.shape[-2:],
        back_shape[::-1] if turned(gbias.shape[1], n_fsdp) else back_shape,
        s_out.shape[-2:],
        (2, width // n_fsdp),
        (1, gbias.shape[1] // (n_dp * n_fsdp)),
    ]
    kinds = [
        (*s_in.shape[-2:], "x", bf16),
        (*back_shape, "y", bf16),
        (*s_out.shape[-2:], "y", bf16),
        (r, part, "x", bf16),
        (r, c_all - part, "y", bf16),
        (8, 128, "x", f32),
    ]
    bufs = [b for k in kinds for b in Scatter.scratch(n_dp, n_fsdp, *k)]
    got = lambda *s: (nh, 2, m, 2, *s)

    def const(*shape):
        return pl.BlockSpec(shape, lambda i: (0,) * len(shape))

    def kept(*shape):
        return pl.BlockSpec(shape, lambda i: (0,) * len(shape), pipeline_mode=pl.Buffered(1))

    one = lambda i: jnp.minimum(i, steps - 1)
    end = lambda i: jnp.maximum(i - final, 0)
    per_tile = tile // HALO
    top = rows // HALO - 1

    def halo(col):
        return [
            pl.BlockSpec((HALO, width), lambda i: (jnp.maximum(one(i) * per_tile - 1, 0), col)),
            pl.BlockSpec((tile, width), lambda i: (one(i), col)),
            pl.BlockSpec((HALO, width), lambda i: (jnp.minimum((one(i) + 1) * per_tile, top), col)),
        ]

    block = pl.BlockSpec((tile, width), lambda i: (one(i), 0))
    late = pl.BlockSpec((last_tile, width), lambda i: (end(i), 0))
    head = width // HEADS
    sds = jax.ShapeDtypeStruct
    return pl.pallas_call(
        functools.partial(back_kernel, ways, plan, late_plan),
        grid=(final + rows // last_tile,),
        in_specs=[
            pl.BlockSpec(memory_space=pltpu.SMEM),
            block,
            *halo(1),
            *halo(2),
            pl.BlockSpec((tile // QB, KW, width), lambda i: (one(i), 0, 0)),
            block,
            block,
            block,
            late,
            late,
            kept(width, rows),
            kept(groups, 2 * GW, GW),
            kept(groups, GW, GW),
            kept(groups, GW, GW),
            kept(groups, GW, GW),
            const(groups, 8, GW),
            const(groups, 8, GW),
            const(8, width),
            kept(width, 3 * width),
            const(GW, GW),
            const(*gv.shape),
            const(*gbias.shape),
            hbm,
            hbm,
            hbm,
        ],
        out_specs=[late] + [const(*s) for s in outs],
        out_shape=[sds((rows, width), bf16)] + [sds(s, f32) for s in outs],
        scratch_shapes=[
            pltpu.VMEM((2, tile + 2 * HALO, width), bf16),
            pltpu.VMEM((2, tile + 2 * HALO, width), bf16),
            pltpu.VMEM((tile, width), f32),
            pltpu.VMEM((groups, tile // QB, KW, GW), f32),
            pltpu.VMEM((groups, tile // QB, KW, GW), bf16),
            pltpu.VMEM((rows + 2 * HALO, 3 * width), bf16),
            pltpu.VMEM((2, QB, width), f32),
            pltpu.VMEM((2, 8, width), f32),
            pltpu.VMEM(got(r, part), bf16),
            pltpu.VMEM(got(r, c_all - part), bf16),
            pltpu.VMEM(got(8, 128), f32),
            pltpu.VMEM((8, width), f32),
            pltpu.VMEM(back_shape, f32),
            pltpu.VMEM((8, 128), f32),
            pltpu.VMEM((n_fsdp, 8, 128), f32),
            pltpu.VMEM((n_dp * n_fsdp, 8, 128), f32),
            *bufs,
            pltpu.SemaphoreType.DMA((6, per)),
            pltpu.SemaphoreType.DMA((6, per)),
            pltpu.SemaphoreType.DMA((6,)),
            pltpu.SemaphoreType.DMA((n_fsdp,)),
            pltpu.SemaphoreType.DMA((n_dp * n_fsdp,)),
        ],
        compiler_params=pltpu.CompilerParams(
            collective_id=1, has_side_effects=True, vmem_limit_bytes=VMEM_LIMIT
        ),
        cost_estimate=pl.CostEstimate(
            flops=2 * rows * width * 14 * width, bytes_accessed=rows * width * 24, transcendentals=0
        ),
        name="back_pass",
    )(
        length,
        qkv,
        qkv,
        qkv,
        qkv,
        qkv,
        qkv,
        qkv,
        p,
        d_mix,
        d_num,
        fa,
        tokens,
        d_attn,
        h1t,
        m1,
        m2,
        m3,
        m4,
        dt,
        c,
        vecs,
        w_qkv,
        jnp.asarray(head_table(head), bf16),
        gv,
        gbias,
        s_in,
        s_back,
        s_out,
    )


def hand_kernel(n, *refs):
    for j in range(n):
        refs[n + j][...] = refs[j][...]


def hand_over(arrays, parts):
    first = arrays[0]
    block = pl.BlockSpec((first.shape[0] // parts, first.shape[1]), lambda i: (i, 0))
    specs = [block] + [pl.BlockSpec(a.shape, lambda i: (0, 0)) for a in arrays[1:]]
    return pl.pallas_call(
        functools.partial(hand_kernel, len(arrays)),
        grid=(parts,),
        in_specs=specs,
        out_specs=specs,
        out_shape=[jax.ShapeDtypeStruct(a.shape, a.dtype) for a in arrays],
        name="hand_over",
    )(*arrays)


FRONT_TILE = 1024
TILE = 512
LAST_TILE = 1024
CHUNK = 512
FRONT_PLAN = {2: [(0, 0), (1, 0)], 3: [(0, 1), (1, 1)], 6: [(0, 2), (1, 2)], 8: [(0, 3), (1, 3)]}
BACK_PLAN = {4: [0], 7: [1], 9: [2], 10: [3]}
LATE_PLAN = {1: [0], 2: [1], 3: [2]}


def shards(
    tokens, cotangent, w_qkv, w_out, w_in, w_back, vec_params, b_in, item_lengths, bucket_counts, *, ways
):
    n_dp, n_fsdp = ways
    (
        qkv,
        near,
        fa,
        fb,
        rn,
        p,
        h1t,
        m1,
        m2,
        c,
        qkv_w,
        vecs,
        in_bias,
        g_in,
        g_back,
        g_out,
    ) = front_pass(
        ways, item_lengths, tokens, w_qkv, w_in, w_back, w_out, vec_params, b_in[None], FRONT_TILE, FRONT_PLAN
    )

    def blocks(g):
        return g.reshape(n_dp, n_fsdp, *g.shape[-2:])

    def pairs(g):
        return g.reshape(n_dp // 2, 2, n_fsdp // 2, 2, *g.shape[-2:])

    (out, d_attn, d_mix, d_num, s_in, s_back, s_out, g_vec, g_bias, m3, m4, dt) = third_pass(
        ways,
        item_lengths,
        tokens,
        cotangent,
        near,
        fa,
        fb,
        rn,
        qkv,
        c,
        vecs,
        in_bias,
        blocks(g_out),
        blocks(g_in),
        blocks(g_back),
        TILE,
        CHUNK,
    )
    d_tok, r_qkv, r_in, r_back, r_out, r_vec, r_bias = back_pass(
        ways,
        item_lengths,
        qkv,
        p,
        d_mix,
        tokens,
        d_attn,
        d_num,
        fa,
        h1t,
        m1,
        m2,
        m3,
        m4,
        dt,
        c,
        vecs,
        qkv_w,
        g_vec,
        g_bias,
        pairs(s_in),
        pairs(s_back),
        pairs(s_out),
        TILE,
        LAST_TILE,
        BACK_PLAN,
        LATE_PLAN,
    )
    d_tok, r_qkv, r_out, r_in, r_back, r_vec, r_bias = hand_over(
        [d_tok, r_qkv, r_out, r_in, r_back, r_vec, r_bias], 4
    )
    return (out, d_tok, r_qkv, r_out, r_in, r_back, r_vec, r_bias[0])


def solution(mesh):
    in_specs = (
        P(("dp", "fsdp"), None),
        P(("dp", "fsdp"), None),
        P("fsdp", "dp"),
        P("fsdp", "dp"),
        P("fsdp", "dp"),
        P("fsdp", "dp"),
        P("dp", "fsdp"),
        P(("dp", "fsdp")),
        P(("dp", "fsdp"), None),
        P(("dp", "fsdp"), None),
    )
    out_specs = (
        P(("dp", "fsdp"), None),
        P(("dp", "fsdp"), None),
        P("fsdp", "dp"),
        P("fsdp", "dp"),
        P("fsdp", "dp"),
        P("fsdp", "dp"),
        P("dp", "fsdp"),
        P(("dp", "fsdp")),
    )
    ways = (mesh.shape["dp"], mesh.shape["fsdp"])
    body = functools.partial(shards, ways=ways)
    return jax.shard_map(body, mesh=mesh, in_specs=in_specs, out_specs=out_specs, check_vma=False)
```

```python
import functools
import math

import jax
import jax.numpy as jnp
import numpy as np
from jax import lax
from jax.experimental import pallas as pl
from jax.experimental.pallas import tpu as pltpu
from jax.sharding import PartitionSpec as P

HEADS = 8
BAND = 30
QB = 64
HALO = 32
KW = QB + 2 * HALO
GW = 256

norm_eps = 1e-05
f32 = jnp.float32
bf16 = jnp.bfloat16
exact = lax.Precision.HIGHEST
VMEM_LIMIT = 60 * 1024 * 1024


def nn(a, b):
    return lax.dot_general(a, b, (((1,), (0,)), ((), ())), preferred_element_type=f32)


def nt(a, b):
    return lax.dot_general(a, b, (((1,), (1,)), ((), ())), preferred_element_type=f32)


def tn(a, b):
    return lax.dot_general(a, b, (((0,), (0,)), ((), ())), preferred_element_type=f32)


def nt_exact(a, b):
    return lax.dot_general(
        a, b, (((1,), (1,)), ((), ())), preferred_element_type=f32, precision=exact
    )


def lift(t):
    return jnp.where(t > 0, t + 1, jnp.exp(jnp.minimum(t, 0)))


def moments(x):
    mean = jnp.mean(x, axis=-1, keepdims=True)
    cen = x - mean
    inv = lax.rsqrt(jnp.mean(cen * cen, axis=-1, keepdims=True) + norm_eps)
    return cen * inv, inv


def fold8(x):
    return jnp.sum(x.reshape(x.shape[0] // 8, 8, x.shape[1]), axis=0)


def fold4(x):
    n = x.shape[0] // 4
    return (x[:n] + x[n : 2 * n]) + (x[2 * n : 3 * n] + x[3 * n :])


def row_valid(step, rows, width, length):
    ids = step * rows + lax.broadcasted_iota(jnp.int32, (rows, width), 0)
    return ids < length


def same_head(head):
    r = lax.broadcasted_iota(jnp.int32, (GW, GW), 0) // head
    c = lax.broadcasted_iota(jnp.int32, (GW, GW), 1) // head
    return r == c


def spread_rows(x, mask_low):
    return jnp.concatenate([x] * (GW // QB), axis=0) * mask_low


def pick_heads(x, head):
    lane = lax.broadcasted_iota(jnp.int32, (QB, GW), 1) // head
    out = x[:QB]
    for h in range(1, GW // QB):
        out = jnp.where(lane == h, x[h * QB : (h + 1) * QB], out)
    return out


def turned(hidden, n_fsdp):
    return hidden // n_fsdp >= 128


def join_blocks(ref, got, lo=0, step=None):
    n_dp, n_fsdp, r, c = got.shape
    step = c if step is None else step
    for d in range(n_dp):
        for f in range(n_fsdp):
            ref[f * r : (f + 1) * r, d * step + lo : d * step + lo + c] = got[d, f]


def cut_blocks(ref, acc):
    n_dp, n_fsdp, r, c = ref.shape
    for d in range(n_dp):
        for f in range(n_fsdp):
            ref[d, f] = acc[f * r : (f + 1) * r, d * c : (d + 1) * c].astype(ref.dtype)


def cut_turned(ref, acc):
    n_dp, n_fsdp, r, c = ref.shape
    width, hidden = acc.shape
    wide, deep = width // n_dp, hidden // n_fsdp
    for d in range(n_dp):
        for f in range(n_fsdp):
            block = acc[d * wide : (d + 1) * wide, f * deep : (f + 1) * deep]
            ref[d, f] = (block if turned(hidden, n_fsdp) else block.T).astype(ref.dtype)


def band_table(head):
    key = np.arange(KW)[:, None] - HALO
    query = np.arange(GW)[None, :] % QB
    return np.where(np.abs(key - query) <= BAND, 0.0, -1e30).astype(np.float32)


def head_table(head):
    r = np.arange(GW)[:, None] // QB
    c = np.arange(GW)[None, :] // head
    return (r == c).astype(np.float32)


MESH = pl.DeviceIdType.MESH


class Place:
    def __init__(self, n_dp, n_fsdp):
        self.m = n_fsdp // 2
        self.nh = n_dp // 2
        d = lax.axis_index("dp")
        f = lax.axis_index("fsdp")
        self.dh, self.dl = d // 2, lax.rem(d, 2)
        self.fh, self.fl = f // 2, lax.rem(f, 2)

    def dev(self, dh=None, dl=None, fh=None, fl=None):
        dh = self.dh if dh is None else dh
        dl = self.dl if dl is None else dl
        fh = self.fh if fh is None else fh
        fl = self.fl if fl is None else fl
        return {"dp": dh * 2 + dl, "fsdp": fh * 2 + fl}

    def partners(self):
        out = [self.dev(fh=lax.rem(self.fh + o, self.m)) for o in range(1, self.m)]
        out += [self.dev(dh=lax.rem(self.dh + o, self.nh)) for o in range(1, self.nh)]
        return out + [self.dev(fl=1 - self.fl), self.dev(dl=1 - self.dl)]


def greet(place):
    barrier = pltpu.get_barrier_semaphore()
    who = place.partners()
    for dev in who:
        pl.semaphore_signal(barrier, inc=1, device_id=dev, device_id_type=MESH)
    pl.semaphore_wait(barrier, len(who))


def copy_to(src, dst, send, recv, dev):
    return pltpu.make_async_remote_copy(
        src_ref=src, dst_ref=dst, send_sem=send, recv_sem=recv, device_id=dev, device_id_type=MESH
    )


class Gather:
    def __init__(self, place, shard, got, send, recv, local, order, way=None):
        self.p, self.shard, self.got, self.order, self.way = place, shard, got, order, way
        self.send, self.recv, self.local = send, recv, local

    @staticmethod
    def count(n_dp, n_fsdp):
        return n_fsdp // 2 - 1 + 1 + n_dp // 2 - 1 + 1

    def own(self):
        p = self.p
        src = self.shard if self.way is None else self.way
        return pltpu.make_async_copy(src, self.got.at[p.dh, p.dl, p.fh, p.fl], self.local)

    def fetch(self):
        return pltpu.make_async_copy(self.shard, self.way, self.local)

    def stage(self, k):
        p, g = self.p, self.got
        if k == 0:
            out = []
            for o in range(1, p.m):
                to = p.dev(fh=lax.rem(p.fh + o, p.m))
                dst = g.at[p.dh, p.dl, p.fh, p.fl]
                out.append(copy_to(self.shard, dst, self.send.at[o - 1], self.recv.at[o - 1], to))
            return out
        i = p.m - 1
        if k == 3:
            ref = g.at[:, p.dl]
            return [copy_to(ref, ref, self.send.at[i], self.recv.at[i], p.dev(dl=1 - p.dl))]
        if (k == 1) == (self.order == "x"):
            ref = g.at[p.dh, p.dl, :, p.fl] if k == 1 else g.at[:, p.dl, :, p.fl]
            return [copy_to(ref, ref, self.send.at[i + 1], self.recv.at[i + 1], p.dev(fl=1 - p.fl))]
        ref = g.at[p.dh, p.dl, :, p.fl] if k == 1 else g.at[p.dh, p.dl]
        out = []
        for o in range(1, p.nh):
            to = p.dev(dh=lax.rem(p.dh + o, p.nh))
            out.append(copy_to(ref, ref, self.send.at[i + 1 + o], self.recv.at[i + 1 + o], to))
        return out

    def start(self, k):
        for c in self.stage(k):
            c.start()

    def wait(self, k):
        if k == 0:
            self.own().wait()
        for c in self.stage(k):
            c.wait()

    def turn(self, k):
        self.wait(k)
        self.start(k + 1)


def front_kernel(
    ways,
    plan,
    qkv_steps,
    len_ref,
    tok_ref,
    wqkv,
    win,
    wback,
    wout,
    vec_in,
    bias_in,
    band_ref,
    hm_ref,
    qkv_ref,
    near_ref,
    fa_ref,
    fb_ref,
    rn_ref,
    p_ref,
    h1t_ref,
    m1_ref,
    m2_ref,
    c_ref,
    w_ref,
    vec_ref,
    bin_ref,
    g_in,
    g_back,
    g_out,
    all_s,
    st_ref,
    t_ref,
    g_qkv,
    small,
    g_small,
    way_in,
    way_back,
    way_out,
    send,
    recv,
    local,
):
    step = pl.program_id(0)
    steps = qkv_steps
    rows, width = tok_ref.shape
    groups = width // GW
    head = width // HEADS
    scale = head ** (-0.5)
    length = len_ref[0, 0]
    n_dp, n_fsdp = ways
    cols = vec_in.shape[1]
    place = Place(n_dp, n_fsdp)
    half_in = win.shape[1] // 2
    half_back = wback.shape[0] // 2

    def piece(j, shard, got, order, way=None):
        return Gather(place, shard, got, send.at[j], recv.at[j], local.at[j], order, way)

    first = [[piece(7, small, g_small, "x")], []]
    for i, (which, cut, order) in enumerate(qkv_parts(*wqkv.shape)):
        first[which].append(piece(8 + i, wqkv.at[cut], g_qkv.at[(slice(None),) * 4 + cut], order))
    rest = []
    for i in range(2):
        cut = pl.ds(i * half_in, half_in)
        rest.append(piece(i, win.at[:, cut], g_in.at[:, :, :, :, :, cut], "x", way_in.at[:, cut]))
    for i in range(2):
        cut = pl.ds(i * half_back, half_back)
        rest.append(piece(2 + i, wback.at[cut], g_back.at[:, :, :, :, cut], "y", way_back.at[cut]))
    rest.append(piece(4, wout, g_out, "y", way_out))
    sets = [[rest[0], rest[2]], [rest[1], rest[3], rest[4]]]

    @pl.when(step == 0)
    def _():
        small[...] = jnp.zeros_like(small)
        small[:2, :cols] = vec_in[...]
        small[2:3, :cols] = bias_in[...]
        for x in first[0] + first[1]:
            x.own().start()
        for x in rest:
            x.fetch().start()
        greet(place)
        for x in first[0] + first[1]:
            x.start(0)
        for x in rest:
            x.fetch().wait()
            x.own().start()
        for k in range(3):
            for group in first:
                for x in group:
                    x.turn(k)
            if k == 0:
                for x in sets[0] + sets[1]:
                    x.start(0)
        st_ref[...] = jnp.zeros_like(st_ref)
        t_ref[...] = jnp.zeros_like(t_ref)
        all_s[:HALO] = jnp.zeros((HALO, 3 * width), bf16)
        all_s[HALO + steps * rows :] = jnp.zeros((HALO, 3 * width), bf16)
        for x in first[0] + first[1]:
            x.wait(3)
        join_pairs(w_ref, g_qkv)
        lane = lax.broadcasted_iota(jnp.int32, (128, width), 0)
        col = lax.broadcasted_iota(jnp.int32, (128, width), 1)

        def place_small(f, total):
            spot = ((lane + f * cols == col) & (lane < cols)).astype(bf16)
            block = jnp.concatenate(
                [g_small[d // 2, d % 2, f // 2, lax.rem(f, 2)] for d in range(n_dp)], axis=0
            )
            return total + nn(block, spot)

        total = lax.fori_loop(0, n_fsdp, place_small, jnp.zeros((16 * n_dp, width), f32))
        for d in range(n_dp):
            vec_ref[2 * d : 2 * d + 2] = total[16 * d : 16 * d + 2]
            bin_ref[0:1, d * width : (d + 1) * width] = total[16 * d + 2 : 16 * d + 3]

    def advance(at, moves):
        @pl.when(step == at)
        def _():
            for which, k in moves:
                for x in sets[which]:
                    if k < 3:
                        x.turn(k)
                    else:
                        x.wait(k)

    for at, moves in plan.items():
        if at < 2 * steps:
            advance(at, moves)

    @pl.when(step < steps)
    def _():
        z, _ = moments(tok_ref[...].astype(f32))
        h = (z * vec_ref[0:1] + vec_ref[1:2]).astype(bf16)
        h1t_ref[...] = h.T
        lo = pl.multiple_of(HALO + step * rows, HALO)
        q = nn(h, w_ref[:, :width]).astype(bf16)
        qkv_ref[:, :width] = q
        all_s[pl.ds(lo, rows), :width] = q
        valid = row_valid(step, rows, GW, length)
        for g in range(groups):
            kc = slice(width + g * GW, width + (g + 1) * GW)
            vc = slice(2 * width + g * GW, 2 * width + (g + 1) * GW)
            k = nn(h, w_ref[:, kc]).astype(bf16)
            v = nn(h, w_ref[:, vc]).astype(bf16)
            qkv_ref[:, kc] = k
            qkv_ref[:, vc] = v
            all_s[pl.ds(lo, rows), kc] = k
            all_s[pl.ds(lo, rows), vc] = v
            phi = jnp.where(valid, lift(k), 0)
            bent = jnp.where(valid, jnp.tanh(k), 0)
            st_ref[g] += tn(v, jnp.concatenate([phi, bent], axis=1))
            t_ref[g] += fold8(phi.astype(f32))

    @pl.when(step == steps - 1)
    def _():
        mask = same_head(head).astype(f32)
        inv_len = 1.0 / length.astype(f32)
        ones = jnp.ones((8, GW), f32)
        for g in range(groups):
            tb = jnp.sum(t_ref[g], axis=0, keepdims=True) * mask
            s1 = st_ref[g][:, :GW] * mask
            s2 = st_ref[g][:, GW:] * mask
            c_row = (nt_exact(ones, s1) / nt_exact(ones, tb)).astype(bf16).astype(f32)
            c_col = jnp.broadcast_to(c_row[0:1], (GW, GW)).T
            m1_ref[g, :GW] = (s1 - c_col * tb).astype(bf16)
            m1_ref[g, GW:] = tb.astype(bf16)
            m2_ref[g] = (s2 * inv_len).astype(bf16)
            c_ref[g] = c_row

    @pl.when(step >= steps)
    def _():
        hm = hm_ref[...]
        at = (step - steps) * rows
        for b in range(rows // QB):
            base = at + b * QB - HALO
            key = base + lax.broadcasted_iota(jnp.int32, (KW, GW), 0)
            bias = jnp.where((key >= 0) & (key < length), band_ref[...], -1e30)
            here = pl.ds(pl.multiple_of(at + b * QB + HALO, HALO), QB)
            window = pl.ds(pl.multiple_of(at + b * QB, QB), KW)
            for g in range(groups):
                cut = slice(g * GW, (g + 1) * GW)
                kc = slice(width + g * GW, width + (g + 1) * GW)
                vc = slice(2 * width + g * GW, 2 * width + (g + 1) * GW)
                qs = spread_rows(all_s[here, cut] * scale, hm)
                s = nt(all_s[window, kc], qs) + bias
                e = jnp.exp(s - jnp.max(s, axis=0, keepdims=True))
                p = (e * (1.0 / jnp.sum(e, axis=0, keepdims=True))).astype(bf16)
                p_ref[b, :, cut] = p
                o = tn(p, all_s[window, vc])
                near_ref[b * QB : (b + 1) * QB, cut] = pick_heads(o, head).astype(bf16)
        for g in range(groups):
            cut = slice(g * GW, (g + 1) * GW)
            q = all_s[pl.ds(pl.multiple_of(at + HALO, HALO), rows), cut]
            both = nt(lift(q), m1_ref[g])
            rn = 1.0 / both[:, GW:]
            rn_ref[:, cut] = rn.astype(bf16)
            fa_ref[:, cut] = (both[:, :GW] * rn).astype(bf16)
            fb_ref[:, cut] = nt(jnp.tanh(q), m2_ref[g]).astype(bf16)

    advance(2 * steps - 1, plan[2 * steps])


def join_pairs(ref, got):
    nh, _, m, _, r, c = got.shape
    for d in range(2 * nh):
        for f in range(2 * m):
            ref[f * r : (f + 1) * r, d * c : (d + 1) * c] = got[d // 2, d % 2, f // 2, f % 2]


def qkv_parts(r, c):
    if c % 384:
        return [(0, (pl.ds(0, r), pl.ds(0, c)), "x")]
    third = c // 3
    whole = pl.ds(0, r)
    parts = [(0, (whole, pl.ds(0, third)), "x"), (0, (whole, pl.ds(third, third)), "y")]
    rest = pl.ds(2 * third, third)
    if r % 32:
        return parts + [(1, (whole, rest), "x")]
    half = r // 2
    return parts + [(1, (pl.ds(0, half), rest), "x"), (1, (pl.ds(half, half), rest), "y")]


def front_pass(ways, length, tokens, w_qkv, w_in, w_back, w_out, vec, bias, tile, plan):
    rows, width = tokens.shape
    groups = width // GW
    n_dp, n_fsdp = ways
    nh, m = n_dp // 2, n_fsdp // 2
    steps = rows // tile
    head = width // HEADS
    const = lambda *shape: pl.BlockSpec(shape, lambda i: (0,) * len(shape))
    early = lambda i: (jnp.minimum(i, steps - 1), 0)
    late = pl.BlockSpec((tile, width), lambda i: (jnp.maximum(i - steps, 0), 0))
    hbm = pl.BlockSpec(memory_space=pl.ANY)
    sds = jax.ShapeDtypeStruct
    got = lambda r, c: (nh, 2, m, 2, r, c)
    hidden = w_in.shape[1] * n_dp
    pieces = 8 + len(qkv_parts(*w_qkv.shape))
    per = Gather.count(n_dp, n_fsdp)
    return pl.pallas_call(
        functools.partial(front_kernel, ways, plan, steps),
        grid=(2 * steps,),
        in_specs=[
            pl.BlockSpec(memory_space=pltpu.SMEM),
            pl.BlockSpec((tile, width), early),
            hbm,
            hbm,
            hbm,
            hbm,
            const(*vec.shape),
            const(*bias.shape),
            const(KW, GW),
            const(GW, GW),
        ],
        out_specs=[
            pl.BlockSpec((tile, 3 * width), early),
            late,
            late,
            late,
            late,
            pl.BlockSpec((tile // QB, KW, width), lambda i: (jnp.maximum(i - steps, 0), 0, 0)),
            pl.BlockSpec((width, tile), lambda i: (0, jnp.minimum(i, steps - 1))),
            const(groups, 2 * GW, GW),
            const(groups, GW, GW),
            const(groups, 8, GW),
            const(width, 3 * width),
            const(8, width),
            const(1, hidden),
            hbm,
            hbm,
            hbm,
        ],
        out_shape=[sds((rows, 3 * width), bf16)]
        + [sds((rows, width), bf16)] * 4
        + [
            sds((rows // QB, KW, width), bf16),
            sds((width, rows), bf16),
            sds((groups, 2 * GW, GW), bf16),
            sds((groups, GW, GW), bf16),
            sds((groups, 8, GW), f32),
            sds((width, 3 * width), bf16),
            sds((8, width), f32),
            sds((1, hidden), f32),
            sds(got(*w_in.shape), bf16),
            sds(got(*w_back.shape), bf16),
            sds(got(*w_out.shape), bf16),
        ],
        scratch_shapes=[
            pltpu.VMEM((rows + 2 * HALO, 3 * width), bf16),
            pltpu.VMEM((groups, GW, 2 * GW), f32),
            pltpu.VMEM((groups, 8, GW), f32),
            pltpu.VMEM(got(*w_qkv.shape), bf16),
            pltpu.VMEM((16, 128), bf16),
            pltpu.VMEM(got(16, 128), bf16),
            pltpu.VMEM(w_in.shape, bf16),
            pltpu.VMEM(w_back.shape, bf16),
            pltpu.VMEM(w_out.shape, bf16),
            pltpu.SemaphoreType.DMA((pieces, per)),
            pltpu.SemaphoreType.DMA((pieces, per)),
            pltpu.SemaphoreType.DMA((pieces,)),
        ],
        compiler_params=pltpu.CompilerParams(
            collective_id=0, has_side_effects=True, vmem_limit_bytes=VMEM_LIMIT
        ),
        cost_estimate=pl.CostEstimate(
            flops=2 * rows * width * 8 * width, bytes_accessed=rows * width * 24, transcendentals=0
        ),
        name="front_pass",
    )(
        length,
        tokens,
        w_qkv,
        w_in,
        w_back,
        w_out,
        vec,
        bias,
        jnp.asarray(band_table(head)),
        jnp.asarray(head_table(head), bf16),
    )


def ffn_kernel(
    chunk,
    len_ref,
    tok_ref,
    cot_ref,
    near_ref,
    fa_ref,
    fb_ref,
    rn_ref,
    q_ref,
    c_ref,
    vec_ref,
    bin_ref,
    gw_out,
    gw_in,
    gw_back,
    out_ref,
    datt_ref,
    dmix_ref,
    dn_ref,
    gin_ref,
    gback_ref,
    gout_ref,
    gvec_ref,
    gbias_ref,
    m3_ref,
    m4_ref,
    dt_ref,
    a_in,
    a_back,
    a_out,
    a_st,
    a_bent,
    wout_ref,
    win_ref,
    wback_ref,
    act_s,
    pre_s,
):
    step = pl.program_id(0)
    rows, width = tok_ref.shape
    hidden = win_ref.shape[1]
    groups = width // GW
    head_size = width // HEADS
    steps = pl.num_programs(0)
    length = len_ref[0, 0]
    c_row = jnp.concatenate([c_ref[g, 0:1] for g in range(groups)], axis=1)
    blend = vec_ref[...].astype(bf16)
    s0 = math.sqrt(2.0 / math.pi)
    s1 = s0 * 0.044715

    @pl.when(step == 0)
    def _():
        join_blocks(wout_ref, gw_out)
        join_blocks(win_ref, gw_in)
        join_blocks(wback_ref, gw_back)
        for ref in (a_in, a_back, a_out, a_st, a_bent, gvec_ref, gbias_ref):
            ref[...] = jnp.zeros_like(ref)

    near = near_ref[...]
    fac = fa_ref[...]
    far_b = fb_ref[...]
    mixed = (
        vec_ref[5:6] * near.astype(f32)
        + vec_ref[6:7] * (fac.astype(f32) + c_row)
        + vec_ref[7:8] * far_b.astype(f32)
    ).astype(bf16)
    resid = tok_ref[...].astype(f32) + nn(mixed, wout_ref[...])
    z2, r2 = moments(resid)
    h2 = (z2 * vec_ref[2:3] + vec_ref[3:4]).astype(bf16)
    valid = row_valid(step, rows, width, length)
    d_ffn = jnp.where(valid, cot_ref[...], 0)
    seed = d_ffn.astype(f32)
    for lo in range(0, hidden, chunk):
        cols = slice(lo, lo + chunk)
        x = nn(h2, win_ref[:, cols]) + bin_ref[0:1, cols]
        x2 = x * x
        half = 0.5 + 0.5 * jnp.tanh(x * (s0 + s1 * x2))
        act = x * half
        slope = half + (act - act * half) * (2 * s0 + 6 * s1 * x2)
        act = act.astype(bf16)
        act_s[:, cols] = act
        a_back[:, cols] += tn(d_ffn, act)
        d_pre = slope * nt(d_ffn, wback_ref[cols, :])
        gbias_ref[:, cols] += fold8(d_pre)
        d_pre = d_pre.astype(bf16)
        pre_s[:, cols] = d_pre
        a_in[:, cols] += tn(h2, d_pre)
    dh2 = nt(pre_s[...], win_ref[...])
    both = dh2 * z2
    gvec_ref[2] += fold8(both)
    gvec_ref[3] += fold8(dh2)
    gvec_ref[4] += fold8(seed)
    dz = dh2 * vec_ref[2:3]
    mean_z = jnp.mean(both * vec_ref[2:3], axis=-1, keepdims=True)
    d_resid = seed + r2 * (dz - jnp.mean(dz, axis=-1, keepdims=True) - z2 * mean_z)
    d_attn = d_resid.astype(bf16)
    datt_ref[...] = d_attn
    ffn = nn(act_s[...], wback_ref[...])
    out_ref[...] = jnp.where(valid, resid + ffn + vec_ref[4:5], 0.0).astype(bf16)
    a_out[...] += tn(mixed, d_attn)
    d_mix = nt(d_attn, wout_ref[...]).astype(bf16)
    dmix_ref[...] = d_mix
    gvec_ref[5] += fold8(fold4(d_mix * near).astype(f32))
    gvec_ref[6] += fold8(fold4(d_mix * fac).astype(f32))
    gvec_ref[7] += fold8(fold4(d_mix * far_b).astype(f32))
    gvec_ref[0] += fold8(fold4(d_mix).astype(f32))
    d_num = blend[6:7] * d_mix * rn_ref[...]
    dn_ref[...] = d_num
    d_den = d_num * fac
    d_far = blend[7:8] * d_mix
    for g in range(groups):
        cols = slice(g * GW, (g + 1) * GW)
        q = q_ref[:, cols]
        a_st[g] += tn(lift(q), jnp.concatenate([d_num[:, cols], d_den[:, cols]], axis=1))
        a_bent[g] += tn(jnp.tanh(q), d_far[:, cols])

    @pl.when(step == steps - 1)
    def _():
        mask = same_head(head_size).astype(f32)
        inv_len = 1.0 / length.astype(f32)
        ones = jnp.ones((8, GW), f32)
        for g in range(groups):
            m3_ref[g] = (a_st[g][:, :GW] * mask).astype(bf16)
            m4_ref[g] = (a_bent[g] * mask * inv_len).astype(bf16)
            dt_ref[g] = -nt_exact(ones, a_st[g][:, GW:] * mask)
        cut_blocks(gin_ref, a_in)
        cut_turned(gback_ref, a_back)
        cut_blocks(gout_ref, a_out)
        gvec_ref[6] += gvec_ref[0] * c_row


def third_pass(
    ways, length, tokens, cot, near, fa, fb, rn, qkv, c, vecs, b_in, w_out, w_in, w_back, tile, chunk
):
    rows, width = tokens.shape
    hidden = w_in.shape[0] * w_in.shape[3]
    groups = width // GW
    steps = rows // tile
    n_dp, n_fsdp = ways
    back = (width // n_dp, hidden // n_fsdp)
    back = back if turned(hidden, n_fsdp) else back[::-1]

    def const(*shape):
        return pl.BlockSpec(shape, lambda i: (0,) * len(shape))

    def kept(*shape):
        return pl.BlockSpec(shape, lambda i: (0,) * len(shape), pipeline_mode=pl.Buffered(1))

    sds = jax.ShapeDtypeStruct
    block = pl.BlockSpec((tile, width), lambda i: (i, 0))
    deep = pltpu.VMEM((tile, hidden), bf16)
    return pl.pallas_call(
        functools.partial(ffn_kernel, chunk),
        grid=(steps,),
        in_specs=[pl.BlockSpec(memory_space=pltpu.SMEM)]
        + [block] * 7
        + [
            const(groups, 8, GW),
            const(8, width),
            const(1, hidden),
            kept(*w_out.shape),
            kept(*w_in.shape),
            kept(*w_back.shape),
        ],
        out_specs=[block] * 4
        + [
            const(n_dp, n_fsdp, width // n_fsdp, hidden // n_dp),
            const(n_dp, n_fsdp, *back),
            const(n_dp, n_fsdp, width // n_fsdp, width // n_dp),
            const(8, 8, width),
            const(8, hidden),
            const(groups, GW, GW),
            const(groups, GW, GW),
            const(groups, 8, GW),
        ],
        out_shape=[sds((rows, width), bf16)] * 4
        + [
            sds((n_dp, n_fsdp, width // n_fsdp, hidden // n_dp), bf16),
            sds((n_dp, n_fsdp, *back), bf16),
            sds((n_dp, n_fsdp, width // n_fsdp, width // n_dp), bf16),
            sds((8, 8, width), f32),
            sds((8, hidden), f32),
            sds((groups, GW, GW), bf16),
            sds((groups, GW, GW), bf16),
            sds((groups, 8, GW), f32),
        ],
        scratch_shapes=[
            pltpu.VMEM((width, hidden), f32),
            pltpu.VMEM((width, hidden), f32),
            pltpu.VMEM((width, width), f32),
            pltpu.VMEM((groups, GW, 2 * GW), f32),
            pltpu.VMEM((groups, GW, GW), f32),
            pltpu.VMEM((width, width), bf16),
            pltpu.VMEM((width, hidden), bf16),
            pltpu.VMEM((hidden, width), bf16),
            deep,
            deep,
        ],
        compiler_params=pltpu.CompilerParams(vmem_limit_bytes=VMEM_LIMIT),
        cost_estimate=pl.CostEstimate(
            flops=2 * rows * width * (6 * hidden + 4 * width),
            bytes_accessed=rows * width * 22,
            transcendentals=0,
        ),
        name="third_pass",
    )(length, tokens, cot, near, fa, fb, rn, qkv, c, vecs, b_in, w_out, w_in, w_back)


class Scatter:
    def __init__(self, place, src, out, bufs, send, recv, local, order):
        self.p, self.src, self.out, self.order = place, src, out, order
        self.acc, self.r0, self.r1, self.r2, self.r3 = bufs
        self.send, self.recv, self.local = send, recv, local

    @staticmethod
    def count(n_dp, n_fsdp):
        return 1 + 1 + (n_dp // 2 - 1) + (n_fsdp // 2 - 1)

    @staticmethod
    def scratch(n_dp, n_fsdp, r, c, order, dtype):
        nh, m = n_dp // 2, n_fsdp // 2
        if order == "x":
            one, two = (nh, m, r, c), (nh - 1, m, r, c)
        else:
            one, two = (nh - 1, m, 2, r, c), (m, r, c)
        shapes = [(nh, m, 2, r, c), (nh, m, 2, r, c), one, two, (m - 1, r, c)]
        return [pltpu.VMEM(s, dtype) for s in shapes]

    def own(self):
        return pltpu.make_async_copy(self.src.at[:, self.p.dl], self.acc, self.local)

    def stage(self, k):
        p = self.p
        if k == 0:
            ref = self.src.at[:, 1 - p.dl]
            return [copy_to(ref, self.r0, self.send.at[0], self.recv.at[0], p.dev(dl=1 - p.dl))]
        if k == 3:
            i = p.nh
            out = []
            for o in range(1, p.m):
                fh = lax.rem(p.fh + o, p.m)
                out.append(
                    copy_to(self.acc.at[p.dh, fh, p.fl], self.r3.at[o - 1], self.send.at[i + o], self.recv.at[i + o],
                            p.dev(fh=fh))
                )
            return out
        if (k == 1) == (self.order == "x"):
            ref = self.acc.at[:, :, 1 - p.fl] if k == 1 else self.acc.at[p.dh, :, 1 - p.fl]
            dst = self.r1 if k == 1 else self.r2
            return [copy_to(ref, dst, self.send.at[1], self.recv.at[1], p.dev(fl=1 - p.fl))]
        out = []
        for o in range(1, p.nh):
            dh = lax.rem(p.dh + o, p.nh)
            ref = self.acc.at[dh] if k == 1 else self.acc.at[dh, :, p.fl]
            dst = self.r1.at[o - 1] if k == 1 else self.r2.at[o - 1]
            out.append(copy_to(ref, dst, self.send.at[1 + o], self.recv.at[1 + o], p.dev(dh=dh)))
        return out

    def start(self, k):
        for c in self.stage(k):
            c.start()

    def turn(self, k):
        if k == 0:
            self.own().wait()
        for c in self.stage(k):
            c.wait()
        self.add(k)
        if k < 3:
            self.start(k + 1)

    def add(self, k):
        p, acc = self.p, self.acc
        nh, m = p.nh, p.m
        dt = acc.dtype

        def put(index, others):
            total = acc[index].astype(f32)
            for o in others:
                total = total + o.astype(f32)
            acc[index] = total.astype(dt)

        if k == 3:
            total = acc[p.dh, p.fh, p.fl].astype(f32)
            for o in range(1, m):
                total = total + self.r3[o - 1].astype(f32)
            self.out[...] = total
            return

        @pl.loop(0, m)
        def _(i):
            if k == 0:
                for a in range(nh):
                    for b in range(2):
                        put((a, i, b), [self.r0[a, i, b]])
            elif k == 1 and self.order == "x":
                for a in range(nh):
                    put((a, i, p.fl), [self.r1[a, i]])
            elif k == 1:
                for b in range(2):
                    put((p.dh, i, b), [self.r1[o - 1, i, b] for o in range(1, nh)])
            elif self.order == "x":
                put((p.dh, i, p.fl), [self.r2[o - 1, i] for o in range(1, nh)])
            else:
                put((p.dh, i, p.fl), [self.r2[i]])


def back_kernel(
    ways,
    plan,
    late_plan,
    len_ref,
    q_ref,
    k_lo,
    k_ref,
    k_hi,
    v_lo,
    v_ref,
    v_hi,
    p_ref,
    dmix_ref,
    dn_ref,
    fa_ref,
    tok_ref,
    datt_ref,
    h1t_ref,
    m1_ref,
    m2_ref,
    m3_ref,
    m4_ref,
    dt_ref,
    c_ref,
    vec_ref,
    w_ref,
    hm_ref,
    gv_ref,
    gbias_ref,
    s_in,
    s_back,
    s_out,
    dtok_ref,
    oqkv_ref,
    oin_ref,
    oback_ref,
    oout_ref,
    ovec_ref,
    obias_ref,
    kk,
    vv,
    far_s,
    dp_s,
    ds_s,
    all_d,
    carry,
    gvec_s,
    gq_ref,
    gs_ref,
    rows_s,
    back_t,
    small_o,
    late_src,
    late_got,
    *rest,
):
    step = pl.program_id(0)
    rows, width = q_ref.shape
    total = h1t_ref.shape[1]
    steps = total // rows
    groups = width // GW
    head = width // HEADS
    scale = head ** (-0.5)
    length = len_ref[0, 0]
    n_dp, n_fsdp = ways
    place = Place(n_dp, n_fsdp)
    cols = ovec_ref.shape[1]
    c_all = oqkv_ref.shape[1]
    send, recv, local, late_send, late_recv = rest[-5:]
    final = steps + 1 + place.nh
    last_rows = tok_ref.shape[0]

    used = [0]

    def piece(src, out, order):
        j = used[0]
        used[0] += 1
        return Scatter(place, src, out, rest[5 * j : 5 * j + 5], send.at[j], recv.at[j], local.at[j], order)

    sets = [[], [], [], []]
    every = (slice(None),) * 4
    for i, (cut_in, cut_back) in enumerate(ffn_parts(s_in.shape[-2:], s_back.shape[-2:])):
        sets[i].append(piece(s_in.at[every + cut_in], oin_ref.at[cut_in], "x"))
        sets[i].append(piece(s_back.at[every + cut_back], back_t.at[cut_back], "y"))
    sets[1].append(piece(s_out, oout_ref, "y"))
    sets[1].append(piece(gs_ref, small_o, "x"))
    for which, cut, order in qkv_parts(*oqkv_ref.shape):
        sets[2 + which].append(piece(gq_ref.at[every + cut], oqkv_ref.at[cut], order))

    @pl.when(step == 0)
    def _():
        for x in sets[0] + sets[1][:-1]:
            x.own().start()
        greet_all(place)
        for x in sets[0] + sets[1][:-1]:
            x.start(0)
        carry[...] = jnp.zeros_like(carry)
        gvec_s[...] = jnp.zeros_like(gvec_s)
        gs_ref[...] = jnp.zeros_like(gs_ref)
        late_src[...] = jnp.zeros_like(late_src)
        rows_s[0:2] = jnp.zeros((2, width), f32)
        rows_s[2:8] = jnp.sum(gv_ref[2:8], axis=1)
        bias = jnp.sum(gbias_ref[...], axis=0, keepdims=True)
        for d in range(n_dp):
            pair = rows_s[2 * d : 2 * d + 2]
            for f in range(n_fsdp):
                spot = slice(f * cols, (f + 1) * cols)
                at = d * width + f * cols
                gs_ref[d // 2, d % 2, f // 2, f % 2, 0:2, :cols] = pair[:, spot]
                gs_ref[d // 2, d % 2, f // 2, f % 2, 2:3, :cols] = bias[:, at : at + cols]
        sets[1][-1].own().start()
        sets[1][-1].start(0)

    for at, moves in plan.items():

        @pl.when(step == at)
        def _(moves=moves):
            for which, k in moves:
                for x in sets[which]:
                    x.turn(k)

    def far_keys(at, slot, live):
        valid = row_valid(at, rows, GW, length) & live
        here = pl.ds(pl.multiple_of(at * rows + HALO, HALO), rows)
        for g in range(groups):
            cut = slice(g * GW, (g + 1) * GW)
            kc = slice(width + g * GW, width + (g + 1) * GW)
            vc = slice(2 * width + g * GW, 2 * width + (g + 1) * GW)
            k = kk[slot, HALO : HALO + rows, cut]
            v = vv[slot, HALO : HALO + rows, cut]
            lift_k = lift(k)
            bent_k = jnp.tanh(k)
            bent = bent_k.astype(f32)
            v_cen = v - c_ref[g, 0:1].astype(bf16)
            dk = (nt(v_cen, m3_ref[g]) + dt_ref[g, 0:1]) * jnp.minimum(lift_k, 1.0).astype(f32)
            dk += nt(v, m4_ref[g]) * (1.0 - bent * bent)
            both = jnp.concatenate([lift_k, bent_k], axis=1)
            dv = nn(both, jnp.concatenate([m3_ref[g], m4_ref[g]], axis=0))
            all_d[here, kc] = (all_d[here, kc].astype(f32) + jnp.where(valid, dk, 0.0)).astype(bf16)
            all_d[here, vc] = (all_d[here, vc].astype(f32) + jnp.where(valid, dv, 0.0)).astype(bf16)

    @pl.when(step < steps)
    def _():
        slot = lax.rem(step, 2)
        kk[slot, :HALO] = k_lo[...]
        kk[slot, HALO : HALO + rows] = k_ref[...]
        kk[slot, HALO + rows :] = k_hi[...]
        vv[slot, :HALO] = v_lo[...]
        vv[slot, HALO : HALO + rows] = v_ref[...]
        vv[slot, HALO + rows :] = v_hi[...]
        hm = hm_ref[...]
        blend = vec_ref[...].astype(bf16)
        base = step * rows
        for g in range(groups):
            cut = slice(g * GW, (g + 1) * GW)
            kc = slice(width + g * GW, width + (g + 1) * GW)
            vc = slice(2 * width + g * GW, 2 * width + (g + 1) * GW)
            q = q_ref[:, cut]
            d_num = dn_ref[:, cut]
            d_den = -d_num * fa_ref[:, cut]
            d_mix = dmix_ref[:, cut]
            bent = jnp.tanh(q).astype(f32)
            far = nn(jnp.concatenate([d_num, d_den], axis=1), m1_ref[g]) * jnp.minimum(lift(q), 1.0).astype(f32)
            far_s[:, cut] = far + nn(blend[7:8, cut] * d_mix, m2_ref[g]) * (1.0 - bent * bent)
            for b in range(rows // QB):
                here = slice(b * QB, (b + 1) * QB)
                window = slice(b * QB, b * QB + KW)
                ds = spread_rows(blend[5:6, cut] * dmix_ref[here, cut], hm)
                dp_s[g, b] = nt(vv[slot, window, cut], ds)
            for b in range(rows // QB):
                pw = p_ref[b, :, cut].astype(f32)
                t = pw * dp_s[g, b]
                ds_s[g, b] = (t - pw * jnp.sum(t, axis=0, keepdims=True)).astype(bf16)
            old_k = carry[0, :, cut]
            old_v = carry[1, :, cut]
            for b in range(rows // QB):
                here = slice(b * QB, (b + 1) * QB)
                window = slice(b * QB, b * QB + KW)
                d_s = ds_s[g, b]
                dk = nn(d_s, spread_rows(q_ref[here, cut] * scale, hm))
                dv = nn(p_ref[b, :, cut], spread_rows(blend[5:6, cut] * dmix_ref[here, cut], hm))
                dq = pick_heads(tn(d_s, kk[slot, window, cut]), head) * scale + far_s[here, cut]
                lo = pl.ds(pl.multiple_of(base + b * QB, QB), QB)
                all_d[pl.ds(pl.multiple_of(base + b * QB + HALO, HALO), QB), cut] = dq.astype(bf16)
                all_d[lo, kc] = (old_k + dk[:QB]).astype(bf16)
                all_d[lo, vc] = (old_v + dv[:QB]).astype(bf16)
                old_k = dk[QB:]
                old_v = dv[QB:]
            carry[0, :, cut] = old_k
            carry[1, :, cut] = old_v
        far_keys(jnp.maximum(step - 1, 0), 1 - slot, step > 0)

    @pl.when(step == steps)
    def _():
        all_d[total:, width : 2 * width] = carry[0].astype(bf16)
        all_d[total:, 2 * width :] = carry[1].astype(bf16)
        far_keys(steps - 1, (steps - 1) % 2, True)

    for dh in range(n_dp // 2):

        @pl.when(step == steps + 1 + dh)
        def _(dh=dh):
            grad = nn(h1t_ref[...], all_d[HALO : HALO + total, dh * 2 * c_all : (dh + 1) * 2 * c_all])
            r = gq_ref.shape[-2]
            for dl in range(2):
                for f in range(n_fsdp):
                    block = grad[f * r : (f + 1) * r, dl * c_all : (dl + 1) * c_all]
                    gq_ref[dh, dl, f // 2, f % 2] = block.astype(bf16)

    @pl.when(step == final)
    def _():
        for x in sets[2] + sets[3]:
            x.own().start()
            x.start(0)

    for at, moves in late_plan.items():
        if at == "end":
            continue

        @pl.when(step == final + at)
        def _(moves=moves):
            for which, k in moves:
                for x in sets[which]:
                    x.turn(k)

    @pl.when(step >= final)
    def _():
        here = pl.ds(pl.multiple_of((step - final) * last_rows + HALO, HALO), last_rows)
        z1, r1 = moments(tok_ref[...].astype(f32))
        dh1 = nt(all_d[here], w_ref[...])
        gvec_s[0] += fold8(dh1 * z1)
        gvec_s[1] += fold8(dh1)
        dz = dh1 * vec_ref[0:1]
        dtok_ref[...] = (
            datt_ref[...].astype(f32)
            + r1
            * (
                dz
                - jnp.mean(dz, axis=-1, keepdims=True)
                - z1 * jnp.mean(dz * z1, axis=-1, keepdims=True)
            )
        ).astype(bf16)

    @pl.when(step == final + total // last_rows - 1)
    def _():
        rows_s[0:2] = jnp.sum(gvec_s[...], axis=1)
        for f in range(n_fsdp):
            late_src[f, 0:2, :cols] = rows_s[0:2, f * cols : (f + 1) * cols]
        d, f = lax.axis_index("dp"), lax.axis_index("fsdp")
        me = d * n_fsdp + f

        def late(o):
            to = lax.rem(f + o, n_fsdp)
            return copy_to(
                late_src.at[to], late_got.at[me], late_send.at[o], late_recv.at[me], {"dp": 0, "fsdp": to}
            )

        @pl.when(d > 0)
        def _():
            late(0).start()

        for o in range(1, n_fsdp):
            late(o).start()
        oback_ref[...] = back_t[...].T if turned(gbias_ref.shape[1], n_fsdp) else back_t[...]
        for which, k in late_plan["end"]:
            for x in sets[which]:
                x.turn(k)

        @pl.when(d > 0)
        def _():
            late(0).wait_send()
            ovec_ref[...] = small_o[0:2, :cols]

        for o in range(1, n_fsdp):
            late(o).wait_send()

        @pl.when(d == 0)
        def _():
            late_got[me] = late_src[f]

            @pl.loop(0, n_dp * n_fsdp)
            def _(s):
                @pl.when(s != me)
                def _():
                    copy_to(
                        late_src.at[0], late_got.at[s], late_send.at[0], late_recv.at[s], {"dp": 0, "fsdp": 0}
                    ).wait_recv()

            ovec_ref[...] = jnp.sum(late_got[...], axis=0)[0:2, :cols]

        obias_ref[...] = small_o[2:3, :cols]


def ffn_parts(shape_in, shape_back):
    (r, c), (rb, cb) = shape_in, shape_back
    out = []
    for i in range(2):
        cut_in = (pl.ds(0, r), pl.ds(i * c // 2, c // 2))
        if cb % 256:
            cut_back = (pl.ds(i * rb // 2, rb // 2), pl.ds(0, cb))
        else:
            cut_back = (pl.ds(0, rb), pl.ds(i * cb // 2, cb // 2))
        out.append((cut_in, cut_back))
    return out


def greet_all(place):
    d, f = lax.axis_index("dp"), lax.axis_index("fsdp")
    n_dp, n_fsdp = 2 * place.nh, 2 * place.m
    barrier = pltpu.get_barrier_semaphore()
    who = place.partners()
    for dev in who:
        pl.semaphore_signal(barrier, inc=1, device_id=dev, device_id_type=MESH)

    @pl.when(d == 0)
    def _():
        @pl.loop(0, n_dp)
        def _(i):
            @pl.loop(0, n_fsdp)
            def _(j):
                @pl.when((i != 0) | (j != f))
                def _():
                    pl.semaphore_signal(barrier, inc=1, device_id={"dp": i, "fsdp": j}, device_id_type=MESH)

    pl.semaphore_wait(barrier, len(who) + n_fsdp - (d == 0).astype(jnp.int32))


def back_pass(
    ways,
    length,
    qkv,
    p,
    d_mix,
    tokens,
    d_attn,
    d_num,
    fa,
    h1t,
    m1,
    m2,
    m3,
    m4,
    dt,
    c,
    vecs,
    w_qkv,
    gv,
    gbias,
    s_in,
    s_back,
    s_out,
    tile,
    last_tile,
    plan,
    late_plan,
):
    rows, width = tokens.shape
    groups = width // GW
    steps = rows // tile
    n_dp, n_fsdp = ways
    nh, m = n_dp // 2, n_fsdp // 2
    r, c_all = width // n_fsdp, 3 * width // n_dp
    per = Scatter.count(n_dp, n_fsdp)
    final = steps + 1 + nh
    hbm = pl.BlockSpec(memory_space=pl.ANY)
    back_shape = s_back.shape[-2:]
    outs = [
        (r, c_all),
        s_in.shape[-2:],
        back_shape[::-1] if turned(gbias.shape[1], n_fsdp) else back_shape,
        s_out.shape[-2:],
        (2, width // n_fsdp),
        (1, gbias.shape[1] // (n_dp * n_fsdp)),
    ]
    kinds = []
    for cut_in, cut_back in ffn_parts(s_in.shape[-2:], back_shape):
        kinds.append((*(x.size for x in cut_in), "x", bf16))
        kinds.append((*(x.size for x in cut_back), "y", bf16))
    kinds.append((*s_out.shape[-2:], "y", bf16))
    kinds.append((8, 128, "x", f32))
    for _, cut, order in qkv_parts(r, c_all):
        kinds.append((*(x.size for x in cut), order, bf16))
    bufs = [b for k in kinds for b in Scatter.scratch(n_dp, n_fsdp, *k)]
    got = lambda *s: (nh, 2, m, 2, *s)

    def const(*shape):
        return pl.BlockSpec(shape, lambda i: (0,) * len(shape))

    def kept(*shape):
        return pl.BlockSpec(shape, lambda i: (0,) * len(shape), pipeline_mode=pl.Buffered(1))

    one = lambda i: jnp.minimum(i, steps - 1)
    end = lambda i: jnp.maximum(i - final, 0)
    per_tile = tile // HALO
    top = rows // HALO - 1

    def halo(col):
        return [
            pl.BlockSpec((HALO, width), lambda i: (jnp.maximum(one(i) * per_tile - 1, 0), col)),
            pl.BlockSpec((tile, width), lambda i: (one(i), col)),
            pl.BlockSpec((HALO, width), lambda i: (jnp.minimum((one(i) + 1) * per_tile, top), col)),
        ]

    block = pl.BlockSpec((tile, width), lambda i: (one(i), 0))
    late = pl.BlockSpec((last_tile, width), lambda i: (end(i), 0))
    head = width // HEADS
    sds = jax.ShapeDtypeStruct
    return pl.pallas_call(
        functools.partial(back_kernel, ways, plan, late_plan),
        grid=(final + rows // last_tile,),
        in_specs=[
            pl.BlockSpec(memory_space=pltpu.SMEM),
            block,
            *halo(1),
            *halo(2),
            pl.BlockSpec((tile // QB, KW, width), lambda i: (one(i), 0, 0)),
            block,
            block,
            block,
            late,
            late,
            kept(width, rows),
            kept(groups, 2 * GW, GW),
            kept(groups, GW, GW),
            kept(groups, GW, GW),
            kept(groups, GW, GW),
            const(groups, 8, GW),
            const(groups, 8, GW),
            const(8, width),
            kept(width, 3 * width),
            const(GW, GW),
            const(*gv.shape),
            const(*gbias.shape),
            hbm,
            hbm,
            hbm,
        ],
        out_specs=[late] + [const(*s) for s in outs],
        out_shape=[sds((rows, width), bf16)] + [sds(s, f32) for s in outs],
        scratch_shapes=[
            pltpu.VMEM((2, tile + 2 * HALO, width), bf16),
            pltpu.VMEM((2, tile + 2 * HALO, width), bf16),
            pltpu.VMEM((tile, width), f32),
            pltpu.VMEM((groups, tile // QB, KW, GW), f32),
            pltpu.VMEM((groups, tile // QB, KW, GW), bf16),
            pltpu.VMEM((rows + 2 * HALO, 3 * width), bf16),
            pltpu.VMEM((2, QB, width), f32),
            pltpu.VMEM((2, 8, width), f32),
            pltpu.VMEM(got(r, c_all), bf16),
            pltpu.VMEM(got(8, 128), f32),
            pltpu.VMEM((8, width), f32),
            pltpu.VMEM(back_shape, f32),
            pltpu.VMEM((8, 128), f32),
            pltpu.VMEM((n_fsdp, 8, 128), f32),
            pltpu.VMEM((n_dp * n_fsdp, 8, 128), f32),
            *bufs,
            pltpu.SemaphoreType.DMA((len(kinds), per)),
            pltpu.SemaphoreType.DMA((len(kinds), per)),
            pltpu.SemaphoreType.DMA((len(kinds),)),
            pltpu.SemaphoreType.DMA((n_fsdp,)),
            pltpu.SemaphoreType.DMA((n_dp * n_fsdp,)),
        ],
        compiler_params=pltpu.CompilerParams(
            collective_id=1, has_side_effects=True, vmem_limit_bytes=VMEM_LIMIT
        ),
        cost_estimate=pl.CostEstimate(
            flops=2 * rows * width * 14 * width, bytes_accessed=rows * width * 24, transcendentals=0
        ),
        name="back_pass",
    )(
        length,
        qkv,
        qkv,
        qkv,
        qkv,
        qkv,
        qkv,
        qkv,
        p,
        d_mix,
        d_num,
        fa,
        tokens,
        d_attn,
        h1t,
        m1,
        m2,
        m3,
        m4,
        dt,
        c,
        vecs,
        w_qkv,
        jnp.asarray(head_table(head), bf16),
        gv,
        gbias,
        s_in,
        s_back,
        s_out,
    )


def hand_kernel(n, *refs):
    for j in range(n):
        refs[n + j][...] = refs[j][...]


def hand_over(arrays, parts):
    first = arrays[0]
    block = pl.BlockSpec((first.shape[0] // parts, first.shape[1]), lambda i: (i, 0))
    specs = [block] + [pl.BlockSpec(a.shape, lambda i: (0, 0)) for a in arrays[1:]]
    return pl.pallas_call(
        functools.partial(hand_kernel, len(arrays)),
        grid=(parts,),
        in_specs=specs,
        out_specs=specs,
        out_shape=[jax.ShapeDtypeStruct(a.shape, a.dtype) for a in arrays],
        name="hand_over",
    )(*arrays)


FRONT_TILE = 1024
TILE = 512
LAST_TILE = 1024
CHUNK = 256
FRONT_PLAN = {1: [(0, 0), (1, 0)], 3: [(0, 1)], 4: [(1, 1)], 5: [(0, 2)], 6: [(1, 2)], 8: [(0, 3), (1, 3)]}
BACK_PLAN = {2: [(0, 0)], 3: [(1, 0)], 4: [(0, 1)], 6: [(1, 1), (0, 2)], 8: [(1, 2), (0, 3)], 10: [(1, 3)]}
LATE_PLAN = {1: [(2, 0), (3, 0)], 3: [(2, 1), (3, 1)], "end": [(2, 2), (3, 2), (2, 3), (3, 3)]}


def shards(
    tokens, cotangent, w_qkv, w_out, w_in, w_back, vec_params, b_in, item_lengths, bucket_counts, *, ways
):
    n_dp, n_fsdp = ways
    (
        qkv,
        near,
        fa,
        fb,
        rn,
        p,
        h1t,
        m1,
        m2,
        c,
        qkv_w,
        vecs,
        in_bias,
        g_in,
        g_back,
        g_out,
    ) = front_pass(
        ways, item_lengths, tokens, w_qkv, w_in, w_back, w_out, vec_params, b_in[None], FRONT_TILE, FRONT_PLAN
    )

    def blocks(g):
        return g.reshape(n_dp, n_fsdp, *g.shape[-2:])

    def pairs(g):
        return g.reshape(n_dp // 2, 2, n_fsdp // 2, 2, *g.shape[-2:])

    (out, d_attn, d_mix, d_num, s_in, s_back, s_out, g_vec, g_bias, m3, m4, dt) = third_pass(
        ways,
        item_lengths,
        tokens,
        cotangent,
        near,
        fa,
        fb,
        rn,
        qkv,
        c,
        vecs,
        in_bias,
        blocks(g_out),
        blocks(g_in),
        blocks(g_back),
        TILE,
        CHUNK,
    )
    d_tok, r_qkv, r_in, r_back, r_out, r_vec, r_bias = back_pass(
        ways,
        item_lengths,
        qkv,
        p,
        d_mix,
        tokens,
        d_attn,
        d_num,
        fa,
        h1t,
        m1,
        m2,
        m3,
        m4,
        dt,
        c,
        vecs,
        qkv_w,
        g_vec,
        g_bias,
        pairs(s_in),
        pairs(s_back),
        pairs(s_out),
        TILE,
        LAST_TILE,
        BACK_PLAN,
        LATE_PLAN,
    )
    d_tok, r_qkv, r_out, r_in, r_back, r_vec, r_bias = hand_over(
        [d_tok, r_qkv, r_out, r_in, r_back, r_vec, r_bias], 8
    )
    return (out, d_tok, r_qkv, r_out, r_in, r_back, r_vec, r_bias[0])


def solution(mesh):
    in_specs = (
        P(("dp", "fsdp"), None),
        P(("dp", "fsdp"), None),
        P("fsdp", "dp"),
        P("fsdp", "dp"),
        P("fsdp", "dp"),
        P("fsdp", "dp"),
        P("dp", "fsdp"),
        P(("dp", "fsdp")),
        P(("dp", "fsdp"), None),
        P(("dp", "fsdp"), None),
    )
    out_specs = (
        P(("dp", "fsdp"), None),
        P(("dp", "fsdp"), None),
        P("fsdp", "dp"),
        P("fsdp", "dp"),
        P("fsdp", "dp"),
        P("fsdp", "dp"),
        P("dp", "fsdp"),
        P(("dp", "fsdp")),
    )
    ways = (mesh.shape["dp"], mesh.shape["fsdp"])
    body = functools.partial(shards, ways=ways)
    return jax.shard_map(body, mesh=mesh, in_specs=in_specs, out_specs=out_specs, check_vma=False)
```

```python
import functools
import math

import jax
import jax.numpy as jnp
import numpy as np
from jax import lax
from jax.experimental import pallas as pl
from jax.experimental.pallas import tpu as pltpu
from jax.sharding import PartitionSpec as P

HEADS = 8
BAND = 30
QB = 64
HALO = 32
KW = QB + 2 * HALO
GW = 256

norm_eps = 1e-05
f32 = jnp.float32
bf16 = jnp.bfloat16
exact = lax.Precision.HIGHEST
VMEM_LIMIT = 60 * 1024 * 1024


def nn(a, b):
    return lax.dot_general(a, b, (((1,), (0,)), ((), ())), preferred_element_type=f32)


def nt(a, b):
    return lax.dot_general(a, b, (((1,), (1,)), ((), ())), preferred_element_type=f32)


def tn(a, b):
    return lax.dot_general(a, b, (((0,), (0,)), ((), ())), preferred_element_type=f32)


def nt_exact(a, b):
    return lax.dot_general(
        a, b, (((1,), (1,)), ((), ())), preferred_element_type=f32, precision=exact
    )


def lift(t):
    return jnp.where(t > 0, t + 1, jnp.exp(jnp.minimum(t, 0)))


def moments(x):
    mean = jnp.mean(x, axis=-1, keepdims=True)
    cen = x - mean
    inv = lax.rsqrt(jnp.mean(cen * cen, axis=-1, keepdims=True) + norm_eps)
    return cen * inv, inv


def fold8(x):
    return jnp.sum(x.reshape(x.shape[0] // 8, 8, x.shape[1]), axis=0)


def fold4(x):
    n = x.shape[0] // 4
    return (x[:n] + x[n : 2 * n]) + (x[2 * n : 3 * n] + x[3 * n :])


def row_valid(step, rows, width, length):
    ids = step * rows + lax.broadcasted_iota(jnp.int32, (rows, width), 0)
    return ids < length


def same_head(head):
    r = lax.broadcasted_iota(jnp.int32, (GW, GW), 0) // head
    c = lax.broadcasted_iota(jnp.int32, (GW, GW), 1) // head
    return r == c


def spread_rows(x, mask_low):
    return jnp.concatenate([x] * (GW // QB), axis=0) * mask_low


def pick_heads(x, head):
    lane = lax.broadcasted_iota(jnp.int32, (QB, GW), 1) // head
    out = x[:QB]
    for h in range(1, GW // QB):
        out = jnp.where(lane == h, x[h * QB : (h + 1) * QB], out)
    return out


def turned(hidden, n_fsdp):
    return hidden // n_fsdp >= 128


def join_blocks(ref, got, lo=0, step=None):
    n_dp, n_fsdp, r, c = got.shape
    step = c if step is None else step
    for d in range(n_dp):
        for f in range(n_fsdp):
            ref[f * r : (f + 1) * r, d * step + lo : d * step + lo + c] = got[d, f]


def cut_blocks(ref, acc):
    n_dp, n_fsdp, r, c = ref.shape
    for d in range(n_dp):
        for f in range(n_fsdp):
            ref[d, f] = acc[f * r : (f + 1) * r, d * c : (d + 1) * c].astype(ref.dtype)


def cut_turned(ref, acc):
    n_dp, n_fsdp, r, c = ref.shape
    width, hidden = acc.shape
    wide, deep = width // n_dp, hidden // n_fsdp
    for d in range(n_dp):
        for f in range(n_fsdp):
            block = acc[d * wide : (d + 1) * wide, f * deep : (f + 1) * deep]
            ref[d, f] = (block if turned(hidden, n_fsdp) else block.T).astype(ref.dtype)


def band_table(head):
    key = np.arange(KW)[:, None] - HALO
    query = np.arange(GW)[None, :] % QB
    return np.where(np.abs(key - query) <= BAND, 0.0, -1e30).astype(np.float32)


def head_table(head):
    r = np.arange(GW)[:, None] // QB
    c = np.arange(GW)[None, :] // head
    return (r == c).astype(np.float32)


MESH = pl.DeviceIdType.MESH


class Place:
    def __init__(self, n_dp, n_fsdp):
        self.m = n_fsdp // 2
        self.nh = n_dp // 2
        d = lax.axis_index("dp")
        f = lax.axis_index("fsdp")
        self.dh, self.dl = d // 2, lax.rem(d, 2)
        self.fh, self.fl = f // 2, lax.rem(f, 2)

    def dev(self, dh=None, dl=None, fh=None, fl=None):
        dh = self.dh if dh is None else dh
        dl = self.dl if dl is None else dl
        fh = self.fh if fh is None else fh
        fl = self.fl if fl is None else fl
        return {"dp": dh * 2 + dl, "fsdp": fh * 2 + fl}

    def partners(self):
        out = [self.dev(fh=lax.rem(self.fh + o, self.m)) for o in range(1, self.m)]
        out += [self.dev(dh=lax.rem(self.dh + o, self.nh)) for o in range(1, self.nh)]
        return out + [self.dev(fl=1 - self.fl), self.dev(dl=1 - self.dl)]


def greet(place):
    barrier = pltpu.get_barrier_semaphore()
    who = place.partners()
    for dev in who:
        pl.semaphore_signal(barrier, inc=1, device_id=dev, device_id_type=MESH)
    pl.semaphore_wait(barrier, len(who))


def copy_to(src, dst, send, recv, dev):
    return pltpu.make_async_remote_copy(
        src_ref=src, dst_ref=dst, send_sem=send, recv_sem=recv, device_id=dev, device_id_type=MESH
    )


class Gather:
    def __init__(self, place, shard, got, send, recv, local, order, way=None):
        self.p, self.shard, self.got, self.order, self.way = place, shard, got, order, way
        self.send, self.recv, self.local = send, recv, local

    @staticmethod
    def count(n_dp, n_fsdp):
        return n_fsdp // 2 - 1 + 1 + n_dp // 2 - 1 + 1

    def own(self):
        p = self.p
        src = self.shard if self.way is None else self.way
        return pltpu.make_async_copy(src, self.got.at[p.dh, p.dl, p.fh, p.fl], self.local)

    def fetch(self):
        return pltpu.make_async_copy(self.shard, self.way, self.local)

    def stage(self, k):
        p, g = self.p, self.got
        if k == 0:
            out = []
            for o in range(1, p.m):
                to = p.dev(fh=lax.rem(p.fh + o, p.m))
                dst = g.at[p.dh, p.dl, p.fh, p.fl]
                out.append(copy_to(self.shard, dst, self.send.at[o - 1], self.recv.at[o - 1], to))
            return out
        i = p.m - 1
        if k == 3:
            ref = g.at[:, p.dl]
            return [copy_to(ref, ref, self.send.at[i], self.recv.at[i], p.dev(dl=1 - p.dl))]
        if (k == 1) == (self.order == "x"):
            ref = g.at[p.dh, p.dl, :, p.fl] if k == 1 else g.at[:, p.dl, :, p.fl]
            return [copy_to(ref, ref, self.send.at[i + 1], self.recv.at[i + 1], p.dev(fl=1 - p.fl))]
        ref = g.at[p.dh, p.dl, :, p.fl] if k == 1 else g.at[p.dh, p.dl]
        out = []
        for o in range(1, p.nh):
            to = p.dev(dh=lax.rem(p.dh + o, p.nh))
            out.append(copy_to(ref, ref, self.send.at[i + 1 + o], self.recv.at[i + 1 + o], to))
        return out

    def start(self, k):
        for c in self.stage(k):
            c.start()

    def wait(self, k):
        if k == 0:
            self.own().wait()
        for c in self.stage(k):
            c.wait()

    def turn(self, k):
        self.wait(k)
        self.start(k + 1)


def front_kernel(
    ways,
    plan,
    qkv_steps,
    len_ref,
    tok_ref,
    wqkv,
    win,
    wback,
    wout,
    vec_in,
    bias_in,
    band_ref,
    qkv_ref,
    near_ref,
    fa_ref,
    fb_ref,
    rn_ref,
    p_ref,
    h1t_ref,
    m1_ref,
    m2_ref,
    c_ref,
    w_ref,
    vec_ref,
    bin_ref,
    g_in,
    g_back,
    g_out,
    all_s,
    st_ref,
    t_ref,
    g_qkv,
    small,
    g_small,
    way_in,
    way_back,
    way_out,
    key_s,
    qq_s,
    send,
    recv,
    local,
):
    step = pl.program_id(0)
    steps = qkv_steps
    rows, width = tok_ref.shape
    groups = width // GW
    head = width // HEADS
    scale = head ** (-0.5)
    length = len_ref[0, 0]
    n_dp, n_fsdp = ways
    cols = vec_in.shape[1]
    place = Place(n_dp, n_fsdp)
    half_in = win.shape[1] // 2
    half_back = wback.shape[0] // 2

    def piece(j, shard, got, order, way=None):
        return Gather(place, shard, got, send.at[j], recv.at[j], local.at[j], order, way)

    first = [[piece(7, small, g_small, "x")], []]
    for i, (which, cut, order) in enumerate(qkv_parts(*wqkv.shape)):
        first[which].append(piece(8 + i, wqkv.at[cut], g_qkv.at[(slice(None),) * 4 + cut], order))
    rest = []
    for i in range(2):
        cut = pl.ds(i * half_in, half_in)
        rest.append(piece(i, win.at[:, cut], g_in.at[:, :, :, :, :, cut], "x", way_in.at[:, cut]))
    for i in range(2):
        cut = pl.ds(i * half_back, half_back)
        rest.append(piece(2 + i, wback.at[cut], g_back.at[:, :, :, :, cut], "y", way_back.at[cut]))
    rest.append(piece(4, wout, g_out, "y", way_out))
    sets = [[rest[0], rest[2]], [rest[1], rest[3], rest[4]]]

    @pl.when(step == 0)
    def _():
        small[...] = jnp.zeros_like(small)
        small[:2, :cols] = vec_in[...]
        small[2:3, :cols] = bias_in[...]
        for x in first[0] + first[1]:
            x.own().start()
        for x in rest:
            x.fetch().start()
        greet(place)
        for x in first[0] + first[1]:
            x.start(0)
        for x in rest:
            x.fetch().wait()
            x.own().start()
        st_ref[...] = jnp.zeros_like(st_ref)
        t_ref[...] = jnp.zeros_like(t_ref)
        all_s[:HALO] = jnp.zeros((HALO, 3 * width), bf16)
        all_s[HALO + steps * rows :] = jnp.zeros((HALO, 3 * width), bf16)
        qq_s[...] = jnp.zeros_like(qq_s)
        key = lax.broadcasted_iota(jnp.int32, key_s.shape, 0) - HALO
        key_s[...] = jnp.where((key >= 0) & (key < length), 0.0, -1e30)
        for k in range(3):
            for group in first:
                for x in group:
                    x.turn(k)
            if k == 0:
                for x in sets[0] + sets[1]:
                    x.start(0)
        for x in first[0] + first[1]:
            x.wait(3)
        join_pairs(w_ref, g_qkv)
        lane = lax.broadcasted_iota(jnp.int32, (128, width), 0)
        col = lax.broadcasted_iota(jnp.int32, (128, width), 1)

        def place_small(f, total):
            spot = ((lane + f * cols == col) & (lane < cols)).astype(bf16)
            block = jnp.concatenate(
                [g_small[d // 2, d % 2, f // 2, lax.rem(f, 2)] for d in range(n_dp)], axis=0
            )
            return total + nn(block, spot)

        total = lax.fori_loop(0, n_fsdp, place_small, jnp.zeros((16 * n_dp, width), f32))
        for d in range(n_dp):
            vec_ref[2 * d : 2 * d + 2] = total[16 * d : 16 * d + 2]
            bin_ref[0:1, d * width : (d + 1) * width] = total[16 * d + 2 : 16 * d + 3]

    def advance(at, moves):
        @pl.when(step == at)
        def _():
            for which, k in moves:
                for x in sets[which]:
                    if k < 3:
                        x.turn(k)
                    else:
                        x.wait(k)

    for at, moves in plan.items():
        if at < 2 * steps:
            advance(at, moves)

    @pl.when(step < steps)
    def _():
        z, _ = moments(tok_ref[...].astype(f32))
        h = (z * vec_ref[0:1] + vec_ref[1:2]).astype(bf16)
        h1t_ref[...] = h.T
        lo = pl.multiple_of(HALO + step * rows, HALO)
        q = nn(h, w_ref[:, :width]).astype(bf16)
        qkv_ref[:, :width] = q
        all_s[pl.ds(lo, rows), :width] = q
        valid = row_valid(step, rows, GW, length)
        for g in range(groups):
            kc = slice(width + g * GW, width + (g + 1) * GW)
            vc = slice(2 * width + g * GW, 2 * width + (g + 1) * GW)
            k = nn(h, w_ref[:, kc]).astype(bf16)
            v = nn(h, w_ref[:, vc]).astype(bf16)
            qkv_ref[:, kc] = k
            qkv_ref[:, vc] = v
            all_s[pl.ds(lo, rows), kc] = k
            all_s[pl.ds(lo, rows), vc] = v
            phi = jnp.where(valid, lift(k), 0)
            bent = jnp.where(valid, jnp.tanh(k), 0)
            st_ref[g] += tn(v, jnp.concatenate([phi, bent], axis=1))
            t_ref[g] += fold8(phi.astype(f32))

    @pl.when(step == steps - 1)
    def _():
        mask = same_head(head).astype(f32)
        inv_len = 1.0 / length.astype(f32)
        ones = jnp.ones((8, GW), f32)
        for g in range(groups):
            tb = jnp.sum(t_ref[g], axis=0, keepdims=True) * mask
            s1 = st_ref[g][:, :GW] * mask
            s2 = st_ref[g][:, GW:] * mask
            c_row = (nt_exact(ones, s1) / nt_exact(ones, tb)).astype(bf16).astype(f32)
            c_col = jnp.broadcast_to(c_row[0:1], (GW, GW)).T
            m1_ref[g, :GW] = (s1 - c_col * tb).astype(bf16)
            m1_ref[g, GW:] = tb.astype(bf16)
            m2_ref[g] = (s2 * inv_len).astype(bf16)
            c_ref[g] = c_row

    @pl.when(step >= steps)
    def _():
        at = (step - steps) * rows
        for b in range(rows // QB):
            here = pl.ds(pl.multiple_of(at + b * QB + HALO, HALO), QB)
            window = pl.ds(pl.multiple_of(at + b * QB, QB), KW)
            out_of_item = key_s[window]
            bias = band_ref[...] + jnp.concatenate([out_of_item] * (GW // 128), axis=1)
            for g in range(groups):
                cut = slice(g * GW, (g + 1) * GW)
                kc = slice(width + g * GW, width + (g + 1) * GW)
                vc = slice(2 * width + g * GW, 2 * width + (g + 1) * GW)
                put_heads(qq_s.at[g, b], all_s[here, cut] * scale, head)
                s = nt(all_s[window, kc], qq_s[g, b]) + bias
                e = jnp.exp(s - jnp.max(s, axis=0, keepdims=True))
                p = (e * (1.0 / jnp.sum(e, axis=0, keepdims=True))).astype(bf16)
                p_ref[b, :, cut] = p
                o = tn(p, all_s[window, vc])
                near_ref[b * QB : (b + 1) * QB, cut] = pick_heads(o, head).astype(bf16)
        for g in range(groups):
            cut = slice(g * GW, (g + 1) * GW)
            q = all_s[pl.ds(pl.multiple_of(at + HALO, HALO), rows), cut]
            both = nt(lift(q), m1_ref[g])
            rn = 1.0 / both[:, GW:]
            rn_ref[:, cut] = rn.astype(bf16)
            fa_ref[:, cut] = (both[:, :GW] * rn).astype(bf16)
            fb_ref[:, cut] = nt(jnp.tanh(q), m2_ref[g]).astype(bf16)

    advance(2 * steps - 1, plan[2 * steps])


def join_pairs(ref, got):
    nh, _, m, _, r, c = got.shape
    for d in range(2 * nh):
        for f in range(2 * m):
            ref[f * r : (f + 1) * r, d * c : (d + 1) * c] = got[d // 2, d % 2, f // 2, f % 2]


def qkv_parts(r, c):
    if c % 384:
        return [(0, (pl.ds(0, r), pl.ds(0, c)), "x")]
    third = c // 3
    whole = pl.ds(0, r)
    parts = [(0, (whole, pl.ds(0, third)), "x"), (0, (whole, pl.ds(third, third)), "y")]
    rest = pl.ds(2 * third, third)
    if r % 32:
        return parts + [(1, (whole, rest), "x")]
    half = r // 2
    return parts + [(1, (pl.ds(0, half), rest), "x"), (1, (pl.ds(half, half), rest), "y")]


def front_pass(ways, length, tokens, w_qkv, w_in, w_back, w_out, vec, bias, tile, plan):
    rows, width = tokens.shape
    groups = width // GW
    n_dp, n_fsdp = ways
    nh, m = n_dp // 2, n_fsdp // 2
    steps = rows // tile
    head = width // HEADS
    const = lambda *shape: pl.BlockSpec(shape, lambda i: (0,) * len(shape))
    early = lambda i: (jnp.minimum(i, steps - 1), 0)
    late = pl.BlockSpec((tile, width), lambda i: (jnp.maximum(i - steps, 0), 0))
    hbm = pl.BlockSpec(memory_space=pl.ANY)
    sds = jax.ShapeDtypeStruct
    got = lambda r, c: (nh, 2, m, 2, r, c)
    hidden = w_in.shape[1] * n_dp
    pieces = 8 + len(qkv_parts(*w_qkv.shape))
    per = Gather.count(n_dp, n_fsdp)
    return pl.pallas_call(
        functools.partial(front_kernel, ways, plan, steps),
        grid=(2 * steps,),
        in_specs=[
            pl.BlockSpec(memory_space=pltpu.SMEM),
            pl.BlockSpec((tile, width), early),
            hbm,
            hbm,
            hbm,
            hbm,
            const(*vec.shape),
            const(*bias.shape),
            const(KW, GW),
        ],
        out_specs=[
            pl.BlockSpec((tile, 3 * width), early),
            late,
            late,
            late,
            late,
            pl.BlockSpec((tile // QB, KW, width), lambda i: (jnp.maximum(i - steps, 0), 0, 0)),
            pl.BlockSpec((width, tile), lambda i: (0, jnp.minimum(i, steps - 1))),
            const(groups, 2 * GW, GW),
            const(groups, GW, GW),
            const(groups, 8, GW),
            const(width, 3 * width),
            const(8, width),
            const(1, hidden),
            hbm,
            hbm,
            hbm,
        ],
        out_shape=[sds((rows, 3 * width), bf16)]
        + [sds((rows, width), bf16)] * 4
        + [
            sds((rows // QB, KW, width), bf16),
            sds((width, rows), bf16),
            sds((groups, 2 * GW, GW), bf16),
            sds((groups, GW, GW), bf16),
            sds((groups, 8, GW), f32),
            sds((width, 3 * width), bf16),
            sds((8, width), f32),
            sds((1, hidden), f32),
            sds(got(*w_in.shape), bf16),
            sds(got(*w_back.shape), bf16),
            sds(got(*w_out.shape), bf16),
        ],
        scratch_shapes=[
            pltpu.VMEM((rows + 2 * HALO, 3 * width), bf16),
            pltpu.VMEM((groups, GW, 2 * GW), f32),
            pltpu.VMEM((groups, 8, GW), f32),
            pltpu.VMEM(got(*w_qkv.shape), bf16),
            pltpu.VMEM((16, 128), bf16),
            pltpu.VMEM(got(16, 128), bf16),
            pltpu.VMEM(w_in.shape, bf16),
            pltpu.VMEM(w_back.shape, bf16),
            pltpu.VMEM(w_out.shape, bf16),
            pltpu.VMEM((rows + 2 * HALO, 128), f32),
            pltpu.VMEM((groups, tile // QB, GW, GW), bf16),
            pltpu.SemaphoreType.DMA((pieces, per)),
            pltpu.SemaphoreType.DMA((pieces, per)),
            pltpu.SemaphoreType.DMA((pieces,)),
        ],
        compiler_params=pltpu.CompilerParams(
            collective_id=0, has_side_effects=True, vmem_limit_bytes=VMEM_LIMIT
        ),
        cost_estimate=pl.CostEstimate(
            flops=2 * rows * width * 8 * width, bytes_accessed=rows * width * 24, transcendentals=0
        ),
        name="front_pass",
    )(
        length,
        tokens,
        w_qkv,
        w_in,
        w_back,
        w_out,
        vec,
        bias,
        jnp.asarray(band_table(head)),
    )


def ffn_kernel(
    chunk,
    len_ref,
    tok_ref,
    cot_ref,
    near_ref,
    fa_ref,
    fb_ref,
    rn_ref,
    q_ref,
    c_ref,
    vec_ref,
    bin_ref,
    gw_out,
    gw_in,
    gw_back,
    out_ref,
    datt_ref,
    dmix_ref,
    dn_ref,
    gin_ref,
    gback_ref,
    gout_ref,
    gvec_ref,
    gbias_ref,
    m3_ref,
    m4_ref,
    dt_ref,
    a_in,
    a_back,
    a_out,
    a_st,
    a_bent,
    wout_ref,
    win_ref,
    wback_ref,
    act_s,
    pre_s,
):
    step = pl.program_id(0)
    rows, width = tok_ref.shape
    hidden = win_ref.shape[1]
    groups = width // GW
    head_size = width // HEADS
    steps = pl.num_programs(0)
    length = len_ref[0, 0]
    c_row = jnp.concatenate([c_ref[g, 0:1] for g in range(groups)], axis=1)
    blend = vec_ref[...].astype(bf16)
    s0 = math.sqrt(2.0 / math.pi)
    s1 = s0 * 0.044715

    @pl.when(step == 0)
    def _():
        join_blocks(wout_ref, gw_out)
        join_blocks(win_ref, gw_in)
        join_blocks(wback_ref, gw_back)
        for ref in (a_in, a_back, a_out, a_st, a_bent, gvec_ref, gbias_ref):
            ref[...] = jnp.zeros_like(ref)

    near = near_ref[...]
    fac = fa_ref[...]
    far_b = fb_ref[...]
    mixed = (
        vec_ref[5:6] * near.astype(f32)
        + vec_ref[6:7] * (fac.astype(f32) + c_row)
        + vec_ref[7:8] * far_b.astype(f32)
    ).astype(bf16)
    resid = tok_ref[...].astype(f32) + nn(mixed, wout_ref[...])
    z2, r2 = moments(resid)
    h2 = (z2 * vec_ref[2:3] + vec_ref[3:4]).astype(bf16)
    valid = row_valid(step, rows, width, length)
    d_ffn = jnp.where(valid, cot_ref[...], 0)
    seed = d_ffn.astype(f32)
    for lo in range(0, hidden, chunk):
        cols = slice(lo, lo + chunk)
        x = nn(h2, win_ref[:, cols]) + bin_ref[0:1, cols]
        x2 = x * x
        half = 0.5 + 0.5 * jnp.tanh(x * (s0 + s1 * x2))
        act = x * half
        slope = half + (act - act * half) * (2 * s0 + 6 * s1 * x2)
        act = act.astype(bf16)
        act_s[:, cols] = act
        a_back[:, cols] += tn(d_ffn, act)
        d_pre = slope * nt(d_ffn, wback_ref[cols, :])
        gbias_ref[:, cols] += fold8(d_pre)
        d_pre = d_pre.astype(bf16)
        pre_s[:, cols] = d_pre
        a_in[:, cols] += tn(h2, d_pre)
    dh2 = nt(pre_s[...], win_ref[...])
    both = dh2 * z2
    gvec_ref[2] += fold8(both)
    gvec_ref[3] += fold8(dh2)
    gvec_ref[4] += fold8(seed)
    dz = dh2 * vec_ref[2:3]
    mean_z = jnp.mean(both * vec_ref[2:3], axis=-1, keepdims=True)
    d_resid = seed + r2 * (dz - jnp.mean(dz, axis=-1, keepdims=True) - z2 * mean_z)
    d_attn = d_resid.astype(bf16)
    datt_ref[...] = d_attn
    ffn = nn(act_s[...], wback_ref[...])
    out_ref[...] = jnp.where(valid, resid + ffn + vec_ref[4:5], 0.0).astype(bf16)
    a_out[...] += tn(mixed, d_attn)
    d_mix = nt(d_attn, wout_ref[...]).astype(bf16)
    dmix_ref[...] = d_mix
    gvec_ref[5] += fold8(fold4(d_mix * near).astype(f32))
    gvec_ref[6] += fold8(fold4(d_mix * fac).astype(f32))
    gvec_ref[7] += fold8(fold4(d_mix * far_b).astype(f32))
    gvec_ref[0] += fold8(fold4(d_mix).astype(f32))
    d_num = blend[6:7] * d_mix * rn_ref[...]
    dn_ref[...] = d_num
    d_den = d_num * fac
    d_far = blend[7:8] * d_mix
    for g in range(groups):
        cols = slice(g * GW, (g + 1) * GW)
        q = q_ref[:, cols]
        a_st[g] += tn(lift(q), jnp.concatenate([d_num[:, cols], d_den[:, cols]], axis=1))
        a_bent[g] += tn(jnp.tanh(q), d_far[:, cols])

    @pl.when(step == steps - 1)
    def _():
        mask = same_head(head_size).astype(f32)
        inv_len = 1.0 / length.astype(f32)
        ones = jnp.ones((8, GW), f32)
        for g in range(groups):
            m3_ref[g] = (a_st[g][:, :GW] * mask).astype(bf16)
            m4_ref[g] = (a_bent[g] * mask * inv_len).astype(bf16)
            dt_ref[g] = -nt_exact(ones, a_st[g][:, GW:] * mask)
        cut_blocks(gin_ref, a_in)
        cut_turned(gback_ref, a_back)
        cut_blocks(gout_ref, a_out)
        gvec_ref[6] += gvec_ref[0] * c_row


def third_pass(
    ways, length, tokens, cot, near, fa, fb, rn, qkv, c, vecs, b_in, w_out, w_in, w_back, tile, chunk
):
    rows, width = tokens.shape
    hidden = w_in.shape[0] * w_in.shape[3]
    groups = width // GW
    steps = rows // tile
    n_dp, n_fsdp = ways
    back = (width // n_dp, hidden // n_fsdp)
    back = back if turned(hidden, n_fsdp) else back[::-1]

    def const(*shape):
        return pl.BlockSpec(shape, lambda i: (0,) * len(shape))

    def kept(*shape):
        return pl.BlockSpec(shape, lambda i: (0,) * len(shape), pipeline_mode=pl.Buffered(1))

    sds = jax.ShapeDtypeStruct
    block = pl.BlockSpec((tile, width), lambda i: (i, 0))
    deep = pltpu.VMEM((tile, hidden), bf16)
    return pl.pallas_call(
        functools.partial(ffn_kernel, chunk),
        grid=(steps,),
        in_specs=[pl.BlockSpec(memory_space=pltpu.SMEM)]
        + [block] * 7
        + [
            const(groups, 8, GW),
            const(8, width),
            const(1, hidden),
            kept(*w_out.shape),
            kept(*w_in.shape),
            kept(*w_back.shape),
        ],
        out_specs=[block] * 4
        + [
            const(n_dp, n_fsdp, width // n_fsdp, hidden // n_dp),
            const(n_dp, n_fsdp, *back),
            const(n_dp, n_fsdp, width // n_fsdp, width // n_dp),
            const(8, 8, width),
            const(8, hidden),
            const(groups, GW, GW),
            const(groups, GW, GW),
            const(groups, 8, GW),
        ],
        out_shape=[sds((rows, width), bf16)] * 4
        + [
            sds((n_dp, n_fsdp, width // n_fsdp, hidden // n_dp), bf16),
            sds((n_dp, n_fsdp, *back), bf16),
            sds((n_dp, n_fsdp, width // n_fsdp, width // n_dp), bf16),
            sds((8, 8, width), f32),
            sds((8, hidden), f32),
            sds((groups, GW, GW), bf16),
            sds((groups, GW, GW), bf16),
            sds((groups, 8, GW), f32),
        ],
        scratch_shapes=[
            pltpu.VMEM((width, hidden), f32),
            pltpu.VMEM((width, hidden), f32),
            pltpu.VMEM((width, width), f32),
            pltpu.VMEM((groups, GW, 2 * GW), f32),
            pltpu.VMEM((groups, GW, GW), f32),
            pltpu.VMEM((width, width), bf16),
            pltpu.VMEM((width, hidden), bf16),
            pltpu.VMEM((hidden, width), bf16),
            deep,
            deep,
        ],
        compiler_params=pltpu.CompilerParams(vmem_limit_bytes=VMEM_LIMIT),
        cost_estimate=pl.CostEstimate(
            flops=2 * rows * width * (6 * hidden + 4 * width),
            bytes_accessed=rows * width * 22,
            transcendentals=0,
        ),
        name="third_pass",
    )(length, tokens, cot, near, fa, fb, rn, qkv, c, vecs, b_in, w_out, w_in, w_back)


class Scatter:
    def __init__(self, place, src, out, bufs, send, recv, local, order):
        self.p, self.src, self.out, self.order = place, src, out, order
        self.acc, self.r0, self.r1, self.r2, self.r3 = bufs
        self.send, self.recv, self.local = send, recv, local

    @staticmethod
    def count(n_dp, n_fsdp):
        return n_dp // 2 + 1 + (n_dp // 2 - 1) + (n_fsdp // 2 - 1)

    @staticmethod
    def scratch(n_dp, n_fsdp, r, c, order, dtype):
        nh, m = n_dp // 2, n_fsdp // 2
        if order == "x":
            one, two = (nh, m, r, c), (nh - 1, m, r, c)
        else:
            one, two = (nh - 1, m, 2, r, c), (m, r, c)
        shapes = [(nh, m, 2, r, c), (nh, m, 2, r, c), one, two, (m - 1, r, c)]
        return [pltpu.VMEM(s, dtype) for s in shapes]

    def own(self):
        return pltpu.make_async_copy(self.src.at[:, self.p.dl], self.acc, self.local)

    def stage(self, k, only=None):
        p = self.p
        if k == 0:
            to = p.dev(dl=1 - p.dl)
            return [
                copy_to(self.src.at[dh, 1 - p.dl], self.r0.at[dh], self.send.at[dh], self.recv.at[dh], to)
                for dh in (range(p.nh) if only is None else [only])
            ]
        first = p.nh - 1
        if k == 3:
            i = first + p.nh
            out = []
            for o in range(1, p.m):
                fh = lax.rem(p.fh + o, p.m)
                out.append(
                    copy_to(self.acc.at[p.dh, fh, p.fl], self.r3.at[o - 1], self.send.at[i + o], self.recv.at[i + o],
                            p.dev(fh=fh))
                )
            return out
        if (k == 1) == (self.order == "x"):
            ref = self.acc.at[:, :, 1 - p.fl] if k == 1 else self.acc.at[p.dh, :, 1 - p.fl]
            dst = self.r1 if k == 1 else self.r2
            i = first + 1
            return [copy_to(ref, dst, self.send.at[i], self.recv.at[i], p.dev(fl=1 - p.fl))]
        out = []
        for o in range(1, p.nh):
            dh = lax.rem(p.dh + o, p.nh)
            ref = self.acc.at[dh] if k == 1 else self.acc.at[dh, :, p.fl]
            dst = self.r1.at[o - 1] if k == 1 else self.r2.at[o - 1]
            i = first + 1 + o
            out.append(copy_to(ref, dst, self.send.at[i], self.recv.at[i], p.dev(dh=dh)))
        return out

    def start(self, k):
        for c in self.stage(k):
            c.start()

    def turn(self, k):
        if k == 0:
            self.own().wait()
        for c in self.stage(k):
            c.wait()
        self.add(k)
        if k < 3:
            self.start(k + 1)

    def add(self, k):
        p, acc = self.p, self.acc
        nh, m = p.nh, p.m
        dt = acc.dtype

        def put(index, others):
            if len(others) == 1:
                acc[index] += others[0]
                return
            total = acc[index].astype(f32)
            for o in others:
                total = total + o.astype(f32)
            acc[index] = total.astype(dt)

        if k == 3:
            total = acc[p.dh, p.fh, p.fl].astype(f32)
            for o in range(1, m):
                total = total + self.r3[o - 1].astype(f32)
            self.out[...] = total
            return

        @pl.loop(0, m)
        def _(i):
            if k == 0:
                for a in range(nh):
                    for b in range(2):
                        put((a, i, b), [self.r0[a, i, b]])
            elif k == 1 and self.order == "x":
                for a in range(nh):
                    put((a, i, p.fl), [self.r1[a, i]])
            elif k == 1:
                for b in range(2):
                    put((p.dh, i, b), [self.r1[o - 1, i, b] for o in range(1, nh)])
            elif self.order == "x":
                put((p.dh, i, p.fl), [self.r2[o - 1, i] for o in range(1, nh)])
            else:
                put((p.dh, i, p.fl), [self.r2[i]])


def back_kernel(
    ways,
    plan,
    late_plan,
    len_ref,
    q_ref,
    k_lo,
    k_ref,
    k_hi,
    v_lo,
    v_ref,
    v_hi,
    p_ref,
    dmix_ref,
    dn_ref,
    fa_ref,
    tok_ref,
    datt_ref,
    h1t_hbm,
    m1_ref,
    m2_ref,
    m3_ref,
    m4_ref,
    dt_ref,
    c_ref,
    vec_ref,
    w_hbm,
    gv_ref,
    gbias_ref,
    s_in,
    s_back,
    s_out,
    dtok_ref,
    oqkv_ref,
    oin_ref,
    oback_ref,
    oout_ref,
    ovec_ref,
    obias_ref,
    h1t_ref,
    w_ref,
    kk,
    vv,
    far_s,
    dp_s,
    ds_s,
    dd_s,
    qq_s,
    all_d,
    carry,
    gvec_s,
    gq_ref,
    gs_ref,
    rows_s,
    back_t,
    small_o,
    late_src,
    late_got,
    *rest,
):
    step = pl.program_id(0)
    rows, width = q_ref.shape
    total = h1t_ref.shape[1]
    steps = total // rows
    groups = width // GW
    head = width // HEADS
    scale = head ** (-0.5)
    length = len_ref[0, 0]
    n_dp, n_fsdp = ways
    place = Place(n_dp, n_fsdp)
    cols = ovec_ref.shape[1]
    c_all = oqkv_ref.shape[1]
    send, recv, local, late_send, late_recv, fetch = rest[-6:]
    fetches = [
        pltpu.make_async_copy(h1t_hbm, h1t_ref, fetch.at[0]),
        pltpu.make_async_copy(w_hbm, w_ref, fetch.at[1]),
    ]
    final = steps + 1 + place.nh
    last_rows = tok_ref.shape[0]

    used = [0]

    def piece(src, out, order):
        j = used[0]
        used[0] += 1
        return Scatter(place, src, out, rest[5 * j : 5 * j + 5], send.at[j], recv.at[j], local.at[j], order)

    sets = [[], [], [], []]
    every = (slice(None),) * 4
    for i, (cut_in, cut_back) in enumerate(ffn_parts(s_in.shape[-2:], s_back.shape[-2:])):
        sets[i].append(piece(s_in.at[every + cut_in], oin_ref.at[cut_in], "x"))
        sets[i].append(piece(s_back.at[every + cut_back], back_t.at[cut_back], "y"))
    sets[1].append(piece(s_out, oout_ref, "y"))
    sets[1].append(piece(gs_ref, small_o, "x"))
    for which, cut, order in qkv_parts(*oqkv_ref.shape):
        sets[2 + which].append(piece(gq_ref.at[every + cut], oqkv_ref.at[cut], order))

    @pl.when(step == 0)
    def _():
        for x in sets[0] + sets[1][:-1]:
            x.own().start()
        greet_all(place)
        for x in sets[0] + sets[1][:-1]:
            x.start(0)
        for x in fetches:
            x.start()
        carry[...] = jnp.zeros_like(carry)
        dd_s[...] = jnp.zeros_like(dd_s)
        qq_s[...] = jnp.zeros_like(qq_s)
        gvec_s[...] = jnp.zeros_like(gvec_s)
        gs_ref[...] = jnp.zeros_like(gs_ref)
        late_src[...] = jnp.zeros_like(late_src)
        rows_s[0:2] = jnp.zeros((2, width), f32)
        rows_s[2:8] = jnp.sum(gv_ref[2:8], axis=1)
        bias = jnp.sum(gbias_ref[...], axis=0, keepdims=True)
        for d in range(n_dp):
            pair = rows_s[2 * d : 2 * d + 2]
            for f in range(n_fsdp):
                spot = slice(f * cols, (f + 1) * cols)
                at = d * width + f * cols
                gs_ref[d // 2, d % 2, f // 2, f % 2, 0:2, :cols] = pair[:, spot]
                gs_ref[d // 2, d % 2, f // 2, f % 2, 2:3, :cols] = bias[:, at : at + cols]
        sets[1][-1].own().start()
        sets[1][-1].start(0)

    for at, moves in plan.items():

        @pl.when(step == at)
        def _(moves=moves):
            for which, k in moves:
                for x in sets[which]:
                    x.turn(k)

    def far_keys(at, slot, live):
        valid = row_valid(at, rows, GW, length) & live
        here = pl.ds(pl.multiple_of(at * rows + HALO, HALO), rows)
        for g in range(groups):
            cut = slice(g * GW, (g + 1) * GW)
            kc = slice(width + g * GW, width + (g + 1) * GW)
            vc = slice(2 * width + g * GW, 2 * width + (g + 1) * GW)
            k = kk[slot, HALO : HALO + rows, cut]
            v = vv[slot, HALO : HALO + rows, cut]
            lift_k = lift(k)
            bent_k = jnp.tanh(k)
            v_cen = v - c_ref[g, 0:1].astype(bf16)
            dk = (nt(v_cen, m3_ref[g]) + dt_ref[g, 0:1]) * jnp.minimum(lift_k, 1).astype(f32)
            dk += nt(v, m4_ref[g]) * (1 - bent_k * bent_k).astype(f32)
            both = jnp.concatenate([lift_k, bent_k], axis=1)
            dv = nn(both, jnp.concatenate([m3_ref[g], m4_ref[g]], axis=0))
            all_d[here, kc] += jnp.where(valid, dk.astype(bf16), 0)
            all_d[here, vc] += jnp.where(valid, dv.astype(bf16), 0)

    @pl.when(step < steps)
    def _():
        slot = lax.rem(step, 2)
        kk[slot, :HALO] = k_lo[...]
        kk[slot, HALO : HALO + rows] = k_ref[...]
        kk[slot, HALO + rows :] = k_hi[...]
        vv[slot, :HALO] = v_lo[...]
        vv[slot, HALO : HALO + rows] = v_ref[...]
        vv[slot, HALO + rows :] = v_hi[...]
        blend = vec_ref[...].astype(bf16)
        base = step * rows
        for g in range(groups):
            cut = slice(g * GW, (g + 1) * GW)
            kc = slice(width + g * GW, width + (g + 1) * GW)
            vc = slice(2 * width + g * GW, 2 * width + (g + 1) * GW)
            q = q_ref[:, cut]
            d_num = dn_ref[:, cut]
            d_den = -d_num * fa_ref[:, cut]
            d_mix = dmix_ref[:, cut]
            bent = jnp.tanh(q)
            far = nn(jnp.concatenate([d_num, d_den], axis=1), m1_ref[g]) * jnp.minimum(lift(q), 1).astype(f32)
            far_s[:, cut] = far + nn(blend[7:8, cut] * d_mix, m2_ref[g]) * (1 - bent * bent).astype(f32)
            for b in range(rows // QB):
                here = slice(b * QB, (b + 1) * QB)
                window = slice(b * QB, b * QB + KW)
                put_heads(dd_s.at[g, b], blend[5:6, cut] * dmix_ref[here, cut], head)
                dp_s[g, b] = nt(vv[slot, window, cut], dd_s[g, b]).astype(bf16)
            for b in range(rows // QB):
                p = p_ref[b, :, cut]
                dp = dp_s[g, b]
                dot = jnp.sum(fold4(p * dp).astype(f32), axis=0, keepdims=True)
                ds_s[g, b] = p * (dp - dot.astype(bf16))
            old_k = carry[0, :, cut]
            old_v = carry[1, :, cut]
            for b in range(rows // QB):
                here = slice(b * QB, (b + 1) * QB)
                window = slice(b * QB, b * QB + KW)
                d_s = ds_s[g, b]
                put_heads(qq_s.at[g, b], q_ref[here, cut] * scale, head)
                dk = nn(d_s, qq_s[g, b])
                dv = nn(p_ref[b, :, cut], dd_s[g, b])
                dq = pick_heads(tn(d_s, kk[slot, window, cut]), head) * scale + far_s[here, cut]
                lo = pl.ds(pl.multiple_of(base + b * QB, QB), QB)
                all_d[pl.ds(pl.multiple_of(base + b * QB + HALO, HALO), QB), cut] = dq.astype(bf16)
                all_d[lo, kc] = (old_k + dk[:QB]).astype(bf16)
                all_d[lo, vc] = (old_v + dv[:QB]).astype(bf16)
                old_k = dk[QB:]
                old_v = dv[QB:]
            carry[0, :, cut] = old_k
            carry[1, :, cut] = old_v
        far_keys(jnp.maximum(step - 1, 0), 1 - slot, step > 0)

    @pl.when(step == steps)
    def _():
        all_d[total:, width : 2 * width] = carry[0].astype(bf16)
        all_d[total:, 2 * width :] = carry[1].astype(bf16)
        far_keys(steps - 1, (steps - 1) % 2, True)

    for dh in range(n_dp // 2):

        @pl.when(step == steps + 1 + dh)
        def _(dh=dh):
            if dh == 0:
                fetches[0].wait()
            grad = nn(h1t_ref[...], all_d[HALO : HALO + total, dh * 2 * c_all : (dh + 1) * 2 * c_all])
            r = gq_ref.shape[-2]
            for dl in range(2):
                for f in range(n_fsdp):
                    block = grad[f * r : (f + 1) * r, dl * c_all : (dl + 1) * c_all]
                    gq_ref[dh, dl, f // 2, f % 2] = block.astype(bf16)
            for x in sets[2] + sets[3]:
                x.stage(0, dh)[0].start()

    @pl.when(step == final)
    def _():
        fetches[1].wait()
        for x in sets[2] + sets[3]:
            x.own().start()

    for at, moves in late_plan.items():
        if at == "end":
            continue

        @pl.when(step == final + at)
        def _(moves=moves):
            for which, k in moves:
                for x in sets[which]:
                    x.turn(k)

    @pl.when(step >= final)
    def _():
        here = pl.ds(pl.multiple_of((step - final) * last_rows + HALO, HALO), last_rows)
        z1, r1 = moments(tok_ref[...].astype(f32))
        dh1 = nt(all_d[here], w_ref[...])
        gvec_s[0] += fold8(dh1 * z1)
        gvec_s[1] += fold8(dh1)
        dz = dh1 * vec_ref[0:1]
        dtok_ref[...] = (
            datt_ref[...].astype(f32)
            + r1
            * (
                dz
                - jnp.mean(dz, axis=-1, keepdims=True)
                - z1 * jnp.mean(dz * z1, axis=-1, keepdims=True)
            )
        ).astype(bf16)

    @pl.when(step == final + total // last_rows - 1)
    def _():
        rows_s[0:2] = jnp.sum(gvec_s[...], axis=1)
        for f in range(n_fsdp):
            late_src[f, 0:2, :cols] = rows_s[0:2, f * cols : (f + 1) * cols]
        d, f = lax.axis_index("dp"), lax.axis_index("fsdp")
        me = d * n_fsdp + f

        def late(o):
            to = lax.rem(f + o, n_fsdp)
            return copy_to(
                late_src.at[to], late_got.at[me], late_send.at[o], late_recv.at[me], {"dp": 0, "fsdp": to}
            )

        @pl.when(d > 0)
        def _():
            late(0).start()

        for o in range(1, n_fsdp):
            late(o).start()
        oback_ref[...] = back_t[...].T if turned(gbias_ref.shape[1], n_fsdp) else back_t[...]
        for which, k in late_plan["end"]:
            for x in sets[which]:
                x.turn(k)

        @pl.when(d > 0)
        def _():
            late(0).wait_send()
            ovec_ref[...] = small_o[0:2, :cols]

        for o in range(1, n_fsdp):
            late(o).wait_send()

        @pl.when(d == 0)
        def _():
            late_got[me] = late_src[f]

            @pl.loop(0, n_dp * n_fsdp)
            def _(s):
                @pl.when(s != me)
                def _():
                    copy_to(
                        late_src.at[0], late_got.at[s], late_send.at[0], late_recv.at[s], {"dp": 0, "fsdp": 0}
                    ).wait_recv()

            ovec_ref[...] = jnp.sum(late_got[...], axis=0)[0:2, :cols]

        obias_ref[...] = small_o[2:3, :cols]


def put_heads(ref, x, head):
    for h in range(GW // head):
        lanes = slice(h * head, (h + 1) * head)
        ref[h * QB : (h + 1) * QB, lanes] = x[:, lanes]


def ffn_parts(shape_in, shape_back):
    (r, c), (rb, cb) = shape_in, shape_back
    out = []
    for i in range(2):
        cut_in = (pl.ds(0, r), pl.ds(i * c // 2, c // 2))
        if cb % 256:
            cut_back = (pl.ds(i * rb // 2, rb // 2), pl.ds(0, cb))
        else:
            cut_back = (pl.ds(0, rb), pl.ds(i * cb // 2, cb // 2))
        out.append((cut_in, cut_back))
    return out


def greet_all(place):
    d, f = lax.axis_index("dp"), lax.axis_index("fsdp")
    n_dp, n_fsdp = 2 * place.nh, 2 * place.m
    barrier = pltpu.get_barrier_semaphore()
    who = place.partners()
    for dev in who:
        pl.semaphore_signal(barrier, inc=1, device_id=dev, device_id_type=MESH)

    @pl.when(d == 0)
    def _():
        @pl.loop(0, n_dp)
        def _(i):
            @pl.loop(0, n_fsdp)
            def _(j):
                @pl.when((i != 0) | (j != f))
                def _():
                    pl.semaphore_signal(barrier, inc=1, device_id={"dp": i, "fsdp": j}, device_id_type=MESH)

    pl.semaphore_wait(barrier, len(who) + n_fsdp - (d == 0).astype(jnp.int32))


def back_pass(
    ways,
    length,
    qkv,
    p,
    d_mix,
    tokens,
    d_attn,
    d_num,
    fa,
    h1t,
    m1,
    m2,
    m3,
    m4,
    dt,
    c,
    vecs,
    w_qkv,
    gv,
    gbias,
    s_in,
    s_back,
    s_out,
    tile,
    last_tile,
    plan,
    late_plan,
):
    rows, width = tokens.shape
    groups = width // GW
    steps = rows // tile
    n_dp, n_fsdp = ways
    nh, m = n_dp // 2, n_fsdp // 2
    r, c_all = width // n_fsdp, 3 * width // n_dp
    per = Scatter.count(n_dp, n_fsdp)
    final = steps + 1 + nh
    hbm = pl.BlockSpec(memory_space=pl.ANY)
    back_shape = s_back.shape[-2:]
    outs = [
        (r, c_all),
        s_in.shape[-2:],
        back_shape[::-1] if turned(gbias.shape[1], n_fsdp) else back_shape,
        s_out.shape[-2:],
        (2, width // n_fsdp),
        (1, gbias.shape[1] // (n_dp * n_fsdp)),
    ]
    kinds = []
    for cut_in, cut_back in ffn_parts(s_in.shape[-2:], back_shape):
        kinds.append((*(x.size for x in cut_in), "x", bf16))
        kinds.append((*(x.size for x in cut_back), "y", bf16))
    kinds.append((*s_out.shape[-2:], "y", bf16))
    kinds.append((8, 128, "x", f32))
    for _, cut, order in qkv_parts(r, c_all):
        kinds.append((*(x.size for x in cut), order, bf16))
    bufs = [b for k in kinds for b in Scatter.scratch(n_dp, n_fsdp, *k)]
    got = lambda *s: (nh, 2, m, 2, *s)

    def const(*shape):
        return pl.BlockSpec(shape, lambda i: (0,) * len(shape))

    def kept(*shape):
        return pl.BlockSpec(shape, lambda i: (0,) * len(shape), pipeline_mode=pl.Buffered(1))

    one = lambda i: jnp.minimum(i, steps - 1)
    end = lambda i: jnp.maximum(i - final, 0)
    per_tile = tile // HALO
    top = rows // HALO - 1

    def halo(col):
        return [
            pl.BlockSpec((HALO, width), lambda i: (jnp.maximum(one(i) * per_tile - 1, 0), col)),
            pl.BlockSpec((tile, width), lambda i: (one(i), col)),
            pl.BlockSpec((HALO, width), lambda i: (jnp.minimum((one(i) + 1) * per_tile, top), col)),
        ]

    block = pl.BlockSpec((tile, width), lambda i: (one(i), 0))
    late = pl.BlockSpec((last_tile, width), lambda i: (end(i), 0))
    head = width // HEADS
    sds = jax.ShapeDtypeStruct
    return pl.pallas_call(
        functools.partial(back_kernel, ways, plan, late_plan),
        grid=(final + rows // last_tile,),
        in_specs=[
            pl.BlockSpec(memory_space=pltpu.SMEM),
            block,
            *halo(1),
            *halo(2),
            pl.BlockSpec((tile // QB, KW, width), lambda i: (one(i), 0, 0)),
            block,
            block,
            block,
            late,
            late,
            hbm,
            kept(groups, 2 * GW, GW),
            kept(groups, GW, GW),
            kept(groups, GW, GW),
            kept(groups, GW, GW),
            const(groups, 8, GW),
            const(groups, 8, GW),
            const(8, width),
            hbm,
            const(*gv.shape),
            const(*gbias.shape),
            hbm,
            hbm,
            hbm,
        ],
        out_specs=[late] + [const(*s) for s in outs],
        out_shape=[sds((rows, width), bf16)] + [sds(s, f32) for s in outs],
        scratch_shapes=[
            pltpu.VMEM((width, rows), bf16),
            pltpu.VMEM((width, 3 * width), bf16),
            pltpu.VMEM((2, tile + 2 * HALO, width), bf16),
            pltpu.VMEM((2, tile + 2 * HALO, width), bf16),
            pltpu.VMEM((tile, width), f32),
            pltpu.VMEM((groups, tile // QB, KW, GW), bf16),
            pltpu.VMEM((groups, tile // QB, KW, GW), bf16),
            pltpu.VMEM((groups, tile // QB, GW, GW), bf16),
            pltpu.VMEM((groups, tile // QB, GW, GW), bf16),
            pltpu.VMEM((rows + 2 * HALO, 3 * width), bf16),
            pltpu.VMEM((2, QB, width), f32),
            pltpu.VMEM((2, 8, width), f32),
            pltpu.VMEM(got(r, c_all), bf16),
            pltpu.VMEM(got(8, 128), f32),
            pltpu.VMEM((8, width), f32),
            pltpu.VMEM(back_shape, f32),
            pltpu.VMEM((8, 128), f32),
            pltpu.VMEM((n_fsdp, 8, 128), f32),
            pltpu.VMEM((n_dp * n_fsdp, 8, 128), f32),
            *bufs,
            pltpu.SemaphoreType.DMA((len(kinds), per)),
            pltpu.SemaphoreType.DMA((len(kinds), per)),
            pltpu.SemaphoreType.DMA((len(kinds),)),
            pltpu.SemaphoreType.DMA((n_fsdp,)),
            pltpu.SemaphoreType.DMA((n_dp * n_fsdp,)),
            pltpu.SemaphoreType.DMA((2,)),
        ],
        compiler_params=pltpu.CompilerParams(
            collective_id=1, has_side_effects=True, vmem_limit_bytes=VMEM_LIMIT
        ),
        cost_estimate=pl.CostEstimate(
            flops=2 * rows * width * 14 * width, bytes_accessed=rows * width * 24, transcendentals=0
        ),
        name="back_pass",
    )(
        length,
        qkv,
        qkv,
        qkv,
        qkv,
        qkv,
        qkv,
        qkv,
        p,
        d_mix,
        d_num,
        fa,
        tokens,
        d_attn,
        h1t,
        m1,
        m2,
        m3,
        m4,
        dt,
        c,
        vecs,
        w_qkv,
        gv,
        gbias,
        s_in,
        s_back,
        s_out,
    )


def hand_kernel(n, *refs):
    for j in range(n):
        refs[n + j][...] = refs[j][...]


def hand_over(arrays, parts):
    first = arrays[0]
    block = pl.BlockSpec((first.shape[0] // parts, first.shape[1]), lambda i: (i, 0))
    specs = [block] + [pl.BlockSpec(a.shape, lambda i: (0, 0)) for a in arrays[1:]]
    return pl.pallas_call(
        functools.partial(hand_kernel, len(arrays)),
        grid=(parts,),
        in_specs=specs,
        out_specs=specs,
        out_shape=[jax.ShapeDtypeStruct(a.shape, a.dtype) for a in arrays],
        name="hand_over",
    )(*arrays)


FRONT_TILE = 1024
TILE = 512
LAST_TILE = 1024
CHUNK = 256
FRONT_PLAN = {1: [(0, 0)], 2: [(1, 0)], 3: [(0, 1)], 5: [(0, 2), (1, 1)], 7: [(1, 2)], 8: [(0, 3), (1, 3)]}
BACK_PLAN = {2: [(0, 0)], 3: [(1, 0)], 4: [(0, 1)], 6: [(1, 1), (0, 2)], 7: [(1, 2)], 8: [(0, 3)], 12: [(1, 3)]}
LATE_PLAN = {1: [(2, 0), (3, 0)], 2: [(2, 1)], 3: [(3, 1), (2, 2)], "end": [(3, 2), (2, 3), (3, 3)]}


def shards(
    tokens, cotangent, w_qkv, w_out, w_in, w_back, vec_params, b_in, item_lengths, bucket_counts, *, ways
):
    n_dp, n_fsdp = ways
    (
        qkv,
        near,
        fa,
        fb,
        rn,
        p,
        h1t,
        m1,
        m2,
        c,
        qkv_w,
        vecs,
        in_bias,
        g_in,
        g_back,
        g_out,
    ) = front_pass(
        ways, item_lengths, tokens, w_qkv, w_in, w_back, w_out, vec_params, b_in[None], FRONT_TILE, FRONT_PLAN
    )

    def blocks(g):
        return g.reshape(n_dp, n_fsdp, *g.shape[-2:])

    def pairs(g):
        return g.reshape(n_dp // 2, 2, n_fsdp // 2, 2, *g.shape[-2:])

    (out, d_attn, d_mix, d_num, s_in, s_back, s_out, g_vec, g_bias, m3, m4, dt) = third_pass(
        ways,
        item_lengths,
        tokens,
        cotangent,
        near,
        fa,
        fb,
        rn,
        qkv,
        c,
        vecs,
        in_bias,
        blocks(g_out),
        blocks(g_in),
        blocks(g_back),
        TILE,
        CHUNK,
    )
    d_tok, r_qkv, r_in, r_back, r_out, r_vec, r_bias = back_pass(
        ways,
        item_lengths,
        qkv,
        p,
        d_mix,
        tokens,
        d_attn,
        d_num,
        fa,
        h1t,
        m1,
        m2,
        m3,
        m4,
        dt,
        c,
        vecs,
        qkv_w,
        g_vec,
        g_bias,
        pairs(s_in),
        pairs(s_back),
        pairs(s_out),
        TILE,
        LAST_TILE,
        BACK_PLAN,
        LATE_PLAN,
    )
    d_tok, r_qkv, r_out, r_in, r_back, r_vec, r_bias = hand_over(
        [d_tok, r_qkv, r_out, r_in, r_back, r_vec, r_bias], 2
    )
    return (out, d_tok, r_qkv, r_out, r_in, r_back, r_vec, r_bias[0])


def solution(mesh):
    in_specs = (
        P(("dp", "fsdp"), None),
        P(("dp", "fsdp"), None),
        P("fsdp", "dp"),
        P("fsdp", "dp"),
        P("fsdp", "dp"),
        P("fsdp", "dp"),
        P("dp", "fsdp"),
        P(("dp", "fsdp")),
        P(("dp", "fsdp"), None),
        P(("dp", "fsdp"), None),
    )
    out_specs = (
        P(("dp", "fsdp"), None),
        P(("dp", "fsdp"), None),
        P("fsdp", "dp"),
        P("fsdp", "dp"),
        P("fsdp", "dp"),
        P("fsdp", "dp"),
        P("dp", "fsdp"),
        P(("dp", "fsdp")),
    )
    ways = (mesh.shape["dp"], mesh.shape["fsdp"])
    body = functools.partial(shards, ways=ways)
    return jax.shard_map(body, mesh=mesh, in_specs=in_specs, out_specs=out_specs, check_vma=False)
```

```python
import functools
import math

import jax
import jax.numpy as jnp
import numpy as np
from jax import lax
from jax.experimental import pallas as pl
from jax.experimental.pallas import tpu as pltpu
from jax.sharding import PartitionSpec as P

HEADS = 8
BAND = 30
QB = 64
HALO = 32
KW = QB + 2 * HALO
GW = 256

norm_eps = 1e-05
f32 = jnp.float32
bf16 = jnp.bfloat16
exact = lax.Precision.HIGHEST
VMEM_LIMIT = 60 * 1024 * 1024


def nn(a, b):
    return lax.dot_general(a, b, (((1,), (0,)), ((), ())), preferred_element_type=f32)


def nt(a, b):
    return lax.dot_general(a, b, (((1,), (1,)), ((), ())), preferred_element_type=f32)


def tn(a, b):
    return lax.dot_general(a, b, (((0,), (0,)), ((), ())), preferred_element_type=f32)


def nt_exact(a, b):
    return lax.dot_general(
        a, b, (((1,), (1,)), ((), ())), preferred_element_type=f32, precision=exact
    )


def lift(t):
    return jnp.where(t > 0, t + 1, jnp.exp(jnp.minimum(t, 0)))


def moments(x):
    mean = jnp.mean(x, axis=-1, keepdims=True)
    cen = x - mean
    inv = lax.rsqrt(jnp.mean(cen * cen, axis=-1, keepdims=True) + norm_eps)
    return cen * inv, inv


def fold8(x):
    return jnp.sum(x.reshape(x.shape[0] // 8, 8, x.shape[1]), axis=0)


def fold4(x):
    n = x.shape[0] // 4
    return (x[:n] + x[n : 2 * n]) + (x[2 * n : 3 * n] + x[3 * n :])


def row_valid(step, rows, width, length):
    ids = step * rows + lax.broadcasted_iota(jnp.int32, (rows, width), 0)
    return ids < length


def same_head(head):
    r = lax.broadcasted_iota(jnp.int32, (GW, GW), 0) // head
    c = lax.broadcasted_iota(jnp.int32, (GW, GW), 1) // head
    return r == c


def spread_rows(x, mask_low):
    return jnp.concatenate([x] * (GW // QB), axis=0) * mask_low


def pick_heads(x, head):
    lane = lax.broadcasted_iota(jnp.int32, (QB, GW), 1) // head
    out = x[:QB]
    for h in range(1, GW // QB):
        out = jnp.where(lane == h, x[h * QB : (h + 1) * QB], out)
    return out


def turned(hidden, n_fsdp):
    return hidden // n_fsdp >= 128


def join_blocks(ref, got, lo=0, step=None):
    n_dp, n_fsdp, r, c = got.shape
    step = c if step is None else step
    for d in range(n_dp):
        for f in range(n_fsdp):
            ref[f * r : (f + 1) * r, d * step + lo : d * step + lo + c] = got[d, f]


def cut_blocks(ref, acc):
    n_dp, n_fsdp, r, c = ref.shape
    for d in range(n_dp):
        for f in range(n_fsdp):
            ref[d, f] = acc[f * r : (f + 1) * r, d * c : (d + 1) * c].astype(ref.dtype)


def cut_turned(ref, acc):
    n_dp, n_fsdp, r, c = ref.shape
    width, hidden = acc.shape
    wide, deep = width // n_dp, hidden // n_fsdp
    for d in range(n_dp):
        for f in range(n_fsdp):
            block = acc[d * wide : (d + 1) * wide, f * deep : (f + 1) * deep]
            ref[d, f] = (block if turned(hidden, n_fsdp) else block.T).astype(ref.dtype)


def band_table(head):
    key = np.arange(KW)[:, None] - HALO
    query = np.arange(GW)[None, :] % QB
    return np.where(np.abs(key - query) <= BAND, 0.0, -1e30).astype(np.float32)


def head_table(head):
    r = np.arange(GW)[:, None] // QB
    c = np.arange(GW)[None, :] // head
    return (r == c).astype(np.float32)


MESH = pl.DeviceIdType.MESH


class Place:
    def __init__(self, n_dp, n_fsdp):
        self.m = n_fsdp // 2
        self.nh = n_dp // 2
        d = lax.axis_index("dp")
        f = lax.axis_index("fsdp")
        self.dh, self.dl = d // 2, lax.rem(d, 2)
        self.fh, self.fl = f // 2, lax.rem(f, 2)

    def dev(self, dh=None, dl=None, fh=None, fl=None):
        dh = self.dh if dh is None else dh
        dl = self.dl if dl is None else dl
        fh = self.fh if fh is None else fh
        fl = self.fl if fl is None else fl
        return {"dp": dh * 2 + dl, "fsdp": fh * 2 + fl}

    def partners(self):
        out = [self.dev(fh=lax.rem(self.fh + o, self.m)) for o in range(1, self.m)]
        out += [self.dev(dh=lax.rem(self.dh + o, self.nh)) for o in range(1, self.nh)]
        return out + [self.dev(fl=1 - self.fl), self.dev(dl=1 - self.dl)]


def greet(place):
    barrier = pltpu.get_barrier_semaphore()
    who = place.partners()
    for dev in who:
        pl.semaphore_signal(barrier, inc=1, device_id=dev, device_id_type=MESH)
    pl.semaphore_wait(barrier, len(who))


def copy_to(src, dst, send, recv, dev):
    return pltpu.make_async_remote_copy(
        src_ref=src, dst_ref=dst, send_sem=send, recv_sem=recv, device_id=dev, device_id_type=MESH
    )


class Gather:
    def __init__(self, place, shard, got, send, recv, local, order, way=None):
        self.p, self.shard, self.got, self.order, self.way = place, shard, got, order, way
        self.send, self.recv, self.local = send, recv, local

    @staticmethod
    def count(n_dp, n_fsdp):
        return n_fsdp // 2 - 1 + 1 + n_dp // 2 - 1 + 1

    def own(self):
        p = self.p
        src = self.shard if self.way is None else self.way
        return pltpu.make_async_copy(src, self.got.at[p.dh, p.dl, p.fh, p.fl], self.local)

    def fetch(self):
        return pltpu.make_async_copy(self.shard, self.way, self.local)

    def stage(self, k):
        p, g = self.p, self.got
        if k == 0:
            out = []
            for o in range(1, p.m):
                to = p.dev(fh=lax.rem(p.fh + o, p.m))
                dst = g.at[p.dh, p.dl, p.fh, p.fl]
                out.append(copy_to(self.shard, dst, self.send.at[o - 1], self.recv.at[o - 1], to))
            return out
        i = p.m - 1
        if k == 3:
            ref = g.at[:, p.dl]
            return [copy_to(ref, ref, self.send.at[i], self.recv.at[i], p.dev(dl=1 - p.dl))]
        if (k == 1) == (self.order == "x"):
            ref = g.at[p.dh, p.dl, :, p.fl] if k == 1 else g.at[:, p.dl, :, p.fl]
            return [copy_to(ref, ref, self.send.at[i + 1], self.recv.at[i + 1], p.dev(fl=1 - p.fl))]
        ref = g.at[p.dh, p.dl, :, p.fl] if k == 1 else g.at[p.dh, p.dl]
        out = []
        for o in range(1, p.nh):
            to = p.dev(dh=lax.rem(p.dh + o, p.nh))
            out.append(copy_to(ref, ref, self.send.at[i + 1 + o], self.recv.at[i + 1 + o], to))
        return out

    def start(self, k):
        for c in self.stage(k):
            c.start()

    def wait(self, k):
        if k == 0:
            self.own().wait()
        for c in self.stage(k):
            c.wait()

    def turn(self, k):
        self.wait(k)
        self.start(k + 1)


def front_kernel(
    ways,
    plan,
    qkv_steps,
    len_ref,
    tok_ref,
    wqkv,
    win,
    wback,
    wout,
    vec_in,
    bias_in,
    band_ref,
    qkv_ref,
    near_ref,
    fa_ref,
    fb_ref,
    rn_ref,
    p_ref,
    h1t_ref,
    m1_ref,
    m2_ref,
    c_ref,
    w_ref,
    vec_ref,
    bin_ref,
    g_in,
    g_back,
    g_out,
    all_s,
    st_ref,
    t_ref,
    g_qkv,
    small,
    g_small,
    way_in,
    way_back,
    way_out,
    key_s,
    qq_s,
    send,
    recv,
    local,
):
    step = pl.program_id(0)
    steps = qkv_steps
    rows, width = tok_ref.shape
    groups = width // GW
    head = width // HEADS
    scale = head ** (-0.5)
    length = len_ref[0, 0]
    n_dp, n_fsdp = ways
    cols = vec_in.shape[1]
    place = Place(n_dp, n_fsdp)
    half_in = win.shape[1] // 2
    half_back = wback.shape[0] // 2

    def piece(j, shard, got, order, way=None):
        return Gather(place, shard, got, send.at[j], recv.at[j], local.at[j], order, way)

    first = [[piece(7, small, g_small, "x")], []]
    for i, (which, cut, order) in enumerate(qkv_parts(*wqkv.shape)):
        first[which].append(piece(8 + i, wqkv.at[cut], g_qkv.at[(slice(None),) * 4 + cut], order))
    rest = []
    for i in range(2):
        cut = pl.ds(i * half_in, half_in)
        rest.append(piece(i, win.at[:, cut], g_in.at[:, :, :, :, :, cut], "x", way_in.at[:, cut]))
    for i in range(2):
        cut = pl.ds(i * half_back, half_back)
        rest.append(piece(2 + i, wback.at[cut], g_back.at[:, :, :, :, cut], "y", way_back.at[cut]))
    rest.append(piece(4, wout, g_out, "y", way_out))
    sets = [[rest[0], rest[2]], [rest[1], rest[3], rest[4]]]

    @pl.when(step == 0)
    def _():
        small[...] = jnp.zeros_like(small)
        small[:2, :cols] = vec_in[...]
        small[2:3, :cols] = bias_in[...]
        for x in first[0] + first[1]:
            x.own().start()
        for x in rest:
            x.fetch().start()
        greet(place)
        for x in first[0] + first[1]:
            x.start(0)
        for x in rest:
            x.fetch().wait()
            x.own().start()
        st_ref[...] = jnp.zeros_like(st_ref)
        t_ref[...] = jnp.zeros_like(t_ref)
        all_s[:HALO] = jnp.zeros((HALO, 3 * width), bf16)
        all_s[HALO + steps * rows :] = jnp.zeros((HALO, 3 * width), bf16)
        qq_s[...] = jnp.zeros_like(qq_s)
        key = lax.broadcasted_iota(jnp.int32, key_s.shape, 0) - HALO
        key_s[...] = jnp.where((key >= 0) & (key < length), 0.0, -1e30)
        for k in range(3):
            for group in first:
                for x in group:
                    x.turn(k)
            if k == 0:
                for x in sets[0] + sets[1]:
                    x.start(0)
        for x in first[0] + first[1]:
            x.wait(3)
        join_pairs(w_ref, g_qkv)
        lane = lax.broadcasted_iota(jnp.int32, (128, width), 0)
        col = lax.broadcasted_iota(jnp.int32, (128, width), 1)

        def place_small(f, total):
            spot = ((lane + f * cols == col) & (lane < cols)).astype(bf16)
            block = jnp.concatenate(
                [g_small[d // 2, d % 2, f // 2, lax.rem(f, 2)] for d in range(n_dp)], axis=0
            )
            return total + nn(block, spot)

        total = lax.fori_loop(0, n_fsdp, place_small, jnp.zeros((16 * n_dp, width), f32))
        for d in range(n_dp):
            vec_ref[2 * d : 2 * d + 2] = total[16 * d : 16 * d + 2]
            bin_ref[0:1, d * width : (d + 1) * width] = total[16 * d + 2 : 16 * d + 3]

    def advance(at, moves):
        @pl.when(step == at)
        def _():
            for which, k in moves:
                for x in sets[which]:
                    if k < 3:
                        x.turn(k)
                    else:
                        x.wait(k)

    for at, moves in plan.items():
        if at < 2 * steps:
            advance(at, moves)

    @pl.when(step < steps)
    def _():
        z, _ = moments(tok_ref[...].astype(f32))
        h = (z * vec_ref[0:1] + vec_ref[1:2]).astype(bf16)
        h1t_ref[...] = h.T
        lo = pl.multiple_of(HALO + step * rows, HALO)
        q = nn(h, w_ref[:, :width]).astype(bf16)
        qkv_ref[:, :width] = q
        all_s[pl.ds(lo, rows), :width] = q
        valid = row_valid(step, rows, GW, length)
        for g in range(groups):
            kc = slice(width + g * GW, width + (g + 1) * GW)
            vc = slice(2 * width + g * GW, 2 * width + (g + 1) * GW)
            k = nn(h, w_ref[:, kc]).astype(bf16)
            v = nn(h, w_ref[:, vc]).astype(bf16)
            qkv_ref[:, kc] = k
            qkv_ref[:, vc] = v
            all_s[pl.ds(lo, rows), kc] = k
            all_s[pl.ds(lo, rows), vc] = v
            phi = jnp.where(valid, lift(k), 0)
            bent = jnp.where(valid, jnp.tanh(k), 0)
            st_ref[g] += tn(v, jnp.concatenate([phi, bent], axis=1))
            t_ref[g] += fold8(phi.astype(f32))

    @pl.when(step == steps - 1)
    def _():
        mask = same_head(head).astype(f32)
        inv_len = 1.0 / length.astype(f32)
        ones = jnp.ones((8, GW), f32)
        for g in range(groups):
            tb = jnp.sum(t_ref[g], axis=0, keepdims=True) * mask
            s1 = st_ref[g][:, :GW] * mask
            s2 = st_ref[g][:, GW:] * mask
            c_row = (nt_exact(ones, s1) / nt_exact(ones, tb)).astype(bf16).astype(f32)
            c_col = jnp.broadcast_to(c_row[0:1], (GW, GW)).T
            m1_ref[g, :GW] = (s1 - c_col * tb).astype(bf16)
            m1_ref[g, GW:] = tb.astype(bf16)
            m2_ref[g] = (s2 * inv_len).astype(bf16)
            c_ref[g] = c_row

    @pl.when(step >= steps)
    def _():
        at = (step - steps) * rows
        for b in range(rows // QB):
            here = pl.ds(pl.multiple_of(at + b * QB + HALO, HALO), QB)
            window = pl.ds(pl.multiple_of(at + b * QB, QB), KW)
            out_of_item = key_s[window]
            bias = band_ref[...] + jnp.concatenate([out_of_item] * (GW // 128), axis=1)
            for g in range(groups):
                cut = slice(g * GW, (g + 1) * GW)
                kc = slice(width + g * GW, width + (g + 1) * GW)
                vc = slice(2 * width + g * GW, 2 * width + (g + 1) * GW)
                put_heads(qq_s.at[g, b], all_s[here, cut] * scale, head)
                s = nt(all_s[window, kc], qq_s[g, b]) + bias
                e = jnp.exp(s - jnp.max(s, axis=0, keepdims=True))
                p = (e * (1.0 / jnp.sum(e, axis=0, keepdims=True))).astype(bf16)
                p_ref[b, :, cut] = p
                o = tn(p, all_s[window, vc])
                near_ref[b * QB : (b + 1) * QB, cut] = pick_heads(o, head).astype(bf16)
        for g in range(groups):
            cut = slice(g * GW, (g + 1) * GW)
            q = all_s[pl.ds(pl.multiple_of(at + HALO, HALO), rows), cut]
            both = nt(lift(q), m1_ref[g])
            rn = 1.0 / both[:, GW:]
            rn_ref[:, cut] = rn.astype(bf16)
            fa_ref[:, cut] = (both[:, :GW] * rn).astype(bf16)
            fb_ref[:, cut] = nt(jnp.tanh(q), m2_ref[g]).astype(bf16)

    advance(2 * steps - 1, plan[2 * steps])


def join_pairs(ref, got):
    nh, _, m, _, r, c = got.shape
    for d in range(2 * nh):
        for f in range(2 * m):
            ref[f * r : (f + 1) * r, d * c : (d + 1) * c] = got[d // 2, d % 2, f // 2, f % 2]


def qkv_parts(r, c):
    if c % 384:
        return [(0, (pl.ds(0, r), pl.ds(0, c)), "x")]
    third = c // 3
    whole = pl.ds(0, r)
    parts = [(0, (whole, pl.ds(0, third)), "x"), (0, (whole, pl.ds(third, third)), "y")]
    rest = pl.ds(2 * third, third)
    if r % 32:
        return parts + [(1, (whole, rest), "x")]
    half = r // 2
    return parts + [(1, (pl.ds(0, half), rest), "x"), (1, (pl.ds(half, half), rest), "y")]


def front_pass(ways, length, tokens, w_qkv, w_in, w_back, w_out, vec, bias, tile, plan):
    rows, width = tokens.shape
    groups = width // GW
    n_dp, n_fsdp = ways
    nh, m = n_dp // 2, n_fsdp // 2
    steps = rows // tile
    head = width // HEADS
    const = lambda *shape: pl.BlockSpec(shape, lambda i: (0,) * len(shape))
    early = lambda i: (jnp.minimum(i, steps - 1), 0)
    late = pl.BlockSpec((tile, width), lambda i: (jnp.maximum(i - steps, 0), 0))
    hbm = pl.BlockSpec(memory_space=pl.ANY)
    sds = jax.ShapeDtypeStruct
    got = lambda r, c: (nh, 2, m, 2, r, c)
    hidden = w_in.shape[1] * n_dp
    pieces = 8 + len(qkv_parts(*w_qkv.shape))
    per = Gather.count(n_dp, n_fsdp)
    return pl.pallas_call(
        functools.partial(front_kernel, ways, plan, steps),
        grid=(2 * steps,),
        in_specs=[
            pl.BlockSpec(memory_space=pltpu.SMEM),
            pl.BlockSpec((tile, width), early),
            hbm,
            hbm,
            hbm,
            hbm,
            const(*vec.shape),
            const(*bias.shape),
            const(KW, GW),
        ],
        out_specs=[
            pl.BlockSpec((tile, 3 * width), early),
            late,
            late,
            late,
            late,
            pl.BlockSpec((tile // QB, KW, width), lambda i: (jnp.maximum(i - steps, 0), 0, 0)),
            pl.BlockSpec((width, tile), lambda i: (0, jnp.minimum(i, steps - 1))),
            const(groups, 2 * GW, GW),
            const(groups, GW, GW),
            const(groups, 8, GW),
            const(width, 3 * width),
            const(8, width),
            const(1, hidden),
            hbm,
            hbm,
            hbm,
        ],
        out_shape=[sds((rows, 3 * width), bf16)]
        + [sds((rows, width), bf16)] * 4
        + [
            sds((rows // QB, KW, width), bf16),
            sds((width, rows), bf16),
            sds((groups, 2 * GW, GW), bf16),
            sds((groups, GW, GW), bf16),
            sds((groups, 8, GW), f32),
            sds((width, 3 * width), bf16),
            sds((8, width), f32),
            sds((1, hidden), f32),
            sds(got(*w_in.shape), bf16),
            sds(got(*w_back.shape), bf16),
            sds(got(*w_out.shape), bf16),
        ],
        scratch_shapes=[
            pltpu.VMEM((rows + 2 * HALO, 3 * width), bf16),
            pltpu.VMEM((groups, GW, 2 * GW), f32),
            pltpu.VMEM((groups, 8, GW), f32),
            pltpu.VMEM(got(*w_qkv.shape), bf16),
            pltpu.VMEM((16, 128), bf16),
            pltpu.VMEM(got(16, 128), bf16),
            pltpu.VMEM(w_in.shape, bf16),
            pltpu.VMEM(w_back.shape, bf16),
            pltpu.VMEM(w_out.shape, bf16),
            pltpu.VMEM((rows + 2 * HALO, 128), f32),
            pltpu.VMEM((groups, tile // QB, GW, GW), bf16),
            pltpu.SemaphoreType.DMA((pieces, per)),
            pltpu.SemaphoreType.DMA((pieces, per)),
            pltpu.SemaphoreType.DMA((pieces,)),
        ],
        compiler_params=pltpu.CompilerParams(
            collective_id=0, has_side_effects=True, vmem_limit_bytes=VMEM_LIMIT
        ),
        cost_estimate=pl.CostEstimate(
            flops=2 * rows * width * 8 * width, bytes_accessed=rows * width * 24, transcendentals=0
        ),
        name="front_pass",
    )(
        length,
        tokens,
        w_qkv,
        w_in,
        w_back,
        w_out,
        vec,
        bias,
        jnp.asarray(band_table(head)),
    )


def ffn_kernel(
    chunk,
    len_ref,
    tok_ref,
    cot_ref,
    near_ref,
    fa_ref,
    fb_ref,
    rn_ref,
    q_ref,
    c_ref,
    vec_ref,
    bin_ref,
    gw_out,
    gw_in,
    gw_back,
    out_ref,
    datt_ref,
    dmix_ref,
    dn_ref,
    gin_ref,
    gback_ref,
    gout_ref,
    gvec_ref,
    gbias_ref,
    m3_ref,
    m4_ref,
    dt_ref,
    a_in,
    a_back,
    a_out,
    a_st,
    a_bent,
    wout_ref,
    win_ref,
    wback_ref,
    act_s,
    pre_s,
):
    step = pl.program_id(0)
    rows, width = tok_ref.shape
    hidden = win_ref.shape[1]
    groups = width // GW
    head_size = width // HEADS
    steps = pl.num_programs(0)
    length = len_ref[0, 0]
    c_row = jnp.concatenate([c_ref[g, 0:1] for g in range(groups)], axis=1)
    blend = vec_ref[...].astype(bf16)
    s0 = math.sqrt(2.0 / math.pi)
    s1 = s0 * 0.044715

    @pl.when(step == 0)
    def _():
        join_blocks(wout_ref, gw_out)
        join_blocks(win_ref, gw_in)
        join_blocks(wback_ref, gw_back)
        for ref in (a_in, a_back, a_out, a_st, a_bent, gvec_ref, gbias_ref):
            ref[...] = jnp.zeros_like(ref)

    near = near_ref[...]
    fac = fa_ref[...]
    far_b = fb_ref[...]
    mixed = (
        vec_ref[5:6] * near.astype(f32)
        + vec_ref[6:7] * (fac.astype(f32) + c_row)
        + vec_ref[7:8] * far_b.astype(f32)
    ).astype(bf16)
    resid = tok_ref[...].astype(f32) + nn(mixed, wout_ref[...])
    z2, r2 = moments(resid)
    h2 = (z2 * vec_ref[2:3] + vec_ref[3:4]).astype(bf16)
    valid = row_valid(step, rows, width, length)
    d_ffn = jnp.where(valid, cot_ref[...], 0)
    seed = d_ffn.astype(f32)
    def add_grads(cols):
        a_back[:, cols] += tn(d_ffn, act_s[:, cols])
        a_in[:, cols] += tn(h2, pre_s[:, cols])

    for lo in range(0, hidden, chunk):
        cols = slice(lo, lo + chunk)
        x = nn(h2, win_ref[:, cols]) + bin_ref[0:1, cols]
        if lo:
            add_grads(slice(lo - chunk, lo))
        x2 = x * x
        half = 0.5 + 0.5 * jnp.tanh(x * (s0 + s1 * x2))
        act = x * half
        slope = half + (act - act * half) * (2 * s0 + 6 * s1 * x2)
        act = act.astype(bf16)
        act_s[:, cols] = act
        d_pre = slope * nt(d_ffn, wback_ref[cols, :])
        gbias_ref[:, cols] += fold8(d_pre)
        d_pre = d_pre.astype(bf16)
        pre_s[:, cols] = d_pre
    add_grads(slice(hidden - chunk, hidden))
    dh2 = nt(pre_s[...], win_ref[...])
    both = dh2 * z2
    gvec_ref[2] += fold8(both)
    gvec_ref[3] += fold8(dh2)
    gvec_ref[4] += fold8(seed)
    dz = dh2 * vec_ref[2:3]
    mean_z = jnp.mean(both * vec_ref[2:3], axis=-1, keepdims=True)
    d_resid = seed + r2 * (dz - jnp.mean(dz, axis=-1, keepdims=True) - z2 * mean_z)
    d_attn = d_resid.astype(bf16)
    datt_ref[...] = d_attn
    ffn = nn(act_s[...], wback_ref[...])
    out_ref[...] = jnp.where(valid, resid + ffn + vec_ref[4:5], 0.0).astype(bf16)
    a_out[...] += tn(mixed, d_attn)
    d_mix = nt(d_attn, wout_ref[...]).astype(bf16)
    dmix_ref[...] = d_mix
    gvec_ref[5] += fold8(fold4(d_mix * near).astype(f32))
    gvec_ref[6] += fold8(fold4(d_mix * fac).astype(f32))
    gvec_ref[7] += fold8(fold4(d_mix * far_b).astype(f32))
    gvec_ref[0] += fold8(fold4(d_mix).astype(f32))
    d_num = blend[6:7] * d_mix * rn_ref[...]
    dn_ref[...] = d_num
    d_den = d_num * fac
    d_far = blend[7:8] * d_mix
    for g in range(groups):
        cols = slice(g * GW, (g + 1) * GW)
        q = q_ref[:, cols]
        a_st[g] += tn(lift(q), jnp.concatenate([d_num[:, cols], d_den[:, cols]], axis=1))
        a_bent[g] += tn(jnp.tanh(q), d_far[:, cols])

    @pl.when(step == steps - 1)
    def _():
        mask = same_head(head_size).astype(f32)
        inv_len = 1.0 / length.astype(f32)
        ones = jnp.ones((8, GW), f32)
        for g in range(groups):
            m3_ref[g] = (a_st[g][:, :GW] * mask).astype(bf16)
            m4_ref[g] = (a_bent[g] * mask * inv_len).astype(bf16)
            dt_ref[g] = -nt_exact(ones, a_st[g][:, GW:] * mask)
        cut_blocks(gin_ref, a_in)
        cut_turned(gback_ref, a_back)
        cut_blocks(gout_ref, a_out)
        gvec_ref[6] += gvec_ref[0] * c_row


def third_pass(
    ways, length, tokens, cot, near, fa, fb, rn, qkv, c, vecs, b_in, w_out, w_in, w_back, tile, chunk
):
    rows, width = tokens.shape
    hidden = w_in.shape[0] * w_in.shape[3]
    groups = width // GW
    steps = rows // tile
    n_dp, n_fsdp = ways
    back = (width // n_dp, hidden // n_fsdp)
    back = back if turned(hidden, n_fsdp) else back[::-1]

    def const(*shape):
        return pl.BlockSpec(shape, lambda i: (0,) * len(shape))

    def kept(*shape):
        return pl.BlockSpec(shape, lambda i: (0,) * len(shape), pipeline_mode=pl.Buffered(1))

    sds = jax.ShapeDtypeStruct
    block = pl.BlockSpec((tile, width), lambda i: (i, 0))
    deep = pltpu.VMEM((tile, hidden), bf16)
    return pl.pallas_call(
        functools.partial(ffn_kernel, chunk),
        grid=(steps,),
        in_specs=[pl.BlockSpec(memory_space=pltpu.SMEM)]
        + [block] * 7
        + [
            const(groups, 8, GW),
            const(8, width),
            const(1, hidden),
            kept(*w_out.shape),
            kept(*w_in.shape),
            kept(*w_back.shape),
        ],
        out_specs=[block] * 4
        + [
            const(n_dp, n_fsdp, width // n_fsdp, hidden // n_dp),
            const(n_dp, n_fsdp, *back),
            const(n_dp, n_fsdp, width // n_fsdp, width // n_dp),
            const(8, 8, width),
            const(8, hidden),
            const(groups, GW, GW),
            const(groups, GW, GW),
            const(groups, 8, GW),
        ],
        out_shape=[sds((rows, width), bf16)] * 4
        + [
            sds((n_dp, n_fsdp, width // n_fsdp, hidden // n_dp), bf16),
            sds((n_dp, n_fsdp, *back), bf16),
            sds((n_dp, n_fsdp, width // n_fsdp, width // n_dp), bf16),
            sds((8, 8, width), f32),
            sds((8, hidden), f32),
            sds((groups, GW, GW), bf16),
            sds((groups, GW, GW), bf16),
            sds((groups, 8, GW), f32),
        ],
        scratch_shapes=[
            pltpu.VMEM((width, hidden), f32),
            pltpu.VMEM((width, hidden), f32),
            pltpu.VMEM((width, width), f32),
            pltpu.VMEM((groups, GW, 2 * GW), f32),
            pltpu.VMEM((groups, GW, GW), f32),
            pltpu.VMEM((width, width), bf16),
            pltpu.VMEM((width, hidden), bf16),
            pltpu.VMEM((hidden, width), bf16),
            deep,
            deep,
        ],
        compiler_params=pltpu.CompilerParams(vmem_limit_bytes=VMEM_LIMIT),
        cost_estimate=pl.CostEstimate(
            flops=2 * rows * width * (6 * hidden + 4 * width),
            bytes_accessed=rows * width * 22,
            transcendentals=0,
        ),
        name="third_pass",
    )(length, tokens, cot, near, fa, fb, rn, qkv, c, vecs, b_in, w_out, w_in, w_back)


class Scatter:
    def __init__(self, place, src, out, bufs, send, recv, local, order):
        self.p, self.src, self.out, self.order = place, src, out, order
        self.acc, self.r0, self.r1, self.r2, self.r3 = bufs
        self.send, self.recv, self.local = send, recv, local

    @staticmethod
    def count(n_dp, n_fsdp):
        return n_dp // 2 + 1 + (n_dp // 2 - 1) + (n_fsdp // 2 - 1)

    @staticmethod
    def scratch(n_dp, n_fsdp, r, c, order, dtype):
        nh, m = n_dp // 2, n_fsdp // 2
        if order == "x":
            one, two = (nh, m, r, c), (nh - 1, m, r, c)
        else:
            one, two = (nh - 1, m, 2, r, c), (m, r, c)
        shapes = [(nh, m, 2, r, c), (nh, m, 2, r, c), one, two, (m - 1, r, c)]
        return [pltpu.VMEM(s, dtype) for s in shapes]

    def own(self):
        return pltpu.make_async_copy(self.src.at[:, self.p.dl], self.acc, self.local)

    def stage(self, k, only=None):
        p = self.p
        if k == 0:
            to = p.dev(dl=1 - p.dl)
            return [
                copy_to(self.src.at[dh, 1 - p.dl], self.r0.at[dh], self.send.at[dh], self.recv.at[dh], to)
                for dh in (range(p.nh) if only is None else [only])
            ]
        first = p.nh - 1
        if k == 3:
            i = first + p.nh
            out = []
            for o in range(1, p.m):
                fh = lax.rem(p.fh + o, p.m)
                out.append(
                    copy_to(self.acc.at[p.dh, fh, p.fl], self.r3.at[o - 1], self.send.at[i + o], self.recv.at[i + o],
                            p.dev(fh=fh))
                )
            return out
        if (k == 1) == (self.order == "x"):
            ref = self.acc.at[:, :, 1 - p.fl] if k == 1 else self.acc.at[p.dh, :, 1 - p.fl]
            dst = self.r1 if k == 1 else self.r2
            i = first + 1
            return [copy_to(ref, dst, self.send.at[i], self.recv.at[i], p.dev(fl=1 - p.fl))]
        out = []
        for o in range(1, p.nh):
            dh = lax.rem(p.dh + o, p.nh)
            ref = self.acc.at[dh] if k == 1 else self.acc.at[dh, :, p.fl]
            dst = self.r1.at[o - 1] if k == 1 else self.r2.at[o - 1]
            i = first + 1 + o
            out.append(copy_to(ref, dst, self.send.at[i], self.recv.at[i], p.dev(dh=dh)))
        return out

    def start(self, k):
        for c in self.stage(k):
            c.start()

    def turn(self, k):
        if k == 0:
            self.own().wait()
        for c in self.stage(k):
            c.wait()
        self.add(k)
        if k < 3:
            self.start(k + 1)

    def add(self, k):
        p, acc = self.p, self.acc
        nh, m = p.nh, p.m
        dt = acc.dtype

        def put(index, others):
            if len(others) == 1:
                acc[index] += others[0]
                return
            total = acc[index].astype(f32)
            for o in others:
                total = total + o.astype(f32)
            acc[index] = total.astype(dt)

        if k == 3:
            total = acc[p.dh, p.fh, p.fl].astype(f32)
            for o in range(1, m):
                total = total + self.r3[o - 1].astype(f32)
            self.out[...] = total
            return

        @pl.loop(0, m)
        def _(i):
            if k == 0:
                for a in range(nh):
                    for b in range(2):
                        put((a, i, b), [self.r0[a, i, b]])
            elif k == 1 and self.order == "x":
                for a in range(nh):
                    put((a, i, p.fl), [self.r1[a, i]])
            elif k == 1:
                for b in range(2):
                    put((p.dh, i, b), [self.r1[o - 1, i, b] for o in range(1, nh)])
            elif self.order == "x":
                put((p.dh, i, p.fl), [self.r2[o - 1, i] for o in range(1, nh)])
            else:
                put((p.dh, i, p.fl), [self.r2[i]])


def back_kernel(
    ways,
    plan,
    late_plan,
    len_ref,
    q_ref,
    k_lo,
    k_ref,
    k_hi,
    v_lo,
    v_ref,
    v_hi,
    p_ref,
    dmix_ref,
    dn_ref,
    fa_ref,
    tok_ref,
    datt_ref,
    h1t_hbm,
    m1_ref,
    m2_ref,
    m3_ref,
    m4_ref,
    dt_ref,
    c_ref,
    vec_ref,
    w_hbm,
    gv_ref,
    gbias_ref,
    s_in,
    s_back,
    s_out,
    dtok_ref,
    oqkv_ref,
    oin_ref,
    oback_ref,
    oout_ref,
    ovec_ref,
    obias_ref,
    h1t_ref,
    w_ref,
    kk,
    vv,
    far_s,
    dp_s,
    ds_s,
    dd_s,
    qq_s,
    all_d,
    carry,
    gvec_s,
    gq_ref,
    gs_ref,
    rows_s,
    back_t,
    small_o,
    late_src,
    late_got,
    *rest,
):
    step = pl.program_id(0)
    rows, width = q_ref.shape
    total = h1t_ref.shape[1]
    steps = total // rows
    groups = width // GW
    head = width // HEADS
    scale = head ** (-0.5)
    length = len_ref[0, 0]
    n_dp, n_fsdp = ways
    place = Place(n_dp, n_fsdp)
    cols = ovec_ref.shape[1]
    c_all = oqkv_ref.shape[1]
    send, recv, local, late_send, late_recv, fetch = rest[-6:]
    fetches = [
        pltpu.make_async_copy(h1t_hbm, h1t_ref, fetch.at[0]),
        pltpu.make_async_copy(w_hbm, w_ref, fetch.at[1]),
    ]
    final = steps + 1 + place.nh
    last_rows = tok_ref.shape[0]

    used = [0]

    def piece(src, out, order):
        j = used[0]
        used[0] += 1
        return Scatter(place, src, out, rest[5 * j : 5 * j + 5], send.at[j], recv.at[j], local.at[j], order)

    sets = [[], [], [], []]
    every = (slice(None),) * 4
    for i, (cut_in, cut_back) in enumerate(ffn_parts(s_in.shape[-2:], s_back.shape[-2:])):
        sets[i].append(piece(s_in.at[every + cut_in], oin_ref.at[cut_in], "x"))
        sets[i].append(piece(s_back.at[every + cut_back], back_t.at[cut_back], "y"))
    sets[1].append(piece(s_out, oout_ref, "y"))
    sets[1].append(piece(gs_ref, small_o, "x"))
    for which, cut, order in qkv_parts(*oqkv_ref.shape):
        sets[2 + which].append(piece(gq_ref.at[every + cut], oqkv_ref.at[cut], order))

    @pl.when(step == 0)
    def _():
        for x in sets[0] + sets[1][:-1]:
            x.own().start()
        greet_all(place)
        for x in sets[0] + sets[1][:-1]:
            x.start(0)
        for x in fetches:
            x.start()
        carry[...] = jnp.zeros_like(carry)
        dd_s[...] = jnp.zeros_like(dd_s)
        qq_s[...] = jnp.zeros_like(qq_s)
        gvec_s[...] = jnp.zeros_like(gvec_s)
        gs_ref[...] = jnp.zeros_like(gs_ref)
        late_src[...] = jnp.zeros_like(late_src)
        rows_s[0:2] = jnp.zeros((2, width), f32)
        rows_s[2:8] = jnp.sum(gv_ref[2:8], axis=1)
        bias = jnp.sum(gbias_ref[...], axis=0, keepdims=True)
        for d in range(n_dp):
            pair = rows_s[2 * d : 2 * d + 2]
            for f in range(n_fsdp):
                spot = slice(f * cols, (f + 1) * cols)
                at = d * width + f * cols
                gs_ref[d // 2, d % 2, f // 2, f % 2, 0:2, :cols] = pair[:, spot]
                gs_ref[d // 2, d % 2, f // 2, f % 2, 2:3, :cols] = bias[:, at : at + cols]
        sets[1][-1].own().start()
        sets[1][-1].start(0)

    for at, moves in plan.items():

        @pl.when(step == at)
        def _(moves=moves):
            for which, k in moves:
                for x in sets[which]:
                    x.turn(k)

    def far_keys(at, slot, live):
        valid = row_valid(at, rows, GW, length) & live
        here = pl.ds(pl.multiple_of(at * rows + HALO, HALO), rows)
        for g in range(groups):
            cut = slice(g * GW, (g + 1) * GW)
            kc = slice(width + g * GW, width + (g + 1) * GW)
            vc = slice(2 * width + g * GW, 2 * width + (g + 1) * GW)
            k = kk[slot, HALO : HALO + rows, cut]
            v = vv[slot, HALO : HALO + rows, cut]
            lift_k = lift(k)
            bent_k = jnp.tanh(k)
            v_cen = v - c_ref[g, 0:1].astype(bf16)
            dk = (nt(v_cen, m3_ref[g]) + dt_ref[g, 0:1]) * jnp.minimum(lift_k, 1).astype(f32)
            dk += nt(v, m4_ref[g]) * (1 - bent_k * bent_k).astype(f32)
            both = jnp.concatenate([lift_k, bent_k], axis=1)
            dv = nn(both, jnp.concatenate([m3_ref[g], m4_ref[g]], axis=0))
            all_d[here, kc] += jnp.where(valid, dk.astype(bf16), 0)
            all_d[here, vc] += jnp.where(valid, dv.astype(bf16), 0)

    @pl.when(step < steps)
    def _():
        slot = lax.rem(step, 2)
        kk[slot, :HALO] = k_lo[...]
        kk[slot, HALO : HALO + rows] = k_ref[...]
        kk[slot, HALO + rows :] = k_hi[...]
        vv[slot, :HALO] = v_lo[...]
        vv[slot, HALO : HALO + rows] = v_ref[...]
        vv[slot, HALO + rows :] = v_hi[...]
        blend = vec_ref[...].astype(bf16)
        base = step * rows
        for g in range(groups):
            cut = slice(g * GW, (g + 1) * GW)
            kc = slice(width + g * GW, width + (g + 1) * GW)
            vc = slice(2 * width + g * GW, 2 * width + (g + 1) * GW)
            q = q_ref[:, cut]
            d_num = dn_ref[:, cut]
            d_den = -d_num * fa_ref[:, cut]
            d_mix = dmix_ref[:, cut]
            bent = jnp.tanh(q)
            far = nn(jnp.concatenate([d_num, d_den], axis=1), m1_ref[g]) * jnp.minimum(lift(q), 1).astype(f32)
            far_s[:, cut] = far + nn(blend[7:8, cut] * d_mix, m2_ref[g]) * (1 - bent * bent).astype(f32)
            for b in range(rows // QB):
                here = slice(b * QB, (b + 1) * QB)
                window = slice(b * QB, b * QB + KW)
                put_heads(dd_s.at[g, b], blend[5:6, cut] * dmix_ref[here, cut], head)
                dp_s[g, b] = nt(vv[slot, window, cut], dd_s[g, b]).astype(bf16)
            for b in range(rows // QB):
                p = p_ref[b, :, cut]
                dp = dp_s[g, b]
                dot = jnp.sum(fold4(p * dp).astype(f32), axis=0, keepdims=True)
                ds_s[g, b] = p * (dp - dot.astype(bf16))
            old_k = carry[0, :, cut]
            old_v = carry[1, :, cut]
            for b in range(rows // QB):
                here = slice(b * QB, (b + 1) * QB)
                window = slice(b * QB, b * QB + KW)
                d_s = ds_s[g, b]
                put_heads(qq_s.at[g, b], q_ref[here, cut] * scale, head)
                dk = nn(d_s, qq_s[g, b])
                dv = nn(p_ref[b, :, cut], dd_s[g, b])
                dq = pick_heads(tn(d_s, kk[slot, window, cut]), head) * scale + far_s[here, cut]
                lo = pl.ds(pl.multiple_of(base + b * QB, QB), QB)
                all_d[pl.ds(pl.multiple_of(base + b * QB + HALO, HALO), QB), cut] = dq.astype(bf16)
                all_d[lo, kc] = (old_k + dk[:QB]).astype(bf16)
                all_d[lo, vc] = (old_v + dv[:QB]).astype(bf16)
                old_k = dk[QB:]
                old_v = dv[QB:]
            carry[0, :, cut] = old_k
            carry[1, :, cut] = old_v
        far_keys(jnp.maximum(step - 1, 0), 1 - slot, step > 0)

    @pl.when(step == steps)
    def _():
        all_d[total:, width : 2 * width] = carry[0].astype(bf16)
        all_d[total:, 2 * width :] = carry[1].astype(bf16)
        far_keys(steps - 1, (steps - 1) % 2, True)

    for dh in range(n_dp // 2):

        @pl.when(step == steps + 1 + dh)
        def _(dh=dh):
            if dh == 0:
                fetches[0].wait()
            grad = nn(h1t_ref[...], all_d[HALO : HALO + total, dh * 2 * c_all : (dh + 1) * 2 * c_all])
            r = gq_ref.shape[-2]
            for dl in range(2):
                for f in range(n_fsdp):
                    block = grad[f * r : (f + 1) * r, dl * c_all : (dl + 1) * c_all]
                    gq_ref[dh, dl, f // 2, f % 2] = block.astype(bf16)
            for x in sets[2] + sets[3]:
                x.stage(0, dh)[0].start()

    @pl.when(step == final)
    def _():
        fetches[1].wait()
        for x in sets[2] + sets[3]:
            x.own().start()

    for at, moves in late_plan.items():
        if at == "end":
            continue

        @pl.when(step == final + at)
        def _(moves=moves):
            for which, k in moves:
                for x in sets[which]:
                    x.turn(k)

    @pl.when(step >= final)
    def _():
        here = pl.ds(pl.multiple_of((step - final) * last_rows + HALO, HALO), last_rows)
        z1, r1 = moments(tok_ref[...].astype(f32))
        dh1 = nt(all_d[here], w_ref[...])
        gvec_s[0] += fold8(dh1 * z1)
        gvec_s[1] += fold8(dh1)
        dz = dh1 * vec_ref[0:1]
        dtok_ref[...] = (
            datt_ref[...].astype(f32)
            + r1
            * (
                dz
                - jnp.mean(dz, axis=-1, keepdims=True)
                - z1 * jnp.mean(dz * z1, axis=-1, keepdims=True)
            )
        ).astype(bf16)

    @pl.when(step == final + total // last_rows - 1)
    def _():
        rows_s[0:2] = jnp.sum(gvec_s[...], axis=1)
        for f in range(n_fsdp):
            late_src[f, 0:2, :cols] = rows_s[0:2, f * cols : (f + 1) * cols]
        d, f = lax.axis_index("dp"), lax.axis_index("fsdp")
        me = d * n_fsdp + f

        def late(o):
            to = lax.rem(f + o, n_fsdp)
            return copy_to(
                late_src.at[to], late_got.at[me], late_send.at[o], late_recv.at[me], {"dp": 0, "fsdp": to}
            )

        @pl.when(d > 0)
        def _():
            late(0).start()

        for o in range(1, n_fsdp):
            late(o).start()
        oback_ref[...] = back_t[...].T if turned(gbias_ref.shape[1], n_fsdp) else back_t[...]
        for which, k in late_plan["end"]:
            for x in sets[which]:
                x.turn(k)

        @pl.when(d > 0)
        def _():
            late(0).wait_send()
            ovec_ref[...] = small_o[0:2, :cols]

        for o in range(1, n_fsdp):
            late(o).wait_send()

        @pl.when(d == 0)
        def _():
            late_got[me] = late_src[f]

            @pl.loop(0, n_dp * n_fsdp)
            def _(s):
                @pl.when(s != me)
                def _():
                    copy_to(
                        late_src.at[0], late_got.at[s], late_send.at[0], late_recv.at[s], {"dp": 0, "fsdp": 0}
                    ).wait_recv()

            ovec_ref[...] = jnp.sum(late_got[...], axis=0)[0:2, :cols]

        obias_ref[...] = small_o[2:3, :cols]


def put_heads(ref, x, head):
    for h in range(GW // head):
        lanes = slice(h * head, (h + 1) * head)
        ref[h * QB : (h + 1) * QB, lanes] = x[:, lanes]


def ffn_parts(shape_in, shape_back):
    (r, c), (rb, cb) = shape_in, shape_back
    out = []
    for i in range(2):
        cut_in = (pl.ds(0, r), pl.ds(i * c // 2, c // 2))
        if cb % 256:
            cut_back = (pl.ds(i * rb // 2, rb // 2), pl.ds(0, cb))
        else:
            cut_back = (pl.ds(0, rb), pl.ds(i * cb // 2, cb // 2))
        out.append((cut_in, cut_back))
    return out


def greet_all(place):
    d, f = lax.axis_index("dp"), lax.axis_index("fsdp")
    n_dp, n_fsdp = 2 * place.nh, 2 * place.m
    barrier = pltpu.get_barrier_semaphore()
    who = place.partners()
    for dev in who:
        pl.semaphore_signal(barrier, inc=1, device_id=dev, device_id_type=MESH)

    @pl.when(d == 0)
    def _():
        @pl.loop(0, n_dp)
        def _(i):
            @pl.loop(0, n_fsdp)
            def _(j):
                @pl.when((i != 0) | (j != f))
                def _():
                    pl.semaphore_signal(barrier, inc=1, device_id={"dp": i, "fsdp": j}, device_id_type=MESH)

    pl.semaphore_wait(barrier, len(who) + n_fsdp - (d == 0).astype(jnp.int32))


def back_pass(
    ways,
    length,
    qkv,
    p,
    d_mix,
    tokens,
    d_attn,
    d_num,
    fa,
    h1t,
    m1,
    m2,
    m3,
    m4,
    dt,
    c,
    vecs,
    w_qkv,
    gv,
    gbias,
    s_in,
    s_back,
    s_out,
    tile,
    last_tile,
    plan,
    late_plan,
):
    rows, width = tokens.shape
    groups = width // GW
    steps = rows // tile
    n_dp, n_fsdp = ways
    nh, m = n_dp // 2, n_fsdp // 2
    r, c_all = width // n_fsdp, 3 * width // n_dp
    per = Scatter.count(n_dp, n_fsdp)
    final = steps + 1 + nh
    hbm = pl.BlockSpec(memory_space=pl.ANY)
    back_shape = s_back.shape[-2:]
    outs = [
        (r, c_all),
        s_in.shape[-2:],
        back_shape[::-1] if turned(gbias.shape[1], n_fsdp) else back_shape,
        s_out.shape[-2:],
        (2, width // n_fsdp),
        (1, gbias.shape[1] // (n_dp * n_fsdp)),
    ]
    kinds = []
    for cut_in, cut_back in ffn_parts(s_in.shape[-2:], back_shape):
        kinds.append((*(x.size for x in cut_in), "x", bf16))
        kinds.append((*(x.size for x in cut_back), "y", bf16))
    kinds.append((*s_out.shape[-2:], "y", bf16))
    kinds.append((8, 128, "x", f32))
    for _, cut, order in qkv_parts(r, c_all):
        kinds.append((*(x.size for x in cut), order, bf16))
    bufs = [b for k in kinds for b in Scatter.scratch(n_dp, n_fsdp, *k)]
    got = lambda *s: (nh, 2, m, 2, *s)

    def const(*shape):
        return pl.BlockSpec(shape, lambda i: (0,) * len(shape))

    def kept(*shape):
        return pl.BlockSpec(shape, lambda i: (0,) * len(shape), pipeline_mode=pl.Buffered(1))

    one = lambda i: jnp.minimum(i, steps - 1)
    end = lambda i: jnp.maximum(i - final, 0)
    per_tile = tile // HALO
    top = rows // HALO - 1

    def halo(col):
        return [
            pl.BlockSpec((HALO, width), lambda i: (jnp.maximum(one(i) * per_tile - 1, 0), col)),
            pl.BlockSpec((tile, width), lambda i: (one(i), col)),
            pl.BlockSpec((HALO, width), lambda i: (jnp.minimum((one(i) + 1) * per_tile, top), col)),
        ]

    block = pl.BlockSpec((tile, width), lambda i: (one(i), 0))
    late = pl.BlockSpec((last_tile, width), lambda i: (end(i), 0))
    head = width // HEADS
    sds = jax.ShapeDtypeStruct
    return pl.pallas_call(
        functools.partial(back_kernel, ways, plan, late_plan),
        grid=(final + rows // last_tile,),
        in_specs=[
            pl.BlockSpec(memory_space=pltpu.SMEM),
            block,
            *halo(1),
            *halo(2),
            pl.BlockSpec((tile // QB, KW, width), lambda i: (one(i), 0, 0)),
            block,
            block,
            block,
            late,
            late,
            hbm,
            kept(groups, 2 * GW, GW),
            kept(groups, GW, GW),
            kept(groups, GW, GW),
            kept(groups, GW, GW),
            const(groups, 8, GW),
            const(groups, 8, GW),
            const(8, width),
            hbm,
            const(*gv.shape),
            const(*gbias.shape),
            hbm,
            hbm,
            hbm,
        ],
        out_specs=[late] + [const(*s) for s in outs],
        out_shape=[sds((rows, width), bf16)] + [sds(s, f32) for s in outs],
        scratch_shapes=[
            pltpu.VMEM((width, rows), bf16),
            pltpu.VMEM((width, 3 * width), bf16),
            pltpu.VMEM((2, tile + 2 * HALO, width), bf16),
            pltpu.VMEM((2, tile + 2 * HALO, width), bf16),
            pltpu.VMEM((tile, width), f32),
            pltpu.VMEM((groups, tile // QB, KW, GW), bf16),
            pltpu.VMEM((groups, tile // QB, KW, GW), bf16),
            pltpu.VMEM((groups, tile // QB, GW, GW), bf16),
            pltpu.VMEM((groups, tile // QB, GW, GW), bf16),
            pltpu.VMEM((rows + 2 * HALO, 3 * width), bf16),
            pltpu.VMEM((2, QB, width), f32),
            pltpu.VMEM((2, 8, width), f32),
            pltpu.VMEM(got(r, c_all), bf16),
            pltpu.VMEM(got(8, 128), f32),
            pltpu.VMEM((8, width), f32),
            pltpu.VMEM(back_shape, f32),
            pltpu.VMEM((8, 128), f32),
            pltpu.VMEM((n_fsdp, 8, 128), f32),
            pltpu.VMEM((n_dp * n_fsdp, 8, 128), f32),
            *bufs,
            pltpu.SemaphoreType.DMA((len(kinds), per)),
            pltpu.SemaphoreType.DMA((len(kinds), per)),
            pltpu.SemaphoreType.DMA((len(kinds),)),
            pltpu.SemaphoreType.DMA((n_fsdp,)),
            pltpu.SemaphoreType.DMA((n_dp * n_fsdp,)),
            pltpu.SemaphoreType.DMA((2,)),
        ],
        compiler_params=pltpu.CompilerParams(
            collective_id=1, has_side_effects=True, vmem_limit_bytes=VMEM_LIMIT
        ),
        cost_estimate=pl.CostEstimate(
            flops=2 * rows * width * 14 * width, bytes_accessed=rows * width * 24, transcendentals=0
        ),
        name="back_pass",
    )(
        length,
        qkv,
        qkv,
        qkv,
        qkv,
        qkv,
        qkv,
        qkv,
        p,
        d_mix,
        d_num,
        fa,
        tokens,
        d_attn,
        h1t,
        m1,
        m2,
        m3,
        m4,
        dt,
        c,
        vecs,
        w_qkv,
        gv,
        gbias,
        s_in,
        s_back,
        s_out,
    )


def hand_kernel(n, *refs):
    for j in range(n):
        refs[n + j][...] = refs[j][...]


def hand_over(arrays, parts):
    first = arrays[0]
    block = pl.BlockSpec((first.shape[0] // parts, first.shape[1]), lambda i: (i, 0))
    specs = [block] + [pl.BlockSpec(a.shape, lambda i: (0, 0)) for a in arrays[1:]]
    return pl.pallas_call(
        functools.partial(hand_kernel, len(arrays)),
        grid=(parts,),
        in_specs=specs,
        out_specs=specs,
        out_shape=[jax.ShapeDtypeStruct(a.shape, a.dtype) for a in arrays],
        name="hand_over",
    )(*arrays)


FRONT_TILE = 1024
TILE = 512
LAST_TILE = 1024
CHUNK = 256
FRONT_PLAN = {1: [(0, 0)], 2: [(1, 0)], 3: [(0, 1)], 5: [(0, 2), (1, 1)], 7: [(1, 2)], 8: [(0, 3), (1, 3)]}
BACK_PLAN = {2: [(0, 0)], 3: [(1, 0)], 4: [(0, 1)], 6: [(1, 1), (0, 2)], 7: [(1, 2)], 8: [(0, 3)], 12: [(1, 3)]}
LATE_PLAN = {1: [(2, 0), (3, 0)], 2: [(2, 1)], 3: [(3, 1), (2, 2)], "end": [(3, 2), (2, 3), (3, 3)]}


def shards(
    tokens, cotangent, w_qkv, w_out, w_in, w_back, vec_params, b_in, item_lengths, bucket_counts, *, ways
):
    n_dp, n_fsdp = ways
    (
        qkv,
        near,
        fa,
        fb,
        rn,
        p,
        h1t,
        m1,
        m2,
        c,
        qkv_w,
        vecs,
        in_bias,
        g_in,
        g_back,
        g_out,
    ) = front_pass(
        ways, item_lengths, tokens, w_qkv, w_in, w_back, w_out, vec_params, b_in[None], FRONT_TILE, FRONT_PLAN
    )

    def blocks(g):
        return g.reshape(n_dp, n_fsdp, *g.shape[-2:])

    def pairs(g):
        return g.reshape(n_dp // 2, 2, n_fsdp // 2, 2, *g.shape[-2:])

    (out, d_attn, d_mix, d_num, s_in, s_back, s_out, g_vec, g_bias, m3, m4, dt) = third_pass(
        ways,
        item_lengths,
        tokens,
        cotangent,
        near,
        fa,
        fb,
        rn,
        qkv,
        c,
        vecs,
        in_bias,
        blocks(g_out),
        blocks(g_in),
        blocks(g_back),
        TILE,
        CHUNK,
    )
    d_tok, r_qkv, r_in, r_back, r_out, r_vec, r_bias = back_pass(
        ways,
        item_lengths,
        qkv,
        p,
        d_mix,
        tokens,
        d_attn,
        d_num,
        fa,
        h1t,
        m1,
        m2,
        m3,
        m4,
        dt,
        c,
        vecs,
        qkv_w,
        g_vec,
        g_bias,
        pairs(s_in),
        pairs(s_back),
        pairs(s_out),
        TILE,
        LAST_TILE,
        BACK_PLAN,
        LATE_PLAN,
    )
    d_tok, r_qkv, r_out, r_in, r_back, r_vec, r_bias = hand_over(
        [d_tok, r_qkv, r_out, r_in, r_back, r_vec, r_bias], 2
    )
    return (out, d_tok, r_qkv, r_out, r_in, r_back, r_vec, r_bias[0])


def solution(mesh):
    in_specs = (
        P(("dp", "fsdp"), None),
        P(("dp", "fsdp"), None),
        P("fsdp", "dp"),
        P("fsdp", "dp"),
        P("fsdp", "dp"),
        P("fsdp", "dp"),
        P("dp", "fsdp"),
        P(("dp", "fsdp")),
        P(("dp", "fsdp"), None),
        P(("dp", "fsdp"), None),
    )
    out_specs = (
        P(("dp", "fsdp"), None),
        P(("dp", "fsdp"), None),
        P("fsdp", "dp"),
        P("fsdp", "dp"),
        P("fsdp", "dp"),
        P("fsdp", "dp"),
        P("dp", "fsdp"),
        P(("dp", "fsdp")),
    )
    ways = (mesh.shape["dp"], mesh.shape["fsdp"])
    body = functools.partial(shards, ways=ways)
    return jax.shard_map(body, mesh=mesh, in_specs=in_specs, out_specs=out_specs, check_vma=False)
```

```python
import functools
import math

import jax
import jax.numpy as jnp
import numpy as np
from jax import lax
from jax.experimental import pallas as pl
from jax.experimental.pallas import tpu as pltpu
from jax.sharding import PartitionSpec as P

HEADS = 8
BAND = 30
QB = 64
HALO = 32
KW = QB + 2 * HALO
GW = 256

norm_eps = 1e-05
f32 = jnp.float32
bf16 = jnp.bfloat16
exact = lax.Precision.HIGHEST
VMEM_LIMIT = 60 * 1024 * 1024


def nn(a, b):
    return lax.dot_general(a, b, (((1,), (0,)), ((), ())), preferred_element_type=f32)


def nt(a, b):
    return lax.dot_general(a, b, (((1,), (1,)), ((), ())), preferred_element_type=f32)


def tn(a, b):
    return lax.dot_general(a, b, (((0,), (0,)), ((), ())), preferred_element_type=f32)


def nt_exact(a, b):
    return lax.dot_general(
        a, b, (((1,), (1,)), ((), ())), preferred_element_type=f32, precision=exact
    )


def lift(t):
    return jnp.where(t > 0, t + 1, jnp.exp(jnp.minimum(t, 0)))


def moments(x):
    mean = jnp.mean(x, axis=-1, keepdims=True)
    cen = x - mean
    inv = lax.rsqrt(jnp.mean(cen * cen, axis=-1, keepdims=True) + norm_eps)
    return cen * inv, inv


def fold8(x):
    return jnp.sum(x.reshape(x.shape[0] // 8, 8, x.shape[1]), axis=0)


def fold4(x):
    n = x.shape[0] // 4
    return (x[:n] + x[n : 2 * n]) + (x[2 * n : 3 * n] + x[3 * n :])


def row_valid(step, rows, width, length):
    ids = step * rows + lax.broadcasted_iota(jnp.int32, (rows, width), 0)
    return ids < length


def same_head(head):
    r = lax.broadcasted_iota(jnp.int32, (GW, GW), 0) // head
    c = lax.broadcasted_iota(jnp.int32, (GW, GW), 1) // head
    return r == c


def spread_rows(x, mask_low):
    return jnp.concatenate([x] * (GW // QB), axis=0) * mask_low


def pick_heads(x, head):
    lane = lax.broadcasted_iota(jnp.int32, (QB, GW), 1) // head
    out = x[:QB]
    for h in range(1, GW // QB):
        out = jnp.where(lane == h, x[h * QB : (h + 1) * QB], out)
    return out


def turned(hidden, n_fsdp):
    return hidden // n_fsdp >= 128


def join_blocks(ref, got, lo=0, step=None):
    n_dp, n_fsdp, r, c = got.shape
    step = c if step is None else step
    for d in range(n_dp):
        for f in range(n_fsdp):
            ref[f * r : (f + 1) * r, d * step + lo : d * step + lo + c] = got[d, f]


def cut_blocks(ref, acc):
    n_dp, n_fsdp, r, c = ref.shape
    for d in range(n_dp):
        for f in range(n_fsdp):
            ref[d, f] = acc[f * r : (f + 1) * r, d * c : (d + 1) * c].astype(ref.dtype)


def cut_turned(ref, acc):
    n_dp, n_fsdp, r, c = ref.shape
    width, hidden = acc.shape
    wide, deep = width // n_dp, hidden // n_fsdp
    for d in range(n_dp):
        for f in range(n_fsdp):
            block = acc[d * wide : (d + 1) * wide, f * deep : (f + 1) * deep]
            ref[d, f] = (block if turned(hidden, n_fsdp) else block.T).astype(ref.dtype)


def band_table(head):
    key = np.arange(KW)[:, None] - HALO
    query = np.arange(GW)[None, :] % QB
    return np.where(np.abs(key - query) <= BAND, 0.0, -1e30).astype(np.float32)


def head_table(head):
    r = np.arange(GW)[:, None] // QB
    c = np.arange(GW)[None, :] // head
    return (r == c).astype(np.float32)


MESH = pl.DeviceIdType.MESH


class Place:
    def __init__(self, n_dp, n_fsdp):
        self.m = n_fsdp // 2
        self.nh = n_dp // 2
        d = lax.axis_index("dp")
        f = lax.axis_index("fsdp")
        self.dh, self.dl = d // 2, lax.rem(d, 2)
        self.fh, self.fl = f // 2, lax.rem(f, 2)

    def dev(self, dh=None, dl=None, fh=None, fl=None):
        dh = self.dh if dh is None else dh
        dl = self.dl if dl is None else dl
        fh = self.fh if fh is None else fh
        fl = self.fl if fl is None else fl
        return {"dp": dh * 2 + dl, "fsdp": fh * 2 + fl}

    def partners(self):
        out = [self.dev(fh=lax.rem(self.fh + o, self.m)) for o in range(1, self.m)]
        out += [self.dev(dh=lax.rem(self.dh + o, self.nh)) for o in range(1, self.nh)]
        return out + [self.dev(fl=1 - self.fl), self.dev(dl=1 - self.dl)]


def greet(place):
    barrier = pltpu.get_barrier_semaphore()
    who = place.partners()
    for dev in who:
        pl.semaphore_signal(barrier, inc=1, device_id=dev, device_id_type=MESH)
    pl.semaphore_wait(barrier, len(who))


def copy_to(src, dst, send, recv, dev):
    return pltpu.make_async_remote_copy(
        src_ref=src, dst_ref=dst, send_sem=send, recv_sem=recv, device_id=dev, device_id_type=MESH
    )


class Gather:
    def __init__(self, place, shard, got, send, recv, local, order, way=None):
        self.p, self.shard, self.got, self.order, self.way = place, shard, got, order, way
        self.send, self.recv, self.local = send, recv, local

    @staticmethod
    def count(n_dp, n_fsdp):
        return n_fsdp // 2 - 1 + 1 + n_dp // 2 - 1 + 1

    def own(self):
        p = self.p
        src = self.shard if self.way is None else self.way
        return pltpu.make_async_copy(src, self.got.at[p.dh, p.dl, p.fh, p.fl], self.local)

    def fetch(self):
        return pltpu.make_async_copy(self.shard, self.way, self.local)

    def stage(self, k):
        p, g = self.p, self.got
        if k == 0:
            out = []
            for o in range(1, p.m):
                to = p.dev(fh=lax.rem(p.fh + o, p.m))
                dst = g.at[p.dh, p.dl, p.fh, p.fl]
                out.append(copy_to(self.shard, dst, self.send.at[o - 1], self.recv.at[o - 1], to))
            return out
        i = p.m - 1
        if k == 3:
            ref = g.at[:, p.dl]
            return [copy_to(ref, ref, self.send.at[i], self.recv.at[i], p.dev(dl=1 - p.dl))]
        if (k == 1) == (self.order == "x"):
            ref = g.at[p.dh, p.dl, :, p.fl] if k == 1 else g.at[:, p.dl, :, p.fl]
            return [copy_to(ref, ref, self.send.at[i + 1], self.recv.at[i + 1], p.dev(fl=1 - p.fl))]
        ref = g.at[p.dh, p.dl, :, p.fl] if k == 1 else g.at[p.dh, p.dl]
        out = []
        for o in range(1, p.nh):
            to = p.dev(dh=lax.rem(p.dh + o, p.nh))
            out.append(copy_to(ref, ref, self.send.at[i + 1 + o], self.recv.at[i + 1 + o], to))
        return out

    def start(self, k):
        for c in self.stage(k):
            c.start()

    def wait(self, k):
        if k == 0:
            self.own().wait()
        for c in self.stage(k):
            c.wait()

    def turn(self, k):
        self.wait(k)
        self.start(k + 1)


def front_kernel(
    ways,
    plan,
    qkv_steps,
    len_ref,
    tok_ref,
    wqkv,
    win,
    wback,
    wout,
    vec_in,
    bias_in,
    band_ref,
    qkv_ref,
    near_ref,
    fa_ref,
    fb_ref,
    rn_ref,
    p_ref,
    h1t_ref,
    m1_ref,
    m2_ref,
    c_ref,
    w_ref,
    vec_ref,
    bin_ref,
    g_in,
    g_back,
    g_out,
    all_s,
    st_ref,
    t_ref,
    g_qkv,
    small,
    g_small,
    way_in,
    way_back,
    way_out,
    key_s,
    qq_s,
    send,
    recv,
    local,
):
    step = pl.program_id(0)
    steps = qkv_steps
    rows, width = tok_ref.shape
    groups = width // GW
    head = width // HEADS
    scale = head ** (-0.5)
    length = len_ref[0, 0]
    n_dp, n_fsdp = ways
    cols = vec_in.shape[1]
    place = Place(n_dp, n_fsdp)
    half_in = win.shape[1] // 2
    half_back = wback.shape[0] // 2

    def piece(j, shard, got, order, way=None):
        return Gather(place, shard, got, send.at[j], recv.at[j], local.at[j], order, way)

    first = [[piece(7, small, g_small, "x")], []]
    for i, (which, cut, order) in enumerate(qkv_parts(*wqkv.shape)):
        first[which].append(piece(8 + i, wqkv.at[cut], g_qkv.at[(slice(None),) * 4 + cut], order))
    rest = []
    for i in range(2):
        cut = pl.ds(i * half_in, half_in)
        rest.append(piece(i, win.at[:, cut], g_in.at[:, :, :, :, :, cut], "x", way_in.at[:, cut]))
    for i in range(2):
        cut = pl.ds(i * half_back, half_back)
        rest.append(piece(2 + i, wback.at[cut], g_back.at[:, :, :, :, cut], "y", way_back.at[cut]))
    rest.append(piece(4, wout, g_out, "y", way_out))
    sets = [[rest[0], rest[2]], [rest[1], rest[3], rest[4]]]

    @pl.when(step == 0)
    def _():
        small[...] = jnp.zeros_like(small)
        small[:2, :cols] = vec_in[...]
        small[2:3, :cols] = bias_in[...]
        for x in first[0] + first[1]:
            x.own().start()
        for x in rest:
            x.fetch().start()
        greet(place)
        for x in first[0] + first[1]:
            x.start(0)
        for x in rest:
            x.fetch().wait()
            x.own().start()
        st_ref[...] = jnp.zeros_like(st_ref)
        t_ref[...] = jnp.zeros_like(t_ref)
        all_s[:HALO] = jnp.zeros((HALO, 3 * width), bf16)
        all_s[HALO + steps * rows :] = jnp.zeros((HALO, 3 * width), bf16)
        qq_s[...] = jnp.zeros_like(qq_s)
        key = lax.broadcasted_iota(jnp.int32, key_s.shape, 0) - HALO
        key_s[...] = jnp.where((key >= 0) & (key < length), 0.0, -1e30)
        for k in range(3):
            for group in first:
                for x in group:
                    x.turn(k)
            if k == 0:
                for x in sets[0] + sets[1]:
                    x.start(0)
        for x in first[0] + first[1]:
            x.wait(3)
        join_pairs(w_ref, g_qkv)
        lane = lax.broadcasted_iota(jnp.int32, (128, width), 0)
        col = lax.broadcasted_iota(jnp.int32, (128, width), 1)

        def place_small(f, total):
            spot = ((lane + f * cols == col) & (lane < cols)).astype(bf16)
            block = jnp.concatenate(
                [g_small[d // 2, d % 2, f // 2, lax.rem(f, 2)] for d in range(n_dp)], axis=0
            )
            return total + nn(block, spot)

        total = lax.fori_loop(0, n_fsdp, place_small, jnp.zeros((16 * n_dp, width), f32))
        for d in range(n_dp):
            vec_ref[2 * d : 2 * d + 2] = total[16 * d : 16 * d + 2]
            bin_ref[0:1, d * width : (d + 1) * width] = total[16 * d + 2 : 16 * d + 3]

    def advance(at, moves):
        @pl.when(step == at)
        def _():
            for which, k in moves:
                for x in sets[which]:
                    if k < 3:
                        x.turn(k)
                    else:
                        x.wait(k)

    for at, moves in plan.items():
        if at < 2 * steps:
            advance(at, moves)

    @pl.when(step < steps)
    def _():
        z, _ = moments(tok_ref[...].astype(f32))
        h = (z * vec_ref[0:1] + vec_ref[1:2]).astype(bf16)
        h1t_ref[...] = h.T
        lo = pl.multiple_of(HALO + step * rows, HALO)
        q = nn(h, w_ref[:, :width]).astype(bf16)
        qkv_ref[:, :width] = q
        all_s[pl.ds(lo, rows), :width] = q
        valid = row_valid(step, rows, GW, length)
        for g in range(groups):
            kc = slice(width + g * GW, width + (g + 1) * GW)
            vc = slice(2 * width + g * GW, 2 * width + (g + 1) * GW)
            k = nn(h, w_ref[:, kc]).astype(bf16)
            v = nn(h, w_ref[:, vc]).astype(bf16)
            qkv_ref[:, kc] = k
            qkv_ref[:, vc] = v
            all_s[pl.ds(lo, rows), kc] = k
            all_s[pl.ds(lo, rows), vc] = v
            phi = jnp.where(valid, lift(k), 0)
            bent = jnp.where(valid, jnp.tanh(k), 0)
            st_ref[g] += tn(v, jnp.concatenate([phi, bent], axis=1))
            t_ref[g] += fold8(phi.astype(f32))

    @pl.when(step == steps - 1)
    def _():
        mask = same_head(head).astype(f32)
        inv_len = 1.0 / length.astype(f32)
        ones = jnp.ones((8, GW), f32)
        for g in range(groups):
            tb = jnp.sum(t_ref[g], axis=0, keepdims=True) * mask
            s1 = st_ref[g][:, :GW] * mask
            s2 = st_ref[g][:, GW:] * mask
            c_row = (nt_exact(ones, s1) / nt_exact(ones, tb)).astype(bf16).astype(f32)
            c_col = jnp.broadcast_to(c_row[0:1], (GW, GW)).T
            m1_ref[g, :GW] = (s1 - c_col * tb).astype(bf16)
            m1_ref[g, GW:] = tb.astype(bf16)
            m2_ref[g] = (s2 * inv_len).astype(bf16)
            c_ref[g] = c_row

    @pl.when(step >= steps)
    def _():
        at = (step - steps) * rows
        for b in range(rows // QB):
            here = pl.ds(pl.multiple_of(at + b * QB + HALO, HALO), QB)
            window = pl.ds(pl.multiple_of(at + b * QB, QB), KW)
            out_of_item = key_s[window]
            bias = band_ref[...] + jnp.concatenate([out_of_item] * (GW // 128), axis=1)
            for g in range(groups):
                cut = slice(g * GW, (g + 1) * GW)
                kc = slice(width + g * GW, width + (g + 1) * GW)
                vc = slice(2 * width + g * GW, 2 * width + (g + 1) * GW)
                put_heads(qq_s.at[g, b], all_s[here, cut] * scale, head)
                s = nt(all_s[window, kc], qq_s[g, b]) + bias
                e = jnp.exp(s - jnp.max(s, axis=0, keepdims=True))
                p = (e * (1.0 / jnp.sum(e, axis=0, keepdims=True))).astype(bf16)
                p_ref[b, :, cut] = p
                o = tn(p, all_s[window, vc])
                near_ref[b * QB : (b + 1) * QB, cut] = pick_heads(o, head).astype(bf16)
        for g in range(groups):
            cut = slice(g * GW, (g + 1) * GW)
            q = all_s[pl.ds(pl.multiple_of(at + HALO, HALO), rows), cut]
            both = nt(lift(q), m1_ref[g])
            rn = 1.0 / both[:, GW:]
            rn_ref[:, cut] = rn.astype(bf16)
            fa_ref[:, cut] = (both[:, :GW] * rn).astype(bf16)
            fb_ref[:, cut] = nt(jnp.tanh(q), m2_ref[g]).astype(bf16)

    advance(2 * steps - 1, plan[2 * steps])


def join_pairs(ref, got):
    nh, _, m, _, r, c = got.shape
    for d in range(2 * nh):
        for f in range(2 * m):
            ref[f * r : (f + 1) * r, d * c : (d + 1) * c] = got[d // 2, d % 2, f // 2, f % 2]


def qkv_parts(r, c):
    if c % 384:
        return [(0, (pl.ds(0, r), pl.ds(0, c)), "x")]
    third = c // 3
    whole = pl.ds(0, r)
    parts = [(0, (whole, pl.ds(0, third)), "x"), (0, (whole, pl.ds(third, third)), "y")]
    rest = pl.ds(2 * third, third)
    if r % 32:
        return parts + [(1, (whole, rest), "x")]
    half = r // 2
    return parts + [(1, (pl.ds(0, half), rest), "x"), (1, (pl.ds(half, half), rest), "y")]


def front_pass(ways, length, tokens, w_qkv, w_in, w_back, w_out, vec, bias, tile, plan):
    rows, width = tokens.shape
    groups = width // GW
    n_dp, n_fsdp = ways
    nh, m = n_dp // 2, n_fsdp // 2
    steps = rows // tile
    head = width // HEADS
    const = lambda *shape: pl.BlockSpec(shape, lambda i: (0,) * len(shape))
    early = lambda i: (jnp.minimum(i, steps - 1), 0)
    late = pl.BlockSpec((tile, width), lambda i: (jnp.maximum(i - steps, 0), 0))
    hbm = pl.BlockSpec(memory_space=pl.ANY)
    sds = jax.ShapeDtypeStruct
    got = lambda r, c: (nh, 2, m, 2, r, c)
    hidden = w_in.shape[1] * n_dp
    pieces = 8 + len(qkv_parts(*w_qkv.shape))
    per = Gather.count(n_dp, n_fsdp)
    return pl.pallas_call(
        functools.partial(front_kernel, ways, plan, steps),
        grid=(2 * steps,),
        in_specs=[
            pl.BlockSpec(memory_space=pltpu.SMEM),
            pl.BlockSpec((tile, width), early),
            hbm,
            hbm,
            hbm,
            hbm,
            const(*vec.shape),
            const(*bias.shape),
            const(KW, GW),
        ],
        out_specs=[
            pl.BlockSpec((tile, 3 * width), early),
            late,
            late,
            late,
            late,
            pl.BlockSpec((tile // QB, KW, width), lambda i: (jnp.maximum(i - steps, 0), 0, 0)),
            pl.BlockSpec((width, tile), lambda i: (0, jnp.minimum(i, steps - 1))),
            const(groups, 2 * GW, GW),
            const(groups, GW, GW),
            const(groups, 8, GW),
            const(width, 3 * width),
            const(8, width),
            const(1, hidden),
            hbm,
            hbm,
            hbm,
        ],
        out_shape=[sds((rows, 3 * width), bf16)]
        + [sds((rows, width), bf16)] * 4
        + [
            sds((rows // QB, KW, width), bf16),
            sds((width, rows), bf16),
            sds((groups, 2 * GW, GW), bf16),
            sds((groups, GW, GW), bf16),
            sds((groups, 8, GW), f32),
            sds((width, 3 * width), bf16),
            sds((8, width), f32),
            sds((1, hidden), f32),
            sds(got(*w_in.shape), bf16),
            sds(got(*w_back.shape), bf16),
            sds(got(*w_out.shape), bf16),
        ],
        scratch_shapes=[
            pltpu.VMEM((rows + 2 * HALO, 3 * width), bf16),
            pltpu.VMEM((groups, GW, 2 * GW), f32),
            pltpu.VMEM((groups, 8, GW), f32),
            pltpu.VMEM(got(*w_qkv.shape), bf16),
            pltpu.VMEM((16, 128), bf16),
            pltpu.VMEM(got(16, 128), bf16),
            pltpu.VMEM(w_in.shape, bf16),
            pltpu.VMEM(w_back.shape, bf16),
            pltpu.VMEM(w_out.shape, bf16),
            pltpu.VMEM((rows + 2 * HALO, 128), f32),
            pltpu.VMEM((groups, tile // QB, GW, GW), bf16),
            pltpu.SemaphoreType.DMA((pieces, per)),
            pltpu.SemaphoreType.DMA((pieces, per)),
            pltpu.SemaphoreType.DMA((pieces,)),
        ],
        compiler_params=pltpu.CompilerParams(
            collective_id=0, has_side_effects=True, vmem_limit_bytes=VMEM_LIMIT
        ),
        cost_estimate=pl.CostEstimate(
            flops=2 * rows * width * 8 * width, bytes_accessed=rows * width * 24, transcendentals=0
        ),
        name="front_pass",
    )(
        length,
        tokens,
        w_qkv,
        w_in,
        w_back,
        w_out,
        vec,
        bias,
        jnp.asarray(band_table(head)),
    )


def ffn_kernel(
    chunk,
    len_ref,
    tok_ref,
    cot_ref,
    near_ref,
    fa_ref,
    fb_ref,
    rn_ref,
    q_ref,
    c_ref,
    vec_ref,
    bin_ref,
    gw_out,
    gw_in,
    gw_back,
    out_ref,
    datt_ref,
    dmix_ref,
    dn_ref,
    gin_ref,
    gback_ref,
    gout_ref,
    gvec_ref,
    gbias_ref,
    m3_ref,
    m4_ref,
    dt_ref,
    a_in,
    a_back,
    a_out,
    a_st,
    a_bent,
    wout_ref,
    win_ref,
    wback_ref,
    act_s,
    pre_s,
):
    step = pl.program_id(0)
    rows, width = tok_ref.shape
    hidden = win_ref.shape[1]
    groups = width // GW
    head_size = width // HEADS
    steps = pl.num_programs(0)
    length = len_ref[0, 0]
    c_row = jnp.concatenate([c_ref[g, 0:1] for g in range(groups)], axis=1)
    blend = vec_ref[...].astype(bf16)
    s0 = math.sqrt(2.0 / math.pi)
    s1 = s0 * 0.044715

    @pl.when(step == 0)
    def _():
        join_blocks(wout_ref, gw_out)
        join_blocks(win_ref, gw_in)
        join_blocks(wback_ref, gw_back)
        for ref in (a_in, a_back, a_out, a_st, a_bent, gvec_ref, gbias_ref):
            ref[...] = jnp.zeros_like(ref)

    near = near_ref[...]
    fac = fa_ref[...]
    far_b = fb_ref[...]
    mixed = (
        vec_ref[5:6] * near.astype(f32)
        + vec_ref[6:7] * (fac.astype(f32) + c_row)
        + vec_ref[7:8] * far_b.astype(f32)
    ).astype(bf16)
    resid = tok_ref[...].astype(f32) + nn(mixed, wout_ref[...])
    z2, r2 = moments(resid)
    h2 = (z2 * vec_ref[2:3] + vec_ref[3:4]).astype(bf16)
    valid = row_valid(step, rows, width, length)
    d_ffn = jnp.where(valid, cot_ref[...], 0)
    seed = d_ffn.astype(f32)
    def add_grads(cols):
        a_back[:, cols] += tn(d_ffn, act_s[:, cols])
        a_in[:, cols] += tn(h2, pre_s[:, cols])

    for lo in range(0, hidden, chunk):
        cols = slice(lo, lo + chunk)
        x = nn(h2, win_ref[:, cols]) + bin_ref[0:1, cols]
        if lo:
            add_grads(slice(lo - chunk, lo))
        x2 = x * x
        half = 0.5 + 0.5 * jnp.tanh(x * (s0 + s1 * x2))
        act = x * half
        slope = half + (act - act * half) * (2 * s0 + 6 * s1 * x2)
        act = act.astype(bf16)
        act_s[:, cols] = act
        d_pre = slope * nt(d_ffn, wback_ref[cols, :])
        gbias_ref[:, cols] += fold8(d_pre)
        d_pre = d_pre.astype(bf16)
        pre_s[:, cols] = d_pre
    add_grads(slice(hidden - chunk, hidden))
    dh2 = nt(pre_s[...], win_ref[...])
    both = dh2 * z2
    gvec_ref[2] += fold8(both)
    gvec_ref[3] += fold8(dh2)
    gvec_ref[4] += fold8(seed)
    dz = dh2 * vec_ref[2:3]
    mean_z = jnp.mean(both * vec_ref[2:3], axis=-1, keepdims=True)
    d_resid = seed + r2 * (dz - jnp.mean(dz, axis=-1, keepdims=True) - z2 * mean_z)
    d_attn = d_resid.astype(bf16)
    datt_ref[...] = d_attn
    ffn = nn(act_s[...], wback_ref[...])
    out_ref[...] = jnp.where(valid, resid + ffn + vec_ref[4:5], 0.0).astype(bf16)
    a_out[...] += tn(mixed, d_attn)
    d_mix = nt(d_attn, wout_ref[...]).astype(bf16)
    dmix_ref[...] = d_mix
    gvec_ref[5] += fold8(fold4(d_mix * near).astype(f32))
    gvec_ref[6] += fold8(fold4(d_mix * fac).astype(f32))
    gvec_ref[7] += fold8(fold4(d_mix * far_b).astype(f32))
    gvec_ref[0] += fold8(fold4(d_mix).astype(f32))
    d_num = blend[6:7] * d_mix * rn_ref[...]
    dn_ref[...] = d_num
    d_den = d_num * fac
    d_far = blend[7:8] * d_mix
    for g in range(groups):
        cols = slice(g * GW, (g + 1) * GW)
        q = q_ref[:, cols]
        a_st[g] += tn(lift(q), jnp.concatenate([d_num[:, cols], d_den[:, cols]], axis=1))
        a_bent[g] += tn(jnp.tanh(q), d_far[:, cols])

    @pl.when(step == steps - 1)
    def _():
        mask = same_head(head_size).astype(f32)
        inv_len = 1.0 / length.astype(f32)
        ones = jnp.ones((8, GW), f32)
        for g in range(groups):
            m3_ref[g] = (a_st[g][:, :GW] * mask).astype(bf16)
            m4_ref[g] = (a_bent[g] * mask * inv_len).astype(bf16)
            dt_ref[g] = -nt_exact(ones, a_st[g][:, GW:] * mask)
        cut_blocks(gin_ref, a_in)
        cut_turned(gback_ref, a_back)
        cut_blocks(gout_ref, a_out)
        gvec_ref[6] += gvec_ref[0] * c_row


def third_pass(
    ways, length, tokens, cot, near, fa, fb, rn, qkv, c, vecs, b_in, w_out, w_in, w_back, tile, chunk
):
    rows, width = tokens.shape
    hidden = w_in.shape[0] * w_in.shape[3]
    groups = width // GW
    steps = rows // tile
    n_dp, n_fsdp = ways
    back = (width // n_dp, hidden // n_fsdp)
    back = back if turned(hidden, n_fsdp) else back[::-1]

    def const(*shape):
        return pl.BlockSpec(shape, lambda i: (0,) * len(shape))

    def kept(*shape):
        return pl.BlockSpec(shape, lambda i: (0,) * len(shape), pipeline_mode=pl.Buffered(1))

    sds = jax.ShapeDtypeStruct
    block = pl.BlockSpec((tile, width), lambda i: (i, 0))
    deep = pltpu.VMEM((tile, hidden), bf16)
    return pl.pallas_call(
        functools.partial(ffn_kernel, chunk),
        grid=(steps,),
        in_specs=[pl.BlockSpec(memory_space=pltpu.SMEM)]
        + [block] * 7
        + [
            const(groups, 8, GW),
            const(8, width),
            const(1, hidden),
            kept(*w_out.shape),
            kept(*w_in.shape),
            kept(*w_back.shape),
        ],
        out_specs=[block] * 4
        + [
            const(n_dp, n_fsdp, width // n_fsdp, hidden // n_dp),
            const(n_dp, n_fsdp, *back),
            const(n_dp, n_fsdp, width // n_fsdp, width // n_dp),
            const(8, 8, width),
            const(8, hidden),
            const(groups, GW, GW),
            const(groups, GW, GW),
            const(groups, 8, GW),
        ],
        out_shape=[sds((rows, width), bf16)] * 4
        + [
            sds((n_dp, n_fsdp, width // n_fsdp, hidden // n_dp), bf16),
            sds((n_dp, n_fsdp, *back), bf16),
            sds((n_dp, n_fsdp, width // n_fsdp, width // n_dp), bf16),
            sds((8, 8, width), f32),
            sds((8, hidden), f32),
            sds((groups, GW, GW), bf16),
            sds((groups, GW, GW), bf16),
            sds((groups, 8, GW), f32),
        ],
        scratch_shapes=[
            pltpu.VMEM((width, hidden), f32),
            pltpu.VMEM((width, hidden), f32),
            pltpu.VMEM((width, width), f32),
            pltpu.VMEM((groups, GW, 2 * GW), f32),
            pltpu.VMEM((groups, GW, GW), f32),
            pltpu.VMEM((width, width), bf16),
            pltpu.VMEM((width, hidden), bf16),
            pltpu.VMEM((hidden, width), bf16),
            deep,
            deep,
        ],
        compiler_params=pltpu.CompilerParams(vmem_limit_bytes=VMEM_LIMIT),
        cost_estimate=pl.CostEstimate(
            flops=2 * rows * width * (6 * hidden + 4 * width),
            bytes_accessed=rows * width * 22,
            transcendentals=0,
        ),
        name="third_pass",
    )(length, tokens, cot, near, fa, fb, rn, qkv, c, vecs, b_in, w_out, w_in, w_back)


class Scatter:
    def __init__(self, place, src, out, bufs, send, recv, local, order):
        self.p, self.src, self.out, self.order = place, src, out, order
        self.acc, self.r0, self.r1, self.r2, self.r3 = bufs
        self.send, self.recv, self.local = send, recv, local

    @staticmethod
    def count(n_dp, n_fsdp):
        return n_dp // 2 + 1 + (n_dp // 2 - 1) + (n_fsdp // 2 - 1)

    @staticmethod
    def scratch(n_dp, n_fsdp, r, c, order, dtype):
        nh, m = n_dp // 2, n_fsdp // 2
        if order == "x":
            one, two = (nh, m, r, c), (nh - 1, m, r, c)
        else:
            one, two = (nh - 1, m, 2, r, c), (m, r, c)
        shapes = [(nh, m, 2, r, c), (nh, m, 2, r, c), one, two, (m - 1, r, c)]
        return [pltpu.VMEM(s, dtype) for s in shapes]

    def own(self):
        return pltpu.make_async_copy(self.src.at[:, self.p.dl], self.acc, self.local)

    def stage(self, k, only=None):
        p = self.p
        if k == 0:
            to = p.dev(dl=1 - p.dl)
            return [
                copy_to(self.src.at[dh, 1 - p.dl], self.r0.at[dh], self.send.at[dh], self.recv.at[dh], to)
                for dh in (range(p.nh) if only is None else [only])
            ]
        first = p.nh - 1
        if k == 3:
            i = first + p.nh
            out = []
            for o in range(1, p.m):
                fh = lax.rem(p.fh + o, p.m)
                out.append(
                    copy_to(self.acc.at[p.dh, fh, p.fl], self.r3.at[o - 1], self.send.at[i + o], self.recv.at[i + o],
                            p.dev(fh=fh))
                )
            return out
        if (k == 1) == (self.order == "x"):
            ref = self.acc.at[:, :, 1 - p.fl] if k == 1 else self.acc.at[p.dh, :, 1 - p.fl]
            dst = self.r1 if k == 1 else self.r2
            i = first + 1
            return [copy_to(ref, dst, self.send.at[i], self.recv.at[i], p.dev(fl=1 - p.fl))]
        out = []
        for o in range(1, p.nh):
            dh = lax.rem(p.dh + o, p.nh)
            ref = self.acc.at[dh] if k == 1 else self.acc.at[dh, :, p.fl]
            dst = self.r1.at[o - 1] if k == 1 else self.r2.at[o - 1]
            i = first + 1 + o
            out.append(copy_to(ref, dst, self.send.at[i], self.recv.at[i], p.dev(dh=dh)))
        return out

    def start(self, k):
        for c in self.stage(k):
            c.start()

    def turn(self, k):
        if k == 0:
            self.own().wait()
        for c in self.stage(k):
            c.wait()
        self.add(k)
        if k < 3:
            self.start(k + 1)

    def add(self, k):
        p, acc = self.p, self.acc
        nh, m = p.nh, p.m
        dt = acc.dtype

        def put(index, others):
            if len(others) == 1:
                acc[index] += others[0]
                return
            total = acc[index].astype(f32)
            for o in others:
                total = total + o.astype(f32)
            acc[index] = total.astype(dt)

        if k == 3:
            total = acc[p.dh, p.fh, p.fl].astype(f32)
            for o in range(1, m):
                total = total + self.r3[o - 1].astype(f32)
            self.out[...] = total
            return

        @pl.loop(0, m)
        def _(i):
            if k == 0:
                for a in range(nh):
                    for b in range(2):
                        put((a, i, b), [self.r0[a, i, b]])
            elif k == 1 and self.order == "x":
                for a in range(nh):
                    put((a, i, p.fl), [self.r1[a, i]])
            elif k == 1:
                for b in range(2):
                    put((p.dh, i, b), [self.r1[o - 1, i, b] for o in range(1, nh)])
            elif self.order == "x":
                put((p.dh, i, p.fl), [self.r2[o - 1, i] for o in range(1, nh)])
            else:
                put((p.dh, i, p.fl), [self.r2[i]])


def back_kernel(
    ways,
    plan,
    late_plan,
    len_ref,
    q_ref,
    k_lo,
    k_ref,
    k_hi,
    v_lo,
    v_ref,
    v_hi,
    p_ref,
    dmix_ref,
    dn_ref,
    fa_ref,
    tok_ref,
    datt_ref,
    h1t_hbm,
    m1_ref,
    m2_ref,
    m3_ref,
    m4_ref,
    dt_ref,
    c_ref,
    vec_ref,
    w_hbm,
    gv_ref,
    gbias_ref,
    s_in,
    s_back,
    s_out,
    dtok_ref,
    oqkv_ref,
    oin_ref,
    oback_ref,
    oout_ref,
    ovec_ref,
    obias_ref,
    h1t_ref,
    w_ref,
    kk,
    vv,
    far_s,
    dp_s,
    ds_s,
    dd_s,
    qq_s,
    all_d,
    carry,
    gvec_s,
    gq_ref,
    gs_ref,
    rows_s,
    back_t,
    small_o,
    late_src,
    late_got,
    *rest,
):
    step = pl.program_id(0)
    rows, width = q_ref.shape
    total = h1t_ref.shape[1]
    steps = total // rows
    groups = width // GW
    head = width // HEADS
    scale = head ** (-0.5)
    length = len_ref[0, 0]
    n_dp, n_fsdp = ways
    place = Place(n_dp, n_fsdp)
    cols = ovec_ref.shape[1]
    c_all = oqkv_ref.shape[1]
    send, recv, local, late_send, late_recv, fetch = rest[-6:]
    fetches = [
        pltpu.make_async_copy(h1t_hbm, h1t_ref, fetch.at[0]),
        pltpu.make_async_copy(w_hbm, w_ref, fetch.at[1]),
    ]
    final = steps + 1 + place.nh
    last_rows = tok_ref.shape[0]

    used = [0]

    def piece(src, out, order):
        j = used[0]
        used[0] += 1
        return Scatter(place, src, out, rest[5 * j : 5 * j + 5], send.at[j], recv.at[j], local.at[j], order)

    sets = [[], [], [], []]
    every = (slice(None),) * 4
    for i, (cut_in, cut_back) in enumerate(ffn_parts(s_in.shape[-2:], s_back.shape[-2:])):
        sets[i].append(piece(s_in.at[every + cut_in], oin_ref.at[cut_in], "x"))
        sets[i].append(piece(s_back.at[every + cut_back], back_t.at[cut_back], "y"))
    sets[1].append(piece(s_out, oout_ref, "y"))
    sets[1].append(piece(gs_ref, small_o, "x"))
    for which, cut, order in qkv_parts(*oqkv_ref.shape):
        sets[2 + which].append(piece(gq_ref.at[every + cut], oqkv_ref.at[cut], order))

    @pl.when(step == 0)
    def _():
        for x in sets[0] + sets[1][:-1]:
            x.own().start()
        greet_all(place)
        for x in sets[0] + sets[1][:-1]:
            x.start(0)
        for x in fetches:
            x.start()
        carry[...] = jnp.zeros_like(carry)
        dd_s[...] = jnp.zeros_like(dd_s)
        qq_s[...] = jnp.zeros_like(qq_s)
        gvec_s[...] = jnp.zeros_like(gvec_s)
        gs_ref[...] = jnp.zeros_like(gs_ref)
        late_src[...] = jnp.zeros_like(late_src)
        rows_s[0:2] = jnp.zeros((2, width), f32)
        rows_s[2:8] = jnp.sum(gv_ref[2:8], axis=1)
        bias = jnp.sum(gbias_ref[...], axis=0, keepdims=True)
        for d in range(n_dp):
            pair = rows_s[2 * d : 2 * d + 2]
            for f in range(n_fsdp):
                spot = slice(f * cols, (f + 1) * cols)
                at = d * width + f * cols
                gs_ref[d // 2, d % 2, f // 2, f % 2, 0:2, :cols] = pair[:, spot]
                gs_ref[d // 2, d % 2, f // 2, f % 2, 2:3, :cols] = bias[:, at : at + cols]
        sets[1][-1].own().start()
        sets[1][-1].start(0)

    for at, moves in plan.items():

        @pl.when(step == at)
        def _(moves=moves):
            for which, k in moves:
                for x in sets[which]:
                    x.turn(k)

    def far_keys(at, slot, live):
        valid = row_valid(at, rows, GW, length) & live
        here = pl.ds(pl.multiple_of(at * rows + HALO, HALO), rows)
        for g in range(groups):
            cut = slice(g * GW, (g + 1) * GW)
            kc = slice(width + g * GW, width + (g + 1) * GW)
            vc = slice(2 * width + g * GW, 2 * width + (g + 1) * GW)
            k = kk[slot, HALO : HALO + rows, cut]
            v = vv[slot, HALO : HALO + rows, cut]
            lift_k = lift(k)
            bent_k = jnp.tanh(k)
            v_cen = v - c_ref[g, 0:1].astype(bf16)
            dk = (nt(v_cen, m3_ref[g]) + dt_ref[g, 0:1]) * jnp.minimum(lift_k, 1).astype(f32)
            dk += nt(v, m4_ref[g]) * (1 - bent_k * bent_k).astype(f32)
            both = jnp.concatenate([lift_k, bent_k], axis=1)
            dv = nn(both, jnp.concatenate([m3_ref[g], m4_ref[g]], axis=0))
            all_d[here, kc] += jnp.where(valid, dk.astype(bf16), 0)
            all_d[here, vc] += jnp.where(valid, dv.astype(bf16), 0)

    @pl.when(step < steps)
    def _():
        slot = lax.rem(step, 2)
        kk[slot, :HALO] = k_lo[...]
        kk[slot, HALO : HALO + rows] = k_ref[...]
        kk[slot, HALO + rows :] = k_hi[...]
        vv[slot, :HALO] = v_lo[...]
        vv[slot, HALO : HALO + rows] = v_ref[...]
        vv[slot, HALO + rows :] = v_hi[...]
        blend = vec_ref[...].astype(bf16)
        base = step * rows
        for g in range(groups):
            cut = slice(g * GW, (g + 1) * GW)
            kc = slice(width + g * GW, width + (g + 1) * GW)
            vc = slice(2 * width + g * GW, 2 * width + (g + 1) * GW)
            q = q_ref[:, cut]
            d_num = dn_ref[:, cut]
            d_den = -d_num * fa_ref[:, cut]
            d_mix = dmix_ref[:, cut]
            bent = jnp.tanh(q)
            far = nn(jnp.concatenate([d_num, d_den], axis=1), m1_ref[g]) * jnp.minimum(lift(q), 1).astype(f32)
            far_s[:, cut] = far + nn(blend[7:8, cut] * d_mix, m2_ref[g]) * (1 - bent * bent).astype(f32)
            for b in range(rows // QB):
                here = slice(b * QB, (b + 1) * QB)
                window = slice(b * QB, b * QB + KW)
                put_heads(dd_s.at[g, b], blend[5:6, cut] * dmix_ref[here, cut], head)
                dp_s[g, b] = nt(vv[slot, window, cut], dd_s[g, b]).astype(bf16)
            for b in range(rows // QB):
                p = p_ref[b, :, cut]
                dp = dp_s[g, b]
                dot = jnp.sum(fold4(p * dp).astype(f32), axis=0, keepdims=True)
                ds_s[g, b] = p * (dp - dot.astype(bf16))
            old_k = carry[0, :, cut]
            old_v = carry[1, :, cut]
            for b in range(rows // QB):
                here = slice(b * QB, (b + 1) * QB)
                window = slice(b * QB, b * QB + KW)
                d_s = ds_s[g, b]
                put_heads(qq_s.at[g, b], q_ref[here, cut] * scale, head)
                dk = nn(d_s, qq_s[g, b])
                dv = nn(p_ref[b, :, cut], dd_s[g, b])
                dq = pick_heads(tn(d_s, kk[slot, window, cut]), head) * scale + far_s[here, cut]
                lo = pl.ds(pl.multiple_of(base + b * QB, QB), QB)
                all_d[pl.ds(pl.multiple_of(base + b * QB + HALO, HALO), QB), cut] = dq.astype(bf16)
                all_d[lo, kc] = (old_k + dk[:QB]).astype(bf16)
                all_d[lo, vc] = (old_v + dv[:QB]).astype(bf16)
                old_k = dk[QB:]
                old_v = dv[QB:]
            carry[0, :, cut] = old_k
            carry[1, :, cut] = old_v
        far_keys(jnp.maximum(step - 1, 0), 1 - slot, step > 0)

    @pl.when(step == steps)
    def _():
        all_d[total:, width : 2 * width] = carry[0].astype(bf16)
        all_d[total:, 2 * width :] = carry[1].astype(bf16)
        far_keys(steps - 1, (steps - 1) % 2, True)

    for dh in range(n_dp // 2):

        @pl.when(step == steps + 1 + dh)
        def _(dh=dh):
            if dh == 0:
                fetches[0].wait()
            grad = nn(h1t_ref[...], all_d[HALO : HALO + total, dh * 2 * c_all : (dh + 1) * 2 * c_all])
            r = gq_ref.shape[-2]
            for dl in range(2):
                for f in range(n_fsdp):
                    block = grad[f * r : (f + 1) * r, dl * c_all : (dl + 1) * c_all]
                    gq_ref[dh, dl, f // 2, f % 2] = block.astype(bf16)
            for x in sets[2] + sets[3]:
                x.stage(0, dh)[0].start()

    @pl.when(step == final)
    def _():
        fetches[1].wait()
        for x in sets[2] + sets[3]:
            x.own().start()

    for at, moves in late_plan.items():
        if at == "end":
            continue

        @pl.when(step == final + at)
        def _(moves=moves):
            for which, k in moves:
                for x in sets[which]:
                    x.turn(k)

    @pl.when(step >= final)
    def _():
        here = pl.ds(pl.multiple_of((step - final) * last_rows + HALO, HALO), last_rows)
        z1, r1 = moments(tok_ref[...].astype(f32))
        dh1 = nt(all_d[here], w_ref[...])
        gvec_s[0] += fold8(dh1 * z1)
        gvec_s[1] += fold8(dh1)
        dz = dh1 * vec_ref[0:1]
        dtok_ref[...] = (
            datt_ref[...].astype(f32)
            + r1
            * (
                dz
                - jnp.mean(dz, axis=-1, keepdims=True)
                - z1 * jnp.mean(dz * z1, axis=-1, keepdims=True)
            )
        ).astype(bf16)

    @pl.when(step == final + total // last_rows - 1)
    def _():
        rows_s[0:2] = jnp.sum(gvec_s[...], axis=1)
        for f in range(n_fsdp):
            late_src[f, 0:2, :cols] = rows_s[0:2, f * cols : (f + 1) * cols]
        d, f = lax.axis_index("dp"), lax.axis_index("fsdp")
        me = d * n_fsdp + f

        def late(o):
            to = lax.rem(f + o, n_fsdp)
            return copy_to(
                late_src.at[to], late_got.at[me], late_send.at[o], late_recv.at[me], {"dp": 0, "fsdp": to}
            )

        @pl.when(d > 0)
        def _():
            late(0).start()

        for o in range(1, n_fsdp):
            late(o).start()
        oback_ref[...] = back_t[...].T if turned(gbias_ref.shape[1], n_fsdp) else back_t[...]
        for which, k in late_plan["end"]:
            for x in sets[which]:
                x.turn(k)

        @pl.when(d > 0)
        def _():
            late(0).wait_send()
            ovec_ref[...] = small_o[0:2, :cols]

        for o in range(1, n_fsdp):
            late(o).wait_send()

        @pl.when(d == 0)
        def _():
            late_got[me] = late_src[f]

            @pl.loop(0, n_dp * n_fsdp)
            def _(s):
                @pl.when(s != me)
                def _():
                    copy_to(
                        late_src.at[0], late_got.at[s], late_send.at[0], late_recv.at[s], {"dp": 0, "fsdp": 0}
                    ).wait_recv()

            ovec_ref[...] = jnp.sum(late_got[...], axis=0)[0:2, :cols]

        obias_ref[...] = small_o[2:3, :cols]


def put_heads(ref, x, head):
    for h in range(GW // head):
        lanes = slice(h * head, (h + 1) * head)
        ref[h * QB : (h + 1) * QB, lanes] = x[:, lanes]


def ffn_parts(shape_in, shape_back):
    (r, c), (rb, cb) = shape_in, shape_back
    out = []
    for i in range(2):
        cut_in = (pl.ds(0, r), pl.ds(i * c // 2, c // 2))
        if cb % 256:
            cut_back = (pl.ds(i * rb // 2, rb // 2), pl.ds(0, cb))
        else:
            cut_back = (pl.ds(0, rb), pl.ds(i * cb // 2, cb // 2))
        out.append((cut_in, cut_back))
    return out


def greet_all(place):
    d, f = lax.axis_index("dp"), lax.axis_index("fsdp")
    n_dp, n_fsdp = 2 * place.nh, 2 * place.m
    barrier = pltpu.get_barrier_semaphore()
    who = place.partners()
    for dev in who:
        pl.semaphore_signal(barrier, inc=1, device_id=dev, device_id_type=MESH)

    @pl.when(d == 0)
    def _():
        @pl.loop(0, n_dp)
        def _(i):
            @pl.loop(0, n_fsdp)
            def _(j):
                @pl.when((i != 0) | (j != f))
                def _():
                    pl.semaphore_signal(barrier, inc=1, device_id={"dp": i, "fsdp": j}, device_id_type=MESH)

    pl.semaphore_wait(barrier, len(who) + n_fsdp - (d == 0).astype(jnp.int32))


def back_pass(
    ways,
    length,
    qkv,
    p,
    d_mix,
    tokens,
    d_attn,
    d_num,
    fa,
    h1t,
    m1,
    m2,
    m3,
    m4,
    dt,
    c,
    vecs,
    w_qkv,
    gv,
    gbias,
    s_in,
    s_back,
    s_out,
    tile,
    last_tile,
    plan,
    late_plan,
):
    rows, width = tokens.shape
    groups = width // GW
    steps = rows // tile
    n_dp, n_fsdp = ways
    nh, m = n_dp // 2, n_fsdp // 2
    r, c_all = width // n_fsdp, 3 * width // n_dp
    per = Scatter.count(n_dp, n_fsdp)
    final = steps + 1 + nh
    hbm = pl.BlockSpec(memory_space=pl.ANY)
    back_shape = s_back.shape[-2:]
    outs = [
        (r, c_all),
        s_in.shape[-2:],
        back_shape[::-1] if turned(gbias.shape[1], n_fsdp) else back_shape,
        s_out.shape[-2:],
        (2, width // n_fsdp),
        (1, gbias.shape[1] // (n_dp * n_fsdp)),
    ]
    kinds = []
    for cut_in, cut_back in ffn_parts(s_in.shape[-2:], back_shape):
        kinds.append((*(x.size for x in cut_in), "x", bf16))
        kinds.append((*(x.size for x in cut_back), "y", bf16))
    kinds.append((*s_out.shape[-2:], "y", bf16))
    kinds.append((8, 128, "x", f32))
    for _, cut, order in qkv_parts(r, c_all):
        kinds.append((*(x.size for x in cut), order, bf16))
    bufs = [b for k in kinds for b in Scatter.scratch(n_dp, n_fsdp, *k)]
    got = lambda *s: (nh, 2, m, 2, *s)

    def const(*shape):
        return pl.BlockSpec(shape, lambda i: (0,) * len(shape))

    def kept(*shape):
        return pl.BlockSpec(shape, lambda i: (0,) * len(shape), pipeline_mode=pl.Buffered(1))

    one = lambda i: jnp.minimum(i, steps - 1)
    end = lambda i: jnp.maximum(i - final, 0)
    per_tile = tile // HALO
    top = rows // HALO - 1

    def halo(col):
        return [
            pl.BlockSpec((HALO, width), lambda i: (jnp.maximum(one(i) * per_tile - 1, 0), col)),
            pl.BlockSpec((tile, width), lambda i: (one(i), col)),
            pl.BlockSpec((HALO, width), lambda i: (jnp.minimum((one(i) + 1) * per_tile, top), col)),
        ]

    block = pl.BlockSpec((tile, width), lambda i: (one(i), 0))
    late = pl.BlockSpec((last_tile, width), lambda i: (end(i), 0))
    head = width // HEADS
    sds = jax.ShapeDtypeStruct
    return pl.pallas_call(
        functools.partial(back_kernel, ways, plan, late_plan),
        grid=(final + rows // last_tile,),
        in_specs=[
            pl.BlockSpec(memory_space=pltpu.SMEM),
            block,
            *halo(1),
            *halo(2),
            pl.BlockSpec((tile // QB, KW, width), lambda i: (one(i), 0, 0)),
            block,
            block,
            block,
            late,
            late,
            hbm,
            kept(groups, 2 * GW, GW),
            kept(groups, GW, GW),
            kept(groups, GW, GW),
            kept(groups, GW, GW),
            const(groups, 8, GW),
            const(groups, 8, GW),
            const(8, width),
            hbm,
            const(*gv.shape),
            const(*gbias.shape),
            hbm,
            hbm,
            hbm,
        ],
        out_specs=[late] + [const(*s) for s in outs],
        out_shape=[sds((rows, width), bf16)] + [sds(s, f32) for s in outs],
        scratch_shapes=[
            pltpu.VMEM((width, rows), bf16),
            pltpu.VMEM((width, 3 * width), bf16),
            pltpu.VMEM((2, tile + 2 * HALO, width), bf16),
            pltpu.VMEM((2, tile + 2 * HALO, width), bf16),
            pltpu.VMEM((tile, width), f32),
            pltpu.VMEM((groups, tile // QB, KW, GW), bf16),
            pltpu.VMEM((groups, tile // QB, KW, GW), bf16),
            pltpu.VMEM((groups, tile // QB, GW, GW), bf16),
            pltpu.VMEM((groups, tile // QB, GW, GW), bf16),
            pltpu.VMEM((rows + 2 * HALO, 3 * width), bf16),
            pltpu.VMEM((2, QB, width), f32),
            pltpu.VMEM((2, 8, width), f32),
            pltpu.VMEM(got(r, c_all), bf16),
            pltpu.VMEM(got(8, 128), f32),
            pltpu.VMEM((8, width), f32),
            pltpu.VMEM(back_shape, f32),
            pltpu.VMEM((8, 128), f32),
            pltpu.VMEM((n_fsdp, 8, 128), f32),
            pltpu.VMEM((n_dp * n_fsdp, 8, 128), f32),
            *bufs,
            pltpu.SemaphoreType.DMA((len(kinds), per)),
            pltpu.SemaphoreType.DMA((len(kinds), per)),
            pltpu.SemaphoreType.DMA((len(kinds),)),
            pltpu.SemaphoreType.DMA((n_fsdp,)),
            pltpu.SemaphoreType.DMA((n_dp * n_fsdp,)),
            pltpu.SemaphoreType.DMA((2,)),
        ],
        compiler_params=pltpu.CompilerParams(
            collective_id=1, has_side_effects=True, vmem_limit_bytes=VMEM_LIMIT
        ),
        cost_estimate=pl.CostEstimate(
            flops=2 * rows * width * 14 * width, bytes_accessed=rows * width * 24, transcendentals=0
        ),
        name="back_pass",
    )(
        length,
        qkv,
        qkv,
        qkv,
        qkv,
        qkv,
        qkv,
        qkv,
        p,
        d_mix,
        d_num,
        fa,
        tokens,
        d_attn,
        h1t,
        m1,
        m2,
        m3,
        m4,
        dt,
        c,
        vecs,
        w_qkv,
        gv,
        gbias,
        s_in,
        s_back,
        s_out,
    )


def hand_kernel(n, *refs):
    for j in range(n):
        refs[n + j][...] = refs[j][...]


def hand_over(arrays, parts):
    first = arrays[0]
    block = pl.BlockSpec((first.shape[0] // parts, first.shape[1]), lambda i: (i, 0))
    specs = [block] + [pl.BlockSpec(a.shape, lambda i: (0, 0)) for a in arrays[1:]]
    return pl.pallas_call(
        functools.partial(hand_kernel, len(arrays)),
        grid=(parts,),
        in_specs=specs,
        out_specs=specs,
        out_shape=[jax.ShapeDtypeStruct(a.shape, a.dtype) for a in arrays],
        name="hand_over",
    )(*arrays)


FRONT_TILE = 1024
TILE = 512
LAST_TILE = 512
CHUNK = 256
FRONT_PLAN = {1: [(0, 0)], 2: [(1, 0)], 3: [(0, 1)], 4: [(1, 1)], 5: [(0, 2)], 7: [(1, 2)], 8: [(0, 3), (1, 3)]}
BACK_PLAN = {2: [(0, 0)], 3: [(1, 0)], 4: [(0, 1)], 6: [(1, 1), (0, 2)], 7: [(1, 2)], 8: [(0, 3)], 14: [(1, 3)]}
LATE_PLAN = {1: [(2, 0), (3, 0)], 3: [(2, 1)], 4: [(3, 1)], 5: [(2, 2)], 6: [(3, 2)], "end": [(2, 3), (3, 3)]}


def shards(
    tokens, cotangent, w_qkv, w_out, w_in, w_back, vec_params, b_in, item_lengths, bucket_counts, *, ways
):
    n_dp, n_fsdp = ways
    (
        qkv,
        near,
        fa,
        fb,
        rn,
        p,
        h1t,
        m1,
        m2,
        c,
        qkv_w,
        vecs,
        in_bias,
        g_in,
        g_back,
        g_out,
    ) = front_pass(
        ways, item_lengths, tokens, w_qkv, w_in, w_back, w_out, vec_params, b_in[None], FRONT_TILE, FRONT_PLAN
    )

    def blocks(g):
        return g.reshape(n_dp, n_fsdp, *g.shape[-2:])

    def pairs(g):
        return g.reshape(n_dp // 2, 2, n_fsdp // 2, 2, *g.shape[-2:])

    (out, d_attn, d_mix, d_num, s_in, s_back, s_out, g_vec, g_bias, m3, m4, dt) = third_pass(
        ways,
        item_lengths,
        tokens,
        cotangent,
        near,
        fa,
        fb,
        rn,
        qkv,
        c,
        vecs,
        in_bias,
        blocks(g_out),
        blocks(g_in),
        blocks(g_back),
        TILE,
        CHUNK,
    )
    d_tok, r_qkv, r_in, r_back, r_out, r_vec, r_bias = back_pass(
        ways,
        item_lengths,
        qkv,
        p,
        d_mix,
        tokens,
        d_attn,
        d_num,
        fa,
        h1t,
        m1,
        m2,
        m3,
        m4,
        dt,
        c,
        vecs,
        qkv_w,
        g_vec,
        g_bias,
        pairs(s_in),
        pairs(s_back),
        pairs(s_out),
        TILE,
        LAST_TILE,
        BACK_PLAN,
        LATE_PLAN,
    )
    d_tok, r_qkv, r_out, r_in, r_back, r_vec, r_bias = hand_over(
        [d_tok, r_qkv, r_out, r_in, r_back, r_vec, r_bias], 2
    )
    return (out, d_tok, r_qkv, r_out, r_in, r_back, r_vec, r_bias[0])


def solution(mesh):
    in_specs = (
        P(("dp", "fsdp"), None),
        P(("dp", "fsdp"), None),
        P("fsdp", "dp"),
        P("fsdp", "dp"),
        P("fsdp", "dp"),
        P("fsdp", "dp"),
        P("dp", "fsdp"),
        P(("dp", "fsdp")),
        P(("dp", "fsdp"), None),
        P(("dp", "fsdp"), None),
    )
    out_specs = (
        P(("dp", "fsdp"), None),
        P(("dp", "fsdp"), None),
        P("fsdp", "dp"),
        P("fsdp", "dp"),
        P("fsdp", "dp"),
        P("fsdp", "dp"),
        P("dp", "fsdp"),
        P(("dp", "fsdp")),
    )
    ways = (mesh.shape["dp"], mesh.shape["fsdp"])
    body = functools.partial(shards, ways=ways)
    return jax.shard_map(body, mesh=mesh, in_specs=in_specs, out_specs=out_specs, check_vma=False)
```

```python
import functools
import math

import jax
import jax.numpy as jnp
import numpy as np
from jax import lax
from jax.experimental import pallas as pl
from jax.experimental.pallas import tpu as pltpu
from jax.sharding import PartitionSpec as P

HEADS = 8
BAND = 30
QB = 64
HALO = 32
KW = QB + 2 * HALO
GW = 256

norm_eps = 1e-05
f32 = jnp.float32
bf16 = jnp.bfloat16
exact = lax.Precision.HIGHEST
VMEM_LIMIT = 60 * 1024 * 1024


def nn(a, b):
    return lax.dot_general(a, b, (((1,), (0,)), ((), ())), preferred_element_type=f32)


def nt(a, b):
    return lax.dot_general(a, b, (((1,), (1,)), ((), ())), preferred_element_type=f32)


def tn(a, b):
    return lax.dot_general(a, b, (((0,), (0,)), ((), ())), preferred_element_type=f32)


def nt_exact(a, b):
    return lax.dot_general(
        a, b, (((1,), (1,)), ((), ())), preferred_element_type=f32, precision=exact
    )


def lift(t):
    return jnp.where(t > 0, t + 1, jnp.exp(jnp.minimum(t, 0)))


def moments(x):
    mean = jnp.mean(x, axis=-1, keepdims=True)
    cen = x - mean
    inv = lax.rsqrt(jnp.mean(cen * cen, axis=-1, keepdims=True) + norm_eps)
    return cen * inv, inv


def fold8(x):
    return jnp.sum(x.reshape(x.shape[0] // 8, 8, x.shape[1]), axis=0)


def fold4(x):
    n = x.shape[0] // 4
    return (x[:n] + x[n : 2 * n]) + (x[2 * n : 3 * n] + x[3 * n :])


def row_valid(step, rows, width, length):
    ids = step * rows + lax.broadcasted_iota(jnp.int32, (rows, width), 0)
    return ids < length


def same_head(head):
    r = lax.broadcasted_iota(jnp.int32, (GW, GW), 0) // head
    c = lax.broadcasted_iota(jnp.int32, (GW, GW), 1) // head
    return r == c


def spread_rows(x, mask_low):
    return jnp.concatenate([x] * (GW // QB), axis=0) * mask_low


def pick_heads(x, head):
    lane = lax.broadcasted_iota(jnp.int32, (QB, GW), 1) // head
    out = x[:QB]
    for h in range(1, GW // QB):
        out = jnp.where(lane == h, x[h * QB : (h + 1) * QB], out)
    return out


def turned(hidden, n_fsdp):
    return hidden // n_fsdp >= 128


def join_blocks(ref, got, lo=0, step=None):
    n_dp, n_fsdp, r, c = got.shape
    step = c if step is None else step
    for d in range(n_dp):
        for f in range(n_fsdp):
            ref[f * r : (f + 1) * r, d * step + lo : d * step + lo + c] = got[d, f]


def cut_blocks(ref, acc):
    n_dp, n_fsdp, r, c = ref.shape
    for d in range(n_dp):
        for f in range(n_fsdp):
            ref[d, f] = acc[f * r : (f + 1) * r, d * c : (d + 1) * c].astype(ref.dtype)


def cut_turned(ref, acc):
    n_dp, n_fsdp, r, c = ref.shape
    width, hidden = acc.shape
    wide, deep = width // n_dp, hidden // n_fsdp
    for d in range(n_dp):
        for f in range(n_fsdp):
            block = acc[d * wide : (d + 1) * wide, f * deep : (f + 1) * deep]
            ref[d, f] = (block if turned(hidden, n_fsdp) else block.T).astype(ref.dtype)


def band_table(head):
    key = np.arange(KW)[:, None] - HALO
    query = np.arange(GW)[None, :] % QB
    return np.where(np.abs(key - query) <= BAND, 0.0, -1e30).astype(np.float32)


def head_table(head):
    r = np.arange(GW)[:, None] // QB
    c = np.arange(GW)[None, :] // head
    return (r == c).astype(np.float32)


MESH = pl.DeviceIdType.MESH


class Place:
    def __init__(self, n_dp, n_fsdp):
        self.m = n_fsdp // 2
        self.nh = n_dp // 2
        d = lax.axis_index("dp")
        f = lax.axis_index("fsdp")
        self.dh, self.dl = d // 2, lax.rem(d, 2)
        self.fh, self.fl = f // 2, lax.rem(f, 2)

    def dev(self, dh=None, dl=None, fh=None, fl=None):
        dh = self.dh if dh is None else dh
        dl = self.dl if dl is None else dl
        fh = self.fh if fh is None else fh
        fl = self.fl if fl is None else fl
        return {"dp": dh * 2 + dl, "fsdp": fh * 2 + fl}

    def partners(self):
        out = [self.dev(fh=lax.rem(self.fh + o, self.m)) for o in range(1, self.m)]
        out += [self.dev(dh=lax.rem(self.dh + o, self.nh)) for o in range(1, self.nh)]
        return out + [self.dev(fl=1 - self.fl), self.dev(dl=1 - self.dl)]


def greet(place):
    barrier = pltpu.get_barrier_semaphore()
    who = place.partners()
    for dev in who:
        pl.semaphore_signal(barrier, inc=1, device_id=dev, device_id_type=MESH)
    pl.semaphore_wait(barrier, len(who))


def copy_to(src, dst, send, recv, dev):
    return pltpu.make_async_remote_copy(
        src_ref=src, dst_ref=dst, send_sem=send, recv_sem=recv, device_id=dev, device_id_type=MESH
    )


class Gather:
    def __init__(self, place, shard, got, send, recv, local, order, way=None):
        self.p, self.shard, self.got, self.order, self.way = place, shard, got, order, way
        self.send, self.recv, self.local = send, recv, local

    @staticmethod
    def count(n_dp, n_fsdp):
        return n_fsdp // 2 - 1 + 1 + n_dp // 2 - 1 + 1

    def own(self):
        p = self.p
        src = self.shard if self.way is None else self.way
        return pltpu.make_async_copy(src, self.got.at[p.dh, p.dl, p.fh, p.fl], self.local)

    def fetch(self):
        return pltpu.make_async_copy(self.shard, self.way, self.local)

    def stage(self, k):
        p, g = self.p, self.got
        if k == 0:
            out = []
            for o in range(1, p.m):
                to = p.dev(fh=lax.rem(p.fh + o, p.m))
                dst = g.at[p.dh, p.dl, p.fh, p.fl]
                out.append(copy_to(self.shard, dst, self.send.at[o - 1], self.recv.at[o - 1], to))
            return out
        i = p.m - 1
        if k == 3:
            ref = g.at[:, p.dl]
            return [copy_to(ref, ref, self.send.at[i], self.recv.at[i], p.dev(dl=1 - p.dl))]
        if (k == 1) == (self.order == "x"):
            ref = g.at[p.dh, p.dl, :, p.fl] if k == 1 else g.at[:, p.dl, :, p.fl]
            return [copy_to(ref, ref, self.send.at[i + 1], self.recv.at[i + 1], p.dev(fl=1 - p.fl))]
        ref = g.at[p.dh, p.dl, :, p.fl] if k == 1 else g.at[p.dh, p.dl]
        out = []
        for o in range(1, p.nh):
            to = p.dev(dh=lax.rem(p.dh + o, p.nh))
            out.append(copy_to(ref, ref, self.send.at[i + 1 + o], self.recv.at[i + 1 + o], to))
        return out

    def start(self, k):
        for c in self.stage(k):
            c.start()

    def wait(self, k):
        if k == 0:
            self.own().wait()
        for c in self.stage(k):
            c.wait()

    def turn(self, k):
        self.wait(k)
        self.start(k + 1)


def front_kernel(
    ways,
    plan,
    qkv_steps,
    len_ref,
    tok_ref,
    wqkv,
    win,
    wback,
    wout,
    vec_in,
    bias_in,
    band_ref,
    qkv_ref,
    near_ref,
    fa_ref,
    fb_ref,
    rn_ref,
    p_ref,
    h1t_ref,
    m1_ref,
    m2_ref,
    c_ref,
    w_ref,
    vec_ref,
    bin_ref,
    g_in,
    g_back,
    g_out,
    all_s,
    st_ref,
    t_ref,
    g_qkv,
    small,
    g_small,
    way_in,
    way_back,
    way_out,
    key_s,
    qq_s,
    send,
    recv,
    local,
):
    step = pl.program_id(0)
    steps = qkv_steps
    rows, width = tok_ref.shape
    groups = width // GW
    head = width // HEADS
    scale = head ** (-0.5)
    length = len_ref[0, 0]
    n_dp, n_fsdp = ways
    cols = vec_in.shape[1]
    place = Place(n_dp, n_fsdp)
    half_in = win.shape[1] // 2
    half_back = wback.shape[0] // 2

    def piece(j, shard, got, order, way=None):
        return Gather(place, shard, got, send.at[j], recv.at[j], local.at[j], order, way)

    first = [[piece(7, small, g_small, "x")], []]
    for i, (which, cut, order) in enumerate(qkv_parts(*wqkv.shape)):
        first[which].append(piece(8 + i, wqkv.at[cut], g_qkv.at[(slice(None),) * 4 + cut], order))
    rest = []
    for i in range(2):
        cut = pl.ds(i * half_in, half_in)
        rest.append(piece(i, win.at[:, cut], g_in.at[:, :, :, :, :, cut], "x", way_in.at[:, cut]))
    for i in range(2):
        cut = pl.ds(i * half_back, half_back)
        rest.append(piece(2 + i, wback.at[cut], g_back.at[:, :, :, :, cut], "y", way_back.at[cut]))
    rest.append(piece(4, wout, g_out, "y", way_out))
    sets = [[rest[0], rest[2]], [rest[1], rest[3], rest[4]]]

    @pl.when(step == 0)
    def _():
        small[...] = jnp.zeros_like(small)
        small[:2, :cols] = vec_in[...]
        small[2:3, :cols] = bias_in[...]
        for x in first[0] + first[1]:
            x.own().start()
        for x in rest:
            x.fetch().start()
        greet(place)
        for x in first[0] + first[1]:
            x.start(0)
        for x in rest:
            x.fetch().wait()
            x.own().start()
        st_ref[...] = jnp.zeros_like(st_ref)
        t_ref[...] = jnp.zeros_like(t_ref)
        all_s[:HALO] = jnp.zeros((HALO, 3 * width), bf16)
        all_s[HALO + steps * rows :] = jnp.zeros((HALO, 3 * width), bf16)
        qq_s[...] = jnp.zeros_like(qq_s)
        key = lax.broadcasted_iota(jnp.int32, key_s.shape, 0) - HALO
        key_s[...] = jnp.where((key >= 0) & (key < length), 0.0, -1e30)
        for k in range(3):
            for group in first:
                for x in group:
                    x.turn(k)
            if k == 0:
                for x in sets[0] + sets[1]:
                    x.start(0)
        for x in first[0] + first[1]:
            x.wait(3)
        join_pairs(w_ref, g_qkv)
        lane = lax.broadcasted_iota(jnp.int32, (128, width), 0)
        col = lax.broadcasted_iota(jnp.int32, (128, width), 1)

        def place_small(f, total):
            spot = ((lane + f * cols == col) & (lane < cols)).astype(bf16)
            block = jnp.concatenate(
                [g_small[d // 2, d % 2, f // 2, lax.rem(f, 2)] for d in range(n_dp)], axis=0
            )
            return total + nn(block, spot)

        total = lax.fori_loop(0, n_fsdp, place_small, jnp.zeros((16 * n_dp, width), f32))
        for d in range(n_dp):
            vec_ref[2 * d : 2 * d + 2] = total[16 * d : 16 * d + 2]
            bin_ref[0:1, d * width : (d + 1) * width] = total[16 * d + 2 : 16 * d + 3]

    def advance(at, moves):
        @pl.when(step == at)
        def _():
            for which, k in moves:
                for x in sets[which]:
                    if k < 3:
                        x.turn(k)
                    else:
                        x.wait(k)

    for at, moves in plan.items():
        if at < 2 * steps:
            advance(at, moves)

    @pl.when(step < steps)
    def _():
        z, _ = moments(tok_ref[...].astype(f32))
        h = (z * vec_ref[0:1] + vec_ref[1:2]).astype(bf16)
        h1t_ref[...] = h.T
        lo = pl.multiple_of(HALO + step * rows, HALO)
        q = nn(h, w_ref[:, :width]).astype(bf16)
        qkv_ref[:, :width] = q
        all_s[pl.ds(lo, rows), :width] = q
        valid = row_valid(step, rows, GW, length)
        for g in range(groups):
            kc = slice(width + g * GW, width + (g + 1) * GW)
            vc = slice(2 * width + g * GW, 2 * width + (g + 1) * GW)
            k = nn(h, w_ref[:, kc]).astype(bf16)
            v = nn(h, w_ref[:, vc]).astype(bf16)
            qkv_ref[:, kc] = k
            qkv_ref[:, vc] = v
            all_s[pl.ds(lo, rows), kc] = k
            all_s[pl.ds(lo, rows), vc] = v
            phi = jnp.where(valid, lift(k), 0)
            bent = jnp.where(valid, jnp.tanh(k), 0)
            st_ref[g] += tn(v, jnp.concatenate([phi, bent], axis=1))
            t_ref[g] += fold8(phi.astype(f32))

    @pl.when(step == steps - 1)
    def _():
        mask = same_head(head).astype(f32)
        inv_len = 1.0 / length.astype(f32)
        ones = jnp.ones((8, GW), f32)
        for g in range(groups):
            tb = jnp.sum(t_ref[g], axis=0, keepdims=True) * mask
            s1 = st_ref[g][:, :GW] * mask
            s2 = st_ref[g][:, GW:] * mask
            c_row = (nt_exact(ones, s1) / nt_exact(ones, tb)).astype(bf16).astype(f32)
            c_col = jnp.broadcast_to(c_row[0:1], (GW, GW)).T
            m1_ref[g, :GW] = (s1 - c_col * tb).astype(bf16)
            m1_ref[g, GW:] = tb.astype(bf16)
            m2_ref[g] = (s2 * inv_len).astype(bf16)
            c_ref[g] = c_row

    @pl.when(step >= steps)
    def _():
        at = (step - steps) * rows
        for b in range(rows // QB):
            here = pl.ds(pl.multiple_of(at + b * QB + HALO, HALO), QB)
            window = pl.ds(pl.multiple_of(at + b * QB, QB), KW)
            out_of_item = key_s[window]
            bias = band_ref[...] + jnp.concatenate([out_of_item] * (GW // 128), axis=1)
            for g in range(groups):
                cut = slice(g * GW, (g + 1) * GW)
                kc = slice(width + g * GW, width + (g + 1) * GW)
                vc = slice(2 * width + g * GW, 2 * width + (g + 1) * GW)
                put_heads(qq_s.at[g, b], all_s[here, cut] * scale, head)
                s = nt(all_s[window, kc], qq_s[g, b]) + bias
                e = jnp.exp(s - jnp.max(s, axis=0, keepdims=True))
                p = (e * (1.0 / jnp.sum(e, axis=0, keepdims=True))).astype(bf16)
                p_ref[b, :, cut] = p
                o = tn(p, all_s[window, vc])
                near_ref[b * QB : (b + 1) * QB, cut] = pick_heads(o, head).astype(bf16)
        for g in range(groups):
            cut = slice(g * GW, (g + 1) * GW)
            q = all_s[pl.ds(pl.multiple_of(at + HALO, HALO), rows), cut]
            both = nt(lift(q), m1_ref[g])
            rn = 1.0 / both[:, GW:]
            rn_ref[:, cut] = rn.astype(bf16)
            fa_ref[:, cut] = (both[:, :GW] * rn).astype(bf16)
            fb_ref[:, cut] = nt(jnp.tanh(q), m2_ref[g]).astype(bf16)

    advance(2 * steps - 1, plan[2 * steps])


def join_pairs(ref, got):
    nh, _, m, _, r, c = got.shape
    for d in range(2 * nh):
        for f in range(2 * m):
            ref[f * r : (f + 1) * r, d * c : (d + 1) * c] = got[d // 2, d % 2, f // 2, f % 2]


def qkv_parts(r, c):
    if c % 384:
        return [(0, (pl.ds(0, r), pl.ds(0, c)), "x")]
    third = c // 3
    whole = pl.ds(0, r)
    parts = [(0, (whole, pl.ds(0, third)), "x"), (0, (whole, pl.ds(third, third)), "y")]
    rest = pl.ds(2 * third, third)
    if r % 32:
        return parts + [(1, (whole, rest), "x")]
    half = r // 2
    return parts + [(1, (pl.ds(0, half), rest), "x"), (1, (pl.ds(half, half), rest), "y")]


def front_pass(ways, length, tokens, w_qkv, w_in, w_back, w_out, vec, bias, tile, plan):
    rows, width = tokens.shape
    groups = width // GW
    n_dp, n_fsdp = ways
    nh, m = n_dp // 2, n_fsdp // 2
    steps = rows // tile
    head = width // HEADS
    const = lambda *shape: pl.BlockSpec(shape, lambda i: (0,) * len(shape))
    early = lambda i: (jnp.minimum(i, steps - 1), 0)
    late = pl.BlockSpec((tile, width), lambda i: (jnp.maximum(i - steps, 0), 0))
    hbm = pl.BlockSpec(memory_space=pl.ANY)
    sds = jax.ShapeDtypeStruct
    got = lambda r, c: (nh, 2, m, 2, r, c)
    hidden = w_in.shape[1] * n_dp
    pieces = 8 + len(qkv_parts(*w_qkv.shape))
    per = Gather.count(n_dp, n_fsdp)
    return pl.pallas_call(
        functools.partial(front_kernel, ways, plan, steps),
        grid=(2 * steps,),
        in_specs=[
            pl.BlockSpec(memory_space=pltpu.SMEM),
            pl.BlockSpec((tile, width), early),
            hbm,
            hbm,
            hbm,
            hbm,
            const(*vec.shape),
            const(*bias.shape),
            const(KW, GW),
        ],
        out_specs=[
            pl.BlockSpec((tile, 3 * width), early),
            late,
            late,
            late,
            late,
            pl.BlockSpec((tile // QB, KW, width), lambda i: (jnp.maximum(i - steps, 0), 0, 0)),
            pl.BlockSpec((width, tile), lambda i: (0, jnp.minimum(i, steps - 1))),
            const(groups, 2 * GW, GW),
            const(groups, GW, GW),
            const(groups, 8, GW),
            const(width, 3 * width),
            const(8, width),
            const(1, hidden),
            hbm,
            hbm,
            hbm,
        ],
        out_shape=[sds((rows, 3 * width), bf16)]
        + [sds((rows, width), bf16)] * 4
        + [
            sds((rows // QB, KW, width), bf16),
            sds((width, rows), bf16),
            sds((groups, 2 * GW, GW), bf16),
            sds((groups, GW, GW), bf16),
            sds((groups, 8, GW), f32),
            sds((width, 3 * width), bf16),
            sds((8, width), f32),
            sds((1, hidden), f32),
            sds(got(*w_in.shape), bf16),
            sds(got(*w_back.shape), bf16),
            sds(got(*w_out.shape), bf16),
        ],
        scratch_shapes=[
            pltpu.VMEM((rows + 2 * HALO, 3 * width), bf16),
            pltpu.VMEM((groups, GW, 2 * GW), f32),
            pltpu.VMEM((groups, 8, GW), f32),
            pltpu.VMEM(got(*w_qkv.shape), bf16),
            pltpu.VMEM((16, 128), bf16),
            pltpu.VMEM(got(16, 128), bf16),
            pltpu.VMEM(w_in.shape, bf16),
            pltpu.VMEM(w_back.shape, bf16),
            pltpu.VMEM(w_out.shape, bf16),
            pltpu.VMEM((rows + 2 * HALO, 128), f32),
            pltpu.VMEM((groups, tile // QB, GW, GW), bf16),
            pltpu.SemaphoreType.DMA((pieces, per)),
            pltpu.SemaphoreType.DMA((pieces, per)),
            pltpu.SemaphoreType.DMA((pieces,)),
        ],
        compiler_params=pltpu.CompilerParams(
            collective_id=0, has_side_effects=True, vmem_limit_bytes=VMEM_LIMIT
        ),
        cost_estimate=pl.CostEstimate(
            flops=2 * rows * width * 8 * width, bytes_accessed=rows * width * 24, transcendentals=0
        ),
        name="front_pass",
    )(
        length,
        tokens,
        w_qkv,
        w_in,
        w_back,
        w_out,
        vec,
        bias,
        jnp.asarray(band_table(head)),
    )


def ffn_kernel(
    chunk,
    len_ref,
    tok_ref,
    cot_ref,
    near_ref,
    fa_ref,
    fb_ref,
    rn_ref,
    q_ref,
    c_ref,
    vec_ref,
    bin_ref,
    gw_out,
    gw_in,
    gw_back,
    out_ref,
    datt_ref,
    dmix_ref,
    dn_ref,
    gin_ref,
    gback_ref,
    gout_ref,
    gvec_ref,
    gbias_ref,
    m3_ref,
    m4_ref,
    dt_ref,
    a_in,
    a_back,
    a_out,
    a_st,
    a_bent,
    wout_ref,
    win_ref,
    wback_ref,
    act_s,
    pre_s,
):
    step = pl.program_id(0)
    rows, width = tok_ref.shape
    hidden = win_ref.shape[1]
    groups = width // GW
    head_size = width // HEADS
    steps = pl.num_programs(0)
    length = len_ref[0, 0]
    c_row = jnp.concatenate([c_ref[g, 0:1] for g in range(groups)], axis=1)
    blend = vec_ref[...].astype(bf16)
    s0 = math.sqrt(2.0 / math.pi)
    s1 = s0 * 0.044715

    @pl.when(step == 0)
    def _():
        join_blocks(wout_ref, gw_out)
        join_blocks(win_ref, gw_in)
        join_blocks(wback_ref, gw_back)
        for ref in (a_in, a_back, a_out, a_st, a_bent, gvec_ref, gbias_ref):
            ref[...] = jnp.zeros_like(ref)

    near = near_ref[...]
    fac = fa_ref[...]
    far_b = fb_ref[...]
    mixed = (
        vec_ref[5:6] * near.astype(f32)
        + vec_ref[6:7] * (fac.astype(f32) + c_row)
        + vec_ref[7:8] * far_b.astype(f32)
    ).astype(bf16)
    resid = tok_ref[...].astype(f32) + nn(mixed, wout_ref[...])
    z2, r2 = moments(resid)
    h2 = (z2 * vec_ref[2:3] + vec_ref[3:4]).astype(bf16)
    valid = row_valid(step, rows, width, length)
    d_ffn = jnp.where(valid, cot_ref[...], 0)
    seed = d_ffn.astype(f32)
    h2_t = h2.T
    seed_t = d_ffn.T

    def add_grads(cols):
        a_back[:, cols] += nn(seed_t, act_s[:, cols])
        a_in[:, cols] += nn(h2_t, pre_s[:, cols])

    for lo in range(0, hidden, chunk):
        cols = slice(lo, lo + chunk)
        x = nn(h2, win_ref[:, cols]) + bin_ref[0:1, cols]
        if lo:
            add_grads(slice(lo - chunk, lo))
        x2 = x * x
        half = 0.5 + 0.5 * jnp.tanh(x * (s0 + s1 * x2))
        act = x * half
        slope = half + (act - act * half) * (2 * s0 + 6 * s1 * x2)
        act = act.astype(bf16)
        act_s[:, cols] = act
        d_pre = slope * nt(d_ffn, wback_ref[cols, :])
        gbias_ref[:, cols] += fold8(d_pre)
        d_pre = d_pre.astype(bf16)
        pre_s[:, cols] = d_pre
    add_grads(slice(hidden - chunk, hidden))
    dh2 = nt(pre_s[...], win_ref[...])
    both = dh2 * z2
    gvec_ref[2] += fold8(both)
    gvec_ref[3] += fold8(dh2)
    gvec_ref[4] += fold8(seed)
    dz = dh2 * vec_ref[2:3]
    mean_z = jnp.mean(both * vec_ref[2:3], axis=-1, keepdims=True)
    d_resid = seed + r2 * (dz - jnp.mean(dz, axis=-1, keepdims=True) - z2 * mean_z)
    d_attn = d_resid.astype(bf16)
    datt_ref[...] = d_attn
    ffn = nn(act_s[...], wback_ref[...])
    out_ref[...] = jnp.where(valid, resid + ffn + vec_ref[4:5], 0.0).astype(bf16)
    a_out[...] += tn(mixed, d_attn)
    d_mix = nt(d_attn, wout_ref[...]).astype(bf16)
    dmix_ref[...] = d_mix
    gvec_ref[5] += fold8(fold4(d_mix * near).astype(f32))
    gvec_ref[6] += fold8(fold4(d_mix * fac).astype(f32))
    gvec_ref[7] += fold8(fold4(d_mix * far_b).astype(f32))
    gvec_ref[0] += fold8(fold4(d_mix).astype(f32))
    d_num = blend[6:7] * d_mix * rn_ref[...]
    dn_ref[...] = d_num
    d_den = d_num * fac
    d_far = blend[7:8] * d_mix
    for g in range(groups):
        cols = slice(g * GW, (g + 1) * GW)
        q = q_ref[:, cols]
        a_st[g] += tn(lift(q), jnp.concatenate([d_num[:, cols], d_den[:, cols]], axis=1))
        a_bent[g] += tn(jnp.tanh(q), d_far[:, cols])

    @pl.when(step == steps - 1)
    def _():
        mask = same_head(head_size).astype(f32)
        inv_len = 1.0 / length.astype(f32)
        ones = jnp.ones((8, GW), f32)
        for g in range(groups):
            m3_ref[g] = (a_st[g][:, :GW] * mask).astype(bf16)
            m4_ref[g] = (a_bent[g] * mask * inv_len).astype(bf16)
            dt_ref[g] = -nt_exact(ones, a_st[g][:, GW:] * mask)
        cut_blocks(gin_ref, a_in)
        cut_turned(gback_ref, a_back)
        cut_blocks(gout_ref, a_out)
        gvec_ref[6] += gvec_ref[0] * c_row


def third_pass(
    ways, length, tokens, cot, near, fa, fb, rn, qkv, c, vecs, b_in, w_out, w_in, w_back, tile, chunk
):
    rows, width = tokens.shape
    hidden = w_in.shape[0] * w_in.shape[3]
    groups = width // GW
    steps = rows // tile
    n_dp, n_fsdp = ways
    back = (width // n_dp, hidden // n_fsdp)
    back = back if turned(hidden, n_fsdp) else back[::-1]

    def const(*shape):
        return pl.BlockSpec(shape, lambda i: (0,) * len(shape))

    def kept(*shape):
        return pl.BlockSpec(shape, lambda i: (0,) * len(shape), pipeline_mode=pl.Buffered(1))

    sds = jax.ShapeDtypeStruct
    block = pl.BlockSpec((tile, width), lambda i: (i, 0))
    deep = pltpu.VMEM((tile, hidden), bf16)
    return pl.pallas_call(
        functools.partial(ffn_kernel, chunk),
        grid=(steps,),
        in_specs=[pl.BlockSpec(memory_space=pltpu.SMEM)]
        + [block] * 7
        + [
            const(groups, 8, GW),
            const(8, width),
            const(1, hidden),
            kept(*w_out.shape),
            kept(*w_in.shape),
            kept(*w_back.shape),
        ],
        out_specs=[block] * 4
        + [
            const(n_dp, n_fsdp, width // n_fsdp, hidden // n_dp),
            const(n_dp, n_fsdp, *back),
            const(n_dp, n_fsdp, width // n_fsdp, width // n_dp),
            const(8, 8, width),
            const(8, hidden),
            const(groups, GW, GW),
            const(groups, GW, GW),
            const(groups, 8, GW),
        ],
        out_shape=[sds((rows, width), bf16)] * 4
        + [
            sds((n_dp, n_fsdp, width // n_fsdp, hidden // n_dp), bf16),
            sds((n_dp, n_fsdp, *back), bf16),
            sds((n_dp, n_fsdp, width // n_fsdp, width // n_dp), bf16),
            sds((8, 8, width), f32),
            sds((8, hidden), f32),
            sds((groups, GW, GW), bf16),
            sds((groups, GW, GW), bf16),
            sds((groups, 8, GW), f32),
        ],
        scratch_shapes=[
            pltpu.VMEM((width, hidden), f32),
            pltpu.VMEM((width, hidden), f32),
            pltpu.VMEM((width, width), f32),
            pltpu.VMEM((groups, GW, 2 * GW), f32),
            pltpu.VMEM((groups, GW, GW), f32),
            pltpu.VMEM((width, width), bf16),
            pltpu.VMEM((width, hidden), bf16),
            pltpu.VMEM((hidden, width), bf16),
            deep,
            deep,
        ],
        compiler_params=pltpu.CompilerParams(vmem_limit_bytes=VMEM_LIMIT),
        cost_estimate=pl.CostEstimate(
            flops=2 * rows * width * (6 * hidden + 4 * width),
            bytes_accessed=rows * width * 22,
            transcendentals=0,
        ),
        name="third_pass",
    )(length, tokens, cot, near, fa, fb, rn, qkv, c, vecs, b_in, w_out, w_in, w_back)


class Scatter:
    def __init__(self, place, src, out, bufs, send, recv, local, order):
        self.p, self.src, self.out, self.order = place, src, out, order
        self.acc, self.r0, self.r1, self.r2, self.r3 = bufs
        self.send, self.recv, self.local = send, recv, local

    @staticmethod
    def count(n_dp, n_fsdp):
        return n_dp // 2 + 1 + (n_dp // 2 - 1) + (n_fsdp // 2 - 1)

    @staticmethod
    def scratch(n_dp, n_fsdp, r, c, order, dtype):
        nh, m = n_dp // 2, n_fsdp // 2
        if order == "x":
            one, two = (nh, m, r, c), (nh - 1, m, r, c)
        else:
            one, two = (nh - 1, m, 2, r, c), (m, r, c)
        shapes = [(nh, m, 2, r, c), (nh, m, 2, r, c), one, two, (m - 1, r, c)]
        return [pltpu.VMEM(s, dtype) for s in shapes]

    def own(self):
        return pltpu.make_async_copy(self.src.at[:, self.p.dl], self.acc, self.local)

    def stage(self, k, only=None):
        p = self.p
        if k == 0:
            to = p.dev(dl=1 - p.dl)
            return [
                copy_to(self.src.at[dh, 1 - p.dl], self.r0.at[dh], self.send.at[dh], self.recv.at[dh], to)
                for dh in (range(p.nh) if only is None else [only])
            ]
        first = p.nh - 1
        if k == 3:
            i = first + p.nh
            out = []
            for o in range(1, p.m):
                fh = lax.rem(p.fh + o, p.m)
                out.append(
                    copy_to(self.acc.at[p.dh, fh, p.fl], self.r3.at[o - 1], self.send.at[i + o], self.recv.at[i + o],
                            p.dev(fh=fh))
                )
            return out
        if (k == 1) == (self.order == "x"):
            ref = self.acc.at[:, :, 1 - p.fl] if k == 1 else self.acc.at[p.dh, :, 1 - p.fl]
            dst = self.r1 if k == 1 else self.r2
            i = first + 1
            return [copy_to(ref, dst, self.send.at[i], self.recv.at[i], p.dev(fl=1 - p.fl))]
        out = []
        for o in range(1, p.nh):
            dh = lax.rem(p.dh + o, p.nh)
            ref = self.acc.at[dh] if k == 1 else self.acc.at[dh, :, p.fl]
            dst = self.r1.at[o - 1] if k == 1 else self.r2.at[o - 1]
            i = first + 1 + o
            out.append(copy_to(ref, dst, self.send.at[i], self.recv.at[i], p.dev(dh=dh)))
        return out

    def start(self, k):
        for c in self.stage(k):
            c.start()

    def turn(self, k):
        if k == 0:
            self.own().wait()
        for c in self.stage(k):
            c.wait()
        self.add(k)
        if k < 3:
            self.start(k + 1)

    def add(self, k):
        p, acc = self.p, self.acc
        nh, m = p.nh, p.m
        dt = acc.dtype

        def put(index, others):
            if len(others) == 1:
                acc[index] += others[0]
                return
            total = acc[index].astype(f32)
            for o in others:
                total = total + o.astype(f32)
            acc[index] = total.astype(dt)

        if k == 3:
            total = acc[p.dh, p.fh, p.fl].astype(f32)
            for o in range(1, m):
                total = total + self.r3[o - 1].astype(f32)
            self.out[...] = total
            return

        @pl.loop(0, m)
        def _(i):
            if k == 0:
                for a in range(nh):
                    for b in range(2):
                        put((a, i, b), [self.r0[a, i, b]])
            elif k == 1 and self.order == "x":
                for a in range(nh):
                    put((a, i, p.fl), [self.r1[a, i]])
            elif k == 1:
                for b in range(2):
                    put((p.dh, i, b), [self.r1[o - 1, i, b] for o in range(1, nh)])
            elif self.order == "x":
                put((p.dh, i, p.fl), [self.r2[o - 1, i] for o in range(1, nh)])
            else:
                put((p.dh, i, p.fl), [self.r2[i]])


def back_kernel(
    ways,
    plan,
    late_plan,
    len_ref,
    q_ref,
    k_lo,
    k_ref,
    k_hi,
    v_lo,
    v_ref,
    v_hi,
    p_ref,
    dmix_ref,
    dn_ref,
    fa_ref,
    tok_ref,
    datt_ref,
    h1t_hbm,
    m1_ref,
    m2_ref,
    m3_ref,
    m4_ref,
    dt_ref,
    c_ref,
    vec_ref,
    w_hbm,
    gv_ref,
    gbias_ref,
    s_in,
    s_back,
    s_out,
    dtok_ref,
    oqkv_ref,
    oin_ref,
    oback_ref,
    oout_ref,
    ovec_ref,
    obias_ref,
    h1t_ref,
    w_ref,
    kk,
    vv,
    far_s,
    dp_s,
    ds_s,
    dd_s,
    qq_s,
    all_d,
    carry,
    gvec_s,
    gq_ref,
    gs_ref,
    rows_s,
    back_t,
    small_o,
    late_src,
    late_got,
    *rest,
):
    step = pl.program_id(0)
    rows, width = q_ref.shape
    total = h1t_ref.shape[1]
    steps = total // rows
    groups = width // GW
    head = width // HEADS
    scale = head ** (-0.5)
    length = len_ref[0, 0]
    n_dp, n_fsdp = ways
    place = Place(n_dp, n_fsdp)
    cols = ovec_ref.shape[1]
    c_all = oqkv_ref.shape[1]
    send, recv, local, late_send, late_recv, fetch = rest[-6:]
    fetches = [
        pltpu.make_async_copy(h1t_hbm, h1t_ref, fetch.at[0]),
        pltpu.make_async_copy(w_hbm, w_ref, fetch.at[1]),
    ]
    final = steps + 1 + place.nh
    last_rows = tok_ref.shape[0]

    used = [0]

    def piece(src, out, order):
        j = used[0]
        used[0] += 1
        return Scatter(place, src, out, rest[5 * j : 5 * j + 5], send.at[j], recv.at[j], local.at[j], order)

    sets = [[], [], [], []]
    every = (slice(None),) * 4
    for i, (cut_in, cut_back) in enumerate(ffn_parts(s_in.shape[-2:], s_back.shape[-2:])):
        sets[i].append(piece(s_in.at[every + cut_in], oin_ref.at[cut_in], "x"))
        sets[i].append(piece(s_back.at[every + cut_back], back_t.at[cut_back], "y"))
    sets[1].append(piece(s_out, oout_ref, "y"))
    sets[1].append(piece(gs_ref, small_o, "x"))
    for which, cut, order in qkv_parts(*oqkv_ref.shape):
        sets[2 + which].append(piece(gq_ref.at[every + cut], oqkv_ref.at[cut], order))

    @pl.when(step == 0)
    def _():
        for x in sets[0] + sets[1][:-1]:
            x.own().start()
        greet_all(place)
        for x in sets[0] + sets[1][:-1]:
            x.start(0)
        for x in fetches:
            x.start()
        carry[...] = jnp.zeros_like(carry)
        dd_s[...] = jnp.zeros_like(dd_s)
        qq_s[...] = jnp.zeros_like(qq_s)
        gvec_s[...] = jnp.zeros_like(gvec_s)
        gs_ref[...] = jnp.zeros_like(gs_ref)
        late_src[...] = jnp.zeros_like(late_src)
        rows_s[0:2] = jnp.zeros((2, width), f32)
        rows_s[2:8] = jnp.sum(gv_ref[2:8], axis=1)
        bias = jnp.sum(gbias_ref[...], axis=0, keepdims=True)
        for d in range(n_dp):
            pair = rows_s[2 * d : 2 * d + 2]
            for f in range(n_fsdp):
                spot = slice(f * cols, (f + 1) * cols)
                at = d * width + f * cols
                gs_ref[d // 2, d % 2, f // 2, f % 2, 0:2, :cols] = pair[:, spot]
                gs_ref[d // 2, d % 2, f // 2, f % 2, 2:3, :cols] = bias[:, at : at + cols]
        sets[1][-1].own().start()
        sets[1][-1].start(0)

    for at, moves in plan.items():

        @pl.when(step == at)
        def _(moves=moves):
            for which, k in moves:
                for x in sets[which]:
                    x.turn(k)

    def far_keys(at, slot, live):
        valid = row_valid(at, rows, GW, length) & live
        here = pl.ds(pl.multiple_of(at * rows + HALO, HALO), rows)
        for g in range(groups):
            cut = slice(g * GW, (g + 1) * GW)
            kc = slice(width + g * GW, width + (g + 1) * GW)
            vc = slice(2 * width + g * GW, 2 * width + (g + 1) * GW)
            k = kk[slot, HALO : HALO + rows, cut]
            v = vv[slot, HALO : HALO + rows, cut]
            lift_k = lift(k)
            bent_k = jnp.tanh(k)
            v_cen = v - c_ref[g, 0:1].astype(bf16)
            dk = (nt(v_cen, m3_ref[g]) + dt_ref[g, 0:1]) * jnp.minimum(lift_k, 1).astype(f32)
            dk += nt(v, m4_ref[g]) * (1 - bent_k * bent_k).astype(f32)
            both = jnp.concatenate([lift_k, bent_k], axis=1)
            dv = nn(both, jnp.concatenate([m3_ref[g], m4_ref[g]], axis=0))
            all_d[here, kc] += jnp.where(valid, dk.astype(bf16), 0)
            all_d[here, vc] += jnp.where(valid, dv.astype(bf16), 0)

    @pl.when(step < steps)
    def _():
        slot = lax.rem(step, 2)
        kk[slot, :HALO] = k_lo[...]
        kk[slot, HALO : HALO + rows] = k_ref[...]
        kk[slot, HALO + rows :] = k_hi[...]
        vv[slot, :HALO] = v_lo[...]
        vv[slot, HALO : HALO + rows] = v_ref[...]
        vv[slot, HALO + rows :] = v_hi[...]
        blend = vec_ref[...].astype(bf16)
        base = step * rows
        for g in range(groups):
            cut = slice(g * GW, (g + 1) * GW)
            kc = slice(width + g * GW, width + (g + 1) * GW)
            vc = slice(2 * width + g * GW, 2 * width + (g + 1) * GW)
            q = q_ref[:, cut]
            d_num = dn_ref[:, cut]
            d_den = -d_num * fa_ref[:, cut]
            d_mix = dmix_ref[:, cut]
            bent = jnp.tanh(q)
            far = nn(jnp.concatenate([d_num, d_den], axis=1), m1_ref[g]) * jnp.minimum(lift(q), 1).astype(f32)
            far_s[:, cut] = far + nn(blend[7:8, cut] * d_mix, m2_ref[g]) * (1 - bent * bent).astype(f32)
            for b in range(rows // QB):
                here = slice(b * QB, (b + 1) * QB)
                window = slice(b * QB, b * QB + KW)
                put_heads(dd_s.at[g, b], blend[5:6, cut] * dmix_ref[here, cut], head)
                dp_s[g, b] = nt(vv[slot, window, cut], dd_s[g, b]).astype(bf16)
            for b in range(rows // QB):
                p = p_ref[b, :, cut]
                dp = dp_s[g, b]
                dot = jnp.sum(fold4(p * dp).astype(f32), axis=0, keepdims=True)
                ds_s[g, b] = p * (dp - dot.astype(bf16))
            old_k = carry[0, :, cut]
            old_v = carry[1, :, cut]
            for b in range(rows // QB):
                here = slice(b * QB, (b + 1) * QB)
                window = slice(b * QB, b * QB + KW)
                d_s = ds_s[g, b]
                put_heads(qq_s.at[g, b], q_ref[here, cut] * scale, head)
                dk = nn(d_s, qq_s[g, b])
                dv = nn(p_ref[b, :, cut], dd_s[g, b])
                dq = pick_heads(tn(d_s, kk[slot, window, cut]), head) * scale + far_s[here, cut]
                lo = pl.ds(pl.multiple_of(base + b * QB, QB), QB)
                all_d[pl.ds(pl.multiple_of(base + b * QB + HALO, HALO), QB), cut] = dq.astype(bf16)
                all_d[lo, kc] = (old_k + dk[:QB]).astype(bf16)
                all_d[lo, vc] = (old_v + dv[:QB]).astype(bf16)
                old_k = dk[QB:]
                old_v = dv[QB:]
            carry[0, :, cut] = old_k
            carry[1, :, cut] = old_v
        far_keys(jnp.maximum(step - 1, 0), 1 - slot, step > 0)

    @pl.when(step == steps)
    def _():
        all_d[total:, width : 2 * width] = carry[0].astype(bf16)
        all_d[total:, 2 * width :] = carry[1].astype(bf16)
        far_keys(steps - 1, (steps - 1) % 2, True)

    for dh in range(n_dp // 2):

        @pl.when(step == steps + 1 + dh)
        def _(dh=dh):
            if dh == 0:
                fetches[0].wait()
            grad = nn(h1t_ref[...], all_d[HALO : HALO + total, dh * 2 * c_all : (dh + 1) * 2 * c_all])
            r = gq_ref.shape[-2]
            for dl in range(2):
                for f in range(n_fsdp):
                    block = grad[f * r : (f + 1) * r, dl * c_all : (dl + 1) * c_all]
                    gq_ref[dh, dl, f // 2, f % 2] = block.astype(bf16)
            for x in sets[2] + sets[3]:
                x.stage(0, dh)[0].start()

    @pl.when(step == final)
    def _():
        fetches[1].wait()
        for x in sets[2] + sets[3]:
            x.own().start()

    for at, moves in late_plan.items():
        if at == "end":
            continue

        @pl.when(step == final + at)
        def _(moves=moves):
            for which, k in moves:
                for x in sets[which]:
                    x.turn(k)

    @pl.when(step >= final)
    def _():
        here = pl.ds(pl.multiple_of((step - final) * last_rows + HALO, HALO), last_rows)
        z1, r1 = moments(tok_ref[...].astype(f32))
        dh1 = nt(all_d[here], w_ref[...])
        gvec_s[0] += fold8(dh1 * z1)
        gvec_s[1] += fold8(dh1)
        dz = dh1 * vec_ref[0:1]
        dtok_ref[...] = (
            datt_ref[...].astype(f32)
            + r1
            * (
                dz
                - jnp.mean(dz, axis=-1, keepdims=True)
                - z1 * jnp.mean(dz * z1, axis=-1, keepdims=True)
            )
        ).astype(bf16)

    @pl.when(step == final + total // last_rows - 1)
    def _():
        rows_s[0:2] = jnp.sum(gvec_s[...], axis=1)
        for f in range(n_fsdp):
            late_src[f, 0:2, :cols] = rows_s[0:2, f * cols : (f + 1) * cols]
        d, f = lax.axis_index("dp"), lax.axis_index("fsdp")
        me = d * n_fsdp + f

        def late(o):
            to = lax.rem(f + o, n_fsdp)
            return copy_to(
                late_src.at[to], late_got.at[me], late_send.at[o], late_recv.at[me], {"dp": 0, "fsdp": to}
            )

        @pl.when(d > 0)
        def _():
            late(0).start()

        for o in range(1, n_fsdp):
            late(o).start()
        oback_ref[...] = back_t[...].T if turned(gbias_ref.shape[1], n_fsdp) else back_t[...]
        for which, k in late_plan["end"]:
            for x in sets[which]:
                x.turn(k)

        @pl.when(d > 0)
        def _():
            late(0).wait_send()
            ovec_ref[...] = small_o[0:2, :cols]

        for o in range(1, n_fsdp):
            late(o).wait_send()

        @pl.when(d == 0)
        def _():
            late_got[me] = late_src[f]

            @pl.loop(0, n_dp * n_fsdp)
            def _(s):
                @pl.when(s != me)
                def _():
                    copy_to(
                        late_src.at[0], late_got.at[s], late_send.at[0], late_recv.at[s], {"dp": 0, "fsdp": 0}
                    ).wait_recv()

            ovec_ref[...] = jnp.sum(late_got[...], axis=0)[0:2, :cols]

        obias_ref[...] = small_o[2:3, :cols]


def put_heads(ref, x, head):
    for h in range(GW // head):
        lanes = slice(h * head, (h + 1) * head)
        ref[h * QB : (h + 1) * QB, lanes] = x[:, lanes]


def ffn_parts(shape_in, shape_back):
    (r, c), (rb, cb) = shape_in, shape_back
    out = []
    for i in range(2):
        cut_in = (pl.ds(0, r), pl.ds(i * c // 2, c // 2))
        if cb % 256:
            cut_back = (pl.ds(i * rb // 2, rb // 2), pl.ds(0, cb))
        else:
            cut_back = (pl.ds(0, rb), pl.ds(i * cb // 2, cb // 2))
        out.append((cut_in, cut_back))
    return out


def greet_all(place):
    d, f = lax.axis_index("dp"), lax.axis_index("fsdp")
    n_dp, n_fsdp = 2 * place.nh, 2 * place.m
    barrier = pltpu.get_barrier_semaphore()
    who = place.partners()
    for dev in who:
        pl.semaphore_signal(barrier, inc=1, device_id=dev, device_id_type=MESH)

    @pl.when(d == 0)
    def _():
        @pl.loop(0, n_dp)
        def _(i):
            @pl.loop(0, n_fsdp)
            def _(j):
                @pl.when((i != 0) | (j != f))
                def _():
                    pl.semaphore_signal(barrier, inc=1, device_id={"dp": i, "fsdp": j}, device_id_type=MESH)

    pl.semaphore_wait(barrier, len(who) + n_fsdp - (d == 0).astype(jnp.int32))


def back_pass(
    ways,
    length,
    qkv,
    p,
    d_mix,
    tokens,
    d_attn,
    d_num,
    fa,
    h1t,
    m1,
    m2,
    m3,
    m4,
    dt,
    c,
    vecs,
    w_qkv,
    gv,
    gbias,
    s_in,
    s_back,
    s_out,
    tile,
    last_tile,
    plan,
    late_plan,
):
    rows, width = tokens.shape
    groups = width // GW
    steps = rows // tile
    n_dp, n_fsdp = ways
    nh, m = n_dp // 2, n_fsdp // 2
    r, c_all = width // n_fsdp, 3 * width // n_dp
    per = Scatter.count(n_dp, n_fsdp)
    final = steps + 1 + nh
    hbm = pl.BlockSpec(memory_space=pl.ANY)
    back_shape = s_back.shape[-2:]
    outs = [
        (r, c_all),
        s_in.shape[-2:],
        back_shape[::-1] if turned(gbias.shape[1], n_fsdp) else back_shape,
        s_out.shape[-2:],
        (2, width // n_fsdp),
        (1, gbias.shape[1] // (n_dp * n_fsdp)),
    ]
    kinds = []
    for cut_in, cut_back in ffn_parts(s_in.shape[-2:], back_shape):
        kinds.append((*(x.size for x in cut_in), "x", bf16))
        kinds.append((*(x.size for x in cut_back), "y", bf16))
    kinds.append((*s_out.shape[-2:], "y", bf16))
    kinds.append((8, 128, "x", f32))
    for _, cut, order in qkv_parts(r, c_all):
        kinds.append((*(x.size for x in cut), order, bf16))
    bufs = [b for k in kinds for b in Scatter.scratch(n_dp, n_fsdp, *k)]
    got = lambda *s: (nh, 2, m, 2, *s)

    def const(*shape):
        return pl.BlockSpec(shape, lambda i: (0,) * len(shape))

    def kept(*shape):
        return pl.BlockSpec(shape, lambda i: (0,) * len(shape), pipeline_mode=pl.Buffered(1))

    one = lambda i: jnp.minimum(i, steps - 1)
    end = lambda i: jnp.maximum(i - final, 0)
    per_tile = tile // HALO
    top = rows // HALO - 1

    def halo(col):
        return [
            pl.BlockSpec((HALO, width), lambda i: (jnp.maximum(one(i) * per_tile - 1, 0), col)),
            pl.BlockSpec((tile, width), lambda i: (one(i), col)),
            pl.BlockSpec((HALO, width), lambda i: (jnp.minimum((one(i) + 1) * per_tile, top), col)),
        ]

    block = pl.BlockSpec((tile, width), lambda i: (one(i), 0))
    late = pl.BlockSpec((last_tile, width), lambda i: (end(i), 0))
    head = width // HEADS
    sds = jax.ShapeDtypeStruct
    return pl.pallas_call(
        functools.partial(back_kernel, ways, plan, late_plan),
        grid=(final + rows // last_tile,),
        in_specs=[
            pl.BlockSpec(memory_space=pltpu.SMEM),
            block,
            *halo(1),
            *halo(2),
            pl.BlockSpec((tile // QB, KW, width), lambda i: (one(i), 0, 0)),
            block,
            block,
            block,
            late,
            late,
            hbm,
            kept(groups, 2 * GW, GW),
            kept(groups, GW, GW),
            kept(groups, GW, GW),
            kept(groups, GW, GW),
            const(groups, 8, GW),
            const(groups, 8, GW),
            const(8, width),
            hbm,
            const(*gv.shape),
            const(*gbias.shape),
            hbm,
            hbm,
            hbm,
        ],
        out_specs=[late] + [const(*s) for s in outs],
        out_shape=[sds((rows, width), bf16)] + [sds(s, f32) for s in outs],
        scratch_shapes=[
            pltpu.VMEM((width, rows), bf16),
            pltpu.VMEM((width, 3 * width), bf16),
            pltpu.VMEM((2, tile + 2 * HALO, width), bf16),
            pltpu.VMEM((2, tile + 2 * HALO, width), bf16),
            pltpu.VMEM((tile, width), f32),
            pltpu.VMEM((groups, tile // QB, KW, GW), bf16),
            pltpu.VMEM((groups, tile // QB, KW, GW), bf16),
            pltpu.VMEM((groups, tile // QB, GW, GW), bf16),
            pltpu.VMEM((groups, tile // QB, GW, GW), bf16),
            pltpu.VMEM((rows + 2 * HALO, 3 * width), bf16),
            pltpu.VMEM((2, QB, width), f32),
            pltpu.VMEM((2, 8, width), f32),
            pltpu.VMEM(got(r, c_all), bf16),
            pltpu.VMEM(got(8, 128), f32),
            pltpu.VMEM((8, width), f32),
            pltpu.VMEM(back_shape, f32),
            pltpu.VMEM((8, 128), f32),
            pltpu.VMEM((n_fsdp, 8, 128), f32),
            pltpu.VMEM((n_dp * n_fsdp, 8, 128), f32),
            *bufs,
            pltpu.SemaphoreType.DMA((len(kinds), per)),
            pltpu.SemaphoreType.DMA((len(kinds), per)),
            pltpu.SemaphoreType.DMA((len(kinds),)),
            pltpu.SemaphoreType.DMA((n_fsdp,)),
            pltpu.SemaphoreType.DMA((n_dp * n_fsdp,)),
            pltpu.SemaphoreType.DMA((2,)),
        ],
        compiler_params=pltpu.CompilerParams(
            collective_id=1, has_side_effects=True, vmem_limit_bytes=VMEM_LIMIT
        ),
        cost_estimate=pl.CostEstimate(
            flops=2 * rows * width * 14 * width, bytes_accessed=rows * width * 24, transcendentals=0
        ),
        name="back_pass",
    )(
        length,
        qkv,
        qkv,
        qkv,
        qkv,
        qkv,
        qkv,
        qkv,
        p,
        d_mix,
        d_num,
        fa,
        tokens,
        d_attn,
        h1t,
        m1,
        m2,
        m3,
        m4,
        dt,
        c,
        vecs,
        w_qkv,
        gv,
        gbias,
        s_in,
        s_back,
        s_out,
    )


def hand_kernel(n, *refs):
    for j in range(n):
        refs[n + j][...] = refs[j][...]


def hand_over(arrays, parts):
    first = arrays[0]
    block = pl.BlockSpec((first.shape[0] // parts, first.shape[1]), lambda i: (i, 0))
    specs = [block] + [pl.BlockSpec(a.shape, lambda i: (0, 0)) for a in arrays[1:]]
    return pl.pallas_call(
        functools.partial(hand_kernel, len(arrays)),
        grid=(parts,),
        in_specs=specs,
        out_specs=specs,
        out_shape=[jax.ShapeDtypeStruct(a.shape, a.dtype) for a in arrays],
        name="hand_over",
    )(*arrays)


FRONT_TILE = 1024
TILE = 512
LAST_TILE = 512
CHUNK = 256
FRONT_PLAN = {1: [(0, 0)], 2: [(1, 0)], 3: [(0, 1)], 4: [(1, 1)], 5: [(0, 2)], 7: [(1, 2)], 8: [(0, 3), (1, 3)]}
BACK_PLAN = {2: [(0, 0)], 3: [(1, 0)], 4: [(0, 1)], 6: [(1, 1), (0, 2)], 7: [(1, 2)], 8: [(0, 3)], 14: [(1, 3)]}
LATE_PLAN = {1: [(2, 0), (3, 0)], 3: [(2, 1)], 4: [(3, 1)], 5: [(2, 2)], 6: [(3, 2)], "end": [(2, 3), (3, 3)]}


def shards(
    tokens, cotangent, w_qkv, w_out, w_in, w_back, vec_params, b_in, item_lengths, bucket_counts, *, ways
):
    n_dp, n_fsdp = ways
    (
        qkv,
        near,
        fa,
        fb,
        rn,
        p,
        h1t,
        m1,
        m2,
        c,
        qkv_w,
        vecs,
        in_bias,
        g_in,
        g_back,
        g_out,
    ) = front_pass(
        ways, item_lengths, tokens, w_qkv, w_in, w_back, w_out, vec_params, b_in[None], FRONT_TILE, FRONT_PLAN
    )

    def blocks(g):
        return g.reshape(n_dp, n_fsdp, *g.shape[-2:])

    def pairs(g):
        return g.reshape(n_dp // 2, 2, n_fsdp // 2, 2, *g.shape[-2:])

    (out, d_attn, d_mix, d_num, s_in, s_back, s_out, g_vec, g_bias, m3, m4, dt) = third_pass(
        ways,
        item_lengths,
        tokens,
        cotangent,
        near,
        fa,
        fb,
        rn,
        qkv,
        c,
        vecs,
        in_bias,
        blocks(g_out),
        blocks(g_in),
        blocks(g_back),
        TILE,
        CHUNK,
    )
    d_tok, r_qkv, r_in, r_back, r_out, r_vec, r_bias = back_pass(
        ways,
        item_lengths,
        qkv,
        p,
        d_mix,
        tokens,
        d_attn,
        d_num,
        fa,
        h1t,
        m1,
        m2,
        m3,
        m4,
        dt,
        c,
        vecs,
        qkv_w,
        g_vec,
        g_bias,
        pairs(s_in),
        pairs(s_back),
        pairs(s_out),
        TILE,
        LAST_TILE,
        BACK_PLAN,
        LATE_PLAN,
    )
    d_tok, r_qkv, r_out, r_in, r_back, r_vec, r_bias = hand_over(
        [d_tok, r_qkv, r_out, r_in, r_back, r_vec, r_bias], 2
    )
    return (out, d_tok, r_qkv, r_out, r_in, r_back, r_vec, r_bias[0])


def solution(mesh):
    in_specs = (
        P(("dp", "fsdp"), None),
        P(("dp", "fsdp"), None),
        P("fsdp", "dp"),
        P("fsdp", "dp"),
        P("fsdp", "dp"),
        P("fsdp", "dp"),
        P("dp", "fsdp"),
        P(("dp", "fsdp")),
        P(("dp", "fsdp"), None),
        P(("dp", "fsdp"), None),
    )
    out_specs = (
        P(("dp", "fsdp"), None),
        P(("dp", "fsdp"), None),
        P("fsdp", "dp"),
        P("fsdp", "dp"),
        P("fsdp", "dp"),
        P("fsdp", "dp"),
        P("dp", "fsdp"),
        P(("dp", "fsdp")),
    )
    ways = (mesh.shape["dp"], mesh.shape["fsdp"])
    body = functools.partial(shards, ways=ways)
    return jax.shard_map(body, mesh=mesh, in_specs=in_specs, out_specs=out_specs, check_vma=False)
```
